32 devices in a mesh: ctx: 16 (over z, y, x), tp: 2 (over core).
Axes of the slice: x: 2, y: 2, z: 4, core: 2. Of those that a mesh axis runs over, the one named last changes fastest.
Arguments:
- tokens: bfloat16 [2048, 2048], P('ctx'), may hold values from -6 to 6
- w_proj: bfloat16 [2048, 4, 2048], P('ctx', None, 'tp'), may hold values from -3 to 3
- w_out: bfloat16 [2048, 2048], P('tp', 'ctx'), may hold values from -0.125 to 0.125
- positions: int32 [2048], P('ctx'), may hold values from 0 to 2047, as said below
- neg_emb: bfloat16 [1024, 2048], P('ctx', 'tp'), may hold values from -7 to 7
- neg_ids: int32 [1024], replicated, may hold values from 0 to 65535, as said below
- target_emb: bfloat16 [2048, 2048], P('ctx', 'tp'), may hold values from -6 to 6
- target_ids: int32 [2048], P(('ctx', 'tp')), may hold values from 0 to 65535, as said below
Outputs:
- hidden: bfloat16 [2048, 2048], P('ctx', 'tp')
- loss: float32 [2048], P(('ctx', 'tp'))
The draws below stay inside these ranges and needn't reach their ends.
Inputs may be any that keep to these rules, and one draw needn't show every extreme that they name: positions never fall and rise by at most two from one event to the next; at the first event of every aligned block of 128 events and at the last event the position equals the event's index. `neg_ids`: item ids; some items are far more common than others. `target_ids`: item ids, drawn by the same popularity as the negatives.
All inputs are finite; a program needn't handle non-finite values.
Results may differ from the reference program's by a relative error of at most 0.0045.
Values may be sent and summed in bfloat16 or wider, within the bound.
No kernel may reach another device: no remote copies, remote signals or barrier semaphores. Data moves between devices by JAX's collectives and lax.ppermute only.
A program may use at most 64 MiB of HBM per device.

```python
import jax
import jax.numpy as jnp
from jax import lax

D = 2048
HEADS = 16
HEAD_DIM = 128
TOK_DEV = 128
NEG = 1024
VOCAB = 65536
TOKENS = 2048
N_CTX = 16


def popular_ids(order, key, count):
    key_exp, key_rank = jax.random.split(key)
    expo = jax.random.randint(key_exp, (count,), 0, 17)
    limit = jnp.left_shift(jnp.ones((count,), jnp.int32), expo)
    ranks = jax.random.randint(key_rank, (count,), 0, limit)
    ids = order[ranks].astype(jnp.int32)
    return ids.at[0].set(0).at[count - 1].set(VOCAB - 1)


def shared_basis(key, rank):
    key = jax.random.fold_in(key, 101)
    key_load, key_basis = jax.random.split(key)
    loadings = jax.random.normal(key_load, (TOKENS, rank), jnp.float32)
    basis = jax.random.normal(key_basis, (rank, D), jnp.float32)
    return (loadings, basis)


def column_offset(key):
    key = jax.random.fold_in(key, 103)
    return jax.random.uniform(key, (D,), jnp.float32, -1.5, 1.5)


def combine(loadings, basis, rank):
    summed = loadings[:, 0:1] * basis[0][None, :]
    for member in range(1, rank):
        summed = summed + loadings[:, member:member + 1] * basis[member][None, :]
    return summed * rank ** (-0.5)


def draw_neg_ids(key, part):
    order = jax.random.permutation(key, VOCAB)
    key = jax.random.fold_in(key, 11)
    return popular_ids(order, key, NEG)


def draw_target_ids(key, part):
    order = jax.random.permutation(key, VOCAB)
    key = jax.random.fold_in(key, 12)
    return popular_ids(order, key, TOKENS)


def draw_positions(key, part):
    key = jax.random.fold_in(key, 13)
    steps = jax.random.randint(key, (TOKENS,), 0, 2)
    index = jnp.arange(TOKENS, dtype=jnp.int32)
    steps = jnp.where(index % TOK_DEV == 0, 0, steps)
    steps = jnp.where(index == TOKENS - 1, 0, steps)
    return (index - steps).astype(jnp.int32)


def draw_w_proj(key, part):
    offset = column_offset(key)
    key = jax.random.fold_in(key, 17)
    key_noise, key_bias = jax.random.split(key)
    width = HEADS * HEAD_DIM
    noise = jnp.clip(jax.random.normal(key_noise, (D, 4, width), jnp.float32), -4.0, 4.0)
    scales = jnp.array([1.0, 2.5, 4.0, 4.0], jnp.float32)
    lows = jnp.array([0.0, 4.5, 5.0, 5.0], jnp.float32)
    spans = jnp.array([0.0, 2.0, 6.0, 6.0], jnp.float32)
    unit = jax.random.uniform(key_bias, (4, width), jnp.float32)
    bias = lows[:, None] + spans[:, None] * unit
    values = noise * (scales[None, :, None] * D ** (-0.5))
    values = values - bias[None, :, :] * offset[:, None, None] / (0.75 * D)
    return values.astype(jnp.bfloat16)


def draw_tokens(key, part):
    rank = 6
    loadings, basis = shared_basis(key, rank)
    offset = column_offset(key)
    key = jax.random.fold_in(key, 15)
    common = combine(loadings, basis, rank)
    noise = 0.7 * jax.random.normal(key, (TOKENS, D), jnp.float32)
    return jnp.clip(common + noise + offset[None, :], -6.0, 6.0).astype(jnp.bfloat16)


def draw_target_emb(key, part):
    rank = 6
    loadings, basis = shared_basis(key, rank)
    key = jax.random.fold_in(key, 16)
    key_load, key_noise = jax.random.split(key)
    fresh = jax.random.normal(key_load, (TOKENS, rank), jnp.float32)
    common = combine(0.7 * loadings + 0.7 * fresh, basis, rank)
    noise = 0.7 * jax.random.normal(key_noise, (TOKENS, D), jnp.float32)
    return jnp.clip(common + noise, -6.0, 6.0).astype(jnp.bfloat16)


def draw_neg_emb(key, part):
    rank = 6
    loadings, basis = shared_basis(key, rank)
    key = jax.random.fold_in(key, 14)
    key_load, key_noise = jax.random.split(key)
    neg_load = jax.random.normal(key_load, (NEG, rank), jnp.float32)
    common = combine(neg_load, basis, rank)
    column = jnp.arange(D, dtype=jnp.float32) / (D - 1.0)
    ratio = 3.0
    noise = 0.7 * jax.random.normal(key_noise, (NEG, D), jnp.float32)
    values = jnp.clip(common + noise, -4.0, 4.0)
    scale = jnp.exp(jnp.log(ratio) * (column - 0.5))
    return (values * scale[None, :]).astype(jnp.bfloat16)


def levels(key, extent, pieces, low, high):
    level = 1.0
    for axis_at, blocks in pieces:
        draws = jax.random.uniform(jax.random.fold_in(jax.random.fold_in(key, 6), axis_at), (blocks,), jnp.float32, low / len(pieces), high / len(pieces))
        level = level * jnp.repeat(jnp.exp(draws), extent[axis_at] // blocks).reshape((-1,) + (1,) * (len(extent) - 1 - axis_at))
    return level


def bell_draw(key, extent, spread, reach, pieces=(), kind=jnp.bfloat16):
    values = jax.random.normal(key, extent, jnp.float32) * spread
    if len(pieces) > 0:
        values = levels(key, extent, pieces, -0.22, 0.18) * values
    return jnp.clip(values, min=-reach, max=reach).astype(kind)


def setup_inputs(seed: int = 0) -> dict:
    key_of = jax.random.split(jax.random.key(seed), 9)
    return {
        "tokens": draw_tokens(jax.random.fold_in(key_of[8], 71), 0),
        "w_proj": draw_w_proj(jax.random.fold_in(key_of[8], 71), 0),
        "w_out": bell_draw(key_of[2], (HEADS * HEAD_DIM, D), (HEADS * HEAD_DIM) ** -0.5, 0.125, ((0, 2), (1, 16))),
        "positions": draw_positions(jax.random.fold_in(key_of[8], 71), 0),
        "neg_emb": draw_neg_emb(jax.random.fold_in(key_of[8], 71), 0),
        "neg_ids": draw_neg_ids(jax.random.fold_in(key_of[8], 71), 0),
        "target_emb": draw_target_emb(jax.random.fold_in(key_of[8], 71), 0),
        "target_ids": draw_target_ids(jax.random.fold_in(key_of[8], 71), 0),
    }


def reference(tokens, w_proj, w_out, positions, neg_emb, neg_ids, target_emb, target_ids):
    proj = jax.nn.silu(jnp.einsum('td,dfh->tfh', tokens.astype(jnp.float32), w_proj.astype(jnp.float32))).astype(jnp.bfloat16)
    gate = proj[:, 0].reshape(TOKENS, HEADS, HEAD_DIM)
    value = proj[:, 1].reshape(TOKENS, HEADS, HEAD_DIM)
    query = proj[:, 2].reshape(TOKENS, HEADS, HEAD_DIM)
    key_all = proj[:, 3].reshape(TOKENS, HEADS, HEAD_DIM)
    score_scale = HEAD_DIM ** (-0.5)
    key_f = key_all.astype(jnp.float32)
    value_f = value.astype(jnp.float32)

    def one_block(block):
        q_block, p_block = block
        scores = jnp.einsum('thd,khd->htk', q_block.astype(jnp.float32), key_f) * score_scale
        visible = positions[None, None, :] <= p_block[None, :, None]
        weight = jnp.where(visible, jax.nn.silu(scores), 0.0).astype(jnp.bfloat16)
        return jnp.einsum('htk,khd->thd', weight.astype(jnp.float32), value_f)
    attn = lax.map(one_block, (query.reshape(N_CTX, TOK_DEV, HEADS, HEAD_DIM), positions.reshape(N_CTX, TOK_DEV)))
    attn = attn.reshape(TOKENS, HEADS, HEAD_DIM)
    normed = attn * lax.rsqrt(lax.optimization_barrier(jnp.mean(attn * attn, axis=-1, keepdims=True)) + 1e-06)
    gated = (normed * gate.astype(jnp.float32)).astype(jnp.bfloat16).reshape(TOKENS, HEADS * HEAD_DIM)
    hidden = (tokens.astype(jnp.float32) + jnp.dot(gated, w_out, preferred_element_type=jnp.float32)).astype(jnp.bfloat16)
    hidden_f = hidden.astype(jnp.float32)
    target_f = target_emb.astype(jnp.float32)
    dots = jnp.dot(hidden, neg_emb.T, preferred_element_type=jnp.float32)
    hh = lax.optimization_barrier(jnp.sum(hidden_f * hidden_f, axis=1))
    he = lax.optimization_barrier(jnp.sum(hidden_f * target_f, axis=1))
    ee = lax.optimization_barrier(jnp.sum(target_f * target_f, axis=1))
    nn_sq = lax.optimization_barrier(jnp.sum(jnp.square(neg_emb.astype(jnp.float32)), axis=1))
    pos_logit = he / jnp.sqrt(hh + 1e-06) / jnp.sqrt(ee + 1e-06) / 0.05
    neg_logit = dots / jnp.sqrt(hh + 1e-06)[:, None] / jnp.sqrt(nn_sq + 1e-06)[None, :] / 0.05
    keep = neg_ids[None, :] != target_ids[:, None]
    total = jnp.exp(pos_logit) + lax.optimization_barrier(jnp.sum(jnp.where(keep, jnp.exp(neg_logit), 0.0), axis=1))
    loss = jnp.log(total) - pos_logit
    return (hidden, loss)
```

```python
import jax
import jax.numpy as jnp
from jax import lax
from jax.experimental import pallas as pl
from jax.experimental.pallas import tpu as pltpu
from jax.sharding import PartitionSpec as P

HEAD_DIM = 128
VMEM_LIMIT = 48 * 1024 * 1024
BF16 = jnp.bfloat16
F32 = jnp.float32


def attend_piece(q_group, q_pos, k_piece, v_piece, p_piece):
    heads = q_group.shape[1]
    width = q_group.shape[2]
    key_heads = k_piece.reshape(k_piece.shape[0], heads, width)
    value_heads = v_piece.reshape(v_piece.shape[0], heads, width)
    scores = jnp.einsum(
        "thd,khd->htk", q_group, key_heads, preferred_element_type=jnp.float32
    ) * width ** (-0.5)
    visible = p_piece[None, None, :] <= q_pos[None, :, None]
    weight = jnp.where(visible, jax.nn.silu(scores), 0.0).astype(jnp.bfloat16)
    return jnp.einsum("htk,khd->thd", weight, value_heads, preferred_element_type=jnp.float32)


def general_shards(
    tokens, w_proj, w_out, positions, neg_emb, neg_ids, target_emb, target_ids
):
    tok_rows = tokens.shape[0]
    head_cols = w_proj.shape[2]
    local_heads = head_cols // HEAD_DIM
    proj_sum = jnp.einsum(
        "td,dfh->tfh",
        tokens,
        lax.all_gather(w_proj, "ctx", axis=0, tiled=True),
        preferred_element_type=jnp.float32,
    )
    proj = jax.nn.silu(proj_sum).astype(jnp.bfloat16)
    gate = proj[:, 0].reshape(tok_rows, local_heads, HEAD_DIM)
    query = proj[:, 2].reshape(tok_rows, local_heads, HEAD_DIM)
    v_piece = lax.all_gather(proj[:, 1], "ctx", axis=0, tiled=True)
    k_piece = lax.all_gather(proj[:, 3], "ctx", axis=0, tiled=True)
    p_piece = lax.all_gather(positions, "ctx", axis=0, tiled=True)
    attn = attend_piece(query, positions, k_piece, v_piece, p_piece)
    normed = attn * lax.rsqrt(jnp.mean(attn * attn, axis=-1, keepdims=True) + 1e-06)
    gated = (normed * gate.astype(jnp.float32)).astype(jnp.bfloat16).reshape(tok_rows, head_cols)
    out_terms = jnp.dot(
        gated, lax.all_gather(w_out, "ctx", axis=1, tiled=True), preferred_element_type=jnp.float32
    )
    out_share = lax.psum_scatter(out_terms, "tp", scatter_dimension=1, tiled=True)
    feat_cols = out_share.shape[1]
    own_tokens = lax.dynamic_slice_in_dim(tokens, lax.axis_index("tp") * feat_cols, feat_cols, 1)
    hidden = (own_tokens.astype(jnp.float32) + out_share).astype(jnp.bfloat16)
    piece = lax.all_gather(neg_emb, "ctx", axis=0, tiled=True)
    panel_dots = lax.dot_general(
        hidden, piece, (((1,), (1,)), ((), ())), preferred_element_type=jnp.float32
    )
    panel_norms = jnp.sum(jnp.square(piece.astype(jnp.float32)), axis=1)
    hidden_f = hidden.astype(jnp.float32)
    target_f = target_emb.astype(jnp.float32)
    part_hh = jnp.sum(hidden_f * hidden_f, axis=1)
    part_he = jnp.sum(hidden_f * target_f, axis=1)
    part_ee = jnp.sum(target_f * target_f, axis=1)
    dots, hh_sum, he_sum, ee_sum = (
        lax.psum_scatter(panel_dots, "tp", scatter_dimension=0, tiled=True),
        lax.psum_scatter(part_hh, "tp", scatter_dimension=0, tiled=True),
        lax.psum_scatter(part_he, "tp", scatter_dimension=0, tiled=True),
        lax.psum_scatter(part_ee, "tp", scatter_dimension=0, tiled=True),
    )
    neg_sq = lax.psum(panel_norms, "tp")
    pos_logit = he_sum / jnp.sqrt(hh_sum + 1e-06) / jnp.sqrt(ee_sum + 1e-06) / 0.05
    neg_logit = dots / jnp.sqrt(hh_sum + 1e-06)[:, None] / jnp.sqrt(neg_sq + 1e-06)[None, :] / 0.05
    keep_mask = neg_ids[None, :] != target_ids[:, None]
    total_mass = jnp.exp(pos_logit) + jnp.sum(jnp.where(keep_mask, jnp.exp(neg_logit), 0.0), axis=1)
    loss = jnp.log(total_mass) - pos_logit
    return (hidden, loss)


NZ, NY, NX = 4, 2, 2
CHIPS = NZ * NY * NX
SWAP = [(0, 1), (1, 0)]
RELATIVE = [(by, bx, s) for by in range(NY) for bx in range(NX) for s in range(NZ)]


def chip_at(z, y, x):
    return (z * NY + y) * NX + x


def coords(c):
    return c // (NY * NX), (c // NX) % NY, c % NX


def relative_chip(c, by, bx, s):
    z, y, x = coords(c)
    return chip_at((z + NZ - s) % NZ, y ^ by, x ^ bx)


def z_shift(s):
    return [(c, relative_chip(c, 0, 0, NZ - s)) for c in range(CHIPS)]


def flip(by, bx):
    return [(c, relative_chip(c, by, bx, 0)) for c in range(CHIPS)]


def hop(value, perm):
    return lax.ppermute(value, "ctx", perm)


def swap_cores(value):
    return lax.ppermute(value, "tp", SWAP)


def gather_chips(own):
    near = jnp.stack([own] + [hop(own, z_shift(s)) for s in range(1, NZ)])
    beside_x = hop(near, flip(0, 1))
    beside_y = hop(near, flip(1, 0))
    half = NZ // 2
    across_a = hop(beside_x[:half], flip(1, 0))
    across_b = hop(beside_y[half:], flip(0, 1))
    return [near, beside_x, beside_y, across_a, across_b]


def silu(v):
    return 0.5 * v * (1.0 + jnp.tanh(0.5 * v))


def proj_kernel(where, *refs):
    tok, (w_own, w_other), (gate_query, value_key), w_all = (
        refs[:5], refs[5:7], refs[7:9], refs[9],
    )
    low, u = where[0], where[1]
    block = HEAD_DIM
    count = w_own.shape[0]
    for d in range(count):
        spot = lax.bitwise_xor(low, d)
        for half, src in ((u, w_own), (1 - u, w_other)):
            start = pl.multiple_of((half * count + spot) * block, block)
            w_all[pl.ds(start, block), :] = src[d]
    base = 0
    for ref in tok:
        pieces, rows, _ = ref.shape
        for at in range(pieces):
            proj = silu(jnp.dot(ref[at], w_all[...], preferred_element_type=F32)).astype(BF16)
            out = pl.ds(base, rows)
            gate_query[out, :HEAD_DIM] = proj[:, :HEAD_DIM]
            value_key[out, :HEAD_DIM] = proj[:, HEAD_DIM : 2 * HEAD_DIM]
            gate_query[out, HEAD_DIM:] = proj[:, 2 * HEAD_DIM : 3 * HEAD_DIM]
            value_key[out, HEAD_DIM:] = proj[:, 3 * HEAD_DIM :]
            base += rows


def attend_kernel(gate_query, kv_own, kv_other, pos_col, pos_own, pos_other, gated):
    rows = gate_query.shape[0]
    tile = min(256, rows)

    def step(at, carry):
        span = pl.ds(pl.multiple_of(at * tile, tile), tile)
        query = gate_query[span, HEAD_DIM:]
        q_pos = pos_col[span, :]
        attn = jnp.zeros((tile, HEAD_DIM), F32)
        for kv, pos in ((kv_own, pos_own), (kv_other, pos_other)):
            scores = lax.dot_general(
                query, kv[:, HEAD_DIM:], (((1,), (1,)), ((), ())), preferred_element_type=F32
            ) * HEAD_DIM ** (-0.5)
            weight = jnp.where(pos[...] <= q_pos, silu(scores), 0.0).astype(BF16)
            attn += jnp.dot(weight, kv[:, :HEAD_DIM], preferred_element_type=F32)
        normed = attn * lax.rsqrt(jnp.mean(attn * attn, axis=-1, keepdims=True) + 1e-06)
        gate = gate_query[span, :HEAD_DIM].astype(F32)
        gated[span, :] = (normed * gate).astype(BF16)
        return carry

    lax.fori_loop(0, rows // tile, step, 0)


def hidden_kernel(where, *refs):
    pieces = refs[:CHIPS]
    w_own, w_other = refs[CHIPS : CHIPS + 5], refs[CHIPS + 5 : CHIPS + 10]
    tokens, keep, send, gated, hidden = refs[CHIPS + 10 :]
    c, u = where[0], where[1]
    width = HEAD_DIM
    half = hidden.shape[1] // 2
    for ref, (by, bx, s) in zip(pieces, RELATIVE):
        head = relative_chip(c, by, bx, NZ - s)
        gated[:, pl.ds(pl.multiple_of(head * width, width), width)] = ref[...]
    g_own = gated[:, pl.ds(pl.multiple_of(u * half, half), half)]
    g_other = gated[:, pl.ds(pl.multiple_of((1 - u) * half, half), half)]
    at = 0
    for own, other in zip(w_own, w_other):
        for i in range(own.shape[0]):
            block = relative_chip(c, *RELATIVE[at])
            cols = pl.ds(pl.multiple_of(block * width, width), width)
            total = jnp.dot(g_own, own[i], preferred_element_type=F32)
            total += jnp.dot(g_other, other[i], preferred_element_type=F32)
            hidden[:, cols] = (tokens[:, cols].astype(F32) + total).astype(BF16)
            at += 1
    keep[...] = hidden[:, pl.ds(pl.multiple_of(u * half, half), half)]
    send[...] = hidden[:, pl.ds(pl.multiple_of((1 - u) * half, half), half)]


def loss_kernel(*refs):
    h_keep, h_send, t_keep, t_send, t_ids, n_ids, nn = refs[:7]
    n_own, n_other = refs[7:12], refs[12:17]
    loss, dots = refs[17:]
    keep, send = h_keep[...], h_send[...]
    at = 0
    for own, other in zip(n_own, n_other):
        for i in range(0, own.shape[0], 2):
            rows = 2 * own.shape[1]
            total = jnp.zeros((keep.shape[0], rows), F32)
            for part, ref in ((keep, own), (send, other)):
                neg = ref[pl.ds(i, 2)].reshape(rows, part.shape[1])
                total += lax.dot_general(
                    part, neg, (((1,), (1,)), ((), ())), preferred_element_type=F32
                )
            dots[:, pl.ds(at, rows)] = total
            at += rows
    hh = he = ee = 0.0
    for part, ref in ((keep, t_keep), (send, t_send)):
        h_f, t_f = part.astype(F32), ref[...].astype(F32)
        hh += jnp.sum(h_f * h_f, axis=1, keepdims=True)
        he += jnp.sum(h_f * t_f, axis=1, keepdims=True)
        ee += jnp.sum(t_f * t_f, axis=1, keepdims=True)
    h_scale = lax.rsqrt(hh + 1e-06) * 20.0
    pos_logit = he * lax.rsqrt(ee + 1e-06) * h_scale
    neg_logit = dots[...] * h_scale * lax.rsqrt(nn[...] + 1e-06)
    mass = jnp.where(n_ids[...] != t_ids[...], jnp.exp(neg_logit), 0.0)
    total = jnp.exp(pos_logit) + jnp.sum(mass, axis=1, keepdims=True)
    loss[...] = jnp.log(total) - pos_logit


def call(kernel, outs, scratch, args, scalars=0, flops=0, name=None):
    specs = [pl.BlockSpec(memory_space=pltpu.SMEM)] * scalars
    specs += [pl.BlockSpec(memory_space=pltpu.VMEM)] * (len(args) - scalars)
    moved = sum(a.size * a.dtype.itemsize for a in args)
    return pl.pallas_call(
        kernel,
        out_shape=[jax.ShapeDtypeStruct(shape, dtype) for shape, dtype in outs],
        in_specs=specs,
        out_specs=[pl.BlockSpec(memory_space=pltpu.VMEM)] * len(outs),
        scratch_shapes=scratch,
        compiler_params=pltpu.CompilerParams(vmem_limit_bytes=VMEM_LIMIT),
        cost_estimate=pl.CostEstimate(flops=flops, bytes_accessed=moved, transcendentals=0),
        name=name,
    )(*args)


def head_shards(
    tokens, w_proj, w_out, positions, neg_emb, neg_ids, target_emb, target_ids
):
    c, u = lax.axis_index("ctx"), lax.axis_index("tp")
    model = tokens.shape[1]
    rows = tokens.shape[0] // 2
    events = rows * CHIPS
    low_heads = w_proj.shape[2] // HEAD_DIM
    low = c % low_heads

    mine = lax.dynamic_slice_in_dim(tokens, u * rows, rows, 0)
    tok = gather_chips(mine)
    pos = jnp.concatenate(gather_chips(positions.reshape(2, rows)))

    w_heads = w_proj.reshape(-1, 4, low_heads, HEAD_DIM).transpose(2, 0, 1, 3)
    w_heads = w_heads.reshape(low_heads, -1, 4 * HEAD_DIM)
    w_mine = []
    for d in range(low_heads):
        perm = [
            (2 * src + t, 2 * (t * low_heads + ((src ^ d) % low_heads)) + src // low_heads)
            for src in range(CHIPS)
            for t in range(2)
        ]
        piece = lax.dynamic_index_in_dim(w_heads, low ^ d, 0, keepdims=False)
        w_mine.append(lax.ppermute(piece, ("ctx", "tp"), perm))
    w_mine = jnp.stack(w_mine)
    w_other = swap_cores(w_mine)

    w_out, neg_emb, _ = lax.optimization_barrier((w_out, neg_emb, tok[0]))
    out_own = gather_chips(w_out)
    out_other = [swap_cores(piece) for piece in out_own]
    neg_own = gather_chips(neg_emb)
    neg_other = [swap_cores(piece) for piece in neg_own]
    t_rows = target_emb.reshape(2, rows, -1)
    t_keep = lax.dynamic_index_in_dim(t_rows, u, 0, keepdims=False)
    t_send = swap_cores(lax.dynamic_index_in_dim(t_rows, 1 - u, 0, keepdims=False))
    order = jnp.stack([relative_chip(c, *at) for at in RELATIVE])
    n_ids = neg_ids.reshape(CHIPS, -1)[order].reshape(1, -1)
    nn = sum(
        jnp.concatenate([jnp.sum(jnp.square(p.astype(F32)), axis=-1) for p in side])
        for side in (neg_own, neg_other)
    ).reshape(1, -1)

    where_low = jnp.stack([low, u]).astype(jnp.int32)
    where = jnp.stack([c, u]).astype(jnp.int32)
    gate_query, value_key = call(
        proj_kernel,
        [((events, 2 * HEAD_DIM), BF16)] * 2,
        [pltpu.VMEM((model, 4 * HEAD_DIM), BF16)],
        [where_low, *tok, w_mine, w_other],
        scalars=1,
        flops=2 * events * model * 4 * HEAD_DIM,
        name="project",
    )
    kv_other = swap_cores(value_key)
    pos_mine = lax.dynamic_index_in_dim(pos, u, 1, keepdims=False).reshape(-1)
    pos_theirs = lax.dynamic_index_in_dim(pos, 1 - u, 1, keepdims=False).reshape(-1)
    (gated,) = call(
        attend_kernel,
        [((events, HEAD_DIM), BF16)],
        [],
        [gate_query, value_key, kv_other, pos_mine[:, None], pos_mine[None], pos_theirs[None]],
        flops=8 * events * events * HEAD_DIM,
        name="attend",
    )
    gated = gated.reshape(CHIPS, rows, HEAD_DIM)
    pieces = [gated[0]]
    for at in range(1, CHIPS):
        perm = [(src, relative_chip(src, *RELATIVE[at])) for src in range(CHIPS)]
        pieces.append(hop(gated[at], perm))
    half = model // 2
    h_keep, h_send = call(
        hidden_kernel,
        [((rows, half), BF16)] * 2,
        [pltpu.VMEM((rows, model), BF16)] * 2,
        [where, *pieces, *out_own, *out_other, mine],
        scalars=1,
        flops=2 * rows * model * model,
        name="hidden",
    )
    h_theirs = swap_cores(h_send)
    (loss,) = call(
        loss_kernel,
        [((rows, 1), F32)],
        [pltpu.VMEM((rows, neg_ids.shape[0]), F32)],
        [h_keep, h_send, t_keep, t_send, target_ids[:, None], n_ids, nn, *neg_own, *neg_other],
        flops=2 * rows * model * neg_ids.shape[0],
        name="loss",
    )
    hidden = jnp.where(
        u == 0,
        jnp.concatenate([h_keep, h_theirs]),
        jnp.concatenate([h_theirs, h_keep]),
    )
    return hidden, loss.reshape(-1)


def shards(tokens, w_proj, *rest):
    n_ctx, n_tp = lax.axis_size("ctx"), lax.axis_size("tp")
    heads = w_proj.shape[2] * n_tp // HEAD_DIM
    plan = head_shards if (n_ctx, n_tp, heads) == (CHIPS, 2, CHIPS) else general_shards
    return plan(tokens, w_proj, *rest)


def solution(mesh):
    placed = (
        P("ctx", None),
        P("ctx", None, "tp"),
        P("tp", "ctx"),
        P("ctx"),
        P("ctx", "tp"),
        P(),
        P("ctx", "tp"),
        P(("ctx", "tp")),
    )
    return jax.shard_map(
        shards,
        mesh=mesh,
        in_specs=placed,
        out_specs=(P("ctx", "tp"), P(("ctx", "tp"))),
        check_vma=False,
    )
```

```python
import jax
import jax.numpy as jnp
from jax import lax
from jax.experimental import pallas as pl
from jax.experimental.pallas import tpu as pltpu
from jax.sharding import PartitionSpec as P

HEAD_DIM = 128
VMEM_LIMIT = 48 * 1024 * 1024
BF16 = jnp.bfloat16
F32 = jnp.float32


def attend_piece(q_group, q_pos, k_piece, v_piece, p_piece):
    heads = q_group.shape[1]
    width = q_group.shape[2]
    key_heads = k_piece.reshape(k_piece.shape[0], heads, width)
    value_heads = v_piece.reshape(v_piece.shape[0], heads, width)
    scores = jnp.einsum(
        "thd,khd->htk", q_group, key_heads, preferred_element_type=jnp.float32
    ) * width ** (-0.5)
    visible = p_piece[None, None, :] <= q_pos[None, :, None]
    weight = jnp.where(visible, jax.nn.silu(scores), 0.0).astype(jnp.bfloat16)
    return jnp.einsum("htk,khd->thd", weight, value_heads, preferred_element_type=jnp.float32)


def general_shards(
    tokens, w_proj, w_out, positions, neg_emb, neg_ids, target_emb, target_ids
):
    tok_rows = tokens.shape[0]
    head_cols = w_proj.shape[2]
    local_heads = head_cols // HEAD_DIM
    proj_sum = jnp.einsum(
        "td,dfh->tfh",
        tokens,
        lax.all_gather(w_proj, "ctx", axis=0, tiled=True),
        preferred_element_type=jnp.float32,
    )
    proj = jax.nn.silu(proj_sum).astype(jnp.bfloat16)
    gate = proj[:, 0].reshape(tok_rows, local_heads, HEAD_DIM)
    query = proj[:, 2].reshape(tok_rows, local_heads, HEAD_DIM)
    v_piece = lax.all_gather(proj[:, 1], "ctx", axis=0, tiled=True)
    k_piece = lax.all_gather(proj[:, 3], "ctx", axis=0, tiled=True)
    p_piece = lax.all_gather(positions, "ctx", axis=0, tiled=True)
    attn = attend_piece(query, positions, k_piece, v_piece, p_piece)
    normed = attn * lax.rsqrt(jnp.mean(attn * attn, axis=-1, keepdims=True) + 1e-06)
    gated = (normed * gate.astype(jnp.float32)).astype(jnp.bfloat16).reshape(tok_rows, head_cols)
    out_terms = jnp.dot(
        gated, lax.all_gather(w_out, "ctx", axis=1, tiled=True), preferred_element_type=jnp.float32
    )
    out_share = lax.psum_scatter(out_terms, "tp", scatter_dimension=1, tiled=True)
    feat_cols = out_share.shape[1]
    own_tokens = lax.dynamic_slice_in_dim(tokens, lax.axis_index("tp") * feat_cols, feat_cols, 1)
    hidden = (own_tokens.astype(jnp.float32) + out_share).astype(jnp.bfloat16)
    piece = lax.all_gather(neg_emb, "ctx", axis=0, tiled=True)
    panel_dots = lax.dot_general(
        hidden, piece, (((1,), (1,)), ((), ())), preferred_element_type=jnp.float32
    )
    panel_norms = jnp.sum(jnp.square(piece.astype(jnp.float32)), axis=1)
    hidden_f = hidden.astype(jnp.float32)
    target_f = target_emb.astype(jnp.float32)
    part_hh = jnp.sum(hidden_f * hidden_f, axis=1)
    part_he = jnp.sum(hidden_f * target_f, axis=1)
    part_ee = jnp.sum(target_f * target_f, axis=1)
    dots, hh_sum, he_sum, ee_sum = (
        lax.psum_scatter(panel_dots, "tp", scatter_dimension=0, tiled=True),
        lax.psum_scatter(part_hh, "tp", scatter_dimension=0, tiled=True),
        lax.psum_scatter(part_he, "tp", scatter_dimension=0, tiled=True),
        lax.psum_scatter(part_ee, "tp", scatter_dimension=0, tiled=True),
    )
    neg_sq = lax.psum(panel_norms, "tp")
    pos_logit = he_sum / jnp.sqrt(hh_sum + 1e-06) / jnp.sqrt(ee_sum + 1e-06) / 0.05
    neg_logit = dots / jnp.sqrt(hh_sum + 1e-06)[:, None] / jnp.sqrt(neg_sq + 1e-06)[None, :] / 0.05
    keep_mask = neg_ids[None, :] != target_ids[:, None]
    total_mass = jnp.exp(pos_logit) + jnp.sum(jnp.where(keep_mask, jnp.exp(neg_logit), 0.0), axis=1)
    loss = jnp.log(total_mass) - pos_logit
    return (hidden, loss)


NZ, NY, NX = 4, 2, 2
CHIPS = NZ * NY * NX
PLANE = [(by, bx) for by in range(NY) for bx in range(NX)]
SWAP = [(0, 1), (1, 0)]
RELATIVE = [(by, bx, s) for by, bx in PLANE for s in range(NZ)]
W = HEAD_DIM


def chip_at(z, y, x):
    return (z * NY + y) * NX + x


def coords(c):
    return c // (NY * NX), (c // NX) % NY, c % NX


def relative_chip(c, by, bx, s):
    z, y, x = coords(c)
    return chip_at((z + NZ - s) % NZ, y ^ by, x ^ bx)


def z_shift(s):
    return [(c, relative_chip(c, 0, 0, NZ - s)) for c in range(CHIPS)]


def flip(by, bx):
    return [(c, relative_chip(c, by, bx, 0)) for c in range(CHIPS)]


def hop(value, perm):
    return lax.ppermute(value, "ctx", perm)


def swap_cores(value):
    return lax.ppermute(value, "tp", SWAP)


def gather_chips(own):
    near = jnp.concatenate([own] + [hop(own, z_shift(s)) for s in range(1, NZ)])
    beside_x = hop(near, flip(0, 1))
    beside_y = hop(near, flip(1, 0))
    half = near.shape[0] // 2
    across_a = hop(beside_x[:half], flip(1, 0))
    across_b = hop(beside_y[half:], flip(0, 1))
    return [near, beside_x, beside_y, across_a, across_b]


def scatter_heads(w_proj, z, y, x, after):
    plane = NY * NX
    heads = w_proj.reshape(-1, 4, 2 * plane, W).transpose(2, 0, 1, 3)
    heads = heads.reshape(2, plane, -1, 4 * W)
    heads, _ = lax.optimization_barrier((heads, after))
    arrived = []
    for e in range(2):
        perm = []
        for src in range(CHIPS):
            sz, sy, sx = coords(src)
            for t in range(2):
                dst = chip_at(2 * t + (e ^ (sz & 1)), sy, sx)
                perm.append((2 * src + t, 2 * dst + (sz >> 1)))
        piece = lax.dynamic_index_in_dim(heads, e ^ (z & 1), 0, keepdims=False)
        arrived.append(lax.ppermute(piece, ("ctx", "tp"), perm))
    both = jnp.stack(arrived, 1)
    out = []
    for by, bx in PLANE:
        spot = (y ^ by) * NX + (x ^ bx)
        piece = lax.dynamic_index_in_dim(both, spot, 0, keepdims=False)
        out.append(piece if (by, bx) == (0, 0) else hop(piece, flip(by, bx)))
    return jnp.stack(out)


def silu(v):
    return 0.5 * v * (1.0 + jnp.tanh(0.5 * v))


def start_all(copies):
    for copy in copies:
        copy.start()
    return copies


def proj_kernel(where, *refs):
    tok, (w_own, w_other), (gate_query, value_key, marks) = refs[:5], refs[5:7], refs[7:10]
    x_all, w_all, tok_sem, w_sem = refs[10:]
    z, y, x, u = (where[i] for i in range(4))
    copies = []
    for side, (half, src) in enumerate(((u, w_own), (1 - u, w_other))):
        for k, (by, bx) in enumerate(PLANE):
            for e in range(2):
                block = chip_at(2 * half + (e ^ (z & 1)), y ^ by, x ^ bx)
                rows = pl.ds(pl.multiple_of(block * W, W), W)
                sem = w_sem.at[(side * len(PLANE) + k) * 2 + e]
                copies.append(pltpu.make_async_copy(src.at[k, e], w_all.at[rows, :], sem))
    loads, base = [], 0
    for i, ref in enumerate(tok):
        rows = pl.ds(base, ref.shape[0])
        loads.append(pltpu.make_async_copy(ref, x_all.at[rows, :], tok_sem.at[i]))
        base += ref.shape[0]
    start_all(copies)
    start_all(loads)
    for copy in copies + loads:
        copy.wait()
    model = w_all.shape[0]
    tile = 256

    def step(at, carry):
        span = pl.ds(pl.multiple_of(at * tile, tile), tile)
        total = jnp.dot(x_all[span, :model], w_all[...], preferred_element_type=F32)
        proj = silu(total).astype(BF16)
        gate_query[span, :W] = proj[:, :W]
        value_key[span, :W] = proj[:, W : 2 * W]
        gate_query[span, W:] = proj[:, 2 * W : 3 * W]
        value_key[span, W:] = proj[:, 3 * W :]
        marks[span, :] = x_all[span, model:]
        return carry

    lax.fori_loop(0, base // tile, step, 0)


def attend_kernel(where, gate_query, kv_own, kv_other, marks, gated):
    rows = gate_query.shape[0]
    tile = rows // len(PLANE)
    piece = tile // NZ
    lane = lax.broadcasted_iota(jnp.int32, (8, W), 1)
    line = lax.broadcasted_iota(jnp.int32, (8, W), 0)
    pick = jnp.where(lane == 2 * line, 128.0, jnp.where(lane == 2 * line + 1, 1.0, 0.0))
    pick = jnp.where(line < 2, pick, 0.0).astype(BF16)
    across = (((1,), (1,)), ((), ()))
    key_pos = lax.dot_general(pick, marks[...], across, preferred_element_type=F32)
    z, y, x = (where[i] for i in range(3))
    for k, (by, bx) in enumerate(PLANE):
        span = pl.ds(k * tile, tile)
        query = gate_query[span, W:]
        q_pos = lax.dot_general(marks[span, :], pick, across, preferred_element_type=F32)[:, :1]
        attn = jnp.zeros((tile, W), F32)
        for side, kv in enumerate((kv_own, kv_other)):
            scores = lax.dot_general(
                query, kv[:, W:], across, preferred_element_type=F32
            ) * W ** (-0.5)
            visible = key_pos[side : side + 1, :] <= q_pos
            weight = jnp.where(visible, silu(scores), 0.0).astype(BF16)
            attn += jnp.dot(weight, kv[:, :W], preferred_element_type=F32)
        normed = attn * lax.rsqrt(jnp.mean(attn * attn, axis=-1, keepdims=True) + 1e-06)
        out = (normed * gate_query[span, :W].astype(F32)).astype(BF16)
        for s in range(NZ):
            chip = chip_at((z + NZ - s) % NZ, y ^ by, x ^ bx)
            gated[pl.ds(chip, 1)] = out[s * piece : (s + 1) * piece][None]


def hidden_kernel(where, gated, w_own, w_other, tokens, keep, send, g_all, h_all, w_all, sems):
    u = where[3]
    chips, rows, _ = gated.shape
    half = chips * W // 2
    copies = []
    for side, src in enumerate((w_own, w_other)):
        for chip in range(chips):
            copies.append(
                pltpu.make_async_copy(
                    src.at[chip, pl.ds(0, half), :],
                    w_all.at[side, :, pl.ds(chip * W, W)],
                    sems.at[side * chips + chip],
                )
            )
    start_all(copies)
    for chip in range(chips):
        g_all[:, chip * W : (chip + 1) * W] = gated[chip]
    g_own = g_all[:, pl.ds(pl.multiple_of(u * half, half), half)]
    g_other = g_all[:, pl.ds(pl.multiple_of((1 - u) * half, half), half)]
    for chip in range(0, chips, 2):
        cols = pl.ds(chip * W, 2 * W)
        for i in (chip, chip + 1, chips + chip, chips + chip + 1):
            copies[i].wait()
        total = jnp.dot(g_own, w_all[0, :, cols], preferred_element_type=F32)
        total += jnp.dot(g_other, w_all[1, :, cols], preferred_element_type=F32)
        h_all[:, cols] = (tokens[:, cols].astype(F32) + total).astype(BF16)
    keep[...] = h_all[:, pl.ds(pl.multiple_of(u * half, half), half)]
    send[...] = h_all[:, pl.ds(pl.multiple_of((1 - u) * half, half), half)]


def loss_kernel(h_keep, h_send, t_keep, t_send, t_ids, n_ids, nn, n_own, n_other, loss, n_all, sems):
    keep, send = h_keep[...], h_send[...]
    chips, panels, negs, _ = n_own.shape
    copies = []
    for side, src in enumerate((n_own, n_other)):
        for panel in range(panels):
            copies.append(
                pltpu.make_async_copy(
                    src.at[:, panel],
                    n_all.at[side, :, :, pl.ds(panel * W, W)],
                    sems.at[side * panels + panel],
                )
            )
    start_all(copies)
    hh = he = ee = 0.0
    for part, ref in ((keep, t_keep), (send, t_send)):
        h_f, t_f = part.astype(F32), ref[...].astype(F32)
        hh += jnp.sum(h_f * h_f, axis=1, keepdims=True)
        he += jnp.sum(h_f * t_f, axis=1, keepdims=True)
        ee += jnp.sum(t_f * t_f, axis=1, keepdims=True)
    h_scale = lax.rsqrt(hh + 1e-06) * 20.0
    pos_logit = he * lax.rsqrt(ee + 1e-06) * h_scale
    for copy in copies:
        copy.wait()
    dots = 0.0
    for side, part in enumerate((keep, send)):
        neg = n_all[side].reshape(chips * negs, panels * W)
        dots += lax.dot_general(part, neg, (((1,), (1,)), ((), ())), preferred_element_type=F32)
    neg_logit = dots * h_scale * lax.rsqrt(nn[...] + 1e-06)
    mass = jnp.where(n_ids[...] != t_ids[...], jnp.exp(neg_logit), 0.0)
    total = jnp.exp(pos_logit) + jnp.sum(mass, axis=1, keepdims=True)
    loss[...] = jnp.log(total) - pos_logit


def call(kernel, name, outs, scratch, args, places, flops):
    space = {"s": pltpu.SMEM, "v": pltpu.VMEM, "h": pl.ANY}
    moved = sum(a.size * a.dtype.itemsize for a in args)
    return pl.pallas_call(
        kernel,
        out_shape=[jax.ShapeDtypeStruct(shape, dtype) for shape, dtype in outs],
        in_specs=[pl.BlockSpec(memory_space=space[p]) for p in places],
        out_specs=[pl.BlockSpec(memory_space=pltpu.VMEM)] * len(outs),
        scratch_shapes=scratch,
        compiler_params=pltpu.CompilerParams(vmem_limit_bytes=VMEM_LIMIT),
        cost_estimate=pl.CostEstimate(flops=flops, bytes_accessed=moved, transcendentals=0),
        name=name,
    )(*args)


def position_marks(pos):
    return [(pos // 128).astype(BF16), (pos % 128).astype(BF16)]


def head_shards(
    tokens, w_proj, w_out, positions, neg_emb, neg_ids, target_emb, target_ids
):
    c, u = lax.axis_index("ctx"), lax.axis_index("tp")
    z, y, x = coords(c)
    where = jnp.stack([z, y, x, u]).astype(jnp.int32)
    model = tokens.shape[1]
    rows = tokens.shape[0] // 2
    events = rows * CHIPS
    half = model // 2

    mine = lax.dynamic_slice_in_dim(tokens, u * rows, rows, 0)
    p_own = lax.dynamic_slice_in_dim(positions, u * rows, rows, 0)
    p_other = lax.dynamic_slice_in_dim(positions, (1 - u) * rows, rows, 0)
    marks = jnp.stack(position_marks(p_own) + position_marks(p_other), 1)
    marks = jnp.pad(marks, ((0, 0), (0, W - marks.shape[1])))
    tok = gather_chips(jnp.concatenate([mine, marks], 1))
    w_mine = scatter_heads(w_proj, z, y, x, tok[0])
    w_theirs = swap_cores(w_mine)

    negs, panels = neg_emb.shape[0], neg_emb.shape[1] // W
    neg_panels = neg_emb.reshape(negs, panels, W).transpose(1, 0, 2).reshape(-1, W)
    late_own = lax.all_gather(jnp.concatenate([w_out, neg_panels]), "ctx", axis=0)
    t_rows = target_emb.reshape(2, rows, -1)
    t_keep = lax.dynamic_index_in_dim(t_rows, u, 0, keepdims=False)
    t_send = swap_cores(lax.dynamic_index_in_dim(t_rows, 1 - u, 0, keepdims=False))

    gate_query, value_key, marks_all = call(
        proj_kernel,
        "project",
        [((events, 2 * W), BF16)] * 2 + [((events, W), BF16)],
        [
            pltpu.VMEM((events, model + W), BF16),
            pltpu.VMEM((model, 4 * W), BF16),
            pltpu.SemaphoreType.DMA((5,)),
            pltpu.SemaphoreType.DMA((16,)),
        ],
        [where, *tok, w_mine, w_theirs],
        "s" + 7 * "h",
        2 * events * model * 4 * W,
    )
    kv_theirs = swap_cores(value_key)
    late_own, _ = lax.optimization_barrier((late_own, value_key))
    late_other = swap_cores(late_own)
    split = w_out.shape[0]
    n_own = late_own[:, split:].reshape(CHIPS, panels, negs, W)
    n_other = late_other[:, split:].reshape(CHIPS, panels, negs, W)
    nn = sum(jnp.sum(jnp.square(n.astype(F32)), axis=(1, 3)) for n in (n_own, n_other))
    (gated,) = call(
        attend_kernel,
        "attend",
        [((CHIPS, rows, W), BF16)],
        [],
        [where, gate_query, value_key, kv_theirs, marks_all],
        "svvvv",
        8 * events * events * W,
    )
    gated = lax.all_to_all(gated, "ctx", 0, 0, tiled=True)
    h_keep, h_send = call(
        hidden_kernel,
        "hidden",
        [((rows, half), BF16)] * 2,
        [
            pltpu.VMEM((rows, model), BF16),
            pltpu.VMEM((rows, model), BF16),
            pltpu.VMEM((2, half, model), BF16),
            pltpu.SemaphoreType.DMA((2 * CHIPS,)),
        ],
        [where, gated, late_own, late_other, mine],
        "svhhv",
        2 * rows * model * model,
    )
    h_theirs = swap_cores(h_send)
    (loss,) = call(
        loss_kernel,
        "loss",
        [((rows, 1), F32)],
        [
            pltpu.VMEM((2, CHIPS, negs, half), BF16),
            pltpu.SemaphoreType.DMA((2 * panels,)),
        ],
        [
            h_keep,
            h_send,
            t_keep,
            t_send,
            target_ids[:, None],
            neg_ids[None],
            nn.reshape(1, -1),
            n_own,
            n_other,
        ],
        "vvvvvvvhh",
        2 * rows * model * neg_ids.shape[0],
    )
    hidden = jnp.where(
        u == 0,
        jnp.concatenate([h_keep, h_theirs]),
        jnp.concatenate([h_theirs, h_keep]),
    )
    return hidden, loss.reshape(-1)


def shards(tokens, w_proj, *rest):
    n_ctx, n_tp = lax.axis_size("ctx"), lax.axis_size("tp")
    heads = w_proj.shape[2] * n_tp // HEAD_DIM
    plan = head_shards if (n_ctx, n_tp, heads) == (CHIPS, 2, CHIPS) else general_shards
    return plan(tokens, w_proj, *rest)


def solution(mesh):
    placed = (
        P("ctx", None),
        P("ctx", None, "tp"),
        P("tp", "ctx"),
        P("ctx"),
        P("ctx", "tp"),
        P(),
        P("ctx", "tp"),
        P(("ctx", "tp")),
    )
    return jax.shard_map(
        shards,
        mesh=mesh,
        in_specs=placed,
        out_specs=(P("ctx", "tp"), P(("ctx", "tp"))),
        check_vma=False,
    )
```

```python
import jax
import jax.numpy as jnp
from jax import lax
from jax.experimental import pallas as pl
from jax.experimental.pallas import tpu as pltpu
from jax.sharding import PartitionSpec as P

HEAD_DIM = 128
VMEM_LIMIT = 48 * 1024 * 1024
BF16 = jnp.bfloat16
F32 = jnp.float32


def attend_piece(q_group, q_pos, k_piece, v_piece, p_piece):
    heads = q_group.shape[1]
    width = q_group.shape[2]
    key_heads = k_piece.reshape(k_piece.shape[0], heads, width)
    value_heads = v_piece.reshape(v_piece.shape[0], heads, width)
    scores = jnp.einsum(
        "thd,khd->htk", q_group, key_heads, preferred_element_type=jnp.float32
    ) * width ** (-0.5)
    visible = p_piece[None, None, :] <= q_pos[None, :, None]
    weight = jnp.where(visible, jax.nn.silu(scores), 0.0).astype(jnp.bfloat16)
    return jnp.einsum("htk,khd->thd", weight, value_heads, preferred_element_type=jnp.float32)


def general_shards(
    tokens, w_proj, w_out, positions, neg_emb, neg_ids, target_emb, target_ids
):
    tok_rows = tokens.shape[0]
    head_cols = w_proj.shape[2]
    local_heads = head_cols // HEAD_DIM
    proj_sum = jnp.einsum(
        "td,dfh->tfh",
        tokens,
        lax.all_gather(w_proj, "ctx", axis=0, tiled=True),
        preferred_element_type=jnp.float32,
    )
    proj = jax.nn.silu(proj_sum).astype(jnp.bfloat16)
    gate = proj[:, 0].reshape(tok_rows, local_heads, HEAD_DIM)
    query = proj[:, 2].reshape(tok_rows, local_heads, HEAD_DIM)
    v_piece = lax.all_gather(proj[:, 1], "ctx", axis=0, tiled=True)
    k_piece = lax.all_gather(proj[:, 3], "ctx", axis=0, tiled=True)
    p_piece = lax.all_gather(positions, "ctx", axis=0, tiled=True)
    attn = attend_piece(query, positions, k_piece, v_piece, p_piece)
    normed = attn * lax.rsqrt(jnp.mean(attn * attn, axis=-1, keepdims=True) + 1e-06)
    gated = (normed * gate.astype(jnp.float32)).astype(jnp.bfloat16).reshape(tok_rows, head_cols)
    out_terms = jnp.dot(
        gated, lax.all_gather(w_out, "ctx", axis=1, tiled=True), preferred_element_type=jnp.float32
    )
    out_share = lax.psum_scatter(out_terms, "tp", scatter_dimension=1, tiled=True)
    feat_cols = out_share.shape[1]
    own_tokens = lax.dynamic_slice_in_dim(tokens, lax.axis_index("tp") * feat_cols, feat_cols, 1)
    hidden = (own_tokens.astype(jnp.float32) + out_share).astype(jnp.bfloat16)
    piece = lax.all_gather(neg_emb, "ctx", axis=0, tiled=True)
    panel_dots = lax.dot_general(
        hidden, piece, (((1,), (1,)), ((), ())), preferred_element_type=jnp.float32
    )
    panel_norms = jnp.sum(jnp.square(piece.astype(jnp.float32)), axis=1)
    hidden_f = hidden.astype(jnp.float32)
    target_f = target_emb.astype(jnp.float32)
    part_hh = jnp.sum(hidden_f * hidden_f, axis=1)
    part_he = jnp.sum(hidden_f * target_f, axis=1)
    part_ee = jnp.sum(target_f * target_f, axis=1)
    dots, hh_sum, he_sum, ee_sum = (
        lax.psum_scatter(panel_dots, "tp", scatter_dimension=0, tiled=True),
        lax.psum_scatter(part_hh, "tp", scatter_dimension=0, tiled=True),
        lax.psum_scatter(part_he, "tp", scatter_dimension=0, tiled=True),
        lax.psum_scatter(part_ee, "tp", scatter_dimension=0, tiled=True),
    )
    neg_sq = lax.psum(panel_norms, "tp")
    pos_logit = he_sum / jnp.sqrt(hh_sum + 1e-06) / jnp.sqrt(ee_sum + 1e-06) / 0.05
    neg_logit = dots / jnp.sqrt(hh_sum + 1e-06)[:, None] / jnp.sqrt(neg_sq + 1e-06)[None, :] / 0.05
    keep_mask = neg_ids[None, :] != target_ids[:, None]
    total_mass = jnp.exp(pos_logit) + jnp.sum(jnp.where(keep_mask, jnp.exp(neg_logit), 0.0), axis=1)
    loss = jnp.log(total_mass) - pos_logit
    return (hidden, loss)


NZ, NY, NX = 4, 2, 2
CHIPS = NZ * NY * NX
PLANE = [(by, bx) for by in range(NY) for bx in range(NX)]
SWAP = [(0, 1), (1, 0)]
RELATIVE = [(by, bx, s) for by, bx in PLANE for s in range(NZ)]
W = HEAD_DIM


def chip_at(z, y, x):
    return (z * NY + y) * NX + x


def coords(c):
    return c // (NY * NX), (c // NX) % NY, c % NX


def relative_chip(c, by, bx, s):
    z, y, x = coords(c)
    return chip_at((z + NZ - s) % NZ, y ^ by, x ^ bx)


def z_shift(s):
    return [(c, relative_chip(c, 0, 0, NZ - s)) for c in range(CHIPS)]


def flip(by, bx):
    return [(c, relative_chip(c, by, bx, 0)) for c in range(CHIPS)]


def hop(value, perm):
    return lax.ppermute(value, "ctx", perm)


def swap_cores(value):
    return lax.ppermute(value, "tp", SWAP)


def gather_chips(own):
    near = jnp.concatenate([own] + [hop(own, z_shift(s)) for s in range(1, NZ)])
    beside_x = hop(near, flip(0, 1))
    beside_y = hop(near, flip(1, 0))
    half = near.shape[0] // 2
    across_a = hop(beside_x[:half], flip(1, 0))
    across_b = hop(beside_y[half:], flip(0, 1))
    return [near, beside_x, beside_y, across_a, across_b]


def scatter_heads(w_proj, u):
    depth, _, cols = w_proj.shape
    count = cols // W
    heads = w_proj.reshape(2, depth // 2, 4, count, W).transpose(0, 3, 1, 2, 4)
    heads = heads.reshape(2, count, depth // 2, 4 * W)
    theirs = swap_cores(lax.dynamic_index_in_dim(heads, 1 - u, 0, keepdims=False))
    ours = lax.dynamic_index_in_dim(heads, u, 0, keepdims=False)
    return jnp.where(
        u == 0, jnp.concatenate([ours, theirs]), jnp.concatenate([theirs, ours])
    )


def silu(v):
    return 0.5 * v * (1.0 + jnp.tanh(0.5 * v))


def start_all(copies):
    for copy in copies:
        copy.start()
    return copies


def proj_kernel(where, *refs):
    count = len(refs) - 9
    tok, (w_own, w_other) = refs[:count], refs[count : count + 2]
    gate_query, value_key, marks, x_all, w_all, tok_sem, w_sem = refs[count + 2 :]
    u = where[3]
    copies, base = [], 0
    for side, (half, src) in enumerate(((u, w_own), (1 - u, w_other))):
        copies.append(pltpu.make_async_copy(src, w_all.at[:, half], w_sem.at[side]))
    for i, ref in enumerate(tok):
        rows = pl.ds(base, ref.shape[0])
        copies.append(pltpu.make_async_copy(ref, x_all.at[rows, :], tok_sem.at[i]))
        base += ref.shape[0]
    start_all(copies)
    for copy in copies:
        copy.wait()
    weights = w_all[...].reshape(-1, w_all.shape[-1])
    model = weights.shape[0]
    total = jnp.dot(x_all[:, :model], weights, preferred_element_type=F32)
    proj = silu(total).astype(BF16)
    gate_query[:, :W] = proj[:, :W]
    value_key[:, :W] = proj[:, W : 2 * W]
    gate_query[:, W:] = proj[:, 2 * W : 3 * W]
    value_key[:, W:] = proj[:, 3 * W :]
    marks[...] = x_all[:, model:]


def attend_kernel(where, *refs):
    gate_query, kv_own, kv_other, marks = refs[:2], refs[2:4], refs[4:6], refs[6:8]
    gated = refs[8]
    lane = lax.broadcasted_iota(jnp.int32, (8, W), 1)
    line = lax.broadcasted_iota(jnp.int32, (8, W), 0)
    pick = jnp.where(lane == 2 * line, 128.0, jnp.where(lane == 2 * line + 1, 1.0, 0.0))
    pick = jnp.where(line < 2, pick, 0.0).astype(BF16)
    across = (((1,), (1,)), ((), ()))
    z, y, x = (where[i] for i in range(3))
    piece = gated.shape[1]
    tile = NZ * piece
    groups = []
    for group in range(2):
        key_pos = lax.dot_general(pick, marks[group][...], across, preferred_element_type=F32)
        groups.append((kv_own[group], key_pos[0:1]))
        groups.append((kv_other[group], key_pos[1:2]))
    for k, (by, bx) in enumerate(PLANE):
        group, base = (0, k * tile) if k < len(PLANE) - 1 else (1, 0)
        span = pl.ds(base, tile)
        query = gate_query[group][span, W:]
        q_pos = lax.dot_general(
            marks[group][span, :], pick, across, preferred_element_type=F32
        )[:, :1]
        attn = jnp.zeros((tile, W), F32)
        for kv, key_pos in groups:
            scores = lax.dot_general(
                query, kv[:, W:], across, preferred_element_type=F32
            ) * W ** (-0.5)
            weight = jnp.where(key_pos <= q_pos, silu(scores), 0.0).astype(BF16)
            attn += jnp.dot(weight, kv[:, :W], preferred_element_type=F32)
        normed = attn * lax.rsqrt(jnp.mean(attn * attn, axis=-1, keepdims=True) + 1e-06)
        out = (normed * gate_query[group][span, :W].astype(F32)).astype(BF16)
        for s in range(NZ):
            chip = chip_at((z + NZ - s) % NZ, y ^ by, x ^ bx)
            gated[pl.ds(chip, 1)] = out[s * piece : (s + 1) * piece][None]


def hidden_kernel(where, gated, w_own, w_other, tokens, keep, send, g_all, h_all, w_all, sems):
    u = where[3]
    chips, rows, _ = gated.shape
    half = chips * W // 2
    copies = []
    for side, src in enumerate((w_own, w_other)):
        for chip in range(chips):
            panel = (chip % (NY * NX)) * NZ + chip // (NY * NX)
            copies.append(
                pltpu.make_async_copy(
                    src.at[panel, pl.ds(0, half), :],
                    w_all.at[side, :, pl.ds(chip * W, W)],
                    sems.at[side * chips + chip],
                )
            )
    start_all(copies)
    for chip in range(chips):
        g_all[:, chip * W : (chip + 1) * W] = gated[chip]
    g_own = g_all[:, pl.ds(pl.multiple_of(u * half, half), half)]
    g_other = g_all[:, pl.ds(pl.multiple_of((1 - u) * half, half), half)]
    for chip in range(0, chips, 2):
        cols = pl.ds(chip * W, 2 * W)
        for i in (chip, chip + 1, chips + chip, chips + chip + 1):
            copies[i].wait()
        total = jnp.dot(g_own, w_all[0, :, cols], preferred_element_type=F32)
        total += jnp.dot(g_other, w_all[1, :, cols], preferred_element_type=F32)
        h_all[:, cols] = (tokens[:, cols].astype(F32) + total).astype(BF16)
    keep[...] = h_all[:, pl.ds(pl.multiple_of(u * half, half), half)]
    send[...] = h_all[:, pl.ds(pl.multiple_of((1 - u) * half, half), half)]


def loss_kernel(
    h_keep, h_send, t_keep, t_send, t_ids, n_ids, nn, late_own, late_other, loss, n_all, sems
):
    keep, send = h_keep[...], h_send[...]
    _, chips, negs, half = n_all.shape
    panels = half // W
    split = late_own.shape[1] - panels * negs
    copies = []
    for side, src in enumerate((late_own, late_other)):
        for panel in range(panels):
            copies.append(
                pltpu.make_async_copy(
                    src.at[:, pl.ds(split + panel * negs, negs), :],
                    n_all.at[side, :, :, pl.ds(panel * W, W)],
                    sems.at[side * panels + panel],
                )
            )
    start_all(copies)
    hh = he = ee = 0.0
    for part, ref in ((keep, t_keep), (send, t_send)):
        h_f, t_f = part.astype(F32), ref[...].astype(F32)
        hh += jnp.sum(h_f * h_f, axis=1, keepdims=True)
        he += jnp.sum(h_f * t_f, axis=1, keepdims=True)
        ee += jnp.sum(t_f * t_f, axis=1, keepdims=True)
    h_scale = lax.rsqrt(hh + 1e-06) * 20.0
    pos_logit = he * lax.rsqrt(ee + 1e-06) * h_scale
    for copy in copies:
        copy.wait()
    dots = 0.0
    for side, part in enumerate((keep, send)):
        neg = n_all[side].reshape(chips * negs, half)
        dots += lax.dot_general(part, neg, (((1,), (1,)), ((), ())), preferred_element_type=F32)
    neg_logit = dots * h_scale * lax.rsqrt(nn[...] + 1e-06)
    mass = jnp.where(n_ids[...] != t_ids[...], jnp.exp(neg_logit), 0.0)
    total = jnp.exp(pos_logit) + jnp.sum(mass, axis=1, keepdims=True)
    loss[...] = jnp.log(total) - pos_logit


def call(kernel, name, outs, scratch, args, places, flops):
    space = {"s": pltpu.SMEM, "v": pltpu.VMEM, "h": pl.ANY}
    moved = sum(a.size * a.dtype.itemsize for a in args)
    return pl.pallas_call(
        kernel,
        out_shape=[jax.ShapeDtypeStruct(shape, dtype) for shape, dtype in outs],
        in_specs=[pl.BlockSpec(memory_space=space[p]) for p in places],
        out_specs=[pl.BlockSpec(memory_space=pltpu.VMEM)] * len(outs),
        scratch_shapes=scratch,
        compiler_params=pltpu.CompilerParams(vmem_limit_bytes=VMEM_LIMIT),
        cost_estimate=pl.CostEstimate(flops=flops, bytes_accessed=moved, transcendentals=0),
        name=name,
    )(*args)


def position_marks(pos):
    return [(pos // 128).astype(BF16), (pos % 128).astype(BF16)]


def head_shards(
    tokens, w_proj, w_out, positions, neg_emb, neg_ids, target_emb, target_ids
):
    c, u = lax.axis_index("ctx"), lax.axis_index("tp")
    z, y, x = coords(c)
    where = jnp.stack([z, y, x, u]).astype(jnp.int32)
    model = tokens.shape[1]
    rows = tokens.shape[0] // 2
    events = rows * CHIPS
    half = model // 2

    mine = lax.dynamic_slice_in_dim(tokens, u * rows, rows, 0)
    p_own = lax.dynamic_slice_in_dim(positions, u * rows, rows, 0)
    p_other = lax.dynamic_slice_in_dim(positions, (1 - u) * rows, rows, 0)
    marks = jnp.stack(position_marks(p_own) + position_marks(p_other), 1)
    marks = jnp.pad(marks, ((0, 0), (0, W - marks.shape[1])))
    w_heads = scatter_heads(w_proj, u)
    tok = gather_chips(jnp.concatenate([mine, marks], 1))
    w_heads, w_out, neg_emb, _ = lax.optimization_barrier((w_heads, w_out, neg_emb, tok[0]))
    w_mine = lax.all_to_all(w_heads, "ctx", 0, 0, tiled=True)
    w_theirs = swap_cores(w_mine)

    negs, panels = neg_emb.shape[0], neg_emb.shape[1] // W
    neg_panels = neg_emb.reshape(negs, panels, W).transpose(1, 0, 2).reshape(-1, W)
    late = jnp.concatenate([w_out, neg_panels])
    plane = NY * NX
    lines = [[zz * plane + p for zz in range(NZ)] for p in range(plane)]
    planes = [[zz * plane + p for p in range(plane)] for zz in range(NZ)]
    late = lax.all_gather(late, "ctx", axis=0, axis_index_groups=lines)
    late, _ = lax.optimization_barrier((late, tok[1:3]))
    late = lax.all_gather(late, "ctx", axis=0, axis_index_groups=planes)
    late = late.reshape(CHIPS, -1, W)
    t_rows = target_emb.reshape(2, rows, -1)
    t_keep = lax.dynamic_index_in_dim(t_rows, u, 0, keepdims=False)
    t_send = swap_cores(lax.dynamic_index_in_dim(t_rows, 1 - u, 0, keepdims=False))

    def project(pieces):
        count = sum(p.shape[0] for p in pieces)
        return call(
            proj_kernel,
            "project",
            [((count, 2 * W), BF16)] * 2 + [((count, W), BF16)],
            [
                pltpu.VMEM((count, model + W), BF16),
                pltpu.VMEM((CHIPS, 2, model // (2 * CHIPS), 4 * W), BF16),
                pltpu.SemaphoreType.DMA((len(pieces),)),
                pltpu.SemaphoreType.DMA((2,)),
            ],
            [where, *pieces, w_mine, w_theirs],
            "s" + (len(pieces) + 2) * "h",
            2 * count * model * 4 * W,
        )

    gq_early, kv_early, marks_early = project(tok[:3])
    kv_early_theirs = swap_cores(kv_early)
    last, kv_early = lax.optimization_barrier((tok[3:], kv_early))
    gq_last, kv_last, marks_last = project(last)
    kv_last_theirs = swap_cores(kv_last)
    (gated,) = call(
        attend_kernel,
        "attend",
        [((CHIPS, rows, W), BF16)],
        [],
        [where, gq_early, gq_last, kv_early, kv_last, kv_early_theirs, kv_last_theirs]
        + [marks_early, marks_last],
        "s" + 8 * "v",
        8 * events * events * W,
    )
    late_own, _ = lax.optimization_barrier((late, gated))
    late_other = swap_cores(late_own)
    split = w_out.shape[0]
    nn = sum(
        jnp.sum(jnp.square(n[:, split:].astype(F32)).reshape(CHIPS, panels, negs, W), axis=(1, 3))
        for n in (late_own, late_other)
    )
    order = [zz * plane + p for p in range(plane) for zz in range(NZ)]
    n_ids = neg_ids.reshape(CHIPS, -1)[jnp.array(order)].reshape(1, -1)
    gated = lax.all_to_all(gated, "ctx", 0, 0, tiled=True)
    h_keep, h_send = call(
        hidden_kernel,
        "hidden",
        [((rows, half), BF16)] * 2,
        [
            pltpu.VMEM((rows, model), BF16),
            pltpu.VMEM((rows, model), BF16),
            pltpu.VMEM((2, half, model), BF16),
            pltpu.SemaphoreType.DMA((2 * CHIPS,)),
        ],
        [where, gated, late_own, late_other, mine],
        "svhhv",
        2 * rows * model * model,
    )
    h_theirs = swap_cores(h_send)
    (loss,) = call(
        loss_kernel,
        "loss",
        [((rows, 1), F32)],
        [
            pltpu.VMEM((2, CHIPS, negs, half), BF16),
            pltpu.SemaphoreType.DMA((2 * panels,)),
        ],
        [
            h_keep,
            h_send,
            t_keep,
            t_send,
            target_ids[:, None],
            n_ids,
            nn.reshape(1, -1),
            late_own,
            late_other,
        ],
        "vvvvvvvhh",
        2 * rows * model * neg_ids.shape[0],
    )
    hidden = jnp.where(
        u == 0,
        jnp.concatenate([h_keep, h_theirs]),
        jnp.concatenate([h_theirs, h_keep]),
    )
    return hidden, loss.reshape(-1)


def shards(tokens, w_proj, *rest):
    n_ctx, n_tp = lax.axis_size("ctx"), lax.axis_size("tp")
    heads = w_proj.shape[2] * n_tp // HEAD_DIM
    plan = head_shards if (n_ctx, n_tp, heads) == (CHIPS, 2, CHIPS) else general_shards
    return plan(tokens, w_proj, *rest)


def solution(mesh):
    placed = (
        P("ctx", None),
        P("ctx", None, "tp"),
        P("tp", "ctx"),
        P("ctx"),
        P("ctx", "tp"),
        P(),
        P("ctx", "tp"),
        P(("ctx", "tp")),
    )
    return jax.shard_map(
        shards,
        mesh=mesh,
        in_specs=placed,
        out_specs=(P("ctx", "tp"), P(("ctx", "tp"))),
        check_vma=False,
    )
```

```python
import jax
import jax.numpy as jnp
from jax import lax
from jax.experimental import pallas as pl
from jax.experimental.pallas import tpu as pltpu
from jax.sharding import PartitionSpec as P

HEAD_DIM = 128
VMEM_LIMIT = 48 * 1024 * 1024
BF16 = jnp.bfloat16
F32 = jnp.float32


def attend_piece(q_group, q_pos, k_piece, v_piece, p_piece):
    heads = q_group.shape[1]
    width = q_group.shape[2]
    key_heads = k_piece.reshape(k_piece.shape[0], heads, width)
    value_heads = v_piece.reshape(v_piece.shape[0], heads, width)
    scores = jnp.einsum(
        "thd,khd->htk", q_group, key_heads, preferred_element_type=jnp.float32
    ) * width ** (-0.5)
    visible = p_piece[None, None, :] <= q_pos[None, :, None]
    weight = jnp.where(visible, jax.nn.silu(scores), 0.0).astype(jnp.bfloat16)
    return jnp.einsum("htk,khd->thd", weight, value_heads, preferred_element_type=jnp.float32)


def general_shards(
    tokens, w_proj, w_out, positions, neg_emb, neg_ids, target_emb, target_ids
):
    tok_rows = tokens.shape[0]
    head_cols = w_proj.shape[2]
    local_heads = head_cols // HEAD_DIM
    proj_sum = jnp.einsum(
        "td,dfh->tfh",
        tokens,
        lax.all_gather(w_proj, "ctx", axis=0, tiled=True),
        preferred_element_type=jnp.float32,
    )
    proj = jax.nn.silu(proj_sum).astype(jnp.bfloat16)
    gate = proj[:, 0].reshape(tok_rows, local_heads, HEAD_DIM)
    query = proj[:, 2].reshape(tok_rows, local_heads, HEAD_DIM)
    v_piece = lax.all_gather(proj[:, 1], "ctx", axis=0, tiled=True)
    k_piece = lax.all_gather(proj[:, 3], "ctx", axis=0, tiled=True)
    p_piece = lax.all_gather(positions, "ctx", axis=0, tiled=True)
    attn = attend_piece(query, positions, k_piece, v_piece, p_piece)
    normed = attn * lax.rsqrt(jnp.mean(attn * attn, axis=-1, keepdims=True) + 1e-06)
    gated = (normed * gate.astype(jnp.float32)).astype(jnp.bfloat16).reshape(tok_rows, head_cols)
    out_terms = jnp.dot(
        gated, lax.all_gather(w_out, "ctx", axis=1, tiled=True), preferred_element_type=jnp.float32
    )
    out_share = lax.psum_scatter(out_terms, "tp", scatter_dimension=1, tiled=True)
    feat_cols = out_share.shape[1]
    own_tokens = lax.dynamic_slice_in_dim(tokens, lax.axis_index("tp") * feat_cols, feat_cols, 1)
    hidden = (own_tokens.astype(jnp.float32) + out_share).astype(jnp.bfloat16)
    piece = lax.all_gather(neg_emb, "ctx", axis=0, tiled=True)
    panel_dots = lax.dot_general(
        hidden, piece, (((1,), (1,)), ((), ())), preferred_element_type=jnp.float32
    )
    panel_norms = jnp.sum(jnp.square(piece.astype(jnp.float32)), axis=1)
    hidden_f = hidden.astype(jnp.float32)
    target_f = target_emb.astype(jnp.float32)
    part_hh = jnp.sum(hidden_f * hidden_f, axis=1)
    part_he = jnp.sum(hidden_f * target_f, axis=1)
    part_ee = jnp.sum(target_f * target_f, axis=1)
    dots, hh_sum, he_sum, ee_sum = (
        lax.psum_scatter(panel_dots, "tp", scatter_dimension=0, tiled=True),
        lax.psum_scatter(part_hh, "tp", scatter_dimension=0, tiled=True),
        lax.psum_scatter(part_he, "tp", scatter_dimension=0, tiled=True),
        lax.psum_scatter(part_ee, "tp", scatter_dimension=0, tiled=True),
    )
    neg_sq = lax.psum(panel_norms, "tp")
    pos_logit = he_sum / jnp.sqrt(hh_sum + 1e-06) / jnp.sqrt(ee_sum + 1e-06) / 0.05
    neg_logit = dots / jnp.sqrt(hh_sum + 1e-06)[:, None] / jnp.sqrt(neg_sq + 1e-06)[None, :] / 0.05
    keep_mask = neg_ids[None, :] != target_ids[:, None]
    total_mass = jnp.exp(pos_logit) + jnp.sum(jnp.where(keep_mask, jnp.exp(neg_logit), 0.0), axis=1)
    loss = jnp.log(total_mass) - pos_logit
    return (hidden, loss)


NZ, NY, NX = 4, 2, 2
CHIPS = NZ * NY * NX
PLANE = [(by, bx) for by in range(NY) for bx in range(NX)]
SWAP = [(0, 1), (1, 0)]
W = HEAD_DIM
ACROSS = (((1,), (1,)), ((), ()))


def chip_at(z, y, x):
    return (z * NY + y) * NX + x


def coords(c):
    return c // (NY * NX), (c // NX) % NY, c % NX


def relative_chip(c, by, bx, s):
    z, y, x = coords(c)
    return chip_at((z + NZ - s) % NZ, y ^ by, x ^ bx)


def z_shift(s):
    return [(c, relative_chip(c, 0, 0, NZ - s)) for c in range(CHIPS)]


def flip(by, bx):
    return [(c, relative_chip(c, by, bx, 0)) for c in range(CHIPS)]


def hop(value, perm):
    return lax.ppermute(value, "ctx", perm)


def swap_cores(value):
    return lax.ppermute(value, "tp", SWAP)


def pick_row(value, at):
    return lax.dynamic_index_in_dim(value, at, 0, keepdims=False)


def after(values, *others):
    return lax.optimization_barrier((values, others))[0]


def along_z(own):
    return [own] + [hop(own, z_shift(s)) for s in range(1, NZ)]


def beside(near):
    return [near, hop(near, flip(0, 1)), hop(near, flip(1, 0))]


def across(near, beside_x, beside_y):
    half = near.shape[0] // 2
    first = hop(beside_x[:half], flip(1, 0))
    second = hop(beside_y[half:], flip(0, 1))
    return [near, beside_x, beside_y, first, second]


def heads_in_plane(w_proj, y, x):
    plane = NY * NX
    heads = w_proj.reshape(-1, 4, 2, plane, W).transpose(3, 2, 0, 1, 4)
    heads = heads.reshape(plane, 2, -1, 4 * W)
    out = []
    for by, bx in PLANE:
        piece = pick_row(heads, (y ^ by) * NX + (x ^ bx))
        if (by, bx) == PLANE[-1]:
            piece = after(piece, out[1])
        out.append(piece if (by, bx) == (0, 0) else hop(piece, flip(by, bx)))
    return jnp.stack(out, 1)


def heads_along_z(heads, z):
    arrived = []
    for e in range(2):
        perm = []
        for src in range(CHIPS):
            sz, sy, sx = coords(src)
            for t in range(2):
                dst = chip_at(2 * t + (e ^ (sz & 1)), sy, sx)
                perm.append((2 * src + t, 2 * dst + (sz >> 1)))
        arrived.append(lax.ppermute(pick_row(heads, e ^ (z & 1)), ("ctx", "tp"), perm))
    return jnp.stack(arrived)


def silu(v):
    return 0.5 * v * (1.0 + jnp.tanh(0.5 * v))


def run_copies(copies):
    for copy in copies:
        copy.start()
    for copy in copies:
        copy.wait()


def proj_kernel(where, *refs):
    count = len(refs) - 9
    tok, (w_own, w_other) = refs[:count], refs[count : count + 2]
    gate_query, value_key, marks, x_all, w_all, tok_sem, w_sem = refs[count + 2 :]
    z, y, x, u = (where[i] for i in range(4))
    copies, base = [], 0
    for side, (half, src) in enumerate(((u, w_own), (1 - u, w_other))):
        for e in range(2):
            for k, (by, bx) in enumerate(PLANE):
                block = chip_at(2 * half + (e ^ (z & 1)), y ^ by, x ^ bx)
                sem = w_sem.at[(side * 2 + e) * len(PLANE) + k]
                copies.append(pltpu.make_async_copy(src.at[e, k], w_all.at[block], sem))
    for i, ref in enumerate(tok):
        rows = pl.ds(base, ref.shape[0])
        copies.append(pltpu.make_async_copy(ref, x_all.at[rows, :], tok_sem.at[i]))
        base += ref.shape[0]
    run_copies(copies)
    weights = w_all[...].reshape(-1, w_all.shape[-1])
    model = weights.shape[0]
    total = jnp.dot(x_all[:, :model], weights, preferred_element_type=F32)
    proj = silu(total).astype(BF16)
    gate_query[:, :W] = proj[:, :W]
    value_key[:, :W] = proj[:, W : 2 * W]
    gate_query[:, W:] = proj[:, 2 * W : 3 * W]
    value_key[:, W:] = proj[:, 3 * W :]
    marks[...] = x_all[:, model:]


def pick_columns(*weights):
    lane = lax.broadcasted_iota(jnp.int32, (8, W), 1)
    line = lax.broadcasted_iota(jnp.int32, (8, W), 0)
    pick = jnp.zeros((8, W), F32)
    for i, row in enumerate(weights):
        for at, weight in row.items():
            pick = jnp.where((line == i) & (lane == at), weight, pick)
    return pick.astype(BF16)


def attend_kernel(*refs):
    gate_query, kv_own, kv_other, marks = refs[:2], refs[2:4], refs[4:6], refs[6:8]
    gated = refs[8]
    pick = pick_columns({0: 128.0, 1: 1.0}, {2: 128.0, 3: 1.0})
    piece = gated.shape[2]
    tile = NZ * piece
    groups = []
    for group in range(2):
        key_pos = lax.dot_general(pick, marks[group][...], ACROSS, preferred_element_type=F32)
        groups.append((kv_own[group], key_pos[0:1]))
        groups.append((kv_other[group], key_pos[1:2]))
    for k in range(len(PLANE)):
        group, base = (0, k * tile) if k < len(PLANE) - 1 else (1, 0)
        span = pl.ds(base, tile)
        query = gate_query[group][span, W:]
        q_pos = lax.dot_general(
            marks[group][span, :], pick, ACROSS, preferred_element_type=F32
        )[:, :1]
        attn = jnp.zeros((tile, W), F32)
        for kv, key_pos in groups:
            scores = lax.dot_general(
                query, kv[:, W:], ACROSS, preferred_element_type=F32
            ) * W ** (-0.5)
            weight = jnp.where(key_pos <= q_pos, silu(scores), 0.0).astype(BF16)
            attn += jnp.dot(weight, kv[:, :W], preferred_element_type=F32)
        normed = attn * lax.rsqrt(jnp.mean(attn * attn, axis=-1, keepdims=True) + 1e-06)
        out = (normed * gate_query[group][span, :W].astype(F32)).astype(BF16)
        for s in range(NZ):
            gated[s, k] = out[s * piece : (s + 1) * piece]


def hidden_kernel(where, *refs):
    n = len(PLANE)
    gated, w_own, w_other, tok = refs[:n], refs[n], refs[n + 1], refs[n + 2 : 2 * n + 2]
    hidden, g_all, t_all, w_all, sems = refs[-5:]
    z, y, x, u = (where[i] for i in range(4))
    c = chip_at(z, y, x)
    rows = hidden.shape[1]
    half = w_all.shape[1]
    copies = []
    for s in range(NZ):
        cols = pl.ds(s * W, W)
        for side, src in enumerate((w_own, w_other)):
            copies.append((src.at[s], w_all.at[side, :, cols]))
        block = relative_chip(c, 0, 0, s)
        from_cols = pl.ds(pl.multiple_of(block * W, W), W)
        for k in range(n):
            copies.append((tok[k].at[pl.ds(0, rows), from_cols], t_all.at[k, :, cols]))
    copies = [pltpu.make_async_copy(a, b, sems.at[i]) for i, (a, b) in enumerate(copies)]
    for copy in copies:
        copy.start()
    for k, (by, bx) in enumerate(PLANE):
        for s in range(NZ):
            head = relative_chip(c, by, bx, NZ - s)
            cols = pl.ds(pl.multiple_of(head * W, W), W)
            for j, (jy, jx) in enumerate(PLANE):
                block = (jy ^ by) * NX + (jx ^ bx)
                g_all[block * rows : (block + 1) * rows, cols] = gated[k][s, j]
    for copy in copies:
        copy.wait()
    total = 0.0
    for side, at in enumerate((u, 1 - u)):
        part = g_all[:, pl.ds(pl.multiple_of(at * half, half), half)]
        total += jnp.dot(part, w_all[side], preferred_element_type=F32)
    for k in range(n):
        for s in range(NZ):
            term = total[k * rows : (k + 1) * rows, s * W : (s + 1) * W]
            cols = pl.ds(pl.multiple_of(((z + NZ - s) % NZ) * W, W), W)
            hidden[k, :, cols] = (t_all[k, :, s * W : (s + 1) * W].astype(F32) + term).astype(BF16)


def order_kernel(where, *refs):
    pieces, (keep, send, h_all) = refs[: len(PLANE)], refs[len(PLANE) :]
    y, x, u = (where[i] for i in range(1, 4))
    half = keep.shape[1]
    for (by, bx), ref in zip(PLANE, pieces):
        for at in range(NZ):
            block = chip_at(at, y ^ by, x ^ bx)
            h_all[:, pl.ds(pl.multiple_of(block * W, W), W)] = ref[:, at * W : (at + 1) * W]
    keep[...] = h_all[:, pl.ds(pl.multiple_of(u * half, half), half)]
    send[...] = h_all[:, pl.ds(pl.multiple_of((1 - u) * half, half), half)]


def loss_kernel(h_keep, h_send, t_keep, t_send, t_ids, n_own, n_other, loss, n_all, sems):
    keep, send = h_keep[...], h_send[...]
    half = keep.shape[1]
    copies = []
    for side, src in enumerate((n_own, n_other)):
        copies.append(pltpu.make_async_copy(src, n_all.at[side], sems.at[side]))
    for copy in copies:
        copy.start()
    hh = he = ee = 0.0
    for part, ref in ((keep, t_keep), (send, t_send)):
        h_f, t_f = part.astype(F32), ref[...].astype(F32)
        hh += jnp.sum(h_f * h_f, axis=1, keepdims=True)
        he += jnp.sum(h_f * t_f, axis=1, keepdims=True)
        ee += jnp.sum(t_f * t_f, axis=1, keepdims=True)
    h_scale = lax.rsqrt(hh + 1e-06) * 20.0
    pos_logit = he * lax.rsqrt(ee + 1e-06) * h_scale
    for copy in copies:
        copy.wait()
    pick = pick_columns({0: 1.0, 1: 1.0, 2: 1.0}, {3: 256.0, 4: 1.0})
    dots, read = 0.0, []
    for side, part in enumerate((keep, send)):
        neg, marks = n_all[side, :, :half], n_all[side, :, half:]
        dots += lax.dot_general(part, neg, ACROSS, preferred_element_type=F32)
        read.append(lax.dot_general(pick, marks, ACROSS, preferred_element_type=F32))
    nn = read[0][0:1] + read[1][0:1]
    n_ids = read[0][1:2]
    neg_logit = dots * h_scale * lax.rsqrt(nn + 1e-06)
    mass = jnp.where(n_ids != t_ids[...].astype(F32), jnp.exp(neg_logit), 0.0)
    total = jnp.exp(pos_logit) + jnp.sum(mass, axis=1, keepdims=True)
    loss[...] = jnp.log(total) - pos_logit


def call(kernel, name, outs, scratch, args, places, flops):
    space = {"s": pltpu.SMEM, "v": pltpu.VMEM, "h": pl.ANY}
    moved = sum(a.size * a.dtype.itemsize for a in args)
    return pl.pallas_call(
        kernel,
        out_shape=[jax.ShapeDtypeStruct(shape, dtype) for shape, dtype in outs],
        in_specs=[pl.BlockSpec(memory_space=space[p]) for p in places],
        out_specs=[pl.BlockSpec(memory_space=pltpu.VMEM)] * len(outs),
        scratch_shapes=scratch,
        compiler_params=pltpu.CompilerParams(vmem_limit_bytes=VMEM_LIMIT),
        cost_estimate=pl.CostEstimate(flops=flops, bytes_accessed=moved, transcendentals=0),
        name=name,
    )(*args)


def whole_parts(value, base):
    return [(value // base).astype(BF16), (value % base).astype(BF16)]


def float_parts(value):
    parts = []
    for _ in range(3):
        parts.append(lax.reduce_precision(value, 8, 7))
        value = value - parts[-1]
    return [part.astype(BF16) for part in parts]


def with_marks(rows, marks):
    marks = jnp.stack(marks, 1)
    marks = jnp.pad(marks, ((0, 0), (0, W - marks.shape[1])))
    return jnp.concatenate([rows, marks], 1)


def head_shards(
    tokens, w_proj, w_out, positions, neg_emb, neg_ids, target_emb, target_ids
):
    c, u = lax.axis_index("ctx"), lax.axis_index("tp")
    z, y, x = coords(c)
    where = jnp.stack([z, y, x, u]).astype(jnp.int32)
    model = tokens.shape[1]
    rows = tokens.shape[0] // 2
    events = rows * CHIPS
    half = model // 2
    negs = neg_emb.shape[0]
    plane = len(PLANE)

    mine = lax.dynamic_slice_in_dim(tokens, u * rows, rows, 0)
    p_own = lax.dynamic_slice_in_dim(positions, u * rows, rows, 0)
    p_other = lax.dynamic_slice_in_dim(positions, (1 - u) * rows, rows, 0)
    mine = with_marks(mine, whole_parts(p_own, 128) + whole_parts(p_other, 128))
    near = jnp.concatenate(along_z(mine))

    w_plane, near = lax.optimization_barrier((heads_in_plane(w_proj, y, x), near))
    tok = across(*beside(near))
    w_mine = heads_along_z(w_plane, z)
    w_theirs = swap_cores(w_mine)

    own_ids = lax.dynamic_slice_in_dim(neg_ids, c * negs, negs, 0)
    norms = jnp.sum(jnp.square(neg_emb.astype(F32)), axis=1)
    neg = with_marks(neg_emb, float_parts(norms) + whole_parts(own_ids, 256))
    neg_near = jnp.concatenate(along_z(after(neg, w_mine)))
    out_own = along_z(after(w_out, neg_near))
    neg_beside = beside(after(neg_near, tok))
    t_rows = target_emb.reshape(2, rows, -1)
    t_keep = pick_row(t_rows, u)
    t_send = swap_cores(pick_row(t_rows, 1 - u))

    def project(pieces):
        count = sum(p.shape[0] for p in pieces)
        return call(
            proj_kernel,
            "project",
            [((count, 2 * W), BF16)] * 2 + [((count, W), BF16)],
            [
                pltpu.VMEM((count, model + W), BF16),
                pltpu.VMEM((CHIPS, model // CHIPS, 4 * W), BF16),
                pltpu.SemaphoreType.DMA((len(pieces),)),
                pltpu.SemaphoreType.DMA((CHIPS,)),
            ],
            [where, *pieces, w_mine, w_theirs],
            "s" + (len(pieces) + 2) * "h",
            2 * count * model * 4 * W,
        )

    gq_early, kv_early, marks_early = project(tok[:3])
    kv_early_theirs = swap_cores(kv_early)
    gq_last, kv_last, marks_last = project(after(tok[3:], kv_early))
    kv_last_theirs = swap_cores(kv_last)
    (gated,) = call(
        attend_kernel,
        "attend",
        [((NZ, plane, rows, W), BF16)],
        [],
        [gq_early, gq_last, kv_early, kv_last, kv_early_theirs, kv_last_theirs]
        + [marks_early, marks_last],
        8 * "v",
        8 * events * events * W,
    )
    gated = jnp.stack([gated[0]] + [hop(gated[s], z_shift(NZ - s)) for s in range(1, NZ)])
    neg_own = jnp.concatenate(across(*after(neg_beside, gated)))
    neg_other = swap_cores(neg_own)
    out_own = after(jnp.stack(out_own), gated)
    out_other = swap_cores(out_own)
    gated = [gated] + [hop(gated, flip(by, bx)) for by, bx in PLANE[1:]]
    (hidden,) = call(
        hidden_kernel,
        "hidden",
        [((plane, rows, NZ * W), BF16)],
        [
            pltpu.VMEM((plane * rows, model), BF16),
            pltpu.VMEM((plane, rows, NZ * W), BF16),
            pltpu.VMEM((2, half, NZ * W), BF16),
            pltpu.SemaphoreType.DMA((NZ * (2 + plane),)),
        ],
        [where, *gated, out_own, out_other, *tok[:4]],
        "s" + 4 * "v" + 6 * "h",
        2 * plane * rows * model * NZ * W,
    )
    pieces = [hidden[0]] + [hop(hidden[k], flip(*PLANE[k])) for k in range(1, plane)]
    h_keep, h_send = call(
        order_kernel,
        "order",
        [((rows, half), BF16)] * 2,
        [pltpu.VMEM((rows, model), BF16)],
        [where, *pieces],
        "svvvv",
        0,
    )
    h_theirs = swap_cores(h_send)
    (loss,) = call(
        loss_kernel,
        "loss",
        [((rows, 1), F32)],
        [
            pltpu.VMEM((2, CHIPS * negs, half + W), BF16),
            pltpu.SemaphoreType.DMA((2,)),
        ],
        [h_keep, h_send, t_keep, t_send, target_ids[:, None], neg_own, neg_other],
        "vvvvvhh",
        2 * rows * model * neg_ids.shape[0],
    )
    hidden = jnp.where(
        u == 0,
        jnp.concatenate([h_keep, h_theirs]),
        jnp.concatenate([h_theirs, h_keep]),
    )
    return hidden, loss.reshape(-1)


def shards(tokens, w_proj, *rest):
    n_ctx, n_tp = lax.axis_size("ctx"), lax.axis_size("tp")
    heads = w_proj.shape[2] * n_tp // HEAD_DIM
    plan = head_shards if (n_ctx, n_tp, heads) == (CHIPS, 2, CHIPS) else general_shards
    return plan(tokens, w_proj, *rest)


def solution(mesh):
    placed = (
        P("ctx", None),
        P("ctx", None, "tp"),
        P("tp", "ctx"),
        P("ctx"),
        P("ctx", "tp"),
        P(),
        P("ctx", "tp"),
        P(("ctx", "tp")),
    )
    return jax.shard_map(
        shards,
        mesh=mesh,
        in_specs=placed,
        out_specs=(P("ctx", "tp"), P(("ctx", "tp"))),
        check_vma=False,
    )
```

```python
import jax
import jax.numpy as jnp
from jax import lax
from jax.experimental import pallas as pl
from jax.experimental.pallas import tpu as pltpu
from jax.sharding import PartitionSpec as P

HEAD_DIM = 128
VMEM_LIMIT = 48 * 1024 * 1024
BF16 = jnp.bfloat16
F32 = jnp.float32


def attend_piece(q_group, q_pos, k_piece, v_piece, p_piece):
    heads = q_group.shape[1]
    width = q_group.shape[2]
    key_heads = k_piece.reshape(k_piece.shape[0], heads, width)
    value_heads = v_piece.reshape(v_piece.shape[0], heads, width)
    scores = jnp.einsum(
        "thd,khd->htk", q_group, key_heads, preferred_element_type=jnp.float32
    ) * width ** (-0.5)
    visible = p_piece[None, None, :] <= q_pos[None, :, None]
    weight = jnp.where(visible, jax.nn.silu(scores), 0.0).astype(jnp.bfloat16)
    return jnp.einsum("htk,khd->thd", weight, value_heads, preferred_element_type=jnp.float32)


def general_shards(
    tokens, w_proj, w_out, positions, neg_emb, neg_ids, target_emb, target_ids
):
    tok_rows = tokens.shape[0]
    head_cols = w_proj.shape[2]
    local_heads = head_cols // HEAD_DIM
    proj_sum = jnp.einsum(
        "td,dfh->tfh",
        tokens,
        lax.all_gather(w_proj, "ctx", axis=0, tiled=True),
        preferred_element_type=jnp.float32,
    )
    proj = jax.nn.silu(proj_sum).astype(jnp.bfloat16)
    gate = proj[:, 0].reshape(tok_rows, local_heads, HEAD_DIM)
    query = proj[:, 2].reshape(tok_rows, local_heads, HEAD_DIM)
    v_piece = lax.all_gather(proj[:, 1], "ctx", axis=0, tiled=True)
    k_piece = lax.all_gather(proj[:, 3], "ctx", axis=0, tiled=True)
    p_piece = lax.all_gather(positions, "ctx", axis=0, tiled=True)
    attn = attend_piece(query, positions, k_piece, v_piece, p_piece)
    normed = attn * lax.rsqrt(jnp.mean(attn * attn, axis=-1, keepdims=True) + 1e-06)
    gated = (normed * gate.astype(jnp.float32)).astype(jnp.bfloat16).reshape(tok_rows, head_cols)
    out_terms = jnp.dot(
        gated, lax.all_gather(w_out, "ctx", axis=1, tiled=True), preferred_element_type=jnp.float32
    )
    out_share = lax.psum_scatter(out_terms, "tp", scatter_dimension=1, tiled=True)
    feat_cols = out_share.shape[1]
    own_tokens = lax.dynamic_slice_in_dim(tokens, lax.axis_index("tp") * feat_cols, feat_cols, 1)
    hidden = (own_tokens.astype(jnp.float32) + out_share).astype(jnp.bfloat16)
    piece = lax.all_gather(neg_emb, "ctx", axis=0, tiled=True)
    panel_dots = lax.dot_general(
        hidden, piece, (((1,), (1,)), ((), ())), preferred_element_type=jnp.float32
    )
    panel_norms = jnp.sum(jnp.square(piece.astype(jnp.float32)), axis=1)
    hidden_f = hidden.astype(jnp.float32)
    target_f = target_emb.astype(jnp.float32)
    part_hh = jnp.sum(hidden_f * hidden_f, axis=1)
    part_he = jnp.sum(hidden_f * target_f, axis=1)
    part_ee = jnp.sum(target_f * target_f, axis=1)
    dots, hh_sum, he_sum, ee_sum = (
        lax.psum_scatter(panel_dots, "tp", scatter_dimension=0, tiled=True),
        lax.psum_scatter(part_hh, "tp", scatter_dimension=0, tiled=True),
        lax.psum_scatter(part_he, "tp", scatter_dimension=0, tiled=True),
        lax.psum_scatter(part_ee, "tp", scatter_dimension=0, tiled=True),
    )
    neg_sq = lax.psum(panel_norms, "tp")
    pos_logit = he_sum / jnp.sqrt(hh_sum + 1e-06) / jnp.sqrt(ee_sum + 1e-06) / 0.05
    neg_logit = dots / jnp.sqrt(hh_sum + 1e-06)[:, None] / jnp.sqrt(neg_sq + 1e-06)[None, :] / 0.05
    keep_mask = neg_ids[None, :] != target_ids[:, None]
    total_mass = jnp.exp(pos_logit) + jnp.sum(jnp.where(keep_mask, jnp.exp(neg_logit), 0.0), axis=1)
    loss = jnp.log(total_mass) - pos_logit
    return (hidden, loss)


NZ, NY, NX = 4, 2, 2
CHIPS = NZ * NY * NX
PLANE = [(by, bx) for by in range(NY) for bx in range(NX)]
SWAP = [(0, 1), (1, 0)]
W = HEAD_DIM
ACROSS = (((1,), (1,)), ((), ()))


def chip_at(z, y, x):
    return (z * NY + y) * NX + x


def coords(c):
    return c // (NY * NX), (c // NX) % NY, c % NX


def relative_chip(c, by, bx, s):
    z, y, x = coords(c)
    return chip_at((z + NZ - s) % NZ, y ^ by, x ^ bx)


def z_shift(s):
    return [(c, relative_chip(c, 0, 0, NZ - s)) for c in range(CHIPS)]


def flip(by, bx):
    return [(c, relative_chip(c, by, bx, 0)) for c in range(CHIPS)]


def hop(value, perm):
    return lax.ppermute(value, "ctx", perm)


def swap_cores(value):
    return lax.ppermute(value, "tp", SWAP)


def pick_row(value, at):
    return lax.dynamic_index_in_dim(value, at, 0, keepdims=False)


def after(values, *others):
    return lax.optimization_barrier((values, others))[0]


def along_z(own):
    return [own] + [hop(own, z_shift(s)) for s in range(1, NZ)]


def in_plane(low, high):
    to_x, to_y = flip(0, 1), flip(1, 0)
    low_x, high_y = hop(low, to_x), hop(high, to_y)
    high_x, low_y = hop(high, to_x), hop(low, to_y)
    return [low, high, low_x, high_x, low_y, high_y, hop(low_x, to_y), hop(high_y, to_x)]


def heads_in_plane(w_proj, y, x):
    plane = NY * NX
    heads = w_proj.reshape(-1, 4, 2, plane, W).transpose(3, 2, 0, 1, 4)
    heads = heads.reshape(plane, 2, -1, 4 * W)
    out = jnp.zeros((2, plane, *heads.shape[2:]), heads.dtype)
    first = None
    for by, bx in PLANE:
        spot = (y ^ by) * NX + (x ^ bx)
        piece = pick_row(heads, spot)
        if (by, bx) == PLANE[-1]:
            piece = after(piece, first)
        if (by, bx) != (0, 0):
            piece = hop(piece, flip(by, bx))
            first = piece if first is None else first
        out = lax.dynamic_update_slice_in_dim(out, piece[:, None], spot, 1)
    return out


def heads_along_z(heads, z):
    arrived = []
    for e in range(2):
        perm = []
        for src in range(CHIPS):
            sz, sy, sx = coords(src)
            for t in range(2):
                dst = chip_at(2 * t + (e ^ (sz & 1)), sy, sx)
                perm.append((2 * src + t, 2 * dst + (sz >> 1)))
        arrived.append(lax.ppermute(pick_row(heads, e ^ (z & 1)), ("ctx", "tp"), perm))
    rows = jnp.where(z % 2 == 0, jnp.stack(arrived), jnp.stack(arrived[::-1]))
    return rows.reshape(-1, rows.shape[-1])


def silu(v):
    return 0.5 * v * (1.0 + jnp.tanh(0.5 * v))


def run_copies(copies):
    for copy in copies:
        copy.start()
    for copy in copies:
        copy.wait()


def proj_kernel(where, *refs):
    count = len(refs) - 9
    tok, (w_own, w_other) = refs[:count], refs[count : count + 2]
    gate_query, value_key, marks, x_all, w_all, tok_sem, w_sem = refs[count + 2 :]
    u = where[3]
    copies, base = [], 0
    half = w_own.shape[0]
    for side, (at, src) in enumerate(((u, w_own), (1 - u, w_other))):
        rows = pl.ds(pl.multiple_of(at * half, half), half)
        copies.append(pltpu.make_async_copy(src, w_all.at[rows, :], w_sem.at[side]))
    for i, ref in enumerate(tok):
        rows = pl.ds(base, ref.shape[0])
        copies.append(pltpu.make_async_copy(ref, x_all.at[rows, :], tok_sem.at[i]))
        base += ref.shape[0]
    run_copies(copies)
    model = w_all.shape[0]
    total = jnp.dot(x_all[:, :model], w_all[...], preferred_element_type=F32)
    proj = silu(total).astype(BF16)
    gate_query[:, :W] = proj[:, :W]
    value_key[:, :W] = proj[:, W : 2 * W]
    gate_query[:, W:] = proj[:, 2 * W : 3 * W]
    value_key[:, W:] = proj[:, 3 * W :]
    marks[...] = x_all[:, model:]


def pick_columns(*weights):
    lane = lax.broadcasted_iota(jnp.int32, (8, W), 1)
    line = lax.broadcasted_iota(jnp.int32, (8, W), 0)
    pick = jnp.zeros((8, W), F32)
    for i, row in enumerate(weights):
        for at, weight in row.items():
            pick = jnp.where((line == i) & (lane == at), weight, pick)
    return pick.astype(BF16)


def attend_kernel(*refs):
    gate_query, kv_own, kv_other, marks = refs[:2], refs[2:4], refs[4:6], refs[6:8]
    gated = refs[8]
    pick = pick_columns({0: 128.0, 1: 1.0}, {2: 128.0, 3: 1.0})
    piece = gated.shape[2]
    tile = NZ * piece
    groups = []
    for group in range(2):
        key_pos = lax.dot_general(pick, marks[group][...], ACROSS, preferred_element_type=F32)
        groups.append((kv_own[group], key_pos[0:1]))
        groups.append((kv_other[group], key_pos[1:2]))
    for k in range(len(PLANE)):
        group, base = (0, k * tile) if k < len(PLANE) - 1 else (1, 0)
        span = pl.ds(base, tile)
        query = gate_query[group][span, W:]
        q_pos = lax.dot_general(
            marks[group][span, :], pick, ACROSS, preferred_element_type=F32
        )[:, :1]
        attn = jnp.zeros((tile, W), F32)
        for kv, key_pos in groups:
            scores = lax.dot_general(
                query, kv[:, W:], ACROSS, preferred_element_type=F32
            ) * W ** (-0.5)
            weight = jnp.where(key_pos <= q_pos, silu(scores), 0.0).astype(BF16)
            attn += jnp.dot(weight, kv[:, :W], preferred_element_type=F32)
        normed = attn * lax.rsqrt(jnp.mean(attn * attn, axis=-1, keepdims=True) + 1e-06)
        out = (normed * gate_query[group][span, :W].astype(F32)).astype(BF16)
        for s in range(NZ):
            gated[s, k] = out[s * piece : (s + 1) * piece]


def hidden_kernel(where, *refs):
    n = len(PLANE)
    gated, w_own, w_other, tok = refs[:n], refs[n], refs[n + 1], refs[n + 2 : 2 * n + 2]
    hidden, g_all, t_all, w_all, sems = refs[-5:]
    z, y, x, u = (where[i] for i in range(4))
    c = chip_at(z, y, x)
    rows = hidden.shape[1]
    half = w_all.shape[1]
    copies = []
    for s in range(NZ):
        cols = pl.ds(s * W, W)
        for side, src in enumerate((w_own, w_other)):
            copies.append((src.at[s], w_all.at[side, :, cols]))
        block = relative_chip(c, 0, 0, s)
        from_cols = pl.ds(pl.multiple_of(block * W, W), W)
        for k in range(n):
            copies.append((tok[k].at[pl.ds(0, rows), from_cols], t_all.at[k, :, cols]))
    copies = [pltpu.make_async_copy(a, b, sems.at[i]) for i, (a, b) in enumerate(copies)]
    for copy in copies:
        copy.start()
    for k, (by, bx) in enumerate(PLANE):
        for s in range(NZ):
            head = relative_chip(c, by, bx, NZ - s)
            cols = pl.ds(pl.multiple_of(head * W, W), W)
            for j, (jy, jx) in enumerate(PLANE):
                block = (jy ^ by) * NX + (jx ^ bx)
                g_all[block * rows : (block + 1) * rows, cols] = gated[k][s, j]
    for copy in copies:
        copy.wait()
    total = 0.0
    for side, at in enumerate((u, 1 - u)):
        part = g_all[:, pl.ds(pl.multiple_of(at * half, half), half)]
        total += jnp.dot(part, w_all[side], preferred_element_type=F32)
    for k in range(n):
        for s in range(NZ):
            term = total[k * rows : (k + 1) * rows, s * W : (s + 1) * W]
            cols = pl.ds(pl.multiple_of(((z + NZ - s) % NZ) * W, W), W)
            hidden[k, :, cols] = (t_all[k, :, s * W : (s + 1) * W].astype(F32) + term).astype(BF16)


def order_kernel(where, *refs):
    pieces, (keep, send, h_all) = refs[: len(PLANE)], refs[len(PLANE) :]
    y, x, u = (where[i] for i in range(1, 4))
    half = keep.shape[1]
    for (by, bx), ref in zip(PLANE, pieces):
        for at in range(NZ):
            block = chip_at(at, y ^ by, x ^ bx)
            h_all[:, pl.ds(pl.multiple_of(block * W, W), W)] = ref[:, at * W : (at + 1) * W]
    keep[...] = h_all[:, pl.ds(pl.multiple_of(u * half, half), half)]
    send[...] = h_all[:, pl.ds(pl.multiple_of((1 - u) * half, half), half)]


def loss_kernel(h_keep, h_send, t_keep, t_send, t_ids, n_own, n_other, loss, n_all, sems):
    keep, send = h_keep[...], h_send[...]
    half = keep.shape[1]
    copies = []
    for side, src in enumerate((n_own, n_other)):
        copies.append(pltpu.make_async_copy(src, n_all.at[side], sems.at[side]))
    for copy in copies:
        copy.start()
    hh = he = ee = 0.0
    for part, ref in ((keep, t_keep), (send, t_send)):
        h_f, t_f = part.astype(F32), ref[...].astype(F32)
        hh += jnp.sum(h_f * h_f, axis=1, keepdims=True)
        he += jnp.sum(h_f * t_f, axis=1, keepdims=True)
        ee += jnp.sum(t_f * t_f, axis=1, keepdims=True)
    h_scale = lax.rsqrt(hh + 1e-06) * 20.0
    pos_logit = he * lax.rsqrt(ee + 1e-06) * h_scale
    for copy in copies:
        copy.wait()
    pick = pick_columns({0: 1.0, 1: 1.0, 2: 1.0}, {3: 256.0, 4: 1.0})
    dots, read = 0.0, []
    for side, part in enumerate((keep, send)):
        neg, marks = n_all[side, :, :half], n_all[side, :, half:]
        dots += lax.dot_general(part, neg, ACROSS, preferred_element_type=F32)
        read.append(lax.dot_general(pick, marks, ACROSS, preferred_element_type=F32))
    nn = read[0][0:1] + read[1][0:1]
    n_ids = read[0][1:2]
    neg_logit = dots * h_scale * lax.rsqrt(nn + 1e-06)
    mass = jnp.where(n_ids != t_ids[...].astype(F32), jnp.exp(neg_logit), 0.0)
    total = jnp.exp(pos_logit) + jnp.sum(mass, axis=1, keepdims=True)
    loss[...] = jnp.log(total) - pos_logit


def call(kernel, name, outs, scratch, args, places, flops):
    space = {"s": pltpu.SMEM, "v": pltpu.VMEM, "h": pl.ANY}
    moved = sum(a.size * a.dtype.itemsize for a in args)
    return pl.pallas_call(
        kernel,
        out_shape=[jax.ShapeDtypeStruct(shape, dtype) for shape, dtype in outs],
        in_specs=[pl.BlockSpec(memory_space=space[p]) for p in places],
        out_specs=[pl.BlockSpec(memory_space=pltpu.VMEM)] * len(outs),
        scratch_shapes=scratch,
        compiler_params=pltpu.CompilerParams(vmem_limit_bytes=VMEM_LIMIT),
        cost_estimate=pl.CostEstimate(flops=flops, bytes_accessed=moved, transcendentals=0),
        name=name,
    )(*args)


def whole_parts(value, base):
    return [(value // base).astype(BF16), (value % base).astype(BF16)]


def float_parts(value):
    parts = []
    for _ in range(3):
        parts.append(lax.reduce_precision(value, 8, 7))
        value = value - parts[-1]
    return [part.astype(BF16) for part in parts]


def with_marks(rows, marks):
    marks = jnp.stack(marks, 1)
    marks = jnp.pad(marks, ((0, 0), (0, W - marks.shape[1])))
    return jnp.concatenate([rows, marks], 1)


def head_shards(
    tokens, w_proj, w_out, positions, neg_emb, neg_ids, target_emb, target_ids
):
    c, u = lax.axis_index("ctx"), lax.axis_index("tp")
    z, y, x = coords(c)
    where = jnp.stack([z, y, x, u]).astype(jnp.int32)
    model = tokens.shape[1]
    rows = tokens.shape[0] // 2
    events = rows * CHIPS
    half = model // 2
    negs = neg_emb.shape[0]
    plane = len(PLANE)

    mine = lax.dynamic_slice_in_dim(tokens, u * rows, rows, 0)
    p_own = lax.dynamic_slice_in_dim(positions, u * rows, rows, 0)
    p_other = lax.dynamic_slice_in_dim(positions, (1 - u) * rows, rows, 0)
    mine = with_marks(mine, whole_parts(p_own, 128) + whole_parts(p_other, 128))
    line = along_z(mine)

    w_plane, line = lax.optimization_barrier((heads_in_plane(w_proj, y, x), line))
    tok = in_plane(jnp.concatenate(line[:2]), jnp.concatenate(line[2:]))
    w_mine = heads_along_z(w_plane, z)
    w_mine = after(w_mine, tok[2:6])
    w_theirs = swap_cores(w_mine)

    own_ids = lax.dynamic_slice_in_dim(neg_ids, c * negs, negs, 0)
    norms = jnp.sum(jnp.square(neg_emb.astype(F32)), axis=1)
    neg = with_marks(neg_emb, float_parts(norms) + whole_parts(own_ids, 256))
    neg_own = lax.all_gather(neg, "ctx", axis=0, tiled=True)
    out_own = along_z(after(w_out, w_mine))
    t_rows = target_emb.reshape(2, rows, -1)
    t_keep = pick_row(t_rows, u)
    t_send = swap_cores(pick_row(t_rows, 1 - u))

    def project(pieces):
        count = sum(p.shape[0] for p in pieces)
        return call(
            proj_kernel,
            "project",
            [((count, 2 * W), BF16)] * 2 + [((count, W), BF16)],
            [
                pltpu.VMEM((count, model + W), BF16),
                pltpu.VMEM((model, 4 * W), BF16),
                pltpu.SemaphoreType.DMA((len(pieces),)),
                pltpu.SemaphoreType.DMA((2,)),
            ],
            [where, *pieces, w_mine, w_theirs],
            "s" + (len(pieces) + 2) * "h",
            2 * count * model * 4 * W,
        )

    gq_early, kv_early, marks_early = project(tok[:6])
    kv_early_theirs = swap_cores(kv_early)
    gq_last, kv_last, marks_last = project(after(tok[6:], kv_early))
    kv_last_theirs = swap_cores(kv_last)
    kv_last_theirs = after(kv_last_theirs, out_own)
    (gated,) = call(
        attend_kernel,
        "attend",
        [((NZ, plane, rows, W), BF16)],
        [],
        [gq_early, gq_last, kv_early, kv_last, kv_early_theirs, kv_last_theirs]
        + [marks_early, marks_last],
        8 * "v",
        8 * events * events * W,
    )
    gated = jnp.stack([gated[0]] + [hop(gated[s], z_shift(NZ - s)) for s in range(1, NZ)])
    neg_own = after(neg_own, gated)
    neg_other = swap_cores(neg_own)
    out_own = after(jnp.stack(out_own), gated)
    out_other = swap_cores(out_own)
    gated = [gated] + [hop(gated, flip(by, bx)) for by, bx in PLANE[1:]]
    (hidden,) = call(
        hidden_kernel,
        "hidden",
        [((plane, rows, NZ * W), BF16)],
        [
            pltpu.VMEM((plane * rows, model), BF16),
            pltpu.VMEM((plane, rows, NZ * W), BF16),
            pltpu.VMEM((2, half, NZ * W), BF16),
            pltpu.SemaphoreType.DMA((NZ * (2 + plane),)),
        ],
        [where, *gated, out_own, out_other, *tok[:5:2], tok[6]],
        "s" + 4 * "v" + 6 * "h",
        2 * plane * rows * model * NZ * W,
    )
    pieces = [hidden[0]] + [hop(hidden[k], flip(*PLANE[k])) for k in range(1, plane)]
    h_keep, h_send = call(
        order_kernel,
        "order",
        [((rows, half), BF16)] * 2,
        [pltpu.VMEM((rows, model), BF16)],
        [where, *pieces],
        "svvvv",
        0,
    )
    h_theirs = swap_cores(h_send)
    (loss,) = call(
        loss_kernel,
        "loss",
        [((rows, 1), F32)],
        [
            pltpu.VMEM((2, CHIPS * negs, half + W), BF16),
            pltpu.SemaphoreType.DMA((2,)),
        ],
        [h_keep, h_send, t_keep, t_send, target_ids[:, None], neg_own, neg_other],
        "vvvvvhh",
        2 * rows * model * neg_ids.shape[0],
    )
    hidden = jnp.where(
        u == 0,
        jnp.concatenate([h_keep, h_theirs]),
        jnp.concatenate([h_theirs, h_keep]),
    )
    return hidden, loss.reshape(-1)


def shards(tokens, w_proj, *rest):
    n_ctx, n_tp = lax.axis_size("ctx"), lax.axis_size("tp")
    heads = w_proj.shape[2] * n_tp // HEAD_DIM
    plan = head_shards if (n_ctx, n_tp, heads) == (CHIPS, 2, CHIPS) else general_shards
    return plan(tokens, w_proj, *rest)


def solution(mesh):
    placed = (
        P("ctx", None),
        P("ctx", None, "tp"),
        P("tp", "ctx"),
        P("ctx"),
        P("ctx", "tp"),
        P(),
        P("ctx", "tp"),
        P(("ctx", "tp")),
    )
    return jax.shard_map(
        shards,
        mesh=mesh,
        in_specs=placed,
        out_specs=(P("ctx", "tp"), P(("ctx", "tp"))),
        check_vma=False,
    )
```

```python
import jax
import jax.numpy as jnp
from jax import lax
from jax.experimental import pallas as pl
from jax.experimental.pallas import tpu as pltpu
from jax.sharding import PartitionSpec as P

HEAD_DIM = 128
VMEM_LIMIT = 48 * 1024 * 1024
BF16 = jnp.bfloat16
F32 = jnp.float32


def attend_piece(q_group, q_pos, k_piece, v_piece, p_piece):
    heads = q_group.shape[1]
    width = q_group.shape[2]
    key_heads = k_piece.reshape(k_piece.shape[0], heads, width)
    value_heads = v_piece.reshape(v_piece.shape[0], heads, width)
    scores = jnp.einsum(
        "thd,khd->htk", q_group, key_heads, preferred_element_type=jnp.float32
    ) * width ** (-0.5)
    visible = p_piece[None, None, :] <= q_pos[None, :, None]
    weight = jnp.where(visible, jax.nn.silu(scores), 0.0).astype(jnp.bfloat16)
    return jnp.einsum("htk,khd->thd", weight, value_heads, preferred_element_type=jnp.float32)


def general_shards(
    tokens, w_proj, w_out, positions, neg_emb, neg_ids, target_emb, target_ids
):
    tok_rows = tokens.shape[0]
    head_cols = w_proj.shape[2]
    local_heads = head_cols // HEAD_DIM
    proj_sum = jnp.einsum(
        "td,dfh->tfh",
        tokens,
        lax.all_gather(w_proj, "ctx", axis=0, tiled=True),
        preferred_element_type=jnp.float32,
    )
    proj = jax.nn.silu(proj_sum).astype(jnp.bfloat16)
    gate = proj[:, 0].reshape(tok_rows, local_heads, HEAD_DIM)
    query = proj[:, 2].reshape(tok_rows, local_heads, HEAD_DIM)
    v_piece = lax.all_gather(proj[:, 1], "ctx", axis=0, tiled=True)
    k_piece = lax.all_gather(proj[:, 3], "ctx", axis=0, tiled=True)
    p_piece = lax.all_gather(positions, "ctx", axis=0, tiled=True)
    attn = attend_piece(query, positions, k_piece, v_piece, p_piece)
    normed = attn * lax.rsqrt(jnp.mean(attn * attn, axis=-1, keepdims=True) + 1e-06)
    gated = (normed * gate.astype(jnp.float32)).astype(jnp.bfloat16).reshape(tok_rows, head_cols)
    out_terms = jnp.dot(
        gated, lax.all_gather(w_out, "ctx", axis=1, tiled=True), preferred_element_type=jnp.float32
    )
    out_share = lax.psum_scatter(out_terms, "tp", scatter_dimension=1, tiled=True)
    feat_cols = out_share.shape[1]
    own_tokens = lax.dynamic_slice_in_dim(tokens, lax.axis_index("tp") * feat_cols, feat_cols, 1)
    hidden = (own_tokens.astype(jnp.float32) + out_share).astype(jnp.bfloat16)
    piece = lax.all_gather(neg_emb, "ctx", axis=0, tiled=True)
    panel_dots = lax.dot_general(
        hidden, piece, (((1,), (1,)), ((), ())), preferred_element_type=jnp.float32
    )
    panel_norms = jnp.sum(jnp.square(piece.astype(jnp.float32)), axis=1)
    hidden_f = hidden.astype(jnp.float32)
    target_f = target_emb.astype(jnp.float32)
    part_hh = jnp.sum(hidden_f * hidden_f, axis=1)
    part_he = jnp.sum(hidden_f * target_f, axis=1)
    part_ee = jnp.sum(target_f * target_f, axis=1)
    dots, hh_sum, he_sum, ee_sum = (
        lax.psum_scatter(panel_dots, "tp", scatter_dimension=0, tiled=True),
        lax.psum_scatter(part_hh, "tp", scatter_dimension=0, tiled=True),
        lax.psum_scatter(part_he, "tp", scatter_dimension=0, tiled=True),
        lax.psum_scatter(part_ee, "tp", scatter_dimension=0, tiled=True),
    )
    neg_sq = lax.psum(panel_norms, "tp")
    pos_logit = he_sum / jnp.sqrt(hh_sum + 1e-06) / jnp.sqrt(ee_sum + 1e-06) / 0.05
    neg_logit = dots / jnp.sqrt(hh_sum + 1e-06)[:, None] / jnp.sqrt(neg_sq + 1e-06)[None, :] / 0.05
    keep_mask = neg_ids[None, :] != target_ids[:, None]
    total_mass = jnp.exp(pos_logit) + jnp.sum(jnp.where(keep_mask, jnp.exp(neg_logit), 0.0), axis=1)
    loss = jnp.log(total_mass) - pos_logit
    return (hidden, loss)


NZ, NY, NX = 4, 2, 2
CHIPS = NZ * NY * NX
PLANE = [(by, bx) for by in range(NY) for bx in range(NX)]
SWAP = [(0, 1), (1, 0)]
W = HEAD_DIM
ACROSS = (((1,), (1,)), ((), ()))


def chip_at(z, y, x):
    return (z * NY + y) * NX + x


def coords(c):
    return c // (NY * NX), (c // NX) % NY, c % NX


def relative_chip(c, by, bx, s):
    z, y, x = coords(c)
    return chip_at(z ^ s, y ^ by, x ^ bx)


def flip(by, bx, s=0):
    return [(c, relative_chip(c, by, bx, s)) for c in range(CHIPS)]


def hop(value, perm):
    return lax.ppermute(value, "ctx", perm)


def swap_cores(value):
    return lax.ppermute(value, "tp", SWAP)


def pick_row(value, at):
    return lax.dynamic_index_in_dim(value, at, 0, keepdims=False)


def after(values, *others):
    return lax.optimization_barrier((values, others))[0]


def pair_up(own):
    return jnp.concatenate([own, hop(own, flip(0, 0, 1))])


def heads_in_plane(w_proj, y, x):
    plane = NY * NX
    heads = w_proj.reshape(-1, 4, 2, plane, W).transpose(3, 2, 0, 1, 4)
    heads = heads.reshape(plane, 2, -1, 4 * W)
    out = jnp.zeros((2, plane, *heads.shape[2:]), heads.dtype)
    first = None
    for by, bx in PLANE:
        spot = (y ^ by) * NX + (x ^ bx)
        piece = pick_row(heads, spot)
        if (by, bx) == PLANE[-1]:
            piece = after(piece, first)
        if (by, bx) != (0, 0):
            piece = hop(piece, flip(by, bx))
            first = piece if first is None else first
        out = lax.dynamic_update_slice_in_dim(out, piece[:, None], spot, 1)
    return out


def heads_along_z(heads, z):
    arrived = []
    for e in range(2):
        perm = []
        for src in range(CHIPS):
            sz, sy, sx = coords(src)
            for t in range(2):
                dst = chip_at(2 * t + (e ^ (sz & 1)), sy, sx)
                perm.append((2 * src + t, 2 * dst + (sz >> 1)))
        arrived.append(lax.ppermute(pick_row(heads, e ^ (z & 1)), ("ctx", "tp"), perm))
    rows = jnp.where(z % 2 == 0, jnp.stack(arrived), jnp.stack(arrived[::-1]))
    return rows.reshape(-1, rows.shape[-1])


def silu(v):
    return 0.5 * v * (1.0 + jnp.tanh(0.5 * v))


def run_copies(copies):
    for copy in copies:
        copy.start()
    for copy in copies:
        copy.wait()


def proj_kernel(where, *refs):
    count = len(refs) - 9
    tok, (w_own, w_other) = refs[:count], refs[count : count + 2]
    gate_query, value_key, marks, x_all, w_all, tok_sem, w_sem = refs[count + 2 :]
    u = where[3]
    copies, base = [], 0
    half = w_own.shape[0]
    for side, (at, src) in enumerate(((u, w_own), (1 - u, w_other))):
        rows = pl.ds(pl.multiple_of(at * half, half), half)
        copies.append(pltpu.make_async_copy(src, w_all.at[rows, :], w_sem.at[side]))
    for i, ref in enumerate(tok):
        rows = pl.ds(base, ref.shape[0])
        copies.append(pltpu.make_async_copy(ref, x_all.at[rows, :], tok_sem.at[i]))
        base += ref.shape[0]
    run_copies(copies)
    model = w_all.shape[0]
    total = jnp.dot(x_all[:, :model], w_all[...], preferred_element_type=F32)
    proj = silu(total).astype(BF16)
    gate_query[:, :W] = proj[:, :W]
    value_key[:, :W] = proj[:, W : 2 * W]
    gate_query[:, W:] = proj[:, 2 * W : 3 * W]
    value_key[:, W:] = proj[:, 3 * W :]
    marks[...] = x_all[:, model:]


def pick_columns(*weights):
    lane = lax.broadcasted_iota(jnp.int32, (8, W), 1)
    line = lax.broadcasted_iota(jnp.int32, (8, W), 0)
    pick = jnp.zeros((8, W), F32)
    for i, row in enumerate(weights):
        for at, weight in row.items():
            pick = jnp.where((line == i) & (lane == at), weight, pick)
    return pick.astype(BF16)


def attend_kernel(*refs):
    gate_query, kv_own, kv_other, marks = refs[:2], refs[2:4], refs[4:6], refs[6:8]
    gated = refs[8]
    pick = pick_columns({0: 128.0, 1: 1.0}, {2: 128.0, 3: 1.0})
    piece = gated.shape[2]
    tile = NZ * piece
    groups = []
    for group in range(2):
        key_pos = lax.dot_general(pick, marks[group][...], ACROSS, preferred_element_type=F32)
        groups.append((kv_own[group], key_pos[0:1]))
        groups.append((kv_other[group], key_pos[1:2]))
    for k in range(len(PLANE)):
        group, base = (0, k * tile) if k < len(PLANE) - 1 else (1, 0)
        span = pl.ds(base, tile)
        query = gate_query[group][span, W:]
        q_pos = lax.dot_general(
            marks[group][span, :], pick, ACROSS, preferred_element_type=F32
        )[:, :1]
        attn = jnp.zeros((tile, W), F32)
        for kv, key_pos in groups:
            scores = lax.dot_general(
                query, kv[:, W:], ACROSS, preferred_element_type=F32
            ) * W ** (-0.5)
            weight = jnp.where(key_pos <= q_pos, silu(scores), 0.0).astype(BF16)
            attn += jnp.dot(weight, kv[:, :W], preferred_element_type=F32)
        normed = attn * lax.rsqrt(jnp.mean(attn * attn, axis=-1, keepdims=True) + 1e-06)
        out = (normed * gate_query[group][span, :W].astype(F32)).astype(BF16)
        for s in range(NZ):
            gated[s, k] = out[s * piece : (s + 1) * piece]


def hidden_kernel(where, *refs):
    n = len(PLANE)
    gated, w_own, w_other, tok = refs[:n], refs[n : n + 2], refs[n + 2 : n + 4], refs[n + 4 : -5]
    hidden, g_all, t_all, w_all, sems = refs[-5:]
    z, y, x, u = (where[i] for i in range(4))
    c = chip_at(z, y, x)
    rows = hidden.shape[1]
    half = w_all.shape[1]
    copies = []
    for s in range(NZ):
        cols = pl.ds(s * W, W)
        for side, src in enumerate((w_own, w_other)):
            copies.append((src[s // 2].at[s % 2], w_all.at[side, :, cols]))
        block = relative_chip(c, 0, 0, s)
        from_cols = pl.ds(pl.multiple_of(block * W, W), W)
        for k in range(n):
            copies.append((tok[k].at[pl.ds(0, rows), from_cols], t_all.at[k, :, cols]))
    copies = [pltpu.make_async_copy(a, b, sems.at[i]) for i, (a, b) in enumerate(copies)]
    for copy in copies:
        copy.start()
    for k, (by, bx) in enumerate(PLANE):
        for s in range(NZ):
            head = relative_chip(c, by, bx, s)
            cols = pl.ds(pl.multiple_of(head * W, W), W)
            for j, (jy, jx) in enumerate(PLANE):
                block = (jy ^ by) * NX + (jx ^ bx)
                g_all[block * rows : (block + 1) * rows, cols] = gated[k][s, j]
    for copy in copies:
        copy.wait()
    total = 0.0
    for side, at in enumerate((u, 1 - u)):
        part = g_all[:, pl.ds(pl.multiple_of(at * half, half), half)]
        total += jnp.dot(part, w_all[side], preferred_element_type=F32)
    for k in range(n):
        for s in range(NZ):
            term = total[k * rows : (k + 1) * rows, s * W : (s + 1) * W]
            cols = pl.ds(pl.multiple_of((z ^ s) * W, W), W)
            hidden[k, :, cols] = (t_all[k, :, s * W : (s + 1) * W].astype(F32) + term).astype(BF16)


def order_kernel(where, *refs):
    pieces, (keep, send, h_all) = refs[: len(PLANE)], refs[len(PLANE) :]
    y, x, u = (where[i] for i in range(1, 4))
    half = keep.shape[1]
    for (by, bx), ref in zip(PLANE, pieces):
        for at in range(NZ):
            block = chip_at(at, y ^ by, x ^ bx)
            h_all[:, pl.ds(pl.multiple_of(block * W, W), W)] = ref[:, at * W : (at + 1) * W]
    keep[...] = h_all[:, pl.ds(pl.multiple_of(u * half, half), half)]
    send[...] = h_all[:, pl.ds(pl.multiple_of((1 - u) * half, half), half)]


def loss_kernel(h_keep, h_send, t_keep, t_send, t_ids, n_own, n_other, loss, n_all, sems):
    keep, send = h_keep[...], h_send[...]
    half = keep.shape[1]
    copies = []
    for side, src in enumerate((n_own, n_other)):
        copies.append(pltpu.make_async_copy(src, n_all.at[side], sems.at[side]))
    for copy in copies:
        copy.start()
    hh = he = ee = 0.0
    for part, ref in ((keep, t_keep), (send, t_send)):
        h_f, t_f = part.astype(F32), ref[...].astype(F32)
        hh += jnp.sum(h_f * h_f, axis=1, keepdims=True)
        he += jnp.sum(h_f * t_f, axis=1, keepdims=True)
        ee += jnp.sum(t_f * t_f, axis=1, keepdims=True)
    h_scale = lax.rsqrt(hh + 1e-06) * 20.0
    pos_logit = he * lax.rsqrt(ee + 1e-06) * h_scale
    for copy in copies:
        copy.wait()
    pick = pick_columns({0: 1.0, 1: 1.0, 2: 1.0}, {3: 256.0, 4: 1.0})
    dots, read = 0.0, []
    for side, part in enumerate((keep, send)):
        neg, marks = n_all[side, :, :half], n_all[side, :, half:]
        dots += lax.dot_general(part, neg, ACROSS, preferred_element_type=F32)
        read.append(lax.dot_general(pick, marks, ACROSS, preferred_element_type=F32))
    nn = read[0][0:1] + read[1][0:1]
    n_ids = read[0][1:2]
    neg_logit = dots * h_scale * lax.rsqrt(nn + 1e-06)
    mass = jnp.where(n_ids != t_ids[...].astype(F32), jnp.exp(neg_logit), 0.0)
    total = jnp.exp(pos_logit) + jnp.sum(mass, axis=1, keepdims=True)
    loss[...] = jnp.log(total) - pos_logit


def call(kernel, name, outs, scratch, args, places, flops):
    space = {"s": pltpu.SMEM, "v": pltpu.VMEM, "h": pltpu.HBM}
    moved = sum(a.size * a.dtype.itemsize for a in args)
    return pl.pallas_call(
        kernel,
        out_shape=[jax.ShapeDtypeStruct(shape, dtype) for shape, dtype in outs],
        in_specs=[pl.BlockSpec(memory_space=space[p]) for p in places],
        out_specs=[pl.BlockSpec(memory_space=pltpu.VMEM)] * len(outs),
        scratch_shapes=scratch,
        compiler_params=pltpu.CompilerParams(vmem_limit_bytes=VMEM_LIMIT),
        cost_estimate=pl.CostEstimate(flops=flops, bytes_accessed=moved, transcendentals=0),
        name=name,
    )(*args)


def whole_parts(value, base):
    return [(value // base).astype(BF16), (value % base).astype(BF16)]


def float_parts(value):
    parts = []
    for _ in range(3):
        parts.append(lax.reduce_precision(value, 8, 7))
        value = value - parts[-1]
    return [part.astype(BF16) for part in parts]


def with_marks(rows, marks):
    marks = jnp.stack(marks, 1)
    marks = jnp.pad(marks, ((0, 0), (0, W - marks.shape[1])))
    return jnp.concatenate([rows, marks], 1)


def head_shards(
    tokens, w_proj, w_out, positions, neg_emb, neg_ids, target_emb, target_ids
):
    c, u = lax.axis_index("ctx"), lax.axis_index("tp")
    z, y, x = coords(c)
    where = jnp.stack([z, y, x, u]).astype(jnp.int32)
    model = tokens.shape[1]
    rows = tokens.shape[0] // 2
    events = rows * CHIPS
    half = model // 2
    negs = neg_emb.shape[0]
    plane = len(PLANE)

    mine = lax.dynamic_slice_in_dim(tokens, u * rows, rows, 0)
    p_own = lax.dynamic_slice_in_dim(positions, u * rows, rows, 0)
    p_other = lax.dynamic_slice_in_dim(positions, (1 - u) * rows, rows, 0)
    mine = with_marks(mine, whole_parts(p_own, 128) + whole_parts(p_other, 128))
    line = [mine] + [hop(mine, flip(0, 0, s)) for s in range(1, NZ)]
    low = jnp.concatenate(line[:2])

    to_x, to_y = flip(0, 1), flip(1, 0)
    low_x, low_y = hop(low, to_x), hop(low, to_y)
    w_plane = heads_in_plane(w_proj, y, x)
    w_plane, high = lax.optimization_barrier((w_plane, after(line[2:], low_x, low_y)))
    high = jnp.concatenate(high)
    high_x, high_y = hop(high, to_x), hop(high, to_y)
    low_xy, high_xy = hop(low_x, to_y), hop(high_y, to_x)
    tok = [low, high, low_x, high_x, low_y, high_y, low_xy, high_xy]
    w_mine = after(heads_along_z(w_plane, z), high_x, high_y, low_xy)
    w_theirs = swap_cores(w_mine)

    own_ids = lax.dynamic_slice_in_dim(neg_ids, c * negs, negs, 0)
    norms = jnp.sum(jnp.square(neg_emb.astype(F32)), axis=1)
    neg = with_marks(neg_emb, float_parts(norms) + whole_parts(own_ids, 256))
    neg_pair = pair_up(after(neg, w_mine))
    neg_pair = after(neg_pair, w_theirs)
    neg_near = jnp.concatenate([neg_pair, hop(neg_pair, flip(0, 0, 2))])
    out_pair = pair_up(after(w_out[None], neg_pair))
    out_own = [out_pair, hop(after(out_pair, neg_near), flip(0, 0, 2))]
    t_rows = target_emb.reshape(2, rows, -1)
    t_keep = pick_row(t_rows, u)
    t_send = swap_cores(pick_row(t_rows, 1 - u))

    def project(pieces):
        count = sum(p.shape[0] for p in pieces)
        return call(
            proj_kernel,
            "project",
            [((count, 2 * W), BF16)] * 2 + [((count, W), BF16)],
            [
                pltpu.VMEM((count, model + W), BF16),
                pltpu.VMEM((model, 4 * W), BF16),
                pltpu.SemaphoreType.DMA((len(pieces),)),
                pltpu.SemaphoreType.DMA((2,)),
            ],
            [where, *pieces, w_mine, w_theirs],
            "s" + (len(pieces) + 2) * "h",
            2 * count * model * 4 * W,
        )

    gq_early, kv_early, marks_early = project(tok[:6])
    kv_early_theirs = swap_cores(kv_early)
    gq_last, kv_last, marks_last = project(after(tok[6:], kv_early))
    kv_last_theirs = swap_cores(kv_last)
    neg_near = after(neg_near, kv_last)
    neg_x, neg_y = hop(neg_near, flip(0, 1)), hop(neg_near, flip(1, 0))
    (gated,) = call(
        attend_kernel,
        "attend",
        [((NZ, plane, rows, W), BF16)],
        [],
        [gq_early, gq_last, kv_early, kv_last, kv_early_theirs, kv_last_theirs]
        + [marks_early, marks_last],
        8 * "v",
        8 * events * events * W,
    )
    gated = jnp.stack([gated[0]] + [hop(gated[s], flip(0, 0, s)) for s in range(1, NZ)])
    out_other = [swap_cores(w) for w in out_own]
    gated = after(gated, out_own)
    gated = [gated] + [hop(gated, flip(by, bx)) for by, bx in PLANE[1:]]
    neg_x, neg_y = after((neg_x, neg_y), gated, out_other)
    part = neg_x.shape[0] // 2
    neg_own = [neg_near, neg_x, neg_y]
    neg_own += [hop(neg_x[:part], flip(1, 0)), hop(neg_y[part:], flip(0, 1))]
    (hidden,) = call(
        hidden_kernel,
        "hidden",
        [((plane, rows, NZ * W), BF16)],
        [
            pltpu.VMEM((plane * rows, model), BF16),
            pltpu.VMEM((plane, rows, NZ * W), BF16),
            pltpu.VMEM((2, half, NZ * W), BF16),
            pltpu.SemaphoreType.DMA((NZ * (2 + plane),)),
        ],
        [where, *gated, *out_own, *out_other, *tok[::2]],
        "s" + 4 * "v" + 8 * "h",
        2 * plane * rows * model * NZ * W,
    )
    pieces = [hidden[0]] + [hop(hidden[k], flip(*PLANE[k])) for k in range(1, plane)]
    neg_own = jnp.concatenate(after(neg_own, hidden))
    neg_other = swap_cores(neg_own)
    h_keep, h_send = call(
        order_kernel,
        "order",
        [((rows, half), BF16)] * 2,
        [pltpu.VMEM((rows, model), BF16)],
        [where, *pieces],
        "svvvv",
        0,
    )
    h_theirs = swap_cores(h_send)
    (loss,) = call(
        loss_kernel,
        "loss",
        [((rows, 1), F32)],
        [
            pltpu.VMEM((2, CHIPS * negs, half + W), BF16),
            pltpu.SemaphoreType.DMA((2,)),
        ],
        [h_keep, h_send, t_keep, t_send, target_ids[:, None], neg_own, neg_other],
        "vvvvvhh",
        2 * rows * model * neg_ids.shape[0],
    )
    hidden = jnp.where(
        u == 0,
        jnp.concatenate([h_keep, h_theirs]),
        jnp.concatenate([h_theirs, h_keep]),
    )
    return hidden, loss.reshape(-1)


def shards(tokens, w_proj, *rest):
    n_ctx, n_tp = lax.axis_size("ctx"), lax.axis_size("tp")
    heads = w_proj.shape[2] * n_tp // HEAD_DIM
    plan = head_shards if (n_ctx, n_tp, heads) == (CHIPS, 2, CHIPS) else general_shards
    return plan(tokens, w_proj, *rest)


def solution(mesh):
    placed = (
        P("ctx", None),
        P("ctx", None, "tp"),
        P("tp", "ctx"),
        P("ctx"),
        P("ctx", "tp"),
        P(),
        P("ctx", "tp"),
        P(("ctx", "tp")),
    )
    return jax.shard_map(
        shards,
        mesh=mesh,
        in_specs=placed,
        out_specs=(P("ctx", "tp"), P(("ctx", "tp"))),
        check_vma=False,
    )
```

```python
import jax
import jax.numpy as jnp
from jax import lax
from jax.experimental import pallas as pl
from jax.experimental.pallas import tpu as pltpu
from jax.sharding import PartitionSpec as P

HEAD_DIM = 128
VMEM_LIMIT = 48 * 1024 * 1024
BF16 = jnp.bfloat16
F32 = jnp.float32


def attend_piece(q_group, q_pos, k_piece, v_piece, p_piece):
    heads = q_group.shape[1]
    width = q_group.shape[2]
    key_heads = k_piece.reshape(k_piece.shape[0], heads, width)
    value_heads = v_piece.reshape(v_piece.shape[0], heads, width)
    scores = jnp.einsum(
        "thd,khd->htk", q_group, key_heads, preferred_element_type=jnp.float32
    ) * width ** (-0.5)
    visible = p_piece[None, None, :] <= q_pos[None, :, None]
    weight = jnp.where(visible, jax.nn.silu(scores), 0.0).astype(jnp.bfloat16)
    return jnp.einsum("htk,khd->thd", weight, value_heads, preferred_element_type=jnp.float32)


def general_shards(
    tokens, w_proj, w_out, positions, neg_emb, neg_ids, target_emb, target_ids
):
    tok_rows = tokens.shape[0]
    head_cols = w_proj.shape[2]
    local_heads = head_cols // HEAD_DIM
    proj_sum = jnp.einsum(
        "td,dfh->tfh",
        tokens,
        lax.all_gather(w_proj, "ctx", axis=0, tiled=True),
        preferred_element_type=jnp.float32,
    )
    proj = jax.nn.silu(proj_sum).astype(jnp.bfloat16)
    gate = proj[:, 0].reshape(tok_rows, local_heads, HEAD_DIM)
    query = proj[:, 2].reshape(tok_rows, local_heads, HEAD_DIM)
    v_piece = lax.all_gather(proj[:, 1], "ctx", axis=0, tiled=True)
    k_piece = lax.all_gather(proj[:, 3], "ctx", axis=0, tiled=True)
    p_piece = lax.all_gather(positions, "ctx", axis=0, tiled=True)
    attn = attend_piece(query, positions, k_piece, v_piece, p_piece)
    normed = attn * lax.rsqrt(jnp.mean(attn * attn, axis=-1, keepdims=True) + 1e-06)
    gated = (normed * gate.astype(jnp.float32)).astype(jnp.bfloat16).reshape(tok_rows, head_cols)
    out_terms = jnp.dot(
        gated, lax.all_gather(w_out, "ctx", axis=1, tiled=True), preferred_element_type=jnp.float32
    )
    out_share = lax.psum_scatter(out_terms, "tp", scatter_dimension=1, tiled=True)
    feat_cols = out_share.shape[1]
    own_tokens = lax.dynamic_slice_in_dim(tokens, lax.axis_index("tp") * feat_cols, feat_cols, 1)
    hidden = (own_tokens.astype(jnp.float32) + out_share).astype(jnp.bfloat16)
    piece = lax.all_gather(neg_emb, "ctx", axis=0, tiled=True)
    panel_dots = lax.dot_general(
        hidden, piece, (((1,), (1,)), ((), ())), preferred_element_type=jnp.float32
    )
    panel_norms = jnp.sum(jnp.square(piece.astype(jnp.float32)), axis=1)
    hidden_f = hidden.astype(jnp.float32)
    target_f = target_emb.astype(jnp.float32)
    part_hh = jnp.sum(hidden_f * hidden_f, axis=1)
    part_he = jnp.sum(hidden_f * target_f, axis=1)
    part_ee = jnp.sum(target_f * target_f, axis=1)
    dots, hh_sum, he_sum, ee_sum = (
        lax.psum_scatter(panel_dots, "tp", scatter_dimension=0, tiled=True),
        lax.psum_scatter(part_hh, "tp", scatter_dimension=0, tiled=True),
        lax.psum_scatter(part_he, "tp", scatter_dimension=0, tiled=True),
        lax.psum_scatter(part_ee, "tp", scatter_dimension=0, tiled=True),
    )
    neg_sq = lax.psum(panel_norms, "tp")
    pos_logit = he_sum / jnp.sqrt(hh_sum + 1e-06) / jnp.sqrt(ee_sum + 1e-06) / 0.05
    neg_logit = dots / jnp.sqrt(hh_sum + 1e-06)[:, None] / jnp.sqrt(neg_sq + 1e-06)[None, :] / 0.05
    keep_mask = neg_ids[None, :] != target_ids[:, None]
    total_mass = jnp.exp(pos_logit) + jnp.sum(jnp.where(keep_mask, jnp.exp(neg_logit), 0.0), axis=1)
    loss = jnp.log(total_mass) - pos_logit
    return (hidden, loss)


NZ, NY, NX = 4, 2, 2
CHIPS = NZ * NY * NX
PLANE = [(by, bx) for by in range(NY) for bx in range(NX)]
SWAP = [(0, 1), (1, 0)]
W = HEAD_DIM
ACROSS = (((1,), (1,)), ((), ()))


def chip_at(z, y, x):
    return (z * NY + y) * NX + x


def coords(c):
    return c // (NY * NX), (c // NX) % NY, c % NX


def relative_chip(c, by, bx, s):
    z, y, x = coords(c)
    return chip_at(z ^ s, y ^ by, x ^ bx)


def flip(by, bx, s=0):
    return [(c, relative_chip(c, by, bx, s)) for c in range(CHIPS)]


def hop(value, perm):
    return lax.ppermute(value, "ctx", perm)


def swap_cores(value):
    return lax.ppermute(value, "tp", SWAP)


def pick_row(value, at):
    return lax.dynamic_index_in_dim(value, at, 0, keepdims=False)


def after(values, *others):
    return lax.optimization_barrier((values, others))[0]


def pair_up(own):
    return jnp.concatenate([own, hop(own, flip(0, 0, 1))])


def relay_pairs(pair, z):
    inner, outer = [], []
    for c in range(CHIPS):
        if coords(c)[0] in (1, 2):
            inner.append((c, relative_chip(c, 0, 0, 3)))
            outer.append((c, relative_chip(c, 0, 0, 1)))
    met = hop(pair, inner)
    return met, lambda met: jnp.where((z == 1) | (z == 2), met, hop(met, outer))


def across(value_x, value_y):
    half = value_x.shape[0] // 2
    return [hop(value_x[:half], flip(1, 0)), hop(value_y[half:], flip(0, 1))]


def heads_in_plane(w_proj, y, x):
    plane = NY * NX
    heads = w_proj.reshape(-1, 4, 2, plane, W).transpose(3, 2, 0, 1, 4)
    heads = heads.reshape(plane, 2, -1, 4 * W)
    out = jnp.zeros((2, plane, *heads.shape[2:]), heads.dtype)
    came = []
    for by, bx in PLANE:
        spot = (y ^ by) * NX + (x ^ bx)
        piece = pick_row(heads, spot)
        if (by, bx) != (0, 0):
            piece = hop(piece, flip(by, bx))
            came.append(piece)
        out = lax.dynamic_update_slice_in_dim(out, piece[:, None], spot, 1)
    return out, came


def heads_along_z(heads, z):
    arrived = []
    for e in range(2):
        perm = []
        for src in range(CHIPS):
            sz, sy, sx = coords(src)
            for t in range(2):
                dst = chip_at(2 * t + (e ^ (sz & 1)), sy, sx)
                perm.append((2 * src + t, 2 * dst + (sz >> 1)))
        arrived.append(lax.ppermute(pick_row(heads, e ^ (z & 1)), ("ctx", "tp"), perm))
    rows = jnp.where(z % 2 == 0, jnp.stack(arrived), jnp.stack(arrived[::-1]))
    return rows.reshape(-1, rows.shape[-1])


def silu(v):
    return 0.5 * v * (1.0 + jnp.tanh(0.5 * v))


def run_copies(copies):
    for copy in copies:
        copy.start()
    for copy in copies:
        copy.wait()


def proj_kernel(where, *refs):
    count = len(refs) - 9
    tok, (w_own, w_other) = refs[:count], refs[count : count + 2]
    gate_query, value_key, marks, x_all, w_all, tok_sem, w_sem = refs[count + 2 :]
    u = where[3]
    copies, base = [], 0
    half = w_own.shape[0]
    for side, (at, src) in enumerate(((u, w_own), (1 - u, w_other))):
        rows = pl.ds(pl.multiple_of(at * half, half), half)
        copies.append(pltpu.make_async_copy(src, w_all.at[rows, :], w_sem.at[side]))
    for i, ref in enumerate(tok):
        rows = pl.ds(base, ref.shape[0])
        copies.append(pltpu.make_async_copy(ref, x_all.at[rows, :], tok_sem.at[i]))
        base += ref.shape[0]
    run_copies(copies)
    model = w_all.shape[0]
    total = jnp.dot(x_all[:, :model], w_all[...], preferred_element_type=F32)
    proj = silu(total).astype(BF16)
    gate_query[:, :W] = proj[:, :W]
    value_key[:, :W] = proj[:, W : 2 * W]
    gate_query[:, W:] = proj[:, 2 * W : 3 * W]
    value_key[:, W:] = proj[:, 3 * W :]
    marks[...] = x_all[:, model:]


def pick_columns(*weights):
    lane = lax.broadcasted_iota(jnp.int32, (8, W), 1)
    line = lax.broadcasted_iota(jnp.int32, (8, W), 0)
    pick = jnp.zeros((8, W), F32)
    for i, row in enumerate(weights):
        for at, weight in row.items():
            pick = jnp.where((line == i) & (lane == at), weight, pick)
    return pick.astype(BF16)


def attend_kernel(gate_query, kv_own, kv_other, marks, gated):
    pick = pick_columns({0: 128.0, 1: 1.0}, {2: 128.0, 3: 1.0})
    piece = gated.shape[2]
    tile = NZ * piece
    key_pos = lax.dot_general(pick, marks[...], ACROSS, preferred_element_type=F32)
    for k in range(len(PLANE)):
        span = pl.ds(k * tile, tile)
        query = gate_query[span, W:]
        q_pos = lax.dot_general(marks[span, :], pick, ACROSS, preferred_element_type=F32)[:, :1]
        attn = jnp.zeros((tile, W), F32)
        for side, kv in enumerate((kv_own, kv_other)):
            scores = lax.dot_general(
                query, kv[:, W:], ACROSS, preferred_element_type=F32
            ) * W ** (-0.5)
            visible = key_pos[side : side + 1] <= q_pos
            weight = jnp.where(visible, silu(scores), 0.0).astype(BF16)
            attn += jnp.dot(weight, kv[:, :W], preferred_element_type=F32)
        normed = attn * lax.rsqrt(jnp.mean(attn * attn, axis=-1, keepdims=True) + 1e-06)
        out = (normed * gate_query[span, :W].astype(F32)).astype(BF16)
        for s in range(NZ):
            gated[s, k] = out[s * piece : (s + 1) * piece]


def hidden_kernel(where, *refs):
    n = len(PLANE)
    gated, w_own, w_other, tok = refs[: n + 1], refs[n + 1 : n + 3], refs[n + 3 : n + 5], refs[n + 5 : -5]
    hidden, g_all, t_all, w_all, sems = refs[-5:]
    z, y, x, u = (where[i] for i in range(4))
    c = chip_at(z, y, x)
    rows = hidden.shape[1]
    half = w_all.shape[1]
    inner = ((z + 1) // 2) % 2
    copies = []
    for s in range(NZ):
        cols = pl.ds(s * W, W)
        for side, src in enumerate((w_own, w_other)):
            panel = src[0].at[s] if s < 2 else src[1].at[(s % 2) ^ inner]
            copies.append((panel, w_all.at[side, :, cols]))
        block = relative_chip(c, 0, 0, s)
        from_cols = pl.ds(pl.multiple_of(block * W, W), W)
        for k in range(n):
            copies.append((tok[k].at[pl.ds(0, rows), from_cols], t_all.at[k, :, cols]))
    copies = [pltpu.make_async_copy(a, b, sems.at[i]) for i, (a, b) in enumerate(copies)]
    for copy in copies:
        copy.start()
    for k, (by, bx) in enumerate(PLANE):
        for s in range(NZ):
            head = relative_chip(c, by, bx, s)
            cols = pl.ds(pl.multiple_of(head * W, W), W)
            for j, (jy, jx) in enumerate(PLANE):
                block = (jy ^ by) * NX + (jx ^ bx)
                piece = gated[k][s, j] if k < n - 1 else gated[k + s // 2][s % 2, j]
                g_all[block * rows : (block + 1) * rows, cols] = piece
    for copy in copies:
        copy.wait()
    total = 0.0
    for side, at in enumerate((u, 1 - u)):
        part = g_all[:, pl.ds(pl.multiple_of(at * half, half), half)]
        total += jnp.dot(part, w_all[side], preferred_element_type=F32)
    for k in range(n):
        for s in range(NZ):
            term = total[k * rows : (k + 1) * rows, s * W : (s + 1) * W]
            cols = pl.ds(pl.multiple_of((z ^ s) * W, W), W)
            hidden[k, :, cols] = (t_all[k, :, s * W : (s + 1) * W].astype(F32) + term).astype(BF16)


def order_kernel(where, *refs):
    pieces, (keep, send, h_all) = refs[: len(PLANE)], refs[len(PLANE) :]
    y, x, u = (where[i] for i in range(1, 4))
    half = keep.shape[1]
    for (by, bx), ref in zip(PLANE, pieces):
        for at in range(NZ):
            block = chip_at(at, y ^ by, x ^ bx)
            h_all[:, pl.ds(pl.multiple_of(block * W, W), W)] = ref[:, at * W : (at + 1) * W]
    keep[...] = h_all[:, pl.ds(pl.multiple_of(u * half, half), half)]
    send[...] = h_all[:, pl.ds(pl.multiple_of((1 - u) * half, half), half)]


def loss_kernel(h_keep, h_send, t_keep, t_send, t_ids, n_own, n_other, loss, n_all, sems):
    keep, send = h_keep[...], h_send[...]
    half = keep.shape[1]
    copies = []
    for side, src in enumerate((n_own, n_other)):
        copies.append(pltpu.make_async_copy(src, n_all.at[side], sems.at[side]))
    for copy in copies:
        copy.start()
    hh = he = ee = 0.0
    for part, ref in ((keep, t_keep), (send, t_send)):
        h_f, t_f = part.astype(F32), ref[...].astype(F32)
        hh += jnp.sum(h_f * h_f, axis=1, keepdims=True)
        he += jnp.sum(h_f * t_f, axis=1, keepdims=True)
        ee += jnp.sum(t_f * t_f, axis=1, keepdims=True)
    h_scale = lax.rsqrt(hh + 1e-06) * 20.0
    pos_logit = he * lax.rsqrt(ee + 1e-06) * h_scale
    for copy in copies:
        copy.wait()
    pick = pick_columns({0: 1.0, 1: 1.0, 2: 1.0}, {3: 256.0, 4: 1.0})
    dots, read = 0.0, []
    for side, part in enumerate((keep, send)):
        neg, marks = n_all[side, :, :half], n_all[side, :, half:]
        dots += lax.dot_general(part, neg, ACROSS, preferred_element_type=F32)
        read.append(lax.dot_general(pick, marks, ACROSS, preferred_element_type=F32))
    nn = read[0][0:1] + read[1][0:1]
    n_ids = read[0][1:2]
    neg_logit = dots * h_scale * lax.rsqrt(nn + 1e-06)
    mass = jnp.where(n_ids != t_ids[...].astype(F32), jnp.exp(neg_logit), 0.0)
    total = jnp.exp(pos_logit) + jnp.sum(mass, axis=1, keepdims=True)
    column = jnp.log(total) - pos_logit
    size = column.shape[0]
    line = lax.broadcasted_iota(jnp.int32, (size, size), 0)
    lane = lax.broadcasted_iota(jnp.int32, (size, size), 1)
    loss[...] = jnp.sum(jnp.where(line == lane, column, 0.0), axis=0, keepdims=True)


def join_kernel(where, keep, theirs, hidden):
    u, rows = where[3], keep.shape[0]
    hidden[pl.ds(pl.multiple_of(u * rows, rows), rows), :] = keep[...]
    hidden[pl.ds(pl.multiple_of((1 - u) * rows, rows), rows), :] = theirs[...]


def call(kernel, name, outs, scratch, args, places, flops):
    space = {"s": pltpu.SMEM, "v": pltpu.VMEM, "h": pltpu.HBM}
    moved = sum(a.size * a.dtype.itemsize for a in args)
    return pl.pallas_call(
        kernel,
        out_shape=[jax.ShapeDtypeStruct(shape, dtype) for shape, dtype in outs],
        in_specs=[pl.BlockSpec(memory_space=space[p]) for p in places],
        out_specs=[pl.BlockSpec(memory_space=pltpu.VMEM)] * len(outs),
        scratch_shapes=scratch,
        compiler_params=pltpu.CompilerParams(vmem_limit_bytes=VMEM_LIMIT),
        cost_estimate=pl.CostEstimate(flops=flops, bytes_accessed=moved, transcendentals=0),
        name=name,
    )(*args)


def whole_parts(value, base):
    return [(value // base).astype(BF16), (value % base).astype(BF16)]


def float_parts(value):
    parts = []
    for _ in range(3):
        parts.append(lax.reduce_precision(value, 8, 7))
        value = value - parts[-1]
    return [part.astype(BF16) for part in parts]


def with_marks(rows, marks):
    marks = jnp.stack(marks, 1)
    marks = jnp.pad(marks, ((0, 0), (0, W - marks.shape[1])))
    return jnp.concatenate([rows, marks], 1)


def head_shards(
    tokens, w_proj, w_out, positions, neg_emb, neg_ids, target_emb, target_ids
):
    c, u = lax.axis_index("ctx"), lax.axis_index("tp")
    z, y, x = coords(c)
    where = jnp.stack([z, y, x, u]).astype(jnp.int32)
    model = tokens.shape[1]
    rows = tokens.shape[0] // 2
    events = rows * CHIPS
    half = model // 2
    negs = neg_emb.shape[0]
    plane = len(PLANE)

    mine = lax.dynamic_slice_in_dim(tokens, u * rows, rows, 0)
    p_own = lax.dynamic_slice_in_dim(positions, u * rows, rows, 0)
    p_other = lax.dynamic_slice_in_dim(positions, (1 - u) * rows, rows, 0)
    mine = with_marks(mine, whole_parts(p_own, 128) + whole_parts(p_other, 128))
    low = pair_up(mine)

    to_x, to_y = flip(0, 1), flip(1, 0)
    high = hop(low, flip(0, 0, 2))
    w_plane, came = heads_in_plane(w_proj, y, x)
    low = after(low, came[:2])
    low_x, low_y = hop(low, to_x), hop(low, to_y)
    low_xy = across(low_x, low_y)
    w_plane = after(w_plane, high)
    high_x, high_y = hop(high, to_x), hop(high, to_y)
    high_xy = across(high_x, high_y)
    tok = [low, high, low_x, high_x, low_y, high_y, *low_xy, *high_xy]
    w_mine = after(heads_along_z(w_plane, z), low_xy, high_xy)
    w_theirs = swap_cores(w_mine)

    t_rows = after(target_emb.reshape(2, rows, -1), high)
    t_keep = pick_row(t_rows, u)
    t_send = swap_cores(pick_row(t_rows, 1 - u))
    own_ids = lax.dynamic_slice_in_dim(neg_ids, c * negs, negs, 0)
    norms = jnp.sum(jnp.square(neg_emb.astype(F32)), axis=1)
    neg = with_marks(neg_emb, float_parts(norms) + whole_parts(own_ids, 256))
    neg_pair = pair_up(after(neg, w_mine, t_send))
    neg_met, neg_far = relay_pairs(after(neg_pair, w_theirs), z)
    out_pair = pair_up(after(w_out[None], neg_pair))

    def project(pieces):
        count = sum(p.shape[0] for p in pieces)
        return call(
            proj_kernel,
            "project",
            [((count, 2 * W), BF16)] * 2 + [((count, W), BF16)],
            [
                pltpu.VMEM((count, model + W), BF16),
                pltpu.VMEM((model, 4 * W), BF16),
                pltpu.SemaphoreType.DMA((len(pieces),)),
                pltpu.SemaphoreType.DMA((2,)),
            ],
            [where, *pieces, w_mine, w_theirs],
            "s" + (len(pieces) + 2) * "h",
            2 * count * model * 4 * W,
        )

    gate_query, value_key, marks = project(tok)
    kv_theirs = swap_cores(value_key)
    out_met, out_far = relay_pairs(after(out_pair, neg_met, value_key), z)
    neg_near = jnp.concatenate([neg_pair, neg_far(after(neg_met, value_key))])
    neg_row = jnp.concatenate([neg_near, hop(neg_near, to_x)])
    neg_own = [neg_row, hop(neg_row, to_y)]
    (gated,) = call(
        attend_kernel,
        "attend",
        [((NZ, plane, rows, W), BF16)],
        [],
        [gate_query, value_key, kv_theirs, marks],
        4 * "v",
        8 * events * events * W,
    )
    gated = after(gated, neg_near)
    gated = jnp.stack([gated[0]] + [hop(gated[s], flip(0, 0, s)) for s in range(1, NZ)])
    out_met = after(out_met, gated)
    gated = [gated, hop(gated, to_x), hop(gated, to_y)]
    gated += across(gated[1], gated[2])
    out_own = [after(out_pair, gated), after(out_far(out_met), gated)]
    out_other = [swap_cores(w) for w in out_own]
    (hidden,) = call(
        hidden_kernel,
        "hidden",
        [((plane, rows, NZ * W), BF16)],
        [
            pltpu.VMEM((plane * rows, model), BF16),
            pltpu.VMEM((plane, rows, NZ * W), BF16),
            pltpu.VMEM((2, half, NZ * W), BF16),
            pltpu.SemaphoreType.DMA((NZ * (2 + plane),)),
        ],
        [where, *gated, *out_own, *out_other, *tok[:7:2]],
        "s" + 5 * "v" + 8 * "h",
        2 * plane * rows * model * NZ * W,
    )
    pieces = [hidden[0]] + [hop(hidden[k], flip(*PLANE[k])) for k in range(1, plane)]
    neg_own = jnp.concatenate(after(neg_own, hidden))
    neg_other = swap_cores(neg_own)
    h_keep, h_send = call(
        order_kernel,
        "order",
        [((rows, half), BF16)] * 2,
        [pltpu.VMEM((rows, model), BF16)],
        [where, *pieces],
        "svvvv",
        0,
    )
    h_theirs = swap_cores(h_send)
    (loss,) = call(
        loss_kernel,
        "loss",
        [((1, rows), F32)],
        [
            pltpu.VMEM((2, CHIPS * negs, half + W), BF16),
            pltpu.SemaphoreType.DMA((2,)),
        ],
        [h_keep, h_send, t_keep, t_send, target_ids[:, None], neg_own, neg_other],
        "vvvvvhh",
        2 * rows * model * neg_ids.shape[0],
    )
    (hidden,) = call(
        join_kernel,
        "join",
        [((2 * rows, half), BF16)],
        [],
        [where, h_keep, after(h_theirs, loss)],
        "svv",
        0,
    )
    return hidden, loss.reshape(-1)


def shards(tokens, w_proj, *rest):
    n_ctx, n_tp = lax.axis_size("ctx"), lax.axis_size("tp")
    heads = w_proj.shape[2] * n_tp // HEAD_DIM
    plan = head_shards if (n_ctx, n_tp, heads) == (CHIPS, 2, CHIPS) else general_shards
    return plan(tokens, w_proj, *rest)


def solution(mesh):
    placed = (
        P("ctx", None),
        P("ctx", None, "tp"),
        P("tp", "ctx"),
        P("ctx"),
        P("ctx", "tp"),
        P(),
        P("ctx", "tp"),
        P(("ctx", "tp")),
    )
    return jax.shard_map(
        shards,
        mesh=mesh,
        in_specs=placed,
        out_specs=(P("ctx", "tp"), P(("ctx", "tp"))),
        check_vma=False,
    )
```

```python
import jax
import jax.numpy as jnp
from jax import lax
from jax.experimental import pallas as pl
from jax.experimental.pallas import tpu as pltpu
from jax.sharding import PartitionSpec as P

HEAD_DIM = 128
VMEM_LIMIT = 48 * 1024 * 1024
BF16 = jnp.bfloat16
F32 = jnp.float32


def attend_piece(q_group, q_pos, k_piece, v_piece, p_piece):
    heads = q_group.shape[1]
    width = q_group.shape[2]
    key_heads = k_piece.reshape(k_piece.shape[0], heads, width)
    value_heads = v_piece.reshape(v_piece.shape[0], heads, width)
    scores = jnp.einsum(
        "thd,khd->htk", q_group, key_heads, preferred_element_type=jnp.float32
    ) * width ** (-0.5)
    visible = p_piece[None, None, :] <= q_pos[None, :, None]
    weight = jnp.where(visible, jax.nn.silu(scores), 0.0).astype(jnp.bfloat16)
    return jnp.einsum("htk,khd->thd", weight, value_heads, preferred_element_type=jnp.float32)


def general_shards(
    tokens, w_proj, w_out, positions, neg_emb, neg_ids, target_emb, target_ids
):
    tok_rows = tokens.shape[0]
    head_cols = w_proj.shape[2]
    local_heads = head_cols // HEAD_DIM
    proj_sum = jnp.einsum(
        "td,dfh->tfh",
        tokens,
        lax.all_gather(w_proj, "ctx", axis=0, tiled=True),
        preferred_element_type=jnp.float32,
    )
    proj = jax.nn.silu(proj_sum).astype(jnp.bfloat16)
    gate = proj[:, 0].reshape(tok_rows, local_heads, HEAD_DIM)
    query = proj[:, 2].reshape(tok_rows, local_heads, HEAD_DIM)
    v_piece = lax.all_gather(proj[:, 1], "ctx", axis=0, tiled=True)
    k_piece = lax.all_gather(proj[:, 3], "ctx", axis=0, tiled=True)
    p_piece = lax.all_gather(positions, "ctx", axis=0, tiled=True)
    attn = attend_piece(query, positions, k_piece, v_piece, p_piece)
    normed = attn * lax.rsqrt(jnp.mean(attn * attn, axis=-1, keepdims=True) + 1e-06)
    gated = (normed * gate.astype(jnp.float32)).astype(jnp.bfloat16).reshape(tok_rows, head_cols)
    out_terms = jnp.dot(
        gated, lax.all_gather(w_out, "ctx", axis=1, tiled=True), preferred_element_type=jnp.float32
    )
    out_share = lax.psum_scatter(out_terms, "tp", scatter_dimension=1, tiled=True)
    feat_cols = out_share.shape[1]
    own_tokens = lax.dynamic_slice_in_dim(tokens, lax.axis_index("tp") * feat_cols, feat_cols, 1)
    hidden = (own_tokens.astype(jnp.float32) + out_share).astype(jnp.bfloat16)
    piece = lax.all_gather(neg_emb, "ctx", axis=0, tiled=True)
    panel_dots = lax.dot_general(
        hidden, piece, (((1,), (1,)), ((), ())), preferred_element_type=jnp.float32
    )
    panel_norms = jnp.sum(jnp.square(piece.astype(jnp.float32)), axis=1)
    hidden_f = hidden.astype(jnp.float32)
    target_f = target_emb.astype(jnp.float32)
    part_hh = jnp.sum(hidden_f * hidden_f, axis=1)
    part_he = jnp.sum(hidden_f * target_f, axis=1)
    part_ee = jnp.sum(target_f * target_f, axis=1)
    dots, hh_sum, he_sum, ee_sum = (
        lax.psum_scatter(panel_dots, "tp", scatter_dimension=0, tiled=True),
        lax.psum_scatter(part_hh, "tp", scatter_dimension=0, tiled=True),
        lax.psum_scatter(part_he, "tp", scatter_dimension=0, tiled=True),
        lax.psum_scatter(part_ee, "tp", scatter_dimension=0, tiled=True),
    )
    neg_sq = lax.psum(panel_norms, "tp")
    pos_logit = he_sum / jnp.sqrt(hh_sum + 1e-06) / jnp.sqrt(ee_sum + 1e-06) / 0.05
    neg_logit = dots / jnp.sqrt(hh_sum + 1e-06)[:, None] / jnp.sqrt(neg_sq + 1e-06)[None, :] / 0.05
    keep_mask = neg_ids[None, :] != target_ids[:, None]
    total_mass = jnp.exp(pos_logit) + jnp.sum(jnp.where(keep_mask, jnp.exp(neg_logit), 0.0), axis=1)
    loss = jnp.log(total_mass) - pos_logit
    return (hidden, loss)


NZ, NY, NX = 4, 2, 2
CHIPS = NZ * NY * NX
PLANE = [(by, bx) for by in range(NY) for bx in range(NX)]
SWAP = [(0, 1), (1, 0)]
W = HEAD_DIM
ACROSS = (((1,), (1,)), ((), ()))


def chip_at(z, y, x):
    return (z * NY + y) * NX + x


def coords(c):
    return c // (NY * NX), (c // NX) % NY, c % NX


def relative_chip(c, by, bx, s):
    z, y, x = coords(c)
    return chip_at(z ^ s, y ^ by, x ^ bx)


def flip(by, bx, s=0):
    return [(c, relative_chip(c, by, bx, s)) for c in range(CHIPS)]


def hop(value, perm):
    return lax.ppermute(value, "ctx", perm)


def swap_cores(value):
    return lax.ppermute(value, "tp", SWAP)


def pick_row(value, at):
    return lax.dynamic_index_in_dim(value, at, 0, keepdims=False)


def after(values, *others):
    return lax.optimization_barrier((values, others))[0]


def pair_up(own):
    return jnp.concatenate([own, hop(own, flip(0, 0, 1))])


def inner_hop(pair):
    return hop(pair, [(c, relative_chip(c, 0, 0, 3)) for c in range(CHIPS) if is_inner(coords(c)[0])])


def outer_hop(pair):
    return hop(pair, [(c, relative_chip(c, 0, 0, 1)) for c in range(CHIPS) if is_inner(coords(c)[0])])


def is_inner(z):
    return ((z + 1) // 2) % 2 == 1


def heads_in_plane(w_proj, y, x):
    plane = NY * NX
    heads = w_proj.reshape(-1, 4, 2, plane, W).transpose(3, 2, 0, 1, 4)
    heads = heads.reshape(plane, 2, -1, 4 * W)
    out = jnp.zeros((2, plane, *heads.shape[2:]), heads.dtype)
    came = []
    for by, bx in PLANE:
        spot = (y ^ by) * NX + (x ^ bx)
        piece = pick_row(heads, spot)
        if (by, bx) != (0, 0):
            piece = hop(piece, flip(by, bx))
            came.append(piece)
        out = lax.dynamic_update_slice_in_dim(out, piece[:, None], spot, 1)
    return out, came


def heads_along_z(heads, z):
    arrived = []
    for e in range(2):
        perm = []
        for src in range(CHIPS):
            sz, sy, sx = coords(src)
            for t in range(2):
                dst = chip_at(2 * t + (e ^ (sz & 1)), sy, sx)
                perm.append((2 * src + t, 2 * dst + (sz >> 1)))
        arrived.append(lax.ppermute(pick_row(heads, e ^ (z & 1)), ("ctx", "tp"), perm))
    rows = jnp.where(z % 2 == 0, jnp.stack(arrived), jnp.stack(arrived[::-1]))
    return rows.reshape(-1, rows.shape[-1])


def silu(v):
    return 0.5 * v * (1.0 + jnp.tanh(0.5 * v))


def run_copies(copies):
    for copy in copies:
        copy.start()
    for copy in copies:
        copy.wait()


def proj_kernel(where, *refs):
    count = len(refs) - 9
    tok, (w_own, w_other) = refs[:count], refs[count : count + 2]
    gate_query, value_key, marks, x_all, w_all, tok_sem, w_sem = refs[count + 2 :]
    u = where[3]
    copies, base = [], 0
    half = w_own.shape[0]
    for side, (at, src) in enumerate(((u, w_own), (1 - u, w_other))):
        rows = pl.ds(pl.multiple_of(at * half, half), half)
        copies.append(pltpu.make_async_copy(src, w_all.at[rows, :], w_sem.at[side]))
    for i, ref in enumerate(tok):
        rows = pl.ds(base, ref.shape[0])
        copies.append(pltpu.make_async_copy(ref, x_all.at[rows, :], tok_sem.at[i]))
        base += ref.shape[0]
    run_copies(copies)
    model = w_all.shape[0]
    total = jnp.dot(x_all[:, :model], w_all[...], preferred_element_type=F32)
    proj = silu(total).astype(BF16)
    gate_query[:, :W] = proj[:, :W]
    value_key[:, :W] = proj[:, W : 2 * W]
    gate_query[:, W:] = proj[:, 2 * W : 3 * W]
    value_key[:, W:] = proj[:, 3 * W :]
    marks[...] = x_all[:, model:]


def pick_columns(*weights):
    lane = lax.broadcasted_iota(jnp.int32, (8, W), 1)
    line = lax.broadcasted_iota(jnp.int32, (8, W), 0)
    pick = jnp.zeros((8, W), F32)
    for i, row in enumerate(weights):
        for at, weight in row.items():
            pick = jnp.where((line == i) & (lane == at), weight, pick)
    return pick.astype(BF16)


def attend_kernel(where, gate_query, kv_own, kv_other, marks, gated):
    pick = pick_columns({0: 128.0, 1: 1.0}, {2: 128.0, 3: 1.0})
    piece = gated.shape[2]
    tile = NZ * piece
    flipped = ((where[0] + 1) // 2) % 2
    key_pos = lax.dot_general(pick, marks[...], ACROSS, preferred_element_type=F32)
    for k in range(len(PLANE)):
        span = pl.ds(k * tile, tile)
        query = gate_query[span, W:]
        q_pos = lax.dot_general(marks[span, :], pick, ACROSS, preferred_element_type=F32)[:, :1]
        attn = jnp.zeros((tile, W), F32)
        for side, kv in enumerate((kv_own, kv_other)):
            scores = lax.dot_general(
                query, kv[:, W:], ACROSS, preferred_element_type=F32
            ) * W ** (-0.5)
            visible = key_pos[side : side + 1] <= q_pos
            weight = jnp.where(visible, silu(scores), 0.0).astype(BF16)
            attn += jnp.dot(weight, kv[:, :W], preferred_element_type=F32)
        normed = attn * lax.rsqrt(jnp.mean(attn * attn, axis=-1, keepdims=True) + 1e-06)
        out = (normed * gate_query[span, :W].astype(F32)).astype(BF16)
        for s in range(NZ):
            part = out[s * piece : (s + 1) * piece]
            if s < 2:
                gated[s, k] = part
            else:
                gated[pl.ds(2 + ((s % 2) ^ flipped), 1), k] = part[None]


def hidden_kernel(where, *refs):
    n = len(PLANE)
    gated, late_own, late_other, tok = refs[:n], refs[n : n + 2], refs[n + 2 : n + 4], refs[n + 4 : -5]
    hidden, g_all, t_all, w_all, sems = refs[-5:]
    z, y, x, u = (where[i] for i in range(4))
    c = chip_at(z, y, x)
    rows = hidden.shape[1]
    half = w_all.shape[1]
    flipped = ((z + 1) // 2) % 2
    copies = []
    for s in range(NZ):
        cols = pl.ds(s * W, W)
        for side, src in enumerate((late_own, late_other)):
            panel = src[0].at[s] if s < 2 else src[1].at[(s % 2) ^ flipped]
            copies.append((panel.at[pl.ds(0, half), :], w_all.at[side, :, cols]))
        block = relative_chip(c, 0, 0, s)
        from_cols = pl.ds(pl.multiple_of(block * W, W), W)
        for k in range(n):
            copies.append((tok[k].at[pl.ds(0, rows), from_cols], t_all.at[k, :, cols]))
    copies = [pltpu.make_async_copy(a, b, sems.at[i]) for i, (a, b) in enumerate(copies)]
    for copy in copies:
        copy.start()
    for k, (by, bx) in enumerate(PLANE):
        for s in range(NZ):
            head = relative_chip(c, by, bx, s)
            cols = pl.ds(pl.multiple_of(head * W, W), W)
            for j, (jy, jx) in enumerate(PLANE):
                block = (jy ^ by) * NX + (jx ^ bx)
                g_all[block * rows : (block + 1) * rows, cols] = gated[k][s, j]
    for copy in copies:
        copy.wait()
    total = 0.0
    for side, at in enumerate((u, 1 - u)):
        part = g_all[:, pl.ds(pl.multiple_of(at * half, half), half)]
        total += jnp.dot(part, w_all[side], preferred_element_type=F32)
    for k in range(n):
        for s in range(NZ):
            term = total[k * rows : (k + 1) * rows, s * W : (s + 1) * W]
            cols = pl.ds(pl.multiple_of((z ^ s) * W, W), W)
            hidden[k, :, cols] = (t_all[k, :, s * W : (s + 1) * W].astype(F32) + term).astype(BF16)


def as_line(column):
    size = column.shape[0]
    line = lax.broadcasted_iota(jnp.int32, (size, size), 0)
    lane = lax.broadcasted_iota(jnp.int32, (size, size), 1)
    return jnp.sum(jnp.where(line == lane, column, 0.0), axis=0, keepdims=True)


def mass_kernel(where, *refs):
    n = len(PLANE)
    pieces, late_own, late_other = refs[:n], refs[n : n + 2], refs[n + 2 : n + 4]
    t_keep, t_send, marks = refs[n + 4 : n + 7]
    keep, send, positive, mass, h_all, raw, n_all, sems = refs[n + 7 :]
    y, x, u = (where[i] for i in range(1, 4))
    rows, half = keep.shape
    negs, panels = n_all.shape[2], half // W
    split = raw.shape[2]
    copies = []
    for side, src in enumerate((late_own, late_other)):
        for pair in range(2):
            rest = src[pair].at[:, pl.ds(src[pair].shape[1] - split, split), :]
            to = raw.at[side, pl.ds(2 * pair, 2)]
            copies.append(pltpu.make_async_copy(rest, to, sems.at[2 * side + pair]))
    for copy in copies:
        copy.start()
    for k, (by, bx) in enumerate(PLANE):
        for at in range(NZ):
            block = chip_at(at, y ^ by, x ^ bx)
            cols = pl.ds(pl.multiple_of(block * W, W), W)
            for j, (jy, jx) in enumerate(PLANE):
                row = ((jy ^ by) * NX + (jx ^ bx)) * rows
                h_all[row : row + rows, cols] = pieces[k][j, :, at * W : (at + 1) * W]
    mine = pl.ds(pl.multiple_of(u * half, half), half)
    theirs = pl.ds(pl.multiple_of((1 - u) * half, half), half)
    keep[...] = h_all[:rows, mine]
    send[...] = h_all[:rows, theirs]
    hh = 0.0
    for part in (mine, theirs):
        h_f = h_all[:, part].astype(F32)
        hh += jnp.sum(h_f * h_f, axis=1, keepdims=True)
    h_scale = lax.rsqrt(hh + 1e-06) * 20.0
    he = ee = 0.0
    for h_ref, ref in ((keep, t_keep), (send, t_send)):
        h_f, t_f = h_ref[...].astype(F32), ref[...].astype(F32)
        he += jnp.sum(h_f * t_f, axis=1, keepdims=True)
        ee += jnp.sum(t_f * t_f, axis=1, keepdims=True)
    positive[...] = as_line(he * lax.rsqrt(ee + 1e-06) * h_scale[:rows])
    first = [marks[k * NZ * rows : (k * NZ + 1) * rows] for k in range(n)]
    pick = pick_columns({4: 256.0, 5: 1.0})
    t_ids = lax.dot_general(
        jnp.concatenate(first), pick, ACROSS, preferred_element_type=F32
    )[:, :1]
    for copy in copies:
        copy.wait()
    total = 0.0
    for s in range(NZ):
        nn, dots = 0.0, 0.0
        for side, part in enumerate((mine, theirs)):
            for panel in range(panels):
                n_all[side, s, :, panel * W : (panel + 1) * W] = raw[
                    side, s, panel * negs : (panel + 1) * negs
                ]
            dots += lax.dot_general(
                h_all[:, part], n_all[side, s], ACROSS, preferred_element_type=F32
            )
            lines = raw[side, s, panels * negs :].astype(F32)
            nn += lines[0:1, :negs] + lines[1:2, :negs] + lines[2:3, :negs]
        n_ids = 256.0 * lines[3:4, :negs] + lines[4:5, :negs]
        neg_logit = dots * h_scale * lax.rsqrt(nn + 1e-06)
        kept = jnp.where(n_ids != t_ids, jnp.exp(neg_logit), 0.0)
        total += jnp.sum(kept, axis=1, keepdims=True)
    for k in range(n):
        mass[k] = as_line(total[k * rows : (k + 1) * rows])


def final_kernel(where, keep, theirs, positive, *refs):
    masses, (hidden, loss) = refs[:-2], refs[-2:]
    u, rows = where[3], keep.shape[0]
    hidden[pl.ds(pl.multiple_of(u * rows, rows), rows), :] = keep[...]
    hidden[pl.ds(pl.multiple_of((1 - u) * rows, rows), rows), :] = theirs[...]
    total = jnp.exp(positive[...])
    for mass in masses:
        total += mass[...]
    loss[...] = jnp.log(total) - positive[...]


def call(kernel, name, outs, scratch, args, places, flops):
    space = {"s": pltpu.SMEM, "v": pltpu.VMEM, "h": pltpu.HBM}
    moved = sum(a.size * a.dtype.itemsize for a in args)
    return pl.pallas_call(
        kernel,
        out_shape=[jax.ShapeDtypeStruct(shape, dtype) for shape, dtype in outs],
        in_specs=[pl.BlockSpec(memory_space=space[p]) for p in places],
        out_specs=[pl.BlockSpec(memory_space=pltpu.VMEM)] * len(outs),
        scratch_shapes=scratch,
        compiler_params=pltpu.CompilerParams(vmem_limit_bytes=VMEM_LIMIT),
        cost_estimate=pl.CostEstimate(flops=flops, bytes_accessed=moved, transcendentals=0),
        name=name,
    )(*args)


def whole_parts(value, base):
    return [(value // base).astype(BF16), (value % base).astype(BF16)]


def float_parts(value):
    parts = []
    for _ in range(3):
        parts.append(lax.reduce_precision(value, 8, 7))
        value = value - parts[-1]
    return [part.astype(BF16) for part in parts]


def with_marks(rows, marks):
    marks = jnp.stack(marks, 1)
    marks = jnp.pad(marks, ((0, 0), (0, W - marks.shape[1])))
    return jnp.concatenate([rows, marks], 1)


def head_shards(
    tokens, w_proj, w_out, positions, neg_emb, neg_ids, target_emb, target_ids
):
    c, u = lax.axis_index("ctx"), lax.axis_index("tp")
    z, y, x = coords(c)
    where = jnp.stack([z, y, x, u]).astype(jnp.int32)
    model = tokens.shape[1]
    rows = tokens.shape[0] // 2
    events = rows * CHIPS
    half = model // 2
    negs = neg_emb.shape[0]
    plane = len(PLANE)

    mine = lax.dynamic_slice_in_dim(tokens, u * rows, rows, 0)
    p_own = lax.dynamic_slice_in_dim(positions, u * rows, rows, 0)
    p_other = lax.dynamic_slice_in_dim(positions, (1 - u) * rows, rows, 0)
    ids = whole_parts(target_ids, 256)
    mine = with_marks(mine, whole_parts(p_own, 128) + whole_parts(p_other, 128) + ids)
    low = pair_up(mine)

    own_ids = lax.dynamic_slice_in_dim(neg_ids, c * negs, negs, 0)
    norms = jnp.sum(jnp.square(neg_emb.astype(F32)), axis=1)
    lines = jnp.stack(float_parts(norms) + whole_parts(own_ids, 256))
    lines = jnp.pad(lines, ((0, 16 - lines.shape[0]), (0, W - negs)))
    panels = neg_emb.reshape(negs, half // W, W).transpose(1, 0, 2).reshape(-1, W)
    late = jnp.concatenate([w_out, panels, lines])[None]

    to_x, to_y = flip(0, 1), flip(1, 0)
    high_met = inner_hop(low)
    w_plane, came = heads_in_plane(w_proj, y, x)
    low_x, low_y = hop(after(low, came), to_x), hop(after(low, came), to_y)
    late_pair = pair_up(after(late, low))
    late_met = inner_hop(after(late_pair, high_met))
    high = jnp.where(is_inner(z), high_met, outer_hop(high_met))
    high_x, high_y = hop(high, to_x), hop(high, to_y)
    low_xy, high_xy = hop(low_x, to_y), hop(high_y, to_x)
    tok = [low, high, low_x, high_x, low_y, high_y, low_xy, high_xy]
    w_mine = heads_along_z(after(w_plane, high, late_met), z)
    late_out = outer_hop(after(late_met, w_mine))
    w_mine = after(w_mine, high_x, low_y, low_xy, high_xy)
    w_theirs = swap_cores(w_mine)
    t_rows = target_emb.reshape(2, rows, -1)
    t_keep = pick_row(t_rows, u)
    t_send = swap_cores(pick_row(after(t_rows, w_theirs), 1 - u))

    def project(pieces):
        count = sum(p.shape[0] for p in pieces)
        return call(
            proj_kernel,
            "project",
            [((count, 2 * W), BF16)] * 2 + [((count, W), BF16)],
            [
                pltpu.VMEM((count, model + W), BF16),
                pltpu.VMEM((model, 4 * W), BF16),
                pltpu.SemaphoreType.DMA((len(pieces),)),
                pltpu.SemaphoreType.DMA((2,)),
            ],
            [where, *pieces, w_mine, w_theirs],
            "s" + (len(pieces) + 2) * "h",
            2 * count * model * 4 * W,
        )

    gate_query, value_key, marks = project(tok)
    kv_theirs = swap_cores(value_key)
    (gated,) = call(
        attend_kernel,
        "attend",
        [((NZ, plane, rows, W), BF16)],
        [],
        [where, gate_query, value_key, kv_theirs, marks],
        "svvvv",
        8 * events * events * W,
    )
    late_out = after(late_out, gated, t_send)
    gated = jnp.stack([gated[0]] + [hop(gated[s], flip(0, 0, s)) for s in range(1, NZ)])
    late_own = [late_pair, jnp.where(is_inner(z), late_met, late_out)]
    late_other = [swap_cores(piece) for piece in after(late_own, gated)]
    gated = [gated] + [hop(gated, flip(by, bx)) for by, bx in PLANE[1:]]
    (hidden,) = call(
        hidden_kernel,
        "hidden",
        [((plane, rows, NZ * W), BF16)],
        [
            pltpu.VMEM((plane * rows, model), BF16),
            pltpu.VMEM((plane, rows, NZ * W), BF16),
            pltpu.VMEM((2, half, NZ * W), BF16),
            pltpu.SemaphoreType.DMA((NZ * (2 + plane),)),
        ],
        [where, *gated, *late_own, *late_other, *tok[::2]],
        "s" + 4 * "v" + 8 * "h",
        2 * plane * rows * model * NZ * W,
    )
    pieces = [hidden] + [hop(hidden, flip(by, bx)) for by, bx in PLANE[1:]]
    h_keep, h_send, positive, mass = call(
        mass_kernel,
        "mass",
        [((rows, half), BF16)] * 2 + [((1, rows), F32), ((plane, 1, rows), F32)],
        [
            pltpu.VMEM((plane * rows, model), BF16),
            pltpu.VMEM((2, NZ, late.shape[1] - half, W), BF16),
            pltpu.VMEM((2, NZ, negs, half), BF16),
            pltpu.SemaphoreType.DMA((4,)),
        ],
        [where, *pieces, *late_own, *late_other, t_keep, t_send, marks],
        "s" + 4 * "v" + 4 * "h" + "vvv",
        2 * plane * rows * model * NZ * negs,
    )
    masses = [mass[0]] + [hop(mass[k], flip(*PLANE[k])) for k in range(1, plane)]
    h_theirs = swap_cores(h_send)
    hidden, loss = call(
        final_kernel,
        "final",
        [((2 * rows, half), BF16), ((1, rows), F32)],
        [],
        [where, h_keep, h_theirs, positive, *masses],
        "s" + 7 * "v",
        0,
    )
    return hidden, loss.reshape(-1)


def shards(tokens, w_proj, *rest):
    n_ctx, n_tp = lax.axis_size("ctx"), lax.axis_size("tp")
    heads = w_proj.shape[2] * n_tp // HEAD_DIM
    plan = head_shards if (n_ctx, n_tp, heads) == (CHIPS, 2, CHIPS) else general_shards
    return plan(tokens, w_proj, *rest)


def solution(mesh):
    placed = (
        P("ctx", None),
        P("ctx", None, "tp"),
        P("tp", "ctx"),
        P("ctx"),
        P("ctx", "tp"),
        P(),
        P("ctx", "tp"),
        P(("ctx", "tp")),
    )
    return jax.shard_map(
        shards,
        mesh=mesh,
        in_specs=placed,
        out_specs=(P("ctx", "tp"), P(("ctx", "tp"))),
        check_vma=False,
    )
```

```python
import jax
import jax.numpy as jnp
from jax import lax
from jax.experimental import pallas as pl
from jax.experimental.pallas import tpu as pltpu
from jax.sharding import PartitionSpec as P

HEAD_DIM = 128
VMEM_LIMIT = 48 * 1024 * 1024
BF16 = jnp.bfloat16
F32 = jnp.float32


def attend_piece(q_group, q_pos, k_piece, v_piece, p_piece):
    heads = q_group.shape[1]
    width = q_group.shape[2]
    key_heads = k_piece.reshape(k_piece.shape[0], heads, width)
    value_heads = v_piece.reshape(v_piece.shape[0], heads, width)
    scores = jnp.einsum(
        "thd,khd->htk", q_group, key_heads, preferred_element_type=jnp.float32
    ) * width ** (-0.5)
    visible = p_piece[None, None, :] <= q_pos[None, :, None]
    weight = jnp.where(visible, jax.nn.silu(scores), 0.0).astype(jnp.bfloat16)
    return jnp.einsum("htk,khd->thd", weight, value_heads, preferred_element_type=jnp.float32)


def general_shards(
    tokens, w_proj, w_out, positions, neg_emb, neg_ids, target_emb, target_ids
):
    tok_rows = tokens.shape[0]
    head_cols = w_proj.shape[2]
    local_heads = head_cols // HEAD_DIM
    proj_sum = jnp.einsum(
        "td,dfh->tfh",
        tokens,
        lax.all_gather(w_proj, "ctx", axis=0, tiled=True),
        preferred_element_type=jnp.float32,
    )
    proj = jax.nn.silu(proj_sum).astype(jnp.bfloat16)
    gate = proj[:, 0].reshape(tok_rows, local_heads, HEAD_DIM)
    query = proj[:, 2].reshape(tok_rows, local_heads, HEAD_DIM)
    v_piece = lax.all_gather(proj[:, 1], "ctx", axis=0, tiled=True)
    k_piece = lax.all_gather(proj[:, 3], "ctx", axis=0, tiled=True)
    p_piece = lax.all_gather(positions, "ctx", axis=0, tiled=True)
    attn = attend_piece(query, positions, k_piece, v_piece, p_piece)
    normed = attn * lax.rsqrt(jnp.mean(attn * attn, axis=-1, keepdims=True) + 1e-06)
    gated = (normed * gate.astype(jnp.float32)).astype(jnp.bfloat16).reshape(tok_rows, head_cols)
    out_terms = jnp.dot(
        gated, lax.all_gather(w_out, "ctx", axis=1, tiled=True), preferred_element_type=jnp.float32
    )
    out_share = lax.psum_scatter(out_terms, "tp", scatter_dimension=1, tiled=True)
    feat_cols = out_share.shape[1]
    own_tokens = lax.dynamic_slice_in_dim(tokens, lax.axis_index("tp") * feat_cols, feat_cols, 1)
    hidden = (own_tokens.astype(jnp.float32) + out_share).astype(jnp.bfloat16)
    piece = lax.all_gather(neg_emb, "ctx", axis=0, tiled=True)
    panel_dots = lax.dot_general(
        hidden, piece, (((1,), (1,)), ((), ())), preferred_element_type=jnp.float32
    )
    panel_norms = jnp.sum(jnp.square(piece.astype(jnp.float32)), axis=1)
    hidden_f = hidden.astype(jnp.float32)
    target_f = target_emb.astype(jnp.float32)
    part_hh = jnp.sum(hidden_f * hidden_f, axis=1)
    part_he = jnp.sum(hidden_f * target_f, axis=1)
    part_ee = jnp.sum(target_f * target_f, axis=1)
    dots, hh_sum, he_sum, ee_sum = (
        lax.psum_scatter(panel_dots, "tp", scatter_dimension=0, tiled=True),
        lax.psum_scatter(part_hh, "tp", scatter_dimension=0, tiled=True),
        lax.psum_scatter(part_he, "tp", scatter_dimension=0, tiled=True),
        lax.psum_scatter(part_ee, "tp", scatter_dimension=0, tiled=True),
    )
    neg_sq = lax.psum(panel_norms, "tp")
    pos_logit = he_sum / jnp.sqrt(hh_sum + 1e-06) / jnp.sqrt(ee_sum + 1e-06) / 0.05
    neg_logit = dots / jnp.sqrt(hh_sum + 1e-06)[:, None] / jnp.sqrt(neg_sq + 1e-06)[None, :] / 0.05
    keep_mask = neg_ids[None, :] != target_ids[:, None]
    total_mass = jnp.exp(pos_logit) + jnp.sum(jnp.where(keep_mask, jnp.exp(neg_logit), 0.0), axis=1)
    loss = jnp.log(total_mass) - pos_logit
    return (hidden, loss)


NZ, NY, NX = 4, 2, 2
CHIPS = NZ * NY * NX
PLANE = [(by, bx) for by in range(NY) for bx in range(NX)]
BITS = [(0, 0), (0, 1), (1, 0), (1, 1)]
SWAP = [(0, 1), (1, 0)]
W = HEAD_DIM
ACROSS = (((1,), (1,)), ((), ()))


def chip_at(z, y, x):
    return (z * NY + y) * NX + x


def coords(c):
    return c // (NY * NX), (c // NX) % NY, c % NX


def relative_chip(c, by, bx, s):
    z, y, x = coords(c)
    return chip_at(z ^ s, y ^ by, x ^ bx)


def flip(by, bx, s=0):
    return [(c, relative_chip(c, by, bx, s)) for c in range(CHIPS)]


def hop(value, perm):
    return lax.ppermute(value, "ctx", perm)


def swap_cores(value):
    return lax.ppermute(value, "tp", SWAP)


def pick_row(value, at):
    return lax.dynamic_index_in_dim(value, at, 0, keepdims=False)


def after(values, *others):
    return lax.optimization_barrier((values, others))[0]


def pair_up(own):
    return jnp.concatenate([own, hop(own, flip(0, 0, 1))])


def across(value_x, value_y):
    half = value_x.shape[0] // 2
    return [hop(value_x[:half], flip(1, 0)), hop(value_y[half:], flip(0, 1))]


def heads_in_plane(w_proj, y, x, first):
    plane = NY * NX
    heads = w_proj.reshape(-1, 4, 2, plane, W).transpose(3, 2, 0, 1, 4)
    heads = heads.reshape(plane, 2, -1, 4 * W)
    out = jnp.zeros((2, plane, *heads.shape[2:]), heads.dtype)
    came = []
    for by, bx in PLANE:
        spot = (y ^ by) * NX + (x ^ bx)
        piece = pick_row(heads, spot)
        if (by, bx) != (0, 0):
            piece = hop(after(piece, first), flip(by, bx))
            came.append(piece)
        out = lax.dynamic_update_slice_in_dim(out, piece[:, None], spot, 1)
    return out, came


def heads_along_z(heads, z):
    arrived = []
    for e in range(2):
        perm = []
        for src in range(CHIPS):
            sz, sy, sx = coords(src)
            for t in range(2):
                dst = chip_at(2 * t + (e ^ (sz & 1)), sy, sx)
                perm.append((2 * src + t, 2 * dst + (sz >> 1)))
        arrived.append(lax.ppermute(pick_row(heads, e ^ (z & 1)), ("ctx", "tp"), perm))
    rows = jnp.where(z % 2 == 0, jnp.stack(arrived), jnp.stack(arrived[::-1]))
    return rows.reshape(-1, rows.shape[-1])


def silu(v):
    return 0.5 * v * (1.0 + jnp.tanh(0.5 * v))


def run_copies(copies):
    for copy in copies:
        copy.start()
    for copy in copies:
        copy.wait()


def proj_kernel(where, *refs):
    count = len(refs) - 9
    tok, (w_own, w_other) = refs[:count], refs[count : count + 2]
    gate_query, value_key, marks, x_all, w_all, tok_sem, w_sem = refs[count + 2 :]
    u = where[3]
    copies, base = [], 0
    half = w_own.shape[0]
    for side, (at, src) in enumerate(((u, w_own), (1 - u, w_other))):
        rows = pl.ds(pl.multiple_of(at * half, half), half)
        copies.append(pltpu.make_async_copy(src, w_all.at[rows, :], w_sem.at[side]))
    for i, ref in enumerate(tok):
        rows = pl.ds(base, ref.shape[0])
        copies.append(pltpu.make_async_copy(ref, x_all.at[rows, :], tok_sem.at[i]))
        base += ref.shape[0]
    run_copies(copies)
    model = w_all.shape[0]
    total = jnp.dot(x_all[:, :model], w_all[...], preferred_element_type=F32)
    proj = silu(total).astype(BF16)
    gate_query[:, :W] = proj[:, :W]
    value_key[:, :W] = proj[:, W : 2 * W]
    gate_query[:, W:] = proj[:, 2 * W : 3 * W]
    value_key[:, W:] = proj[:, 3 * W :]
    marks[...] = x_all[:, model:]


def pick_columns(*weights):
    lane = lax.broadcasted_iota(jnp.int32, (8, W), 1)
    line = lax.broadcasted_iota(jnp.int32, (8, W), 0)
    pick = jnp.zeros((8, W), F32)
    for i, row in enumerate(weights):
        for at, weight in row.items():
            pick = jnp.where((line == i) & (lane == at), weight, pick)
    return pick.astype(BF16)


def attend_kernel(gq_hbm, own_hbm, other_hbm, marks_hbm, gated, gate_query, own, other, marks, sems):
    sources = (gq_hbm, own_hbm, other_hbm, marks_hbm)
    run_copies(
        [
            pltpu.make_async_copy(src, dst, sems.at[i])
            for i, (src, dst) in enumerate(zip(sources, (gate_query, own, other, marks)))
        ]
    )
    pick = pick_columns({0: 128.0, 1: 1.0}, {2: 128.0, 3: 1.0})
    piece = gated.shape[3]
    tile = NZ * piece
    key_pos = lax.dot_general(pick, marks[...], ACROSS, preferred_element_type=F32)
    for k, (by, bx) in enumerate(PLANE):
        span = pl.ds(k * tile, tile)
        query = gate_query[span, W:]
        q_pos = lax.dot_general(marks[span, :], pick, ACROSS, preferred_element_type=F32)[:, :1]
        attn = jnp.zeros((tile, W), F32)
        for side, kv in enumerate((own, other)):
            scores = lax.dot_general(
                query, kv[:, W:], ACROSS, preferred_element_type=F32
            ) * W ** (-0.5)
            visible = key_pos[side : side + 1] <= q_pos
            weight = jnp.where(visible, silu(scores), 0.0).astype(BF16)
            attn += jnp.dot(weight, kv[:, :W], preferred_element_type=F32)
        normed = attn * lax.rsqrt(jnp.mean(attn * attn, axis=-1, keepdims=True) + 1e-06)
        out = (normed * gate_query[span, :W].astype(F32)).astype(BF16)
        for s in range(NZ):
            gated[s % 2, bx, 2 * (s // 2) + by] = out[s * piece : (s + 1) * piece]


def hidden_kernel(where, *refs):
    gated, w_own, w_other, tok = refs[:4], refs[4:6], refs[6:8], refs[8:12]
    hidden, g_raw, g_all, t_all, w_all, sems = refs[12:]
    z, y, x, u = (where[i] for i in range(4))
    rows = hidden.shape[1]
    half = w_all.shape[1]
    copies = [(src, g_raw.at[k]) for k, src in enumerate(gated)]
    for e, d in BITS:
        cols = pl.ds((2 * e + d) * W, W)
        for side, src in enumerate((w_own, w_other)):
            copies.append((src[e].at[d], w_all.at[side, :, cols]))
        block = chip_at(z ^ e, y, x ^ d)
        from_cols = pl.ds(pl.multiple_of(block * W, W), W)
        for k in range(4):
            copies.append((tok[k].at[pl.ds(0, rows), from_cols], t_all.at[k, :, cols]))
    copies = [pltpu.make_async_copy(src, dst, sems.at[i]) for i, (src, dst) in enumerate(copies)]
    for copy in copies:
        copy.start()
    for copy in copies[:4]:
        copy.wait()
    for k, (far, by) in enumerate(BITS):
        for e, d in BITS:
            head = chip_at(z ^ (2 * far + e), y ^ by, x ^ d)
            cols = pl.ds(pl.multiple_of(head * W, W), W)
            for j in range(4):
                block = j ^ k
                g_all[block * rows : (block + 1) * rows, cols] = g_raw[k, e, d, j]
    for copy in copies[4:]:
        copy.wait()
    total = 0.0
    for side, at in enumerate((u, 1 - u)):
        part = g_all[:, pl.ds(pl.multiple_of(at * half, half), half)]
        total += jnp.dot(part, w_all[side], preferred_element_type=F32)
    for k in range(4):
        terms = total[k * rows : (k + 1) * rows]
        hidden[k] = (t_all[k].astype(F32) + terms).astype(BF16)


def order_kernel(where, *refs):
    pieces, (keep, send, h_all) = refs[:4], refs[4:]
    z, y, x, u = (where[i] for i in range(4))
    half = keep.shape[1]
    for (far, by), ref in zip(BITS, pieces):
        for e, d in BITS:
            block = chip_at(z ^ (2 * far + e), y ^ by, x ^ d)
            from_cols = slice((2 * e + d) * W, (2 * e + d + 1) * W)
            h_all[:, pl.ds(pl.multiple_of(block * W, W), W)] = ref[:, from_cols]
    keep[...] = h_all[:, pl.ds(pl.multiple_of(u * half, half), half)]
    send[...] = h_all[:, pl.ds(pl.multiple_of((1 - u) * half, half), half)]


def loss_kernel(h_keep, h_send, t_keep, t_send, t_ids, n_own, n_other, loss, n_all, sems):
    keep, send = h_keep[...], h_send[...]
    half = keep.shape[1]
    copies = []
    for side, src in enumerate((n_own, n_other)):
        copies.append(pltpu.make_async_copy(src, n_all.at[side], sems.at[side]))
    for copy in copies:
        copy.start()
    hh = he = ee = 0.0
    for part, ref in ((keep, t_keep), (send, t_send)):
        h_f, t_f = part.astype(F32), ref[...].astype(F32)
        hh += jnp.sum(h_f * h_f, axis=1, keepdims=True)
        he += jnp.sum(h_f * t_f, axis=1, keepdims=True)
        ee += jnp.sum(t_f * t_f, axis=1, keepdims=True)
    h_scale = lax.rsqrt(hh + 1e-06) * 20.0
    pos_logit = he * lax.rsqrt(ee + 1e-06) * h_scale
    for copy in copies:
        copy.wait()
    pick = pick_columns({0: 1.0, 1: 1.0, 2: 1.0}, {3: 256.0, 4: 1.0})
    dots, read = 0.0, []
    for side, part in enumerate((keep, send)):
        neg, marks = n_all[side, :, :half], n_all[side, :, half:]
        dots += lax.dot_general(part, neg, ACROSS, preferred_element_type=F32)
        read.append(lax.dot_general(pick, marks, ACROSS, preferred_element_type=F32))
    nn = read[0][0:1] + read[1][0:1]
    n_ids = read[0][1:2]
    neg_logit = dots * h_scale * lax.rsqrt(nn + 1e-06)
    mass = jnp.where(n_ids != t_ids[...].astype(F32), jnp.exp(neg_logit), 0.0)
    total = jnp.exp(pos_logit) + jnp.sum(mass, axis=1, keepdims=True)
    column = jnp.log(total) - pos_logit
    size = column.shape[0]
    line = lax.broadcasted_iota(jnp.int32, (size, size), 0)
    lane = lax.broadcasted_iota(jnp.int32, (size, size), 1)
    loss[...] = jnp.sum(jnp.where(line == lane, column, 0.0), axis=0, keepdims=True)


def join_kernel(where, keep, theirs, hidden):
    u, rows = where[3], keep.shape[0]
    hidden[pl.ds(pl.multiple_of(u * rows, rows), rows), :] = keep[...]
    hidden[pl.ds(pl.multiple_of((1 - u) * rows, rows), rows), :] = theirs[...]


def call(kernel, name, outs, scratch, args, places, flops):
    space = {"s": pltpu.SMEM, "v": pltpu.VMEM, "h": pltpu.HBM}
    moved = sum(a.size * a.dtype.itemsize for a in args)
    return pl.pallas_call(
        kernel,
        out_shape=[jax.ShapeDtypeStruct(shape, dtype) for shape, dtype in outs],
        in_specs=[pl.BlockSpec(memory_space=space[p]) for p in places],
        out_specs=[pl.BlockSpec(memory_space=pltpu.VMEM)] * len(outs),
        scratch_shapes=scratch,
        compiler_params=pltpu.CompilerParams(vmem_limit_bytes=VMEM_LIMIT),
        cost_estimate=pl.CostEstimate(flops=flops, bytes_accessed=moved, transcendentals=0),
        name=name,
    )(*args)


def whole_parts(value, base):
    return [(value // base).astype(BF16), (value % base).astype(BF16)]


def float_parts(value):
    parts = []
    for _ in range(3):
        parts.append(lax.reduce_precision(value, 8, 7))
        value = value - parts[-1]
    return [part.astype(BF16) for part in parts]


def with_marks(rows, marks):
    marks = jnp.stack(marks, 1)
    marks = jnp.pad(marks, ((0, 0), (0, W - marks.shape[1])))
    return jnp.concatenate([rows, marks], 1)


def head_shards(
    tokens, w_proj, w_out, positions, neg_emb, neg_ids, target_emb, target_ids
):
    c, u = lax.axis_index("ctx"), lax.axis_index("tp")
    z, y, x = coords(c)
    where = jnp.stack([z, y, x, u]).astype(jnp.int32)
    model = tokens.shape[1]
    rows = tokens.shape[0] // 2
    events = rows * CHIPS
    half = model // 2
    negs = neg_emb.shape[0]
    plane = len(PLANE)

    mine = lax.dynamic_slice_in_dim(tokens, u * rows, rows, 0)
    p_own = lax.dynamic_slice_in_dim(positions, u * rows, rows, 0)
    p_other = lax.dynamic_slice_in_dim(positions, (1 - u) * rows, rows, 0)
    mine = with_marks(mine, whole_parts(p_own, 128) + whole_parts(p_other, 128))
    low = pair_up(mine)

    to_x, to_y = flip(0, 1), flip(1, 0)
    own_ids = lax.dynamic_slice_in_dim(neg_ids, c * negs, negs, 0)
    norms = jnp.sum(jnp.square(neg_emb.astype(F32)), axis=1)
    neg = with_marks(neg_emb, float_parts(norms) + whole_parts(own_ids, 256))
    high = hop(low, flip(0, 0, 2))
    w_plane, came = heads_in_plane(w_proj, y, x, low)
    low_late = after(low, came)
    out_row = jnp.concatenate([w_out[None], hop(after(w_out[None], came), to_x)])
    neg_pair = pair_up(after(neg, came))
    low_x, low_y = hop(low_late, to_x), hop(low_late, to_y)
    low_xy = across(low_x, low_y)
    high = after(high, out_row, neg_pair)
    high_x, high_y = hop(high, to_x), hop(high, to_y)
    high_xy = across(high_x, high_y)
    out_own = [out_row, hop(after(out_row, high), flip(0, 0, 1))]
    tok = [low, high, low_x, high_x, low_y, high_y, *low_xy, *high_xy]
    w_mine = heads_along_z(after(w_plane, high), z)

    t_rows = after(target_emb.reshape(2, rows, -1), high)
    t_keep = pick_row(t_rows, u)
    t_send = swap_cores(pick_row(t_rows, 1 - u))
    w_mine = after(w_mine, low_xy, high_xy, out_own, t_send)
    w_theirs = swap_cores(w_mine)
    neg_far = hop(after(neg_pair, w_mine), flip(0, 0, 2))
    neg_near = jnp.concatenate([neg_pair, neg_far])
    neg_x, neg_y = hop(neg_near, to_x), hop(neg_near, to_y)

    def project(pieces):
        count = sum(p.shape[0] for p in pieces)
        return call(
            proj_kernel,
            "project",
            [((count, 2 * W), BF16)] * 2 + [((count, W), BF16)],
            [
                pltpu.VMEM((count, model + W), BF16),
                pltpu.VMEM((model, 4 * W), BF16),
                pltpu.SemaphoreType.DMA((len(pieces),)),
                pltpu.SemaphoreType.DMA((2,)),
            ],
            [where, *pieces, w_mine, w_theirs],
            "s" + (len(pieces) + 2) * "h",
            2 * count * model * 4 * W,
        )

    gate_query, value_key, marks = project(tok)
    kv_theirs = swap_cores(after(value_key, neg_far))
    (gated,) = call(
        attend_kernel,
        "attend",
        [((2, 2, 4, rows, W), BF16)],
        [pltpu.VMEM((events, 2 * W), BF16)] * 3
        + [pltpu.VMEM((events, W), BF16), pltpu.SemaphoreType.DMA((4,))],
        [gate_query, value_key, kv_theirs, marks],
        4 * "h",
        8 * events * events * W,
    )
    out_other = [swap_cores(w) for w in after(out_own, gated)]
    hops = [hop(gated[e, d], flip(0, d, e)) for e, d in BITS[1:]]
    gated = jnp.stack([gated[0, 0], *hops]).reshape(gated.shape)
    gated = [gated] + [hop(gated, flip(by, 0, 2 * far)) for far, by in BITS[1:]]
    neg_x, neg_y = after((neg_x, neg_y), gated)
    neg_own = [neg_near, neg_x, neg_y, *across(neg_x, neg_y)]
    (hidden,) = call(
        hidden_kernel,
        "hidden",
        [((4, rows, 4 * W), BF16)],
        [
            pltpu.VMEM((4, 2, 2, 4, rows, W), BF16),
            pltpu.VMEM((4 * rows, model), BF16),
            pltpu.VMEM((4, rows, 4 * W), BF16),
            pltpu.VMEM((2, half, 4 * W), BF16),
            pltpu.SemaphoreType.DMA((28,)),
        ],
        [where, *gated, *out_own, *out_other, low, low_y, high, high_y],
        "s" + 12 * "h",
        8 * rows * model * 4 * W,
    )
    pieces = [hidden[0]]
    pieces += [hop(hidden[k], flip(BITS[k][1], 0, 2 * BITS[k][0])) for k in range(1, 4)]
    neg_own = jnp.concatenate(after(neg_own, hidden))
    neg_other = swap_cores(neg_own)
    h_keep, h_send = call(
        order_kernel,
        "order",
        [((rows, half), BF16)] * 2,
        [pltpu.VMEM((rows, model), BF16)],
        [where, *pieces],
        "svvvv",
        0,
    )
    h_theirs = swap_cores(h_send)
    (loss,) = call(
        loss_kernel,
        "loss",
        [((1, rows), F32)],
        [
            pltpu.VMEM((2, CHIPS * negs, half + W), BF16),
            pltpu.SemaphoreType.DMA((2,)),
        ],
        [h_keep, h_send, t_keep, t_send, target_ids[:, None], neg_own, neg_other],
        "vvvvvhh",
        2 * rows * model * neg_ids.shape[0],
    )
    (hidden,) = call(
        join_kernel,
        "join",
        [((2 * rows, half), BF16)],
        [],
        [where, h_keep, after(h_theirs, loss)],
        "svv",
        0,
    )
    return hidden, loss.reshape(-1)


def shards(tokens, w_proj, *rest):
    n_ctx, n_tp = lax.axis_size("ctx"), lax.axis_size("tp")
    heads = w_proj.shape[2] * n_tp // HEAD_DIM
    plan = head_shards if (n_ctx, n_tp, heads) == (CHIPS, 2, CHIPS) else general_shards
    return plan(tokens, w_proj, *rest)


def solution(mesh):
    placed = (
        P("ctx", None),
        P("ctx", None, "tp"),
        P("tp", "ctx"),
        P("ctx"),
        P("ctx", "tp"),
        P(),
        P("ctx", "tp"),
        P(("ctx", "tp")),
    )
    return jax.shard_map(
        shards,
        mesh=mesh,
        in_specs=placed,
        out_specs=(P("ctx", "tp"), P(("ctx", "tp"))),
        check_vma=False,
    )
```

```python
import jax
import jax.numpy as jnp
from jax import lax
from jax.experimental import pallas as pl
from jax.experimental.pallas import tpu as pltpu
from jax.sharding import PartitionSpec as P

HEAD_DIM = 128
VMEM_LIMIT = 48 * 1024 * 1024
BF16 = jnp.bfloat16
F32 = jnp.float32


def attend_piece(q_group, q_pos, k_piece, v_piece, p_piece):
    heads = q_group.shape[1]
    width = q_group.shape[2]
    key_heads = k_piece.reshape(k_piece.shape[0], heads, width)
    value_heads = v_piece.reshape(v_piece.shape[0], heads, width)
    scores = jnp.einsum(
        "thd,khd->htk", q_group, key_heads, preferred_element_type=jnp.float32
    ) * width ** (-0.5)
    visible = p_piece[None, None, :] <= q_pos[None, :, None]
    weight = jnp.where(visible, jax.nn.silu(scores), 0.0).astype(jnp.bfloat16)
    return jnp.einsum("htk,khd->thd", weight, value_heads, preferred_element_type=jnp.float32)


def general_shards(
    tokens, w_proj, w_out, positions, neg_emb, neg_ids, target_emb, target_ids
):
    tok_rows = tokens.shape[0]
    head_cols = w_proj.shape[2]
    local_heads = head_cols // HEAD_DIM
    proj_sum = jnp.einsum(
        "td,dfh->tfh",
        tokens,
        lax.all_gather(w_proj, "ctx", axis=0, tiled=True),
        preferred_element_type=jnp.float32,
    )
    proj = jax.nn.silu(proj_sum).astype(jnp.bfloat16)
    gate = proj[:, 0].reshape(tok_rows, local_heads, HEAD_DIM)
    query = proj[:, 2].reshape(tok_rows, local_heads, HEAD_DIM)
    v_piece = lax.all_gather(proj[:, 1], "ctx", axis=0, tiled=True)
    k_piece = lax.all_gather(proj[:, 3], "ctx", axis=0, tiled=True)
    p_piece = lax.all_gather(positions, "ctx", axis=0, tiled=True)
    attn = attend_piece(query, positions, k_piece, v_piece, p_piece)
    normed = attn * lax.rsqrt(jnp.mean(attn * attn, axis=-1, keepdims=True) + 1e-06)
    gated = (normed * gate.astype(jnp.float32)).astype(jnp.bfloat16).reshape(tok_rows, head_cols)
    out_terms = jnp.dot(
        gated, lax.all_gather(w_out, "ctx", axis=1, tiled=True), preferred_element_type=jnp.float32
    )
    out_share = lax.psum_scatter(out_terms, "tp", scatter_dimension=1, tiled=True)
    feat_cols = out_share.shape[1]
    own_tokens = lax.dynamic_slice_in_dim(tokens, lax.axis_index("tp") * feat_cols, feat_cols, 1)
    hidden = (own_tokens.astype(jnp.float32) + out_share).astype(jnp.bfloat16)
    piece = lax.all_gather(neg_emb, "ctx", axis=0, tiled=True)
    panel_dots = lax.dot_general(
        hidden, piece, (((1,), (1,)), ((), ())), preferred_element_type=jnp.float32
    )
    panel_norms = jnp.sum(jnp.square(piece.astype(jnp.float32)), axis=1)
    hidden_f = hidden.astype(jnp.float32)
    target_f = target_emb.astype(jnp.float32)
    part_hh = jnp.sum(hidden_f * hidden_f, axis=1)
    part_he = jnp.sum(hidden_f * target_f, axis=1)
    part_ee = jnp.sum(target_f * target_f, axis=1)
    dots, hh_sum, he_sum, ee_sum = (
        lax.psum_scatter(panel_dots, "tp", scatter_dimension=0, tiled=True),
        lax.psum_scatter(part_hh, "tp", scatter_dimension=0, tiled=True),
        lax.psum_scatter(part_he, "tp", scatter_dimension=0, tiled=True),
        lax.psum_scatter(part_ee, "tp", scatter_dimension=0, tiled=True),
    )
    neg_sq = lax.psum(panel_norms, "tp")
    pos_logit = he_sum / jnp.sqrt(hh_sum + 1e-06) / jnp.sqrt(ee_sum + 1e-06) / 0.05
    neg_logit = dots / jnp.sqrt(hh_sum + 1e-06)[:, None] / jnp.sqrt(neg_sq + 1e-06)[None, :] / 0.05
    keep_mask = neg_ids[None, :] != target_ids[:, None]
    total_mass = jnp.exp(pos_logit) + jnp.sum(jnp.where(keep_mask, jnp.exp(neg_logit), 0.0), axis=1)
    loss = jnp.log(total_mass) - pos_logit
    return (hidden, loss)


NZ, NY, NX = 4, 2, 2
CHIPS = NZ * NY * NX
PLANE = [(by, bx) for by in range(NY) for bx in range(NX)]
SWAP = [(0, 1), (1, 0)]
W = HEAD_DIM
ACROSS = (((1,), (1,)), ((), ()))


def chip_at(z, y, x):
    return (z * NY + y) * NX + x


def coords(c):
    return c // (NY * NX), (c // NX) % NY, c % NX


def relative_chip(c, by, bx, s):
    z, y, x = coords(c)
    return chip_at(z ^ s, y ^ by, x ^ bx)


def flip(by, bx, s=0):
    return [(c, relative_chip(c, by, bx, s)) for c in range(CHIPS)]


def hop(value, perm):
    return lax.ppermute(value, "ctx", perm)


def swap_cores(value):
    return lax.ppermute(value, "tp", SWAP)


def pick_row(value, at):
    return lax.dynamic_index_in_dim(value, at, 0, keepdims=False)


def after(values, *others):
    return lax.optimization_barrier((values, others))[0]


def pair_up(own):
    return jnp.concatenate([own, hop(own, flip(0, 0, 1))])


def across(value_x, value_y):
    half = value_x.shape[0] // 2
    return [hop(value_x[:half], flip(1, 0)), hop(value_y[half:], flip(0, 1))]


def heads_in_plane(w_proj, y, x, first):
    plane = NY * NX
    heads = w_proj.reshape(-1, 4, 2, plane, W).transpose(3, 2, 0, 1, 4)
    heads = heads.reshape(plane, 2, -1, 4 * W)
    out = jnp.zeros((2, plane, *heads.shape[2:]), heads.dtype)
    came = []
    for by, bx in PLANE:
        spot = (y ^ by) * NX + (x ^ bx)
        piece = pick_row(heads, spot)
        if (by, bx) != (0, 0):
            piece = hop(after(piece, first), flip(by, bx))
            came.append(piece)
        out = lax.dynamic_update_slice_in_dim(out, piece[:, None], spot, 1)
    return out, came


def heads_along_z(heads, z):
    arrived = []
    for e in range(2):
        perm = []
        for src in range(CHIPS):
            sz, sy, sx = coords(src)
            for t in range(2):
                dst = chip_at(2 * t + (e ^ (sz & 1)), sy, sx)
                perm.append((2 * src + t, 2 * dst + (sz >> 1)))
        arrived.append(lax.ppermute(pick_row(heads, e ^ (z & 1)), ("ctx", "tp"), perm))
    rows = jnp.where(z % 2 == 0, jnp.stack(arrived), jnp.stack(arrived[::-1]))
    return rows.reshape(-1, rows.shape[-1])


def silu(v):
    return 0.5 * v * (1.0 + jnp.tanh(0.5 * v))


def run_copies(copies):
    for copy in copies:
        copy.start()
    for copy in copies:
        copy.wait()


def proj_kernel(where, *refs):
    count = len(refs) - 9
    tok, (w_own, w_other) = refs[:count], refs[count : count + 2]
    gate_query, value_key, marks, x_all, w_all, tok_sem, w_sem = refs[count + 2 :]
    u = where[3]
    copies, base = [], 0
    half = w_own.shape[0]
    for side, (at, src) in enumerate(((u, w_own), (1 - u, w_other))):
        rows = pl.ds(pl.multiple_of(at * half, half), half)
        copies.append(pltpu.make_async_copy(src, w_all.at[rows, :], w_sem.at[side]))
    for i, ref in enumerate(tok):
        rows = pl.ds(base, ref.shape[0])
        copies.append(pltpu.make_async_copy(ref, x_all.at[rows, :], tok_sem.at[i]))
        base += ref.shape[0]
    run_copies(copies)
    model = w_all.shape[0]
    total = jnp.dot(x_all[:, :model], w_all[...], preferred_element_type=F32)
    proj = silu(total).astype(BF16)
    gate_query[:, :W] = proj[:, :W]
    value_key[:, :W] = proj[:, W : 2 * W]
    gate_query[:, W:] = proj[:, 2 * W : 3 * W]
    value_key[:, W:] = proj[:, 3 * W :]
    marks[...] = x_all[:, model:]


def pick_columns(*weights):
    lane = lax.broadcasted_iota(jnp.int32, (8, W), 1)
    line = lax.broadcasted_iota(jnp.int32, (8, W), 0)
    pick = jnp.zeros((8, W), F32)
    for i, row in enumerate(weights):
        for at, weight in row.items():
            pick = jnp.where((line == i) & (lane == at), weight, pick)
    return pick.astype(BF16)


def attend_kernel(where, gq_hbm, own_hbm, other_hbm, marks_hbm, gated, gate_query, own, other, marks, sems):
    z, y, x = (where[i] for i in range(3))
    sources = (gq_hbm, own_hbm, other_hbm, marks_hbm)
    run_copies(
        [
            pltpu.make_async_copy(src, dst, sems.at[i])
            for i, (src, dst) in enumerate(zip(sources, (gate_query, own, other, marks)))
        ]
    )
    pick = pick_columns({0: 128.0, 1: 1.0}, {2: 128.0, 3: 1.0})
    piece = gated.shape[1]
    tile = NZ * piece
    key_pos = lax.dot_general(pick, marks[...], ACROSS, preferred_element_type=F32)
    for k, (by, bx) in enumerate(PLANE):
        span = pl.ds(k * tile, tile)
        query = gate_query[span, W:]
        q_pos = lax.dot_general(marks[span, :], pick, ACROSS, preferred_element_type=F32)[:, :1]
        attn = jnp.zeros((tile, W), F32)
        for side, kv in enumerate((own, other)):
            scores = lax.dot_general(
                query, kv[:, W:], ACROSS, preferred_element_type=F32
            ) * W ** (-0.5)
            visible = key_pos[side : side + 1] <= q_pos
            weight = jnp.where(visible, silu(scores), 0.0).astype(BF16)
            attn += jnp.dot(weight, kv[:, :W], preferred_element_type=F32)
        normed = attn * lax.rsqrt(jnp.mean(attn * attn, axis=-1, keepdims=True) + 1e-06)
        out = (normed * gate_query[span, :W].astype(F32)).astype(BF16)
        for s in range(NZ):
            chip = chip_at(z ^ s, y ^ by, x ^ bx)
            gated[pl.ds(chip, 1)] = out[s * piece : (s + 1) * piece][None]


def hidden_kernel(where, gated, low, high, low_other, high_other, tokens, *refs):
    keep, send, g_all, h_all, w_all, sems = refs
    z, y, x, u = (where[i] for i in range(4))
    chips, rows, _ = gated.shape
    half = chips * W // 2
    copies = []
    for group, sides in enumerate(((low, low_other), (high, high_other))):
        for at in range(chips // 2):
            cols = pl.ds((group * chips // 2 + at) * W, W)
            for side, src in enumerate(sides):
                sem = sems.at[len(copies)]
                copies.append(pltpu.make_async_copy(src.at[at], w_all.at[side, :, cols], sem))
    for copy in copies:
        copy.start()
    for chip in range(chips):
        g_all[:, chip * W : (chip + 1) * W] = gated[chip]
    g_own = g_all[:, pl.ds(pl.multiple_of(u * half, half), half)]
    g_other = g_all[:, pl.ds(pl.multiple_of((1 - u) * half, half), half)]
    for group in range(2):
        for k, (by, bx) in enumerate(PLANE):
            at = group * len(PLANE) + k
            for copy in copies[4 * at : 4 * at + 4]:
                copy.wait()
            panels = slice(2 * at * W, 2 * (at + 1) * W)
            total = jnp.dot(g_own, w_all[0, :, panels], preferred_element_type=F32)
            total += jnp.dot(g_other, w_all[1, :, panels], preferred_element_type=F32)
            for j in range(2):
                chip = chip_at(z ^ (2 * group + j), y ^ by, x ^ bx)
                cols = pl.ds(pl.multiple_of(chip * W, W), W)
                term = total[:, j * W : (j + 1) * W]
                h_all[:, cols] = (tokens[:, cols].astype(F32) + term).astype(BF16)
    keep[...] = h_all[:, pl.ds(pl.multiple_of(u * half, half), half)]
    send[...] = h_all[:, pl.ds(pl.multiple_of((1 - u) * half, half), half)]


def loss_kernel(h_keep, h_send, t_keep, t_send, t_ids, n_own, n_other, loss, n_all, sems):
    keep, send = h_keep[...], h_send[...]
    half = keep.shape[1]
    copies = []
    for side, src in enumerate((n_own, n_other)):
        copies.append(pltpu.make_async_copy(src, n_all.at[side], sems.at[side]))
    for copy in copies:
        copy.start()
    hh = he = ee = 0.0
    for part, ref in ((keep, t_keep), (send, t_send)):
        h_f, t_f = part.astype(F32), ref[...].astype(F32)
        hh += jnp.sum(h_f * h_f, axis=1, keepdims=True)
        he += jnp.sum(h_f * t_f, axis=1, keepdims=True)
        ee += jnp.sum(t_f * t_f, axis=1, keepdims=True)
    h_scale = lax.rsqrt(hh + 1e-06) * 20.0
    pos_logit = he * lax.rsqrt(ee + 1e-06) * h_scale
    for copy in copies:
        copy.wait()
    pick = pick_columns({0: 1.0, 1: 1.0, 2: 1.0}, {3: 256.0, 4: 1.0})
    dots, read = 0.0, []
    for side, part in enumerate((keep, send)):
        neg, marks = n_all[side, :, :half], n_all[side, :, half:]
        dots += lax.dot_general(part, neg, ACROSS, preferred_element_type=F32)
        read.append(lax.dot_general(pick, marks, ACROSS, preferred_element_type=F32))
    nn = read[0][0:1] + read[1][0:1]
    n_ids = read[0][1:2]
    neg_logit = dots * h_scale * lax.rsqrt(nn + 1e-06)
    mass = jnp.where(n_ids != t_ids[...].astype(F32), jnp.exp(neg_logit), 0.0)
    total = jnp.exp(pos_logit) + jnp.sum(mass, axis=1, keepdims=True)
    column = jnp.log(total) - pos_logit
    size = column.shape[0]
    line = lax.broadcasted_iota(jnp.int32, (size, size), 0)
    lane = lax.broadcasted_iota(jnp.int32, (size, size), 1)
    loss[...] = jnp.sum(jnp.where(line == lane, column, 0.0), axis=0, keepdims=True)


def join_kernel(where, keep, theirs, hidden):
    u, rows = where[3], keep.shape[0]
    hidden[pl.ds(pl.multiple_of(u * rows, rows), rows), :] = keep[...]
    hidden[pl.ds(pl.multiple_of((1 - u) * rows, rows), rows), :] = theirs[...]


def call(kernel, name, outs, scratch, args, places, flops):
    space = {"s": pltpu.SMEM, "v": pltpu.VMEM, "h": pltpu.HBM}
    moved = sum(a.size * a.dtype.itemsize for a in args)
    return pl.pallas_call(
        kernel,
        out_shape=[jax.ShapeDtypeStruct(shape, dtype) for shape, dtype in outs],
        in_specs=[pl.BlockSpec(memory_space=space[p]) for p in places],
        out_specs=[pl.BlockSpec(memory_space=pltpu.VMEM)] * len(outs),
        scratch_shapes=scratch,
        compiler_params=pltpu.CompilerParams(vmem_limit_bytes=VMEM_LIMIT),
        cost_estimate=pl.CostEstimate(flops=flops, bytes_accessed=moved, transcendentals=0),
        name=name,
    )(*args)


def whole_parts(value, base):
    return [(value // base).astype(BF16), (value % base).astype(BF16)]


def float_parts(value):
    parts = []
    for _ in range(3):
        parts.append(lax.reduce_precision(value, 8, 7))
        value = value - parts[-1]
    return [part.astype(BF16) for part in parts]


def with_marks(rows, marks):
    marks = jnp.stack(marks, 1)
    marks = jnp.pad(marks, ((0, 0), (0, W - marks.shape[1])))
    return jnp.concatenate([rows, marks], 1)


def head_shards(
    tokens, w_proj, w_out, positions, neg_emb, neg_ids, target_emb, target_ids
):
    c, u = lax.axis_index("ctx"), lax.axis_index("tp")
    z, y, x = coords(c)
    where = jnp.stack([z, y, x, u]).astype(jnp.int32)
    model = tokens.shape[1]
    rows = tokens.shape[0] // 2
    events = rows * CHIPS
    half = model // 2
    negs = neg_emb.shape[0]
    plane = len(PLANE)

    mine = lax.dynamic_slice_in_dim(tokens, u * rows, rows, 0)
    p_own = lax.dynamic_slice_in_dim(positions, u * rows, rows, 0)
    p_other = lax.dynamic_slice_in_dim(positions, (1 - u) * rows, rows, 0)
    mine = with_marks(mine, whole_parts(p_own, 128) + whole_parts(p_other, 128))
    low = pair_up(mine)

    to_x, to_y = flip(0, 1), flip(1, 0)
    own_ids = lax.dynamic_slice_in_dim(neg_ids, c * negs, negs, 0)
    norms = jnp.sum(jnp.square(neg_emb.astype(F32)), axis=1)
    neg = with_marks(neg_emb, float_parts(norms) + whole_parts(own_ids, 256))
    high = hop(low, flip(0, 0, 2))
    w_plane, came = heads_in_plane(w_proj, y, x, low)
    low_late = after(low, came)
    low_x, low_y = hop(low_late, to_x), hop(low_late, to_y)
    low_xy = across(low_x, low_y)
    out_low = pair_up(after(w_out[None], came))
    out_low_x, out_low_y = hop(out_low, to_x), hop(out_low, to_y)
    high = after(high, low_xy, out_low)
    high_x, high_y = hop(high, to_x), hop(high, to_y)
    high_xy = across(high_x, high_y)
    tok = [low, high, low_x, high_x, low_y, high_y, *low_xy, *high_xy]
    w_mine = heads_along_z(after(w_plane, high), z)
    w_mine = after(w_mine, high_xy, out_low_x, out_low_y)
    w_theirs = swap_cores(w_mine)
    out_high = hop(after(out_low, w_mine), flip(0, 0, 2))
    out_low = [out_low, out_low_x, out_low_y, *across(*after((out_low_x, out_low_y), w_mine))]
    t_rows = target_emb.reshape(2, rows, -1)
    t_keep = pick_row(t_rows, u)
    t_send = swap_cores(pick_row(after(t_rows, w_theirs), 1 - u))
    neg_pair = pair_up(after(neg, w_mine))

    def project(pieces):
        count = sum(p.shape[0] for p in pieces)
        return call(
            proj_kernel,
            "project",
            [((count, 2 * W), BF16)] * 2 + [((count, W), BF16)],
            [
                pltpu.VMEM((count, model + W), BF16),
                pltpu.VMEM((model, 4 * W), BF16),
                pltpu.SemaphoreType.DMA((len(pieces),)),
                pltpu.SemaphoreType.DMA((2,)),
            ],
            [where, *pieces, w_mine, w_theirs],
            "s" + (len(pieces) + 2) * "h",
            2 * count * model * 4 * W,
        )

    gate_query, value_key, marks = project(tok)
    kv_theirs = swap_cores(value_key)
    (gated,) = call(
        attend_kernel,
        "attend",
        [((CHIPS, rows, W), BF16)],
        [pltpu.VMEM((events, 2 * W), BF16)] * 3
        + [pltpu.VMEM((events, W), BF16), pltpu.SemaphoreType.DMA((4,))],
        [where, gate_query, value_key, kv_theirs, marks],
        "s" + 4 * "h",
        8 * events * events * W,
    )
    out_high, neg_pair, out_low = after((out_high, neg_pair, out_low), gated)
    gated = lax.all_to_all(gated, "ctx", 0, 0, tiled=True)
    out_high_x, out_high_y = hop(out_high, to_x), hop(out_high, to_y)
    out_high_x, out_high_y = after((out_high_x, out_high_y), gated)
    out_high = [out_high, out_high_x, out_high_y, *across(out_high_x, out_high_y)]
    neg_far = hop(after(neg_pair, out_high[0]), flip(0, 0, 2))
    neg_near = jnp.concatenate([neg_pair, neg_far])
    neg_near = after(neg_near, out_high)
    neg_x, neg_y = hop(neg_near, to_x), hop(neg_near, to_y)
    out_own = [jnp.concatenate(out_low), jnp.concatenate(out_high)]
    out_other = [swap_cores(panels) for panels in out_own]
    neg_own = [neg_near, neg_x, neg_y, *across(neg_x, neg_y)]
    h_keep, h_send = call(
        hidden_kernel,
        "hidden",
        [((rows, half), BF16)] * 2,
        [
            pltpu.VMEM((rows, model), BF16),
            pltpu.VMEM((rows, model), BF16),
            pltpu.VMEM((2, half, model), BF16),
            pltpu.SemaphoreType.DMA((2 * CHIPS,)),
        ],
        [where, gated, *out_own, *out_other, mine[:, :model]],
        "sv" + 4 * "h" + "v",
        2 * rows * model * model,
    )
    neg_own = jnp.concatenate(after(neg_own, h_send))
    neg_other = swap_cores(neg_own)
    h_theirs = swap_cores(h_send)
    (loss,) = call(
        loss_kernel,
        "loss",
        [((1, rows), F32)],
        [
            pltpu.VMEM((2, CHIPS * negs, half + W), BF16),
            pltpu.SemaphoreType.DMA((2,)),
        ],
        [h_keep, h_send, t_keep, t_send, target_ids[:, None], neg_own, neg_other],
        "vvvvvhh",
        2 * rows * model * neg_ids.shape[0],
    )
    (hidden,) = call(
        join_kernel,
        "join",
        [((2 * rows, half), BF16)],
        [],
        [where, h_keep, after(h_theirs, loss)],
        "svv",
        0,
    )
    return hidden, loss.reshape(-1)


def shards(tokens, w_proj, *rest):
    n_ctx, n_tp = lax.axis_size("ctx"), lax.axis_size("tp")
    heads = w_proj.shape[2] * n_tp // HEAD_DIM
    plan = head_shards if (n_ctx, n_tp, heads) == (CHIPS, 2, CHIPS) else general_shards
    return plan(tokens, w_proj, *rest)


def solution(mesh):
    placed = (
        P("ctx", None),
        P("ctx", None, "tp"),
        P("tp", "ctx"),
        P("ctx"),
        P("ctx", "tp"),
        P(),
        P("ctx", "tp"),
        P(("ctx", "tp")),
    )
    return jax.shard_map(
        shards,
        mesh=mesh,
        in_specs=placed,
        out_specs=(P("ctx", "tp"), P(("ctx", "tp"))),
        check_vma=False,
    )
```

```python
import jax
import jax.numpy as jnp
from jax import lax
from jax.experimental import pallas as pl
from jax.experimental.pallas import tpu as pltpu
from jax.sharding import PartitionSpec as P

HEAD_DIM = 128
VMEM_LIMIT = 48 * 1024 * 1024
BF16 = jnp.bfloat16
F32 = jnp.float32


def attend_piece(q_group, q_pos, k_piece, v_piece, p_piece):
    heads = q_group.shape[1]
    width = q_group.shape[2]
    key_heads = k_piece.reshape(k_piece.shape[0], heads, width)
    value_heads = v_piece.reshape(v_piece.shape[0], heads, width)
    scores = jnp.einsum(
        "thd,khd->htk", q_group, key_heads, preferred_element_type=jnp.float32
    ) * width ** (-0.5)
    visible = p_piece[None, None, :] <= q_pos[None, :, None]
    weight = jnp.where(visible, jax.nn.silu(scores), 0.0).astype(jnp.bfloat16)
    return jnp.einsum("htk,khd->thd", weight, value_heads, preferred_element_type=jnp.float32)


def general_shards(
    tokens, w_proj, w_out, positions, neg_emb, neg_ids, target_emb, target_ids
):
    tok_rows = tokens.shape[0]
    head_cols = w_proj.shape[2]
    local_heads = head_cols // HEAD_DIM
    proj_sum = jnp.einsum(
        "td,dfh->tfh",
        tokens,
        lax.all_gather(w_proj, "ctx", axis=0, tiled=True),
        preferred_element_type=jnp.float32,
    )
    proj = jax.nn.silu(proj_sum).astype(jnp.bfloat16)
    gate = proj[:, 0].reshape(tok_rows, local_heads, HEAD_DIM)
    query = proj[:, 2].reshape(tok_rows, local_heads, HEAD_DIM)
    v_piece = lax.all_gather(proj[:, 1], "ctx", axis=0, tiled=True)
    k_piece = lax.all_gather(proj[:, 3], "ctx", axis=0, tiled=True)
    p_piece = lax.all_gather(positions, "ctx", axis=0, tiled=True)
    attn = attend_piece(query, positions, k_piece, v_piece, p_piece)
    normed = attn * lax.rsqrt(jnp.mean(attn * attn, axis=-1, keepdims=True) + 1e-06)
    gated = (normed * gate.astype(jnp.float32)).astype(jnp.bfloat16).reshape(tok_rows, head_cols)
    out_terms = jnp.dot(
        gated, lax.all_gather(w_out, "ctx", axis=1, tiled=True), preferred_element_type=jnp.float32
    )
    out_share = lax.psum_scatter(out_terms, "tp", scatter_dimension=1, tiled=True)
    feat_cols = out_share.shape[1]
    own_tokens = lax.dynamic_slice_in_dim(tokens, lax.axis_index("tp") * feat_cols, feat_cols, 1)
    hidden = (own_tokens.astype(jnp.float32) + out_share).astype(jnp.bfloat16)
    piece = lax.all_gather(neg_emb, "ctx", axis=0, tiled=True)
    panel_dots = lax.dot_general(
        hidden, piece, (((1,), (1,)), ((), ())), preferred_element_type=jnp.float32
    )
    panel_norms = jnp.sum(jnp.square(piece.astype(jnp.float32)), axis=1)
    hidden_f = hidden.astype(jnp.float32)
    target_f = target_emb.astype(jnp.float32)
    part_hh = jnp.sum(hidden_f * hidden_f, axis=1)
    part_he = jnp.sum(hidden_f * target_f, axis=1)
    part_ee = jnp.sum(target_f * target_f, axis=1)
    dots, hh_sum, he_sum, ee_sum = (
        lax.psum_scatter(panel_dots, "tp", scatter_dimension=0, tiled=True),
        lax.psum_scatter(part_hh, "tp", scatter_dimension=0, tiled=True),
        lax.psum_scatter(part_he, "tp", scatter_dimension=0, tiled=True),
        lax.psum_scatter(part_ee, "tp", scatter_dimension=0, tiled=True),
    )
    neg_sq = lax.psum(panel_norms, "tp")
    pos_logit = he_sum / jnp.sqrt(hh_sum + 1e-06) / jnp.sqrt(ee_sum + 1e-06) / 0.05
    neg_logit = dots / jnp.sqrt(hh_sum + 1e-06)[:, None] / jnp.sqrt(neg_sq + 1e-06)[None, :] / 0.05
    keep_mask = neg_ids[None, :] != target_ids[:, None]
    total_mass = jnp.exp(pos_logit) + jnp.sum(jnp.where(keep_mask, jnp.exp(neg_logit), 0.0), axis=1)
    loss = jnp.log(total_mass) - pos_logit
    return (hidden, loss)


NZ, NY, NX = 4, 2, 2
CHIPS = NZ * NY * NX
PLANE = [(by, bx) for by in range(NY) for bx in range(NX)]
SWAP = [(0, 1), (1, 0)]
W = HEAD_DIM
ACROSS = (((1,), (1,)), ((), ()))


def chip_at(z, y, x):
    return (z * NY + y) * NX + x


def coords(c):
    return c // (NY * NX), (c // NX) % NY, c % NX


def relative_chip(c, by, bx, s):
    z, y, x = coords(c)
    return chip_at(z ^ s, y ^ by, x ^ bx)


def flip(by, bx, s=0):
    return [(c, relative_chip(c, by, bx, s)) for c in range(CHIPS)]


def hop(value, perm):
    return lax.ppermute(value, "ctx", perm)


def swap_cores(value):
    return lax.ppermute(value, "tp", SWAP)


def pick_row(value, at):
    return lax.dynamic_index_in_dim(value, at, 0, keepdims=False)


def after(values, *others):
    return lax.optimization_barrier((values, others))[0]


def pair_up(own):
    return jnp.concatenate([own, hop(own, flip(0, 0, 1))])


def across(value_x, value_y):
    half = value_x.shape[0] // 2
    return [hop(value_x[:half], flip(1, 0)), hop(value_y[half:], flip(0, 1))]


def heads_in_plane(w_proj, y, x):
    heads = w_proj.reshape(-1, 4, 2, NY, NX, W).transpose(4, 3, 2, 0, 1, 5)
    heads = heads.reshape(NX, NY, 2, -1, 4 * W)
    kept, came = pick_row(heads, x), hop(pick_row(heads, x ^ 1), flip(0, 1))
    lined = jnp.where(x == 0, jnp.stack([kept, came], 1), jnp.stack([came, kept], 1))
    kept, came = pick_row(lined, y), hop(pick_row(lined, y ^ 1), flip(1, 0))
    whole = jnp.where(y == 0, jnp.stack([kept, came]), jnp.stack([came, kept]))
    return whole.transpose(2, 0, 1, 3, 4).reshape(2, NY * NX, *whole.shape[3:])


def heads_along_z(heads, z):
    arrived = []
    for e in range(2):
        perm = []
        for src in range(CHIPS):
            sz, sy, sx = coords(src)
            for t in range(2):
                dst = chip_at(2 * t + (e ^ (sz & 1)), sy, sx)
                perm.append((2 * src + t, 2 * dst + (sz >> 1)))
        arrived.append(lax.ppermute(pick_row(heads, e ^ (z & 1)), ("ctx", "tp"), perm))
    rows = jnp.where(z % 2 == 0, jnp.stack(arrived), jnp.stack(arrived[::-1]))
    return rows.reshape(-1, rows.shape[-1])


def silu(v):
    return 0.5 * v * (1.0 + jnp.tanh(0.5 * v))


def run_copies(copies):
    for copy in copies:
        copy.start()
    for copy in copies:
        copy.wait()


def proj_kernel(where, *refs):
    count = len(refs) - 9
    tok, (w_own, w_other) = refs[:count], refs[count : count + 2]
    gate_query, value_key, marks, x_all, w_all, tok_sem, w_sem = refs[count + 2 :]
    u = where[3]
    copies, base = [], 0
    half = w_own.shape[0]
    for side, (at, src) in enumerate(((u, w_own), (1 - u, w_other))):
        rows = pl.ds(pl.multiple_of(at * half, half), half)
        copies.append(pltpu.make_async_copy(src, w_all.at[rows, :], w_sem.at[side]))
    for i, ref in enumerate(tok):
        rows = pl.ds(base, ref.shape[0])
        copies.append(pltpu.make_async_copy(ref, x_all.at[rows, :], tok_sem.at[i]))
        base += ref.shape[0]
    run_copies(copies)
    model = w_all.shape[0]
    total = jnp.dot(x_all[:, :model], w_all[...], preferred_element_type=F32)
    proj = silu(total).astype(BF16)
    gate_query[:, :W] = proj[:, :W]
    value_key[:, :W] = proj[:, W : 2 * W]
    gate_query[:, W:] = proj[:, 2 * W : 3 * W]
    value_key[:, W:] = proj[:, 3 * W :]
    marks[...] = x_all[:, model:]


def pick_columns(*weights):
    lane = lax.broadcasted_iota(jnp.int32, (8, W), 1)
    line = lax.broadcasted_iota(jnp.int32, (8, W), 0)
    pick = jnp.zeros((8, W), F32)
    for i, row in enumerate(weights):
        for at, weight in row.items():
            pick = jnp.where((line == i) & (lane == at), weight, pick)
    return pick.astype(BF16)


def attend_kernel(gq_hbm, own_hbm, other_hbm, marks_hbm, gated, gate_query, own, other, marks, sems):
    sources = (gq_hbm, own_hbm, other_hbm, marks_hbm)
    run_copies(
        [
            pltpu.make_async_copy(src, dst, sems.at[i])
            for i, (src, dst) in enumerate(zip(sources, (gate_query, own, other, marks)))
        ]
    )
    pick = pick_columns({0: 128.0, 1: 1.0}, {2: 128.0, 3: 1.0})
    piece = gated.shape[2]
    tile = NZ * piece
    key_pos = lax.dot_general(pick, marks[...], ACROSS, preferred_element_type=F32)
    for k in range(len(PLANE)):
        span = pl.ds(k * tile, tile)
        query = gate_query[span, W:]
        q_pos = lax.dot_general(marks[span, :], pick, ACROSS, preferred_element_type=F32)[:, :1]
        attn = jnp.zeros((tile, W), F32)
        for side, kv in enumerate((own, other)):
            scores = lax.dot_general(
                query, kv[:, W:], ACROSS, preferred_element_type=F32
            ) * W ** (-0.5)
            visible = key_pos[side : side + 1] <= q_pos
            weight = jnp.where(visible, silu(scores), 0.0).astype(BF16)
            attn += jnp.dot(weight, kv[:, :W], preferred_element_type=F32)
        normed = attn * lax.rsqrt(jnp.mean(attn * attn, axis=-1, keepdims=True) + 1e-06)
        out = (normed * gate_query[span, :W].astype(F32)).astype(BF16)
        for s in range(NZ):
            gated[s, k] = out[s * piece : (s + 1) * piece]


def hidden_kernel(where, *refs):
    n = len(PLANE)
    gated, w_own, w_other, tok = refs[:n], refs[n : n + 2], refs[n + 2 : n + 4], refs[n + 4 : 2 * n + 4]
    hidden, g_raw, g_all, t_all, w_all, sems = refs[2 * n + 4 :]
    z, y, x, u = (where[i] for i in range(4))
    c = chip_at(z, y, x)
    rows = hidden.shape[1]
    half = w_all.shape[1]
    copies = [(src, g_raw.at[k]) for k, src in enumerate(gated)]
    for s in range(NZ):
        cols = pl.ds(s * W, W)
        for side, src in enumerate((w_own, w_other)):
            copies.append((src[s // 2].at[s % 2], w_all.at[side, :, cols]))
        block = relative_chip(c, 0, 0, s)
        from_cols = pl.ds(pl.multiple_of(block * W, W), W)
        for k in range(n):
            copies.append((tok[k].at[pl.ds(0, rows), from_cols], t_all.at[k, :, cols]))
    copies = [pltpu.make_async_copy(src, dst, sems.at[i]) for i, (src, dst) in enumerate(copies)]
    for copy in copies:
        copy.start()
    for copy in copies[:n]:
        copy.wait()
    for k, (by, bx) in enumerate(PLANE):
        for s in range(NZ):
            head = relative_chip(c, by, bx, s)
            cols = pl.ds(pl.multiple_of(head * W, W), W)
            for j in range(n):
                block = j ^ k
                g_all[block * rows : (block + 1) * rows, cols] = g_raw[k, s, j]
    for copy in copies[n:]:
        copy.wait()
    total = 0.0
    for side, at in enumerate((u, 1 - u)):
        part = g_all[:, pl.ds(pl.multiple_of(at * half, half), half)]
        total += jnp.dot(part, w_all[side], preferred_element_type=F32)
    for k in range(n):
        for s in range(NZ):
            term = total[k * rows : (k + 1) * rows, s * W : (s + 1) * W]
            cols = pl.ds(pl.multiple_of((z ^ s) * W, W), W)
            hidden[k, :, cols] = (t_all[k, :, s * W : (s + 1) * W].astype(F32) + term).astype(BF16)


def order_kernel(where, *refs):
    pieces, (keep, send, h_all) = refs[: len(PLANE)], refs[len(PLANE) :]
    y, x, u = (where[i] for i in range(1, 4))
    half = keep.shape[1]
    for (by, bx), ref in zip(PLANE, pieces):
        for at in range(NZ):
            block = chip_at(at, y ^ by, x ^ bx)
            h_all[:, pl.ds(pl.multiple_of(block * W, W), W)] = ref[:, at * W : (at + 1) * W]
    keep[...] = h_all[:, pl.ds(pl.multiple_of(u * half, half), half)]
    send[...] = h_all[:, pl.ds(pl.multiple_of((1 - u) * half, half), half)]


def loss_kernel(h_keep, h_send, t_keep, t_send, t_ids, n_own, n_other, loss, n_all, sems):
    keep, send = h_keep[...], h_send[...]
    half = keep.shape[1]
    copies = []
    for side, src in enumerate((n_own, n_other)):
        copies.append(pltpu.make_async_copy(src, n_all.at[side], sems.at[side]))
    for copy in copies:
        copy.start()
    hh = he = ee = 0.0
    for part, ref in ((keep, t_keep), (send, t_send)):
        h_f, t_f = part.astype(F32), ref[...].astype(F32)
        hh += jnp.sum(h_f * h_f, axis=1, keepdims=True)
        he += jnp.sum(h_f * t_f, axis=1, keepdims=True)
        ee += jnp.sum(t_f * t_f, axis=1, keepdims=True)
    h_scale = lax.rsqrt(hh + 1e-06) * 20.0
    pos_logit = he * lax.rsqrt(ee + 1e-06) * h_scale
    for copy in copies:
        copy.wait()
    pick = pick_columns({0: 1.0, 1: 1.0, 2: 1.0}, {3: 256.0, 4: 1.0})
    dots, read = 0.0, []
    for side, part in enumerate((keep, send)):
        neg, marks = n_all[side, :, :half], n_all[side, :, half:]
        dots += lax.dot_general(part, neg, ACROSS, preferred_element_type=F32)
        read.append(lax.dot_general(pick, marks, ACROSS, preferred_element_type=F32))
    nn = read[0][0:1] + read[1][0:1]
    n_ids = read[0][1:2]
    neg_logit = dots * h_scale * lax.rsqrt(nn + 1e-06)
    mass = jnp.where(n_ids != t_ids[...].astype(F32), jnp.exp(neg_logit), 0.0)
    total = jnp.exp(pos_logit) + jnp.sum(mass, axis=1, keepdims=True)
    column = jnp.log(total) - pos_logit
    size = column.shape[0]
    line = lax.broadcasted_iota(jnp.int32, (size, size), 0)
    lane = lax.broadcasted_iota(jnp.int32, (size, size), 1)
    loss[...] = jnp.sum(jnp.where(line == lane, column, 0.0), axis=0, keepdims=True)


def join_kernel(where, keep, theirs, hidden):
    u, rows = where[3], keep.shape[0]
    hidden[pl.ds(pl.multiple_of(u * rows, rows), rows), :] = keep[...]
    hidden[pl.ds(pl.multiple_of((1 - u) * rows, rows), rows), :] = theirs[...]


def call(kernel, name, outs, scratch, args, places, flops):
    space = {"s": pltpu.SMEM, "v": pltpu.VMEM, "h": pltpu.HBM}
    moved = sum(a.size * a.dtype.itemsize for a in args)
    return pl.pallas_call(
        kernel,
        out_shape=[jax.ShapeDtypeStruct(shape, dtype) for shape, dtype in outs],
        in_specs=[pl.BlockSpec(memory_space=space[p]) for p in places],
        out_specs=[pl.BlockSpec(memory_space=pltpu.VMEM)] * len(outs),
        scratch_shapes=scratch,
        compiler_params=pltpu.CompilerParams(vmem_limit_bytes=VMEM_LIMIT),
        cost_estimate=pl.CostEstimate(flops=flops, bytes_accessed=moved, transcendentals=0),
        name=name,
    )(*args)


def whole_parts(value, base):
    return [(value // base).astype(BF16), (value % base).astype(BF16)]


def float_parts(value):
    parts = []
    for _ in range(3):
        parts.append(lax.reduce_precision(value, 8, 7))
        value = value - parts[-1]
    return [part.astype(BF16) for part in parts]


def with_marks(rows, marks):
    marks = jnp.stack(marks, 1)
    marks = jnp.pad(marks, ((0, 0), (0, W - marks.shape[1])))
    return jnp.concatenate([rows, marks], 1)


def head_shards(
    tokens, w_proj, w_out, positions, neg_emb, neg_ids, target_emb, target_ids
):
    c, u = lax.axis_index("ctx"), lax.axis_index("tp")
    z, y, x = coords(c)
    where = jnp.stack([z, y, x, u]).astype(jnp.int32)
    model = tokens.shape[1]
    rows = tokens.shape[0] // 2
    events = rows * CHIPS
    half = model // 2
    negs = neg_emb.shape[0]
    plane = len(PLANE)

    mine = lax.dynamic_slice_in_dim(tokens, u * rows, rows, 0)
    p_own = lax.dynamic_slice_in_dim(positions, u * rows, rows, 0)
    p_other = lax.dynamic_slice_in_dim(positions, (1 - u) * rows, rows, 0)
    mine = with_marks(mine, whole_parts(p_own, 128) + whole_parts(p_other, 128))
    low = pair_up(mine)

    to_x, to_y = flip(0, 1), flip(1, 0)
    high = hop(low, flip(0, 0, 2))
    w_plane = heads_in_plane(w_proj, y, x)
    low_x, low_y = hop(low, to_x), hop(low, to_y)
    low_xy = across(low_x, low_y)
    high_x, high_y = hop(high, to_x), hop(high, to_y)
    high_xy = across(high_x, high_y)
    tok = [low, high, low_x, high_x, low_y, high_y, *low_xy, *high_xy]
    w_mine = heads_along_z(after(w_plane, high), z)
    out_pair = pair_up(after(w_out[None], high))
    w_mine = after(w_mine, low_xy, high_xy, out_pair)
    w_theirs = swap_cores(w_mine)
    out_own = [out_pair, hop(after(out_pair, w_mine), flip(0, 0, 2))]

    own_ids = lax.dynamic_slice_in_dim(neg_ids, c * negs, negs, 0)
    norms = jnp.sum(jnp.square(neg_emb.astype(F32)), axis=1)
    neg = with_marks(neg_emb, float_parts(norms) + whole_parts(own_ids, 256))
    neg_pair = pair_up(after(neg, out_pair))
    t_rows = after(target_emb.reshape(2, rows, -1), w_theirs)
    t_keep = pick_row(t_rows, u)
    t_send = swap_cores(pick_row(t_rows, 1 - u))

    def project(pieces):
        count = sum(p.shape[0] for p in pieces)
        return call(
            proj_kernel,
            "project",
            [((count, 2 * W), BF16)] * 2 + [((count, W), BF16)],
            [
                pltpu.VMEM((count, model + W), BF16),
                pltpu.VMEM((model, 4 * W), BF16),
                pltpu.SemaphoreType.DMA((len(pieces),)),
                pltpu.SemaphoreType.DMA((2,)),
            ],
            [where, *pieces, w_mine, w_theirs],
            "s" + (len(pieces) + 2) * "h",
            20 * 2 * count * model * 4 * W,
        )

    gate_query, value_key, marks = project(tok)
    kv_theirs = swap_cores(value_key)
    out_pair_theirs = swap_cores(after(out_pair, value_key))
    (gated,) = call(
        attend_kernel,
        "attend",
        [((NZ, plane, rows, W), BF16)],
        [pltpu.VMEM((events, 2 * W), BF16)] * 3
        + [pltpu.VMEM((events, W), BF16), pltpu.SemaphoreType.DMA((4,))],
        [gate_query, value_key, kv_theirs, marks],
        4 * "h",
        0,
    )
    out_own, out_pair_theirs, gated = lax.optimization_barrier((out_own, out_pair_theirs, gated))
    gated = jnp.stack([gated[0]] + [hop(gated[s], flip(0, 0, s)) for s in range(1, NZ)])
    neg_far = hop(after(neg_pair, gated), flip(0, 0, 2))
    out_other = [out_pair_theirs, swap_cores(after(out_own[1], gated))]
    gated = [gated] + [hop(gated, flip(by, bx)) for by, bx in PLANE[1:]]
    neg_near = after(jnp.concatenate([neg_pair, neg_far]), gated, out_other)
    neg_x, neg_y = hop(neg_near, to_x), hop(neg_near, to_y)
    (hidden,) = call(
        hidden_kernel,
        "hidden",
        [((plane, rows, NZ * W), BF16)],
        [
            pltpu.VMEM((plane, NZ, plane, rows, W), BF16),
            pltpu.VMEM((plane * rows, model), BF16),
            pltpu.VMEM((plane, rows, NZ * W), BF16),
            pltpu.VMEM((2, half, NZ * W), BF16),
            pltpu.SemaphoreType.DMA((28,)),
        ],
        [where, *gated, *out_own, *out_other, low, low_x, low_y, low_xy[0]],
        "s" + 12 * "h",
        2 * plane * rows * model * NZ * W,
    )
    pieces = [hidden[0]] + [hop(hidden[k], flip(*PLANE[k])) for k in range(1, plane)]
    neg_own = [neg_near, neg_x, neg_y, *across(*after((neg_x, neg_y), pieces))]
    neg_own = jnp.concatenate(neg_own)
    neg_other = swap_cores(neg_own)
    h_keep, h_send = call(
        order_kernel,
        "order",
        [((rows, half), BF16)] * 2,
        [pltpu.VMEM((rows, model), BF16)],
        [where, *pieces],
        "svvvv",
        0,
    )
    h_theirs = swap_cores(h_send)
    (loss,) = call(
        loss_kernel,
        "loss",
        [((1, rows), F32)],
        [
            pltpu.VMEM((2, CHIPS * negs, half + W), BF16),
            pltpu.SemaphoreType.DMA((2,)),
        ],
        [h_keep, h_send, t_keep, t_send, target_ids[:, None], neg_own, neg_other],
        "vvvvvhh",
        2 * rows * model * neg_ids.shape[0],
    )
    (hidden,) = call(
        join_kernel,
        "join",
        [((2 * rows, half), BF16)],
        [],
        [where, h_keep, after(h_theirs, loss)],
        "svv",
        0,
    )
    return hidden, loss.reshape(-1)


def shards(tokens, w_proj, *rest):
    n_ctx, n_tp = lax.axis_size("ctx"), lax.axis_size("tp")
    heads = w_proj.shape[2] * n_tp // HEAD_DIM
    plan = head_shards if (n_ctx, n_tp, heads) == (CHIPS, 2, CHIPS) else general_shards
    return plan(tokens, w_proj, *rest)


def solution(mesh):
    placed = (
        P("ctx", None),
        P("ctx", None, "tp"),
        P("tp", "ctx"),
        P("ctx"),
        P("ctx", "tp"),
        P(),
        P("ctx", "tp"),
        P(("ctx", "tp")),
    )
    return jax.shard_map(
        shards,
        mesh=mesh,
        in_specs=placed,
        out_specs=(P("ctx", "tp"), P(("ctx", "tp"))),
        check_vma=False,
    )
```

```python
import jax
import jax.numpy as jnp
from jax import lax
from jax.experimental import pallas as pl
from jax.experimental.pallas import tpu as pltpu
from jax.sharding import PartitionSpec as P

HEAD_DIM = 128
VMEM_LIMIT = 24 * 1024 * 1024
BF16 = jnp.bfloat16
F32 = jnp.float32


def attend_piece(q_group, q_pos, k_piece, v_piece, p_piece):
    heads = q_group.shape[1]
    width = q_group.shape[2]
    key_heads = k_piece.reshape(k_piece.shape[0], heads, width)
    value_heads = v_piece.reshape(v_piece.shape[0], heads, width)
    scores = jnp.einsum(
        "thd,khd->htk", q_group, key_heads, preferred_element_type=jnp.float32
    ) * width ** (-0.5)
    visible = p_piece[None, None, :] <= q_pos[None, :, None]
    weight = jnp.where(visible, jax.nn.silu(scores), 0.0).astype(jnp.bfloat16)
    return jnp.einsum("htk,khd->thd", weight, value_heads, preferred_element_type=jnp.float32)


def general_shards(
    tokens, w_proj, w_out, positions, neg_emb, neg_ids, target_emb, target_ids
):
    tok_rows = tokens.shape[0]
    head_cols = w_proj.shape[2]
    local_heads = head_cols // HEAD_DIM
    proj_sum = jnp.einsum(
        "td,dfh->tfh",
        tokens,
        lax.all_gather(w_proj, "ctx", axis=0, tiled=True),
        preferred_element_type=jnp.float32,
    )
    proj = jax.nn.silu(proj_sum).astype(jnp.bfloat16)
    gate = proj[:, 0].reshape(tok_rows, local_heads, HEAD_DIM)
    query = proj[:, 2].reshape(tok_rows, local_heads, HEAD_DIM)
    v_piece = lax.all_gather(proj[:, 1], "ctx", axis=0, tiled=True)
    k_piece = lax.all_gather(proj[:, 3], "ctx", axis=0, tiled=True)
    p_piece = lax.all_gather(positions, "ctx", axis=0, tiled=True)
    attn = attend_piece(query, positions, k_piece, v_piece, p_piece)
    normed = attn * lax.rsqrt(jnp.mean(attn * attn, axis=-1, keepdims=True) + 1e-06)
    gated = (normed * gate.astype(jnp.float32)).astype(jnp.bfloat16).reshape(tok_rows, head_cols)
    out_terms = jnp.dot(
        gated, lax.all_gather(w_out, "ctx", axis=1, tiled=True), preferred_element_type=jnp.float32
    )
    out_share = lax.psum_scatter(out_terms, "tp", scatter_dimension=1, tiled=True)
    feat_cols = out_share.shape[1]
    own_tokens = lax.dynamic_slice_in_dim(tokens, lax.axis_index("tp") * feat_cols, feat_cols, 1)
    hidden = (own_tokens.astype(jnp.float32) + out_share).astype(jnp.bfloat16)
    piece = lax.all_gather(neg_emb, "ctx", axis=0, tiled=True)
    panel_dots = lax.dot_general(
        hidden, piece, (((1,), (1,)), ((), ())), preferred_element_type=jnp.float32
    )
    panel_norms = jnp.sum(jnp.square(piece.astype(jnp.float32)), axis=1)
    hidden_f = hidden.astype(jnp.float32)
    target_f = target_emb.astype(jnp.float32)
    part_hh = jnp.sum(hidden_f * hidden_f, axis=1)
    part_he = jnp.sum(hidden_f * target_f, axis=1)
    part_ee = jnp.sum(target_f * target_f, axis=1)
    dots, hh_sum, he_sum, ee_sum = (
        lax.psum_scatter(panel_dots, "tp", scatter_dimension=0, tiled=True),
        lax.psum_scatter(part_hh, "tp", scatter_dimension=0, tiled=True),
        lax.psum_scatter(part_he, "tp", scatter_dimension=0, tiled=True),
        lax.psum_scatter(part_ee, "tp", scatter_dimension=0, tiled=True),
    )
    neg_sq = lax.psum(panel_norms, "tp")
    pos_logit = he_sum / jnp.sqrt(hh_sum + 1e-06) / jnp.sqrt(ee_sum + 1e-06) / 0.05
    neg_logit = dots / jnp.sqrt(hh_sum + 1e-06)[:, None] / jnp.sqrt(neg_sq + 1e-06)[None, :] / 0.05
    keep_mask = neg_ids[None, :] != target_ids[:, None]
    total_mass = jnp.exp(pos_logit) + jnp.sum(jnp.where(keep_mask, jnp.exp(neg_logit), 0.0), axis=1)
    loss = jnp.log(total_mass) - pos_logit
    return (hidden, loss)


NZ, NY, NX = 4, 2, 2
CHIPS = NZ * NY * NX
PLANE = [(by, bx) for by in range(NY) for bx in range(NX)]
SWAP = [(0, 1), (1, 0)]
W = HEAD_DIM
ACROSS = (((1,), (1,)), ((), ()))


def chip_at(z, y, x):
    return (z * NY + y) * NX + x


def coords(c):
    return c // (NY * NX), (c // NX) % NY, c % NX


def relative_chip(c, by, bx, s):
    z, y, x = coords(c)
    return chip_at(z ^ s, y ^ by, x ^ bx)


def flip(by, bx, s=0):
    return [(c, relative_chip(c, by, bx, s)) for c in range(CHIPS)]


def hop(value, perm):
    return lax.ppermute(value, "ctx", perm)


def swap_cores(value):
    return lax.ppermute(value, "tp", SWAP)


def pick_row(value, at):
    return lax.dynamic_index_in_dim(value, at, 0, keepdims=False)


def after(values, *others):
    return lax.optimization_barrier((values, others))[0]


def pair_up(own):
    return jnp.concatenate([own, hop(own, flip(0, 0, 1))])


def across(value_x, value_y):
    half = value_x.shape[0] // 2
    return [hop(value_x[:half], flip(1, 0)), hop(value_y[half:], flip(0, 1))]


def heads_in_plane(w_proj, y, x):
    heads = w_proj.reshape(-1, 4, 2, NY, NX, W).transpose(4, 3, 2, 0, 1, 5)
    heads = heads.reshape(NX, NY, 2, -1, 4 * W)
    kept, came = pick_row(heads, x), hop(pick_row(heads, x ^ 1), flip(0, 1))
    lined = jnp.where(x == 0, jnp.stack([kept, came], 1), jnp.stack([came, kept], 1))
    kept, came = pick_row(lined, y), hop(pick_row(lined, y ^ 1), flip(1, 0))
    whole = jnp.where(y == 0, jnp.stack([kept, came]), jnp.stack([came, kept]))
    return whole.transpose(2, 0, 1, 3, 4).reshape(2, NY * NX, *whole.shape[3:])


def heads_along_z(pieces):
    arrived = []
    for e, piece in enumerate(pieces):
        perm = []
        for src in range(CHIPS):
            sz, sy, sx = coords(src)
            for t in range(2):
                dst = chip_at(2 * t + (e ^ (sz & 1)), sy, sx)
                perm.append((2 * src + t, 2 * dst + (sz >> 1)))
        arrived.append(lax.ppermute(piece, ("ctx", "tp"), perm).reshape(-1, piece.shape[-1]))
    return arrived


def silu(v):
    return 0.5 * v * (1.0 + jnp.tanh(0.5 * v))


def run_copies(copies):
    for copy in copies:
        copy.start()
    for copy in copies:
        copy.wait()


def proj_kernel(where, *refs):
    count = len(refs) - 12
    tok, w_own, w_other = refs[:count], refs[count : count + 2], refs[count + 2 : count + 4]
    gate_query, value, key, marks, x_all, w_all, tok_sem, w_sem = refs[count + 4 :]
    z, u = where[0], where[3]
    copies, base = [], 0
    for side, (at, srcs) in enumerate(((u, w_own), (1 - u, w_other))):
        for e, src in enumerate(srcs):
            size = src.shape[0]
            start = pl.multiple_of((2 * at + (e ^ (z & 1))) * size, size)
            to = w_all.at[pl.ds(start, size), :]
            copies.append(pltpu.make_async_copy(src, to, w_sem.at[2 * side + e]))
    for i, ref in enumerate(tok):
        rows = pl.ds(base, ref.shape[0])
        copies.append(pltpu.make_async_copy(ref, x_all.at[rows, :], tok_sem.at[i]))
        base += ref.shape[0]
    run_copies(copies)
    model = w_all.shape[0]
    total = jnp.dot(x_all[:, :model], w_all[...], preferred_element_type=F32)
    proj = silu(total).astype(BF16)
    gate_query[:, :W] = proj[:, :W]
    value[...] = proj[:, W : 2 * W]
    gate_query[:, W:] = proj[:, 2 * W : 3 * W]
    key[...] = proj[:, 3 * W :]
    marks[...] = x_all[:, model:]


def pick_columns(*weights):
    lane = lax.broadcasted_iota(jnp.int32, (8, W), 1)
    line = lax.broadcasted_iota(jnp.int32, (8, W), 0)
    pick = jnp.zeros((8, W), F32)
    for i, row in enumerate(weights):
        for at, weight in row.items():
            pick = jnp.where((line == i) & (lane == at), weight, pick)
    return pick.astype(BF16)


def attend_kernel(*refs):
    sources, gated, copied, sems = refs[:6], refs[6], refs[7:13], refs[13]
    run_copies(
        [
            pltpu.make_async_copy(src, dst, sems.at[i])
            for i, (src, dst) in enumerate(zip(sources, copied))
        ]
    )
    gate_query, key, value, key_theirs, value_theirs, marks = copied
    pick = pick_columns({0: 128.0, 1: 1.0}, {2: 128.0, 3: 1.0})
    piece = gated.shape[2]
    tile = NZ * piece
    key_pos = lax.dot_general(pick, marks[...], ACROSS, preferred_element_type=F32)
    for k in range(len(PLANE)):
        span = pl.ds(k * tile, tile)
        query = gate_query[span, W:]
        q_pos = lax.dot_general(marks[span, :], pick, ACROSS, preferred_element_type=F32)[:, :1]
        attn = jnp.zeros((tile, W), F32)
        for side, (keys, values) in enumerate(((key, value), (key_theirs, value_theirs))):
            scores = lax.dot_general(
                query, keys[...], ACROSS, preferred_element_type=F32
            ) * W ** (-0.5)
            visible = key_pos[side : side + 1] <= q_pos
            weight = jnp.where(visible, silu(scores), 0.0).astype(BF16)
            attn += jnp.dot(weight, values[...], preferred_element_type=F32)
        normed = attn * lax.rsqrt(jnp.mean(attn * attn, axis=-1, keepdims=True) + 1e-06)
        out = (normed * gate_query[span, :W].astype(F32)).astype(BF16)
        for s in range(NZ):
            gated[s, k] = out[s * piece : (s + 1) * piece]


def hidden_kernel(where, *refs):
    n = len(PLANE)
    gated, w_own, w_other, tok = refs[:n], refs[n : n + 2], refs[n + 2 : n + 4], refs[n + 4 : 2 * n + 4]
    hidden, g_raw, g_all, t_all, w_all, sems = refs[2 * n + 4 :]
    z, y, x, u = (where[i] for i in range(4))
    c = chip_at(z, y, x)
    rows = hidden.shape[1]
    half = w_all.shape[1]
    copies = [(src, g_raw.at[k]) for k, src in enumerate(gated)]
    for s in range(NZ):
        cols = pl.ds(s * W, W)
        for side, src in enumerate((w_own, w_other)):
            copies.append((src[s // 2].at[s % 2], w_all.at[side, :, cols]))
        block = relative_chip(c, 0, 0, s)
        from_cols = pl.ds(pl.multiple_of(block * W, W), W)
        for k in range(n):
            copies.append((tok[k].at[pl.ds(0, rows), from_cols], t_all.at[k, :, cols]))
    copies = [pltpu.make_async_copy(src, dst, sems.at[i]) for i, (src, dst) in enumerate(copies)]
    for copy in copies:
        copy.start()
    for copy in copies[:n]:
        copy.wait()
    for k, (by, bx) in enumerate(PLANE):
        for s in range(NZ):
            head = relative_chip(c, by, bx, s)
            cols = pl.ds(pl.multiple_of(head * W, W), W)
            for j in range(n):
                block = j ^ k
                g_all[block * rows : (block + 1) * rows, cols] = g_raw[k, s, j]
    for copy in copies[n:]:
        copy.wait()
    total = 0.0
    for side, at in enumerate((u, 1 - u)):
        part = g_all[:, pl.ds(pl.multiple_of(at * half, half), half)]
        total += jnp.dot(part, w_all[side], preferred_element_type=F32)
    for k in range(n):
        for s in range(NZ):
            term = total[k * rows : (k + 1) * rows, s * W : (s + 1) * W]
            cols = pl.ds(pl.multiple_of((z ^ s) * W, W), W)
            hidden[k, :, cols] = (t_all[k, :, s * W : (s + 1) * W].astype(F32) + term).astype(BF16)


def order_kernel(where, *refs):
    pieces, (keep, send, h_all) = refs[: len(PLANE)], refs[len(PLANE) :]
    y, x, u = (where[i] for i in range(1, 4))
    half = keep.shape[1]
    for (by, bx), ref in zip(PLANE, pieces):
        for at in range(NZ):
            block = chip_at(at, y ^ by, x ^ bx)
            h_all[:, pl.ds(pl.multiple_of(block * W, W), W)] = ref[:, at * W : (at + 1) * W]
    keep[...] = h_all[:, pl.ds(pl.multiple_of(u * half, half), half)]
    send[...] = h_all[:, pl.ds(pl.multiple_of((1 - u) * half, half), half)]


def loss_kernel(h_keep, h_send, t_keep, t_send, t_ids, n_own, n_other, loss, n_all, sems):
    keep, send = h_keep[...], h_send[...]
    half = keep.shape[1]
    copies = []
    for side, src in enumerate((n_own, n_other)):
        copies.append(pltpu.make_async_copy(src, n_all.at[side], sems.at[side]))
    for copy in copies:
        copy.start()
    hh = he = ee = 0.0
    for part, ref in ((keep, t_keep), (send, t_send)):
        h_f, t_f = part.astype(F32), ref[...].astype(F32)
        hh += jnp.sum(h_f * h_f, axis=1, keepdims=True)
        he += jnp.sum(h_f * t_f, axis=1, keepdims=True)
        ee += jnp.sum(t_f * t_f, axis=1, keepdims=True)
    h_scale = lax.rsqrt(hh + 1e-06) * 20.0
    pos_logit = he * lax.rsqrt(ee + 1e-06) * h_scale
    for copy in copies:
        copy.wait()
    pick = pick_columns({0: 1.0, 1: 1.0, 2: 1.0}, {3: 256.0, 4: 1.0})
    dots, read = 0.0, []
    for side, part in enumerate((keep, send)):
        neg, marks = n_all[side, :, :half], n_all[side, :, half:]
        dots += lax.dot_general(part, neg, ACROSS, preferred_element_type=F32)
        read.append(lax.dot_general(pick, marks, ACROSS, preferred_element_type=F32))
    nn = read[0][0:1] + read[1][0:1]
    n_ids = read[0][1:2]
    neg_logit = dots * h_scale * lax.rsqrt(nn + 1e-06)
    mass = jnp.where(n_ids != t_ids[...].astype(F32), jnp.exp(neg_logit), 0.0)
    total = jnp.exp(pos_logit) + jnp.sum(mass, axis=1, keepdims=True)
    column = jnp.log(total) - pos_logit
    size = column.shape[0]
    line = lax.broadcasted_iota(jnp.int32, (size, size), 0)
    lane = lax.broadcasted_iota(jnp.int32, (size, size), 1)
    loss[...] = jnp.sum(jnp.where(line == lane, column, 0.0), axis=0, keepdims=True)


def join_kernel(where, keep, theirs, hidden):
    u, rows = where[3], keep.shape[0]
    hidden[pl.ds(pl.multiple_of(u * rows, rows), rows), :] = keep[...]
    hidden[pl.ds(pl.multiple_of((1 - u) * rows, rows), rows), :] = theirs[...]


def call(kernel, name, outs, scratch, args, places, flops):
    space = {"s": pltpu.SMEM, "v": pltpu.VMEM, "h": pl.ANY}
    moved = sum(a.size * a.dtype.itemsize for a in args)
    return pl.pallas_call(
        kernel,
        out_shape=[jax.ShapeDtypeStruct(shape, dtype) for shape, dtype in outs],
        in_specs=[pl.BlockSpec(memory_space=space[p]) for p in places],
        out_specs=[pl.BlockSpec(memory_space=pltpu.VMEM)] * len(outs),
        scratch_shapes=scratch,
        compiler_params=pltpu.CompilerParams(vmem_limit_bytes=VMEM_LIMIT),
        cost_estimate=pl.CostEstimate(flops=flops, bytes_accessed=moved, transcendentals=0),
        name=name,
    )(*args)


def whole_parts(value, base):
    return [(value // base).astype(BF16), (value % base).astype(BF16)]


def float_parts(value):
    parts = []
    for _ in range(3):
        parts.append(lax.reduce_precision(value, 8, 7))
        value = value - parts[-1]
    return [part.astype(BF16) for part in parts]


def with_marks(rows, marks):
    marks = jnp.stack(marks, 1)
    marks = jnp.pad(marks, ((0, 0), (0, W - marks.shape[1])))
    return jnp.concatenate([rows, marks], 1)


def head_shards(
    tokens, w_proj, w_out, positions, neg_emb, neg_ids, target_emb, target_ids
):
    c, u = lax.axis_index("ctx"), lax.axis_index("tp")
    z, y, x = coords(c)
    where = jnp.stack([z, y, x, u]).astype(jnp.int32)
    model = tokens.shape[1]
    rows = tokens.shape[0] // 2
    events = rows * CHIPS
    half = model // 2
    negs = neg_emb.shape[0]
    plane = len(PLANE)

    mine = lax.dynamic_slice_in_dim(tokens, u * rows, rows, 0)
    p_own = lax.dynamic_slice_in_dim(positions, u * rows, rows, 0)
    p_other = lax.dynamic_slice_in_dim(positions, (1 - u) * rows, rows, 0)
    mine = with_marks(mine, whole_parts(p_own, 128) + whole_parts(p_other, 128))
    low = pair_up(mine)

    to_x, to_y = flip(0, 1), flip(1, 0)
    high = hop(low, flip(0, 0, 2))
    w_plane = heads_in_plane(w_proj, y, x)
    w_pieces = [pick_row(w_plane, e ^ (z & 1)) for e in range(2)]
    low_x, low_y = hop(low, to_x), hop(low, to_y)
    low_xy = across(low_x, low_y)

    out_pair = pair_up(after(w_out[None], low))
    own_ids = lax.dynamic_slice_in_dim(neg_ids, c * negs, negs, 0)
    norms = jnp.sum(jnp.square(neg_emb.astype(F32)), axis=1)
    neg = with_marks(neg_emb, float_parts(norms) + whole_parts(own_ids, 256))
    neg_pair = pair_up(after(neg, out_pair))

    w_pieces, high = lax.optimization_barrier((w_pieces, after(high, neg_pair)))
    high_x, high_y = hop(high, to_x), hop(high, to_y)
    high_xy = across(high_x, high_y)
    tok = [low, high, low_x, high_x, low_y, high_y, *low_xy, *high_xy]
    w_mine = after(heads_along_z(w_pieces), low_xy, high_xy)
    w_theirs = [swap_cores(w) for w in w_mine]
    out_own = [out_pair, hop(after(out_pair, w_mine), flip(0, 0, 2))]
    t_rows = after(target_emb.reshape(2, rows, -1), w_theirs)
    t_keep = pick_row(t_rows, u)
    t_send = swap_cores(pick_row(t_rows, 1 - u))

    def project(pieces):
        count = sum(p.shape[0] for p in pieces)
        return call(
            proj_kernel,
            "project",
            [((count, 2 * W), BF16)] + [((count, W), BF16)] * 3,
            [
                pltpu.VMEM((count, model + W), BF16),
                pltpu.VMEM((model, 4 * W), BF16),
                pltpu.SemaphoreType.DMA((len(pieces),)),
                pltpu.SemaphoreType.DMA((4,)),
            ],
            [where, *pieces, *w_mine, *w_theirs],
            "s" + (len(pieces) + 4) * "h",
            20 * 2 * count * model * 4 * W,
        )

    gate_query, value, key, marks = project(tok)
    key_theirs, value_theirs = swap_cores(key), swap_cores(value)
    out_pair_theirs = swap_cores(after(out_pair, value))
    (gated,) = call(
        attend_kernel,
        "attend",
        [((NZ, plane, rows, W), BF16)],
        [pltpu.VMEM((events, 2 * W), BF16)]
        + [pltpu.VMEM((events, W), BF16)] * 5
        + [pltpu.SemaphoreType.DMA((6,))],
        [gate_query, key, value, key_theirs, value_theirs, marks],
        6 * "h",
        0,
    )
    out_own, out_pair_theirs, gated = lax.optimization_barrier((out_own, out_pair_theirs, gated))
    gated = jnp.stack([gated[0]] + [hop(gated[s], flip(0, 0, s)) for s in range(1, NZ)])
    neg_far = hop(after(neg_pair, gated), flip(0, 0, 2))
    out_other = [out_pair_theirs, swap_cores(after(out_own[1], gated))]
    gated = [gated] + [hop(gated, flip(by, bx)) for by, bx in PLANE[1:]]
    neg_near = after(jnp.concatenate([neg_pair, neg_far]), gated, out_other, t_send)
    neg_x, neg_y = hop(neg_near, to_x), hop(neg_near, to_y)
    (hidden,) = call(
        hidden_kernel,
        "hidden",
        [((plane, rows, NZ * W), BF16)],
        [
            pltpu.VMEM((plane, NZ, plane, rows, W), BF16),
            pltpu.VMEM((plane * rows, model), BF16),
            pltpu.VMEM((plane, rows, NZ * W), BF16),
            pltpu.VMEM((2, half, NZ * W), BF16),
            pltpu.SemaphoreType.DMA((28,)),
        ],
        [where, *gated, *out_own, *out_other, low, low_x, low_y, low_xy[0]],
        "s" + 12 * "h",
        2 * plane * rows * model * NZ * W,
    )
    pieces = [hidden[0]] + [hop(hidden[k], flip(*PLANE[k])) for k in range(1, plane)]
    neg_own = [neg_near, neg_x, neg_y, *across(*after((neg_x, neg_y), pieces))]
    neg_own = jnp.concatenate(neg_own)
    neg_other = swap_cores(neg_own)
    h_keep, h_send = call(
        order_kernel,
        "order",
        [((rows, half), BF16)] * 2,
        [pltpu.VMEM((rows, model), BF16)],
        [where, *pieces],
        "svvvv",
        0,
    )
    h_theirs = swap_cores(h_send)
    (loss,) = call(
        loss_kernel,
        "loss",
        [((1, rows), F32)],
        [
            pltpu.VMEM((2, CHIPS * negs, half + W), BF16),
            pltpu.SemaphoreType.DMA((2,)),
        ],
        [h_keep, h_send, t_keep, t_send, target_ids[:, None], neg_own, neg_other],
        "vvvvvhh",
        2 * rows * model * neg_ids.shape[0],
    )
    (hidden,) = call(
        join_kernel,
        "join",
        [((2 * rows, half), BF16)],
        [],
        [where, h_keep, after(h_theirs, loss)],
        "svv",
        0,
    )
    return hidden, loss.reshape(-1)


def shards(tokens, w_proj, *rest):
    n_ctx, n_tp = lax.axis_size("ctx"), lax.axis_size("tp")
    heads = w_proj.shape[2] * n_tp // HEAD_DIM
    plan = head_shards if (n_ctx, n_tp, heads) == (CHIPS, 2, CHIPS) else general_shards
    return plan(tokens, w_proj, *rest)


def solution(mesh):
    placed = (
        P("ctx", None),
        P("ctx", None, "tp"),
        P("tp", "ctx"),
        P("ctx"),
        P("ctx", "tp"),
        P(),
        P("ctx", "tp"),
        P(("ctx", "tp")),
    )
    return jax.shard_map(
        shards,
        mesh=mesh,
        in_specs=placed,
        out_specs=(P("ctx", "tp"), P(("ctx", "tp"))),
        check_vma=False,
    )
```

```python
import jax
import jax.numpy as jnp
from jax import lax
from jax.experimental import pallas as pl
from jax.experimental.pallas import tpu as pltpu
from jax.sharding import PartitionSpec as P

HEAD_DIM = 128
VMEM_LIMIT = 24 * 1024 * 1024
BF16 = jnp.bfloat16
F32 = jnp.float32


def attend_piece(q_group, q_pos, k_piece, v_piece, p_piece):
    heads = q_group.shape[1]
    width = q_group.shape[2]
    key_heads = k_piece.reshape(k_piece.shape[0], heads, width)
    value_heads = v_piece.reshape(v_piece.shape[0], heads, width)
    scores = jnp.einsum(
        "thd,khd->htk", q_group, key_heads, preferred_element_type=jnp.float32
    ) * width ** (-0.5)
    visible = p_piece[None, None, :] <= q_pos[None, :, None]
    weight = jnp.where(visible, jax.nn.silu(scores), 0.0).astype(jnp.bfloat16)
    return jnp.einsum("htk,khd->thd", weight, value_heads, preferred_element_type=jnp.float32)


def general_shards(
    tokens, w_proj, w_out, positions, neg_emb, neg_ids, target_emb, target_ids
):
    tok_rows = tokens.shape[0]
    head_cols = w_proj.shape[2]
    local_heads = head_cols // HEAD_DIM
    proj_sum = jnp.einsum(
        "td,dfh->tfh",
        tokens,
        lax.all_gather(w_proj, "ctx", axis=0, tiled=True),
        preferred_element_type=jnp.float32,
    )
    proj = jax.nn.silu(proj_sum).astype(jnp.bfloat16)
    gate = proj[:, 0].reshape(tok_rows, local_heads, HEAD_DIM)
    query = proj[:, 2].reshape(tok_rows, local_heads, HEAD_DIM)
    v_piece = lax.all_gather(proj[:, 1], "ctx", axis=0, tiled=True)
    k_piece = lax.all_gather(proj[:, 3], "ctx", axis=0, tiled=True)
    p_piece = lax.all_gather(positions, "ctx", axis=0, tiled=True)
    attn = attend_piece(query, positions, k_piece, v_piece, p_piece)
    normed = attn * lax.rsqrt(jnp.mean(attn * attn, axis=-1, keepdims=True) + 1e-06)
    gated = (normed * gate.astype(jnp.float32)).astype(jnp.bfloat16).reshape(tok_rows, head_cols)
    out_terms = jnp.dot(
        gated, lax.all_gather(w_out, "ctx", axis=1, tiled=True), preferred_element_type=jnp.float32
    )
    out_share = lax.psum_scatter(out_terms, "tp", scatter_dimension=1, tiled=True)
    feat_cols = out_share.shape[1]
    own_tokens = lax.dynamic_slice_in_dim(tokens, lax.axis_index("tp") * feat_cols, feat_cols, 1)
    hidden = (own_tokens.astype(jnp.float32) + out_share).astype(jnp.bfloat16)
    piece = lax.all_gather(neg_emb, "ctx", axis=0, tiled=True)
    panel_dots = lax.dot_general(
        hidden, piece, (((1,), (1,)), ((), ())), preferred_element_type=jnp.float32
    )
    panel_norms = jnp.sum(jnp.square(piece.astype(jnp.float32)), axis=1)
    hidden_f = hidden.astype(jnp.float32)
    target_f = target_emb.astype(jnp.float32)
    part_hh = jnp.sum(hidden_f * hidden_f, axis=1)
    part_he = jnp.sum(hidden_f * target_f, axis=1)
    part_ee = jnp.sum(target_f * target_f, axis=1)
    dots, hh_sum, he_sum, ee_sum = (
        lax.psum_scatter(panel_dots, "tp", scatter_dimension=0, tiled=True),
        lax.psum_scatter(part_hh, "tp", scatter_dimension=0, tiled=True),
        lax.psum_scatter(part_he, "tp", scatter_dimension=0, tiled=True),
        lax.psum_scatter(part_ee, "tp", scatter_dimension=0, tiled=True),
    )
    neg_sq = lax.psum(panel_norms, "tp")
    pos_logit = he_sum / jnp.sqrt(hh_sum + 1e-06) / jnp.sqrt(ee_sum + 1e-06) / 0.05
    neg_logit = dots / jnp.sqrt(hh_sum + 1e-06)[:, None] / jnp.sqrt(neg_sq + 1e-06)[None, :] / 0.05
    keep_mask = neg_ids[None, :] != target_ids[:, None]
    total_mass = jnp.exp(pos_logit) + jnp.sum(jnp.where(keep_mask, jnp.exp(neg_logit), 0.0), axis=1)
    loss = jnp.log(total_mass) - pos_logit
    return (hidden, loss)


NZ, NY, NX = 4, 2, 2
CHIPS = NZ * NY * NX
PLANE = [(by, bx) for by in range(NY) for bx in range(NX)]
SWAP = [(0, 1), (1, 0)]
W = HEAD_DIM
ACROSS = (((1,), (1,)), ((), ()))


def chip_at(z, y, x):
    return (z * NY + y) * NX + x


def coords(c):
    return c // (NY * NX), (c // NX) % NY, c % NX


def relative_chip(c, by, bx, s):
    z, y, x = coords(c)
    return chip_at(z ^ s, y ^ by, x ^ bx)


def flip(by, bx, s=0):
    return [(c, relative_chip(c, by, bx, s)) for c in range(CHIPS)]


def hop(value, perm):
    return lax.ppermute(value, "ctx", perm)


def swap_cores(value):
    return lax.ppermute(value, "tp", SWAP)


def pick_row(value, at):
    return lax.dynamic_index_in_dim(value, at, 0, keepdims=False)


def after(values, *others):
    return lax.optimization_barrier((values, others))[0]


def pair_up(own):
    return jnp.concatenate([own, hop(own, flip(0, 0, 1))])


def across(value_x, value_y):
    half = value_x.shape[0] // 2
    return [hop(value_x[:half], flip(1, 0)), hop(value_y[half:], flip(0, 1))]


def heads_in_plane(w_proj, y, x, first):
    heads = w_proj.reshape(-1, 4, 2, NY, NX, W).transpose(4, 3, 2, 0, 1, 5)
    heads = heads.reshape(NX, NY, 2, -1, 4 * W)
    kept, sent = pick_row(heads, x), after(pick_row(heads, x ^ 1), first)
    came = hop(sent, flip(0, 1))
    lined = jnp.where(x == 0, jnp.stack([kept, came], 1), jnp.stack([came, kept], 1))
    kept, came = pick_row(lined, y), hop(pick_row(lined, y ^ 1), flip(1, 0))
    whole = jnp.where(y == 0, jnp.stack([kept, came]), jnp.stack([came, kept]))
    return whole.transpose(2, 0, 1, 3, 4).reshape(2, NY * NX, *whole.shape[3:])


def heads_along_z(pieces):
    arrived = []
    for e, piece in enumerate(pieces):
        perm = []
        for src in range(CHIPS):
            sz, sy, sx = coords(src)
            for t in range(2):
                dst = chip_at(2 * t + (e ^ (sz & 1)), sy, sx)
                perm.append((2 * src + t, 2 * dst + (sz >> 1)))
        arrived.append(lax.ppermute(piece, ("ctx", "tp"), perm).reshape(-1, piece.shape[-1]))
    return arrived


def silu(v):
    return 0.5 * v * (1.0 + jnp.tanh(0.5 * v))


def run_copies(copies):
    for copy in copies:
        copy.start()
    for copy in copies:
        copy.wait()


def proj_kernel(where, *refs):
    count = len(refs) - 12
    tok, w_own, w_other = refs[:count], refs[count : count + 2], refs[count + 2 : count + 4]
    gate_query, value, key, marks, x_all, w_all, tok_sem, w_sem = refs[count + 4 :]
    z, u = where[0], where[3]
    copies, base = [], 0
    for side, (at, srcs) in enumerate(((u, w_own), (1 - u, w_other))):
        for e, src in enumerate(srcs):
            size = src.shape[0]
            start = pl.multiple_of((2 * at + (e ^ (z & 1))) * size, size)
            to = w_all.at[pl.ds(start, size), :]
            copies.append(pltpu.make_async_copy(src, to, w_sem.at[2 * side + e]))
    for i, ref in enumerate(tok):
        rows = pl.ds(base, ref.shape[0])
        copies.append(pltpu.make_async_copy(ref, x_all.at[rows, :], tok_sem.at[i]))
        base += ref.shape[0]
    run_copies(copies)
    model = w_all.shape[0]
    total = jnp.dot(x_all[:, :model], w_all[...], preferred_element_type=F32)
    proj = silu(total).astype(BF16)
    gate_query[:, :W] = proj[:, :W]
    value[...] = proj[:, W : 2 * W]
    gate_query[:, W:] = proj[:, 2 * W : 3 * W]
    key[...] = proj[:, 3 * W :]
    marks[...] = x_all[:, model:]


def pick_columns(*weights):
    lane = lax.broadcasted_iota(jnp.int32, (8, W), 1)
    line = lax.broadcasted_iota(jnp.int32, (8, W), 0)
    pick = jnp.zeros((8, W), F32)
    for i, row in enumerate(weights):
        for at, weight in row.items():
            pick = jnp.where((line == i) & (lane == at), weight, pick)
    return pick.astype(BF16)


def attend_kernel(*refs):
    sources, gated, copied, sems = refs[:6], refs[6], refs[7:13], refs[13]
    run_copies(
        [
            pltpu.make_async_copy(src, dst, sems.at[i])
            for i, (src, dst) in enumerate(zip(sources, copied))
        ]
    )
    gate_query, key, value, key_theirs, value_theirs, marks = copied
    pick = pick_columns({0: 128.0, 1: 1.0}, {2: 128.0, 3: 1.0})
    piece = gated.shape[2]
    tile = NZ * piece
    key_pos = lax.dot_general(pick, marks[...], ACROSS, preferred_element_type=F32)
    for k in range(len(PLANE)):
        span = pl.ds(k * tile, tile)
        query = gate_query[span, W:]
        q_pos = lax.dot_general(marks[span, :], pick, ACROSS, preferred_element_type=F32)[:, :1]
        attn = jnp.zeros((tile, W), F32)
        for side, (keys, values) in enumerate(((key, value), (key_theirs, value_theirs))):
            scores = lax.dot_general(
                query, keys[...], ACROSS, preferred_element_type=F32
            ) * W ** (-0.5)
            visible = key_pos[side : side + 1] <= q_pos
            weight = jnp.where(visible, silu(scores), 0.0).astype(BF16)
            attn += jnp.dot(weight, values[...], preferred_element_type=F32)
        normed = attn * lax.rsqrt(jnp.mean(attn * attn, axis=-1, keepdims=True) + 1e-06)
        out = (normed * gate_query[span, :W].astype(F32)).astype(BF16)
        for s in range(NZ):
            gated[s, k] = out[s * piece : (s + 1) * piece]


def hidden_kernel(where, *refs):
    n = len(PLANE)
    gated, w_own, w_other, tok = refs[:n], refs[n : n + 2], refs[n + 2 : n + 4], refs[n + 4 : 2 * n + 4]
    hidden, g_raw, g_all, t_all, w_all, sems = refs[2 * n + 4 :]
    z, y, x, u = (where[i] for i in range(4))
    c = chip_at(z, y, x)
    rows = hidden.shape[1]
    half = w_all.shape[1]
    copies = [(src, g_raw.at[k]) for k, src in enumerate(gated)]
    for s in range(NZ):
        cols = pl.ds(s * W, W)
        for side, src in enumerate((w_own, w_other)):
            copies.append((src[s // 2].at[s % 2], w_all.at[side, :, cols]))
        block = relative_chip(c, 0, 0, s)
        from_cols = pl.ds(pl.multiple_of(block * W, W), W)
        for k in range(n):
            copies.append((tok[k].at[pl.ds(0, rows), from_cols], t_all.at[k, :, cols]))
    copies = [pltpu.make_async_copy(src, dst, sems.at[i]) for i, (src, dst) in enumerate(copies)]
    for copy in copies:
        copy.start()
    for copy in copies[:n]:
        copy.wait()
    for k, (by, bx) in enumerate(PLANE):
        for s in range(NZ):
            head = relative_chip(c, by, bx, s)
            cols = pl.ds(pl.multiple_of(head * W, W), W)
            for j in range(n):
                block = j ^ k
                g_all[block * rows : (block + 1) * rows, cols] = g_raw[k, s, j]
    for copy in copies[n:]:
        copy.wait()
    total = 0.0
    for side, at in enumerate((u, 1 - u)):
        part = g_all[:, pl.ds(pl.multiple_of(at * half, half), half)]
        total += jnp.dot(part, w_all[side], preferred_element_type=F32)
    for k in range(n):
        for s in range(NZ):
            term = total[k * rows : (k + 1) * rows, s * W : (s + 1) * W]
            cols = pl.ds(pl.multiple_of((z ^ s) * W, W), W)
            hidden[k, :, cols] = (t_all[k, :, s * W : (s + 1) * W].astype(F32) + term).astype(BF16)


def as_line(column):
    size = column.shape[0]
    line = lax.broadcasted_iota(jnp.int32, (size, size), 0)
    lane = lax.broadcasted_iota(jnp.int32, (size, size), 1)
    return jnp.sum(jnp.where(line == lane, column, 0.0), axis=0, keepdims=True)


def mass_kernel(where, *refs):
    n = len(PLANE)
    pieces, (n_own, n_other, t_keep, t_send, marks) = refs[:n], refs[n : n + 5]
    keep, send, positive, mass, h_all = refs[n + 5 :]
    y, x, u = (where[i] for i in range(1, 4))
    rows, half = keep.shape
    for k, (by, bx) in enumerate(PLANE):
        for at in range(NZ):
            block = chip_at(at, y ^ by, x ^ bx)
            cols = pl.ds(pl.multiple_of(block * W, W), W)
            for j in range(n):
                row = (j ^ k) * rows
                h_all[row : row + rows, cols] = pieces[k][j, :, at * W : (at + 1) * W]
    mine = pl.ds(pl.multiple_of(u * half, half), half)
    theirs = pl.ds(pl.multiple_of((1 - u) * half, half), half)
    keep[...] = h_all[:rows, mine]
    send[...] = h_all[:rows, theirs]
    hh, dots, lines = 0.0, 0.0, []
    pick = pick_columns({0: 1.0, 1: 1.0, 2: 1.0}, {3: 256.0, 4: 1.0})
    for part, neg in ((mine, n_own), (theirs, n_other)):
        h_part = h_all[:, part]
        h_f = h_part.astype(F32)
        hh += jnp.sum(h_f * h_f, axis=1, keepdims=True)
        dots += lax.dot_general(h_part, neg[:, :half], ACROSS, preferred_element_type=F32)
        lines.append(lax.dot_general(pick, neg[:, half:], ACROSS, preferred_element_type=F32))
    h_scale = lax.rsqrt(hh + 1e-06) * 20.0
    he = ee = 0.0
    for h_ref, ref in ((keep, t_keep), (send, t_send)):
        h_f, t_f = h_ref[...].astype(F32), ref[...].astype(F32)
        he += jnp.sum(h_f * t_f, axis=1, keepdims=True)
        ee += jnp.sum(t_f * t_f, axis=1, keepdims=True)
    positive[...] = as_line(he * lax.rsqrt(ee + 1e-06) * h_scale[:rows])
    first = [marks[k * NZ * rows : (k * NZ + 1) * rows] for k in range(n)]
    pick = pick_columns({4: 256.0, 5: 1.0})
    t_ids = lax.dot_general(
        jnp.concatenate(first), pick, ACROSS, preferred_element_type=F32
    )[:, :1]
    neg_logit = dots * h_scale * lax.rsqrt(lines[0][0:1] + lines[1][0:1] + 1e-06)
    kept = jnp.where(lines[0][1:2] != t_ids, jnp.exp(neg_logit), 0.0)
    total = jnp.sum(kept, axis=1, keepdims=True)
    for k in range(n):
        mass[k] = as_line(total[k * rows : (k + 1) * rows])


def final_kernel(where, keep, theirs, positive, *refs):
    masses, (hidden, loss) = refs[:-2], refs[-2:]
    u, rows = where[3], keep.shape[0]
    hidden[pl.ds(pl.multiple_of(u * rows, rows), rows), :] = keep[...]
    hidden[pl.ds(pl.multiple_of((1 - u) * rows, rows), rows), :] = theirs[...]
    total = jnp.exp(positive[...])
    for mass in masses:
        total += mass[...]
    loss[...] = jnp.log(total) - positive[...]


def call(kernel, name, outs, scratch, args, places, flops):
    space = {"s": pltpu.SMEM, "v": pltpu.VMEM, "h": pl.ANY}
    moved = sum(a.size * a.dtype.itemsize for a in args)
    return pl.pallas_call(
        kernel,
        out_shape=[jax.ShapeDtypeStruct(shape, dtype) for shape, dtype in outs],
        in_specs=[pl.BlockSpec(memory_space=space[p]) for p in places],
        out_specs=[pl.BlockSpec(memory_space=pltpu.VMEM)] * len(outs),
        scratch_shapes=scratch,
        compiler_params=pltpu.CompilerParams(vmem_limit_bytes=VMEM_LIMIT),
        cost_estimate=pl.CostEstimate(flops=flops, bytes_accessed=moved, transcendentals=0),
        name=name,
    )(*args)


def whole_parts(value, base):
    return [(value // base).astype(BF16), (value % base).astype(BF16)]


def float_parts(value):
    parts = []
    for _ in range(3):
        parts.append(lax.reduce_precision(value, 8, 7))
        value = value - parts[-1]
    return [part.astype(BF16) for part in parts]


def with_marks(rows, marks):
    marks = jnp.stack(marks, 1)
    marks = jnp.pad(marks, ((0, 0), (0, W - marks.shape[1])))
    return jnp.concatenate([rows, marks], 1)


def head_shards(
    tokens, w_proj, w_out, positions, neg_emb, neg_ids, target_emb, target_ids
):
    c, u = lax.axis_index("ctx"), lax.axis_index("tp")
    z, y, x = coords(c)
    where = jnp.stack([z, y, x, u]).astype(jnp.int32)
    model = tokens.shape[1]
    rows = tokens.shape[0] // 2
    events = rows * CHIPS
    half = model // 2
    negs = neg_emb.shape[0]
    plane = len(PLANE)

    mine = lax.dynamic_slice_in_dim(tokens, u * rows, rows, 0)
    p_own = lax.dynamic_slice_in_dim(positions, u * rows, rows, 0)
    p_other = lax.dynamic_slice_in_dim(positions, (1 - u) * rows, rows, 0)
    ids = whole_parts(target_ids, 256)
    mine = with_marks(mine, whole_parts(p_own, 128) + whole_parts(p_other, 128) + ids)
    low = pair_up(mine)

    to_x, to_y = flip(0, 1), flip(1, 0)
    high = hop(low, flip(0, 0, 2))
    w_plane = heads_in_plane(w_proj, y, x, low)
    w_pieces = [pick_row(w_plane, e ^ (z & 1)) for e in range(2)]
    low_x, low_y = hop(low, to_x), hop(low, to_y)
    low_xy = across(low_x, low_y)

    out_pair = pair_up(after(w_out[None], low))
    own_ids = lax.dynamic_slice_in_dim(neg_ids, c * negs, negs, 0)
    norms = jnp.sum(jnp.square(neg_emb.astype(F32)), axis=1)
    neg = with_marks(neg_emb, float_parts(norms) + whole_parts(own_ids, 256))

    w_pieces, high = lax.optimization_barrier((w_pieces, after(high, out_pair)))
    high_x, high_y = hop(high, to_x), hop(high, to_y)
    high_xy = across(high_x, high_y)
    tok = [low, high, low_x, high_x, low_y, high_y, *low_xy, *high_xy]
    w_mine = after(heads_along_z(w_pieces), low_xy, high_xy)
    w_theirs = [swap_cores(w) for w in w_mine]
    out_own = [out_pair, hop(after(out_pair, w_mine), flip(0, 0, 2))]
    neg_pair = pair_up(after(neg, w_mine))
    t_rows = after(target_emb.reshape(2, rows, -1), w_theirs)
    t_keep = pick_row(t_rows, u)
    t_send = swap_cores(pick_row(t_rows, 1 - u))

    def project(pieces):
        count = sum(p.shape[0] for p in pieces)
        return call(
            proj_kernel,
            "project",
            [((count, 2 * W), BF16)] + [((count, W), BF16)] * 3,
            [
                pltpu.VMEM((count, model + W), BF16),
                pltpu.VMEM((model, 4 * W), BF16),
                pltpu.SemaphoreType.DMA((len(pieces),)),
                pltpu.SemaphoreType.DMA((4,)),
            ],
            [where, *pieces, *w_mine, *w_theirs],
            "s" + (len(pieces) + 4) * "h",
            0,
        )

    gate_query, value, key, marks = project(tok)
    key_theirs, value_theirs = swap_cores(key), swap_cores(value)
    out_pair_theirs = swap_cores(after(out_pair, value))
    (gated,) = call(
        attend_kernel,
        "attend",
        [((NZ, plane, rows, W), BF16)],
        [pltpu.VMEM((events, 2 * W), BF16)]
        + [pltpu.VMEM((events, W), BF16)] * 5
        + [pltpu.SemaphoreType.DMA((6,))],
        [gate_query, key, value, key_theirs, value_theirs, marks],
        6 * "h",
        0,
    )
    out_own, out_pair_theirs, gated = lax.optimization_barrier((out_own, out_pair_theirs, gated))
    gated = jnp.stack([gated[0]] + [hop(gated[s], flip(0, 0, s)) for s in range(1, NZ)])
    neg_far = hop(after(neg_pair, gated), flip(0, 0, 2))
    out_other = [out_pair_theirs, swap_cores(after(out_own[1], gated))]
    gated = [gated] + [hop(gated, flip(by, bx)) for by, bx in PLANE[1:]]
    (hidden,) = call(
        hidden_kernel,
        "hidden",
        [((plane, rows, NZ * W), BF16)],
        [
            pltpu.VMEM((plane, NZ, plane, rows, W), BF16),
            pltpu.VMEM((plane * rows, model), BF16),
            pltpu.VMEM((plane, rows, NZ * W), BF16),
            pltpu.VMEM((2, half, NZ * W), BF16),
            pltpu.SemaphoreType.DMA((28,)),
        ],
        [where, *gated, *out_own, *out_other, low, low_x, low_y, low_xy[0]],
        "s" + 12 * "h",
        2 * plane * rows * model * NZ * W,
    )
    neg_own = jnp.concatenate([neg_pair, after(neg_far, hidden, t_send)])
    neg_other = swap_cores(neg_own)
    pieces = [hidden] + [hop(hidden, flip(by, bx)) for by, bx in PLANE[1:]]
    h_keep, h_send, positive, mass = call(
        mass_kernel,
        "mass",
        [((rows, half), BF16)] * 2 + [((1, rows), F32), ((plane, 1, rows), F32)],
        [pltpu.VMEM((plane * rows, model), BF16)],
        [where, *pieces, neg_own, neg_other, t_keep, t_send, marks],
        "s" + 9 * "v",
        2 * plane * rows * model * NZ * negs,
    )
    masses = [mass[0]] + [hop(mass[k], flip(*PLANE[k])) for k in range(1, plane)]
    h_theirs = swap_cores(h_send)
    hidden, loss = call(
        final_kernel,
        "final",
        [((2 * rows, half), BF16), ((1, rows), F32)],
        [],
        [where, h_keep, h_theirs, positive, *masses],
        "s" + 7 * "v",
        0,
    )
    return hidden, loss.reshape(-1)


def shards(tokens, w_proj, *rest):
    n_ctx, n_tp = lax.axis_size("ctx"), lax.axis_size("tp")
    heads = w_proj.shape[2] * n_tp // HEAD_DIM
    plan = head_shards if (n_ctx, n_tp, heads) == (CHIPS, 2, CHIPS) else general_shards
    return plan(tokens, w_proj, *rest)


def solution(mesh):
    placed = (
        P("ctx", None),
        P("ctx", None, "tp"),
        P("tp", "ctx"),
        P("ctx"),
        P("ctx", "tp"),
        P(),
        P("ctx", "tp"),
        P(("ctx", "tp")),
    )
    return jax.shard_map(
        shards,
        mesh=mesh,
        in_specs=placed,
        out_specs=(P("ctx", "tp"), P(("ctx", "tp"))),
        check_vma=False,
    )
```

```python
import jax
import jax.numpy as jnp
from jax import lax
from jax.experimental import pallas as pl
from jax.experimental.pallas import tpu as pltpu
from jax.sharding import PartitionSpec as P

HEAD_DIM = 128
VMEM_LIMIT = 24 * 1024 * 1024
BF16 = jnp.bfloat16
F32 = jnp.float32


def attend_piece(q_group, q_pos, k_piece, v_piece, p_piece):
    heads = q_group.shape[1]
    width = q_group.shape[2]
    key_heads = k_piece.reshape(k_piece.shape[0], heads, width)
    value_heads = v_piece.reshape(v_piece.shape[0], heads, width)
    scores = jnp.einsum(
        "thd,khd->htk", q_group, key_heads, preferred_element_type=jnp.float32
    ) * width ** (-0.5)
    visible = p_piece[None, None, :] <= q_pos[None, :, None]
    weight = jnp.where(visible, jax.nn.silu(scores), 0.0).astype(jnp.bfloat16)
    return jnp.einsum("htk,khd->thd", weight, value_heads, preferred_element_type=jnp.float32)


def general_shards(
    tokens, w_proj, w_out, positions, neg_emb, neg_ids, target_emb, target_ids
):
    tok_rows = tokens.shape[0]
    head_cols = w_proj.shape[2]
    local_heads = head_cols // HEAD_DIM
    proj_sum = jnp.einsum(
        "td,dfh->tfh",
        tokens,
        lax.all_gather(w_proj, "ctx", axis=0, tiled=True),
        preferred_element_type=jnp.float32,
    )
    proj = jax.nn.silu(proj_sum).astype(jnp.bfloat16)
    gate = proj[:, 0].reshape(tok_rows, local_heads, HEAD_DIM)
    query = proj[:, 2].reshape(tok_rows, local_heads, HEAD_DIM)
    v_piece = lax.all_gather(proj[:, 1], "ctx", axis=0, tiled=True)
    k_piece = lax.all_gather(proj[:, 3], "ctx", axis=0, tiled=True)
    p_piece = lax.all_gather(positions, "ctx", axis=0, tiled=True)
    attn = attend_piece(query, positions, k_piece, v_piece, p_piece)
    normed = attn * lax.rsqrt(jnp.mean(attn * attn, axis=-1, keepdims=True) + 1e-06)
    gated = (normed * gate.astype(jnp.float32)).astype(jnp.bfloat16).reshape(tok_rows, head_cols)
    out_terms = jnp.dot(
        gated, lax.all_gather(w_out, "ctx", axis=1, tiled=True), preferred_element_type=jnp.float32
    )
    out_share = lax.psum_scatter(out_terms, "tp", scatter_dimension=1, tiled=True)
    feat_cols = out_share.shape[1]
    own_tokens = lax.dynamic_slice_in_dim(tokens, lax.axis_index("tp") * feat_cols, feat_cols, 1)
    hidden = (own_tokens.astype(jnp.float32) + out_share).astype(jnp.bfloat16)
    piece = lax.all_gather(neg_emb, "ctx", axis=0, tiled=True)
    panel_dots = lax.dot_general(
        hidden, piece, (((1,), (1,)), ((), ())), preferred_element_type=jnp.float32
    )
    panel_norms = jnp.sum(jnp.square(piece.astype(jnp.float32)), axis=1)
    hidden_f = hidden.astype(jnp.float32)
    target_f = target_emb.astype(jnp.float32)
    part_hh = jnp.sum(hidden_f * hidden_f, axis=1)
    part_he = jnp.sum(hidden_f * target_f, axis=1)
    part_ee = jnp.sum(target_f * target_f, axis=1)
    dots, hh_sum, he_sum, ee_sum = (
        lax.psum_scatter(panel_dots, "tp", scatter_dimension=0, tiled=True),
        lax.psum_scatter(part_hh, "tp", scatter_dimension=0, tiled=True),
        lax.psum_scatter(part_he, "tp", scatter_dimension=0, tiled=True),
        lax.psum_scatter(part_ee, "tp", scatter_dimension=0, tiled=True),
    )
    neg_sq = lax.psum(panel_norms, "tp")
    pos_logit = he_sum / jnp.sqrt(hh_sum + 1e-06) / jnp.sqrt(ee_sum + 1e-06) / 0.05
    neg_logit = dots / jnp.sqrt(hh_sum + 1e-06)[:, None] / jnp.sqrt(neg_sq + 1e-06)[None, :] / 0.05
    keep_mask = neg_ids[None, :] != target_ids[:, None]
    total_mass = jnp.exp(pos_logit) + jnp.sum(jnp.where(keep_mask, jnp.exp(neg_logit), 0.0), axis=1)
    loss = jnp.log(total_mass) - pos_logit
    return (hidden, loss)


NZ, NY, NX = 4, 2, 2
CHIPS = NZ * NY * NX
PLANE = [(by, bx) for by in range(NY) for bx in range(NX)]
SWAP = [(0, 1), (1, 0)]
W = HEAD_DIM
ACROSS = (((1,), (1,)), ((), ()))


def chip_at(z, y, x):
    return (z * NY + y) * NX + x


def coords(c):
    return c // (NY * NX), (c // NX) % NY, c % NX


def relative_chip(c, by, bx, s):
    z, y, x = coords(c)
    return chip_at(z ^ s, y ^ by, x ^ bx)


def flip(by, bx, s=0):
    return [(c, relative_chip(c, by, bx, s)) for c in range(CHIPS)]


def hop(value, perm):
    return lax.ppermute(value, "ctx", perm)


def swap_cores(value):
    return lax.ppermute(value, "tp", SWAP)


def pick_row(value, at):
    return lax.dynamic_index_in_dim(value, at, 0, keepdims=False)


def after(values, *others):
    return lax.optimization_barrier((values, others))[0]


def pair_up(own):
    return jnp.concatenate([own, hop(own, flip(0, 0, 1))])


def across(value_x, value_y):
    half = value_x.shape[0] // 2
    return [hop(value_x[:half], flip(1, 0)), hop(value_y[half:], flip(0, 1))]


def heads_in_plane(w_proj, y, x, first):
    heads = w_proj.reshape(-1, 4, 2, NY, NX, W).transpose(4, 3, 2, 0, 1, 5)
    heads = heads.reshape(NX, NY, 2, -1, 4 * W)
    kept, sent = pick_row(heads, x), after(pick_row(heads, x ^ 1), first)
    came = hop(sent, flip(0, 1))
    lined = jnp.where(x == 0, jnp.stack([kept, came], 2), jnp.stack([came, kept], 2))
    return pick_row(lined, y), hop(pick_row(lined, y ^ 1), flip(1, 0))


def heads_along_z(pieces):
    arrived = []
    for e, piece in enumerate(pieces):
        perm = []
        for src in range(CHIPS):
            sz, sy, sx = coords(src)
            for t in range(2):
                dst = chip_at(2 * t + (e ^ (sz & 1)), sy, sx)
                perm.append((2 * src + t, 2 * dst + (sz >> 1)))
        arrived.append(lax.ppermute(piece, ("ctx", "tp"), perm))
    return arrived


def silu(v):
    return 0.5 * v * (1.0 + jnp.tanh(0.5 * v))


def run_copies(copies):
    for copy in copies:
        copy.start()
    for copy in copies:
        copy.wait()


def mark_kernel(where, tokens, positions, ids, mine):
    u = where[3]
    rows, model = mine.shape[0], tokens.shape[1]
    mine[:, :model] = tokens[pl.ds(pl.multiple_of(u * rows, rows), rows), :]
    line = lax.broadcasted_iota(jnp.int32, (rows, rows), 0)
    across = lax.broadcasted_iota(jnp.int32, (rows, rows), 1)
    lane = lax.broadcasted_iota(jnp.int32, (rows, W), 1)
    marks = jnp.zeros((rows, W), F32)
    values = (positions[pl.ds(u, 1)], positions[pl.ds(1 - u, 1)], ids[...])
    for i, (value, bits) in enumerate(zip(values, (7, 7, 8))):
        column = jnp.sum(jnp.where(line == across, value, 0), axis=1, keepdims=True)
        high = lax.shift_right_logical(column, bits)
        marks = jnp.where(lane == 2 * i, high.astype(F32), marks)
        marks = jnp.where(lane == 2 * i + 1, (column - high * 2**bits).astype(F32), marks)
    mine[:, model:] = marks.astype(BF16)


def proj_kernel(where, *refs):
    count = len(refs) - 12
    tok, w_own, w_other = refs[:count], refs[count : count + 2], refs[count + 2 : count + 4]
    gate_query, value, key, marks, x_all, w_all, tok_sem, w_sem = refs[count + 4 :]
    z, y, u = where[0], where[1], where[3]
    copies, base = [], 0
    for side, (at, srcs) in enumerate(((u, w_own), (1 - u, w_other))):
        for e, src in enumerate(srcs):
            size = src.shape[0] // 2
            for j in range(2):
                start = ((2 * at + (e ^ (z & 1))) * 2 + (y ^ j)) * size
                to = w_all.at[pl.ds(pl.multiple_of(start, size), size), :]
                sem = w_sem.at[4 * side + 2 * e + j]
                copies.append(pltpu.make_async_copy(src.at[pl.ds(j * size, size), :], to, sem))
    for i, ref in enumerate(tok):
        rows = pl.ds(base, ref.shape[0])
        copies.append(pltpu.make_async_copy(ref, x_all.at[rows, :], tok_sem.at[i]))
        base += ref.shape[0]
    run_copies(copies)
    model = w_all.shape[0]
    total = jnp.dot(x_all[:, :model], w_all[...], preferred_element_type=F32)
    proj = silu(total).astype(BF16)
    gate_query[:, :W] = proj[:, :W]
    value[...] = proj[:, W : 2 * W]
    gate_query[:, W:] = proj[:, 2 * W : 3 * W]
    key[...] = proj[:, 3 * W :]
    marks[...] = x_all[:, model:]


def pick_columns(*weights):
    lane = lax.broadcasted_iota(jnp.int32, (8, W), 1)
    line = lax.broadcasted_iota(jnp.int32, (8, W), 0)
    pick = jnp.zeros((8, W), F32)
    for i, row in enumerate(weights):
        for at, weight in row.items():
            pick = jnp.where((line == i) & (lane == at), weight, pick)
    return pick.astype(BF16)


def attend_kernel(*refs):
    sources, gated, copied, sems = refs[:6], refs[6], refs[7:13], refs[13]
    run_copies(
        [
            pltpu.make_async_copy(src, dst, sems.at[i])
            for i, (src, dst) in enumerate(zip(sources, copied))
        ]
    )
    gate_query, key, value, key_theirs, value_theirs, marks = copied
    pick = pick_columns({0: 128.0, 1: 1.0}, {2: 128.0, 3: 1.0})
    piece = gated.shape[2]
    tile = NZ * piece
    key_pos = lax.dot_general(pick, marks[...], ACROSS, preferred_element_type=F32)
    for k in range(len(PLANE)):
        span = pl.ds(k * tile, tile)
        query = gate_query[span, W:]
        q_pos = lax.dot_general(marks[span, :], pick, ACROSS, preferred_element_type=F32)[:, :1]
        attn = jnp.zeros((tile, W), F32)
        for side, (keys, values) in enumerate(((key, value), (key_theirs, value_theirs))):
            scores = lax.dot_general(
                query, keys[...], ACROSS, preferred_element_type=F32
            ) * W ** (-0.5)
            visible = key_pos[side : side + 1] <= q_pos
            weight = jnp.where(visible, silu(scores), 0.0).astype(BF16)
            attn += jnp.dot(weight, values[...], preferred_element_type=F32)
        normed = attn * lax.rsqrt(jnp.mean(attn * attn, axis=-1, keepdims=True) + 1e-06)
        out = (normed * gate_query[span, :W].astype(F32)).astype(BF16)
        for s in range(NZ):
            gated[s, k] = out[s * piece : (s + 1) * piece]


def hidden_kernel(where, *refs):
    n = len(PLANE)
    gated, w_own, w_other, tok = refs[:5], refs[5:7], refs[7:9], refs[9:13]
    hidden, g_raw, g_all, t_all, w_all, sems = refs[13:]
    z, y, x, u = (where[i] for i in range(4))
    c = chip_at(z, y, x)
    rows = hidden.shape[1]
    half = w_all.shape[1]
    copies = [(src, g_raw.at[k]) for k, src in enumerate(gated[:3])]
    copies += [(src, g_raw.at[3, pl.ds(2 * i, 2)]) for i, src in enumerate(gated[3:])]
    for s in range(NZ):
        cols = pl.ds(s * W, W)
        for side, src in enumerate((w_own, w_other)):
            copies.append((src[s // 2].at[s % 2], w_all.at[side, :, cols]))
        block = relative_chip(c, 0, 0, s)
        from_cols = pl.ds(pl.multiple_of(block * W, W), W)
        for k in range(n):
            copies.append((tok[k].at[pl.ds(0, rows), from_cols], t_all.at[k, :, cols]))
    copies = [pltpu.make_async_copy(src, dst, sems.at[i]) for i, (src, dst) in enumerate(copies)]
    for copy in copies:
        copy.start()
    for copy in copies[:5]:
        copy.wait()
    for k, (by, bx) in enumerate(PLANE):
        for s in range(NZ):
            head = relative_chip(c, by, bx, s)
            cols = pl.ds(pl.multiple_of(head * W, W), W)
            for j in range(n):
                block = j ^ k
                g_all[block * rows : (block + 1) * rows, cols] = g_raw[k, s, j]
    for copy in copies[5:]:
        copy.wait()
    total = 0.0
    for side, at in enumerate((u, 1 - u)):
        part = g_all[:, pl.ds(pl.multiple_of(at * half, half), half)]
        total += jnp.dot(part, w_all[side], preferred_element_type=F32)
    for k in range(n):
        for s in range(NZ):
            term = total[k * rows : (k + 1) * rows, s * W : (s + 1) * W]
            cols = pl.ds(pl.multiple_of((z ^ s) * W, W), W)
            hidden[k, :, cols] = (t_all[k, :, s * W : (s + 1) * W].astype(F32) + term).astype(BF16)


def as_line(column):
    size = column.shape[0]
    line = lax.broadcasted_iota(jnp.int32, (size, size), 0)
    lane = lax.broadcasted_iota(jnp.int32, (size, size), 1)
    return jnp.sum(jnp.where(line == lane, column, 0.0), axis=0, keepdims=True)


def mass_kernel(where, *refs):
    n = len(PLANE)
    pieces, (n_own, n_other, t_keep, t_send, marks) = refs[:5], refs[5:10]
    keep, send, positive, mass, h_all = refs[10:]
    y, x, u = (where[i] for i in range(1, 4))
    rows, half = keep.shape
    for k, (by, bx) in enumerate(PLANE):
        for at in range(NZ):
            block = chip_at(at, y ^ by, x ^ bx)
            cols = pl.ds(pl.multiple_of(block * W, W), W)
            for j in range(n):
                row = (j ^ k) * rows
                ref, i = (pieces[k], j) if k < n - 1 else (pieces[k + j // 2], j % 2)
                h_all[row : row + rows, cols] = ref[i, :, at * W : (at + 1) * W]
    mine = pl.ds(pl.multiple_of(u * half, half), half)
    theirs = pl.ds(pl.multiple_of((1 - u) * half, half), half)
    keep[...] = h_all[:rows, mine]
    send[...] = h_all[:rows, theirs]
    hh, dots, lines = 0.0, 0.0, []
    pick = pick_columns({0: 1.0, 1: 1.0, 2: 1.0}, {3: 256.0, 4: 1.0})
    for part, neg in ((mine, n_own), (theirs, n_other)):
        h_part = h_all[:, part]
        h_f = h_part.astype(F32)
        hh += jnp.sum(h_f * h_f, axis=1, keepdims=True)
        dots += lax.dot_general(h_part, neg[:, :half], ACROSS, preferred_element_type=F32)
        lines.append(lax.dot_general(pick, neg[:, half:], ACROSS, preferred_element_type=F32))
    h_scale = lax.rsqrt(hh + 1e-06) * 20.0
    he = ee = 0.0
    for h_ref, ref in ((keep, t_keep), (send, t_send)):
        h_f, t_f = h_ref[...].astype(F32), ref[...].astype(F32)
        he += jnp.sum(h_f * t_f, axis=1, keepdims=True)
        ee += jnp.sum(t_f * t_f, axis=1, keepdims=True)
    positive[...] = as_line(he * lax.rsqrt(ee + 1e-06) * h_scale[:rows])
    first = [marks[k * NZ * rows : (k * NZ + 1) * rows] for k in range(n)]
    pick = pick_columns({4: 256.0, 5: 1.0})
    t_ids = lax.dot_general(
        jnp.concatenate(first), pick, ACROSS, preferred_element_type=F32
    )[:, :1]
    neg_logit = dots * h_scale * lax.rsqrt(lines[0][0:1] + lines[1][0:1] + 1e-06)
    kept = jnp.where(lines[0][1:2] != t_ids, jnp.exp(neg_logit), 0.0)
    total = jnp.sum(kept, axis=1, keepdims=True)
    for k in range(n):
        mass[k] = as_line(total[k * rows : (k + 1) * rows])


def final_kernel(where, keep, theirs, positive, *refs):
    masses, (hidden, loss) = refs[:-2], refs[-2:]
    u, rows = where[3], keep.shape[0]
    hidden[pl.ds(pl.multiple_of(u * rows, rows), rows), :] = keep[...]
    hidden[pl.ds(pl.multiple_of((1 - u) * rows, rows), rows), :] = theirs[...]
    total = jnp.exp(positive[...])
    for mass in masses:
        total += mass[...]
    loss[...] = jnp.log(total) - positive[...]


def call(kernel, name, outs, scratch, args, places, flops):
    space = {"s": pltpu.SMEM, "v": pltpu.VMEM, "h": pl.ANY}
    moved = sum(a.size * a.dtype.itemsize for a in args)
    return pl.pallas_call(
        kernel,
        out_shape=[jax.ShapeDtypeStruct(shape, dtype) for shape, dtype in outs],
        in_specs=[pl.BlockSpec(memory_space=space[p]) for p in places],
        out_specs=[pl.BlockSpec(memory_space=pltpu.VMEM)] * len(outs),
        scratch_shapes=scratch,
        compiler_params=pltpu.CompilerParams(vmem_limit_bytes=VMEM_LIMIT),
        cost_estimate=pl.CostEstimate(flops=flops, bytes_accessed=moved, transcendentals=0),
        name=name,
    )(*args)


def whole_parts(value, base):
    return [(value // base).astype(BF16), (value % base).astype(BF16)]


def float_parts(value):
    parts = []
    for _ in range(3):
        parts.append(lax.reduce_precision(value, 8, 7))
        value = value - parts[-1]
    return [part.astype(BF16) for part in parts]


def with_marks(rows, marks):
    marks = jnp.stack(marks, 1)
    marks = jnp.pad(marks, ((0, 0), (0, W - marks.shape[1])))
    return jnp.concatenate([rows, marks], 1)


def head_shards(
    tokens, w_proj, w_out, positions, neg_emb, neg_ids, target_emb, target_ids
):
    c, u = lax.axis_index("ctx"), lax.axis_index("tp")
    z, y, x = coords(c)
    where = jnp.stack([z, y, x, u]).astype(jnp.int32)
    model = tokens.shape[1]
    rows = tokens.shape[0] // 2
    events = rows * CHIPS
    half = model // 2
    negs = neg_emb.shape[0]
    plane = len(PLANE)

    (mine,) = call(
        mark_kernel,
        "mark",
        [((rows, model + W), BF16)],
        [],
        [where, tokens, positions.reshape(2, rows), target_ids.reshape(1, rows)],
        "svvv",
        0,
    )
    line = [mine] + [hop(mine, flip(0, 0, s)) for s in range(1, NZ)]

    to_x, to_y = flip(0, 1), flip(1, 0)
    w_rows = heads_in_plane(after(w_proj, mine), y, x, line[1])
    w_pieces = [
        jnp.concatenate([pick_row(w, e ^ (z & 1)) for w in w_rows]).reshape(-1, 4 * W)
        for e in range(2)
    ]

    own_ids = lax.dynamic_slice_in_dim(neg_ids, c * negs, negs, 0)
    norms = jnp.sum(jnp.square(neg_emb.astype(F32)), axis=1)
    neg = with_marks(neg_emb, float_parts(norms) + whole_parts(own_ids, 256))

    out_pair = pair_up(after(w_out[None], mine))
    w_pieces, neg, out_pair, line = lax.optimization_barrier((w_pieces, neg, out_pair, line))
    near = jnp.concatenate(line)
    near_x, near_y = hop(near, to_x), hop(near, to_y)
    tok = [near, near_x, near_y, *across(near_x, near_y)]
    w_mine = heads_along_z(w_pieces)
    w_theirs = [swap_cores(w) for w in w_mine]
    out_own = [out_pair, hop(after(out_pair, w_mine), flip(0, 0, 2))]
    neg_pair = pair_up(after(neg, w_mine))
    t_rows = after(target_emb.reshape(2, rows, -1), w_theirs)
    t_keep = pick_row(t_rows, u)
    t_send = swap_cores(pick_row(t_rows, 1 - u))

    def project(pieces):
        count = sum(p.shape[0] for p in pieces)
        return call(
            proj_kernel,
            "project",
            [((count, 2 * W), BF16)] + [((count, W), BF16)] * 3,
            [
                pltpu.VMEM((count, model + W), BF16),
                pltpu.VMEM((model, 4 * W), BF16),
                pltpu.SemaphoreType.DMA((len(pieces),)),
                pltpu.SemaphoreType.DMA((8,)),
            ],
            [where, *pieces, *w_mine, *w_theirs],
            "s" + (len(pieces) + 4) * "h",
            0,
        )

    gate_query, value, key, marks = project(tok)
    key_theirs, value_theirs = swap_cores(key), swap_cores(value)
    out_pair_theirs = swap_cores(after(out_pair, value))
    (gated,) = call(
        attend_kernel,
        "attend",
        [((NZ, plane, rows, W), BF16)],
        [pltpu.VMEM((events, 2 * W), BF16)]
        + [pltpu.VMEM((events, W), BF16)] * 5
        + [pltpu.SemaphoreType.DMA((6,))],
        [gate_query, key, value, key_theirs, value_theirs, marks],
        6 * "h",
        0,
    )
    out_own, out_pair_theirs, gated = lax.optimization_barrier((out_own, out_pair_theirs, gated))
    gated = jnp.stack([gated[0]] + [hop(gated[s], flip(0, 0, s)) for s in range(1, NZ)])
    neg_far = hop(after(neg_pair, gated), flip(0, 0, 2))
    out_other = [out_pair_theirs, swap_cores(after(out_own[1], gated))]
    gated = [gated, hop(gated, to_x), hop(gated, to_y)]
    gated += across(gated[1], gated[2])
    (hidden,) = call(
        hidden_kernel,
        "hidden",
        [((plane, rows, NZ * W), BF16)],
        [
            pltpu.VMEM((plane, NZ, plane, rows, W), BF16),
            pltpu.VMEM((plane * rows, model), BF16),
            pltpu.VMEM((plane, rows, NZ * W), BF16),
            pltpu.VMEM((2, half, NZ * W), BF16),
            pltpu.SemaphoreType.DMA((29,)),
        ],
        [where, *gated, *out_own, *out_other, *tok[:4]],
        "s" + 13 * "h",
        2 * plane * rows * model * NZ * W,
    )
    neg_own = jnp.concatenate([neg_pair, after(neg_far, hidden, t_send)])
    neg_other = swap_cores(neg_own)
    pieces = [hidden, hop(hidden, to_x), hop(hidden, to_y)]
    pieces += across(pieces[1], pieces[2])
    h_keep, h_send, positive, mass = call(
        mass_kernel,
        "mass",
        [((rows, half), BF16)] * 2 + [((1, rows), F32), ((plane, 1, rows), F32)],
        [pltpu.VMEM((plane * rows, model), BF16)],
        [where, *pieces, neg_own, neg_other, t_keep, t_send, marks],
        "s" + 10 * "v",
        2 * plane * rows * model * NZ * negs,
    )
    masses = [mass[0]] + [hop(mass[k], flip(*PLANE[k])) for k in range(1, plane)]
    h_theirs = swap_cores(h_send)
    hidden, loss = call(
        final_kernel,
        "final",
        [((2 * rows, half), BF16), ((1, rows), F32)],
        [],
        [where, h_keep, h_theirs, positive, *masses],
        "s" + 7 * "v",
        0,
    )
    return hidden, loss.reshape(-1)


def shards(tokens, w_proj, *rest):
    n_ctx, n_tp = lax.axis_size("ctx"), lax.axis_size("tp")
    heads = w_proj.shape[2] * n_tp // HEAD_DIM
    plan = head_shards if (n_ctx, n_tp, heads) == (CHIPS, 2, CHIPS) else general_shards
    return plan(tokens, w_proj, *rest)


def solution(mesh):
    placed = (
        P("ctx", None),
        P("ctx", None, "tp"),
        P("tp", "ctx"),
        P("ctx"),
        P("ctx", "tp"),
        P(),
        P("ctx", "tp"),
        P(("ctx", "tp")),
    )
    return jax.shard_map(
        shards,
        mesh=mesh,
        in_specs=placed,
        out_specs=(P("ctx", "tp"), P(("ctx", "tp"))),
        check_vma=False,
    )
```

```python
import jax
import jax.numpy as jnp
from jax import lax
from jax.experimental import pallas as pl
from jax.experimental.pallas import tpu as pltpu
from jax.sharding import PartitionSpec as P

HEAD_DIM = 128
VMEM_LIMIT = 24 * 1024 * 1024
BF16 = jnp.bfloat16
F32 = jnp.float32


def attend_piece(q_group, q_pos, k_piece, v_piece, p_piece):
    heads = q_group.shape[1]
    width = q_group.shape[2]
    key_heads = k_piece.reshape(k_piece.shape[0], heads, width)
    value_heads = v_piece.reshape(v_piece.shape[0], heads, width)
    scores = jnp.einsum(
        "thd,khd->htk", q_group, key_heads, preferred_element_type=jnp.float32
    ) * width ** (-0.5)
    visible = p_piece[None, None, :] <= q_pos[None, :, None]
    weight = jnp.where(visible, jax.nn.silu(scores), 0.0).astype(jnp.bfloat16)
    return jnp.einsum("htk,khd->thd", weight, value_heads, preferred_element_type=jnp.float32)


def general_shards(
    tokens, w_proj, w_out, positions, neg_emb, neg_ids, target_emb, target_ids
):
    tok_rows = tokens.shape[0]
    head_cols = w_proj.shape[2]
    local_heads = head_cols // HEAD_DIM
    proj_sum = jnp.einsum(
        "td,dfh->tfh",
        tokens,
        lax.all_gather(w_proj, "ctx", axis=0, tiled=True),
        preferred_element_type=jnp.float32,
    )
    proj = jax.nn.silu(proj_sum).astype(jnp.bfloat16)
    gate = proj[:, 0].reshape(tok_rows, local_heads, HEAD_DIM)
    query = proj[:, 2].reshape(tok_rows, local_heads, HEAD_DIM)
    v_piece = lax.all_gather(proj[:, 1], "ctx", axis=0, tiled=True)
    k_piece = lax.all_gather(proj[:, 3], "ctx", axis=0, tiled=True)
    p_piece = lax.all_gather(positions, "ctx", axis=0, tiled=True)
    attn = attend_piece(query, positions, k_piece, v_piece, p_piece)
    normed = attn * lax.rsqrt(jnp.mean(attn * attn, axis=-1, keepdims=True) + 1e-06)
    gated = (normed * gate.astype(jnp.float32)).astype(jnp.bfloat16).reshape(tok_rows, head_cols)
    out_terms = jnp.dot(
        gated, lax.all_gather(w_out, "ctx", axis=1, tiled=True), preferred_element_type=jnp.float32
    )
    out_share = lax.psum_scatter(out_terms, "tp", scatter_dimension=1, tiled=True)
    feat_cols = out_share.shape[1]
    own_tokens = lax.dynamic_slice_in_dim(tokens, lax.axis_index("tp") * feat_cols, feat_cols, 1)
    hidden = (own_tokens.astype(jnp.float32) + out_share).astype(jnp.bfloat16)
    piece = lax.all_gather(neg_emb, "ctx", axis=0, tiled=True)
    panel_dots = lax.dot_general(
        hidden, piece, (((1,), (1,)), ((), ())), preferred_element_type=jnp.float32
    )
    panel_norms = jnp.sum(jnp.square(piece.astype(jnp.float32)), axis=1)
    hidden_f = hidden.astype(jnp.float32)
    target_f = target_emb.astype(jnp.float32)
    part_hh = jnp.sum(hidden_f * hidden_f, axis=1)
    part_he = jnp.sum(hidden_f * target_f, axis=1)
    part_ee = jnp.sum(target_f * target_f, axis=1)
    dots, hh_sum, he_sum, ee_sum = (
        lax.psum_scatter(panel_dots, "tp", scatter_dimension=0, tiled=True),
        lax.psum_scatter(part_hh, "tp", scatter_dimension=0, tiled=True),
        lax.psum_scatter(part_he, "tp", scatter_dimension=0, tiled=True),
        lax.psum_scatter(part_ee, "tp", scatter_dimension=0, tiled=True),
    )
    neg_sq = lax.psum(panel_norms, "tp")
    pos_logit = he_sum / jnp.sqrt(hh_sum + 1e-06) / jnp.sqrt(ee_sum + 1e-06) / 0.05
    neg_logit = dots / jnp.sqrt(hh_sum + 1e-06)[:, None] / jnp.sqrt(neg_sq + 1e-06)[None, :] / 0.05
    keep_mask = neg_ids[None, :] != target_ids[:, None]
    total_mass = jnp.exp(pos_logit) + jnp.sum(jnp.where(keep_mask, jnp.exp(neg_logit), 0.0), axis=1)
    loss = jnp.log(total_mass) - pos_logit
    return (hidden, loss)


NZ, NY, NX = 4, 2, 2
CHIPS = NZ * NY * NX
PLANE = [(by, bx) for by in range(NY) for bx in range(NX)]
SWAP = [(0, 1), (1, 0)]
W = HEAD_DIM
ACROSS = (((1,), (1,)), ((), ()))


def chip_at(z, y, x):
    return (z * NY + y) * NX + x


def coords(c):
    return c // (NY * NX), (c // NX) % NY, c % NX


def relative_chip(c, by, bx, s):
    z, y, x = coords(c)
    return chip_at(z ^ s, y ^ by, x ^ bx)


def flip(by, bx, s=0):
    return [(c, relative_chip(c, by, bx, s)) for c in range(CHIPS)]


def hop(value, perm):
    return lax.ppermute(value, "ctx", perm)


def swap_cores(value):
    return lax.ppermute(value, "tp", SWAP)


def pick_row(value, at):
    return lax.dynamic_index_in_dim(value, at, 0, keepdims=False)


def after(values, *others):
    return lax.optimization_barrier((values, others))[0]


def pair_up(own):
    return jnp.concatenate([own, hop(own, flip(0, 0, 1))])


def across(value_x, value_y):
    half = value_x.shape[0] // 2
    return [hop(value_x[:half], flip(1, 0)), hop(value_y[half:], flip(0, 1))]


def heads_in_plane(w_proj, y, x, first):
    heads = w_proj.reshape(-1, 4, 2, NY, NX, W).transpose(4, 3, 2, 0, 1, 5)
    heads = heads.reshape(NX, NY, 2, -1, 4 * W)
    kept, sent = pick_row(heads, x), after(pick_row(heads, x ^ 1), first)
    came = hop(sent, flip(0, 1))
    lined = jnp.where(x == 0, jnp.stack([kept, came], 2), jnp.stack([came, kept], 2))
    return pick_row(lined, y), hop(pick_row(lined, y ^ 1), flip(1, 0))


def heads_along_z(pieces):
    arrived = []
    for e, piece in enumerate(pieces):
        perm = []
        for src in range(CHIPS):
            sz, sy, sx = coords(src)
            for t in range(2):
                dst = chip_at(2 * t + (e ^ (sz & 1)), sy, sx)
                perm.append((2 * src + t, 2 * dst + (sz >> 1)))
        arrived.append(lax.ppermute(piece, ("ctx", "tp"), perm))
    return arrived


def silu(v):
    return 0.5 * v * (1.0 + jnp.tanh(0.5 * v))


def run_copies(copies):
    for copy in copies:
        copy.start()
    for copy in copies:
        copy.wait()


def mark_kernel(where, tokens, positions, ids, mine):
    u = where[3]
    rows, model = mine.shape[0], tokens.shape[1]
    mine[:, :model] = tokens[pl.ds(pl.multiple_of(u * rows, rows), rows), :]
    line = lax.broadcasted_iota(jnp.int32, (rows, rows), 0)
    across = lax.broadcasted_iota(jnp.int32, (rows, rows), 1)
    lane = lax.broadcasted_iota(jnp.int32, (rows, W), 1)
    marks = jnp.zeros((rows, W), F32)
    values = (positions[pl.ds(u, 1)], positions[pl.ds(1 - u, 1)], ids[...])
    for i, (value, bits) in enumerate(zip(values, (7, 7, 8))):
        column = jnp.sum(jnp.where(line == across, value, 0), axis=1, keepdims=True)
        high = lax.shift_right_logical(column, bits)
        marks = jnp.where(lane == 2 * i, high.astype(F32), marks)
        marks = jnp.where(lane == 2 * i + 1, (column - high * 2**bits).astype(F32), marks)
    mine[:, model:] = marks.astype(BF16)


def proj_kernel(where, *refs):
    count = len(refs) - 12
    tok, w_own, w_other = refs[:count], refs[count : count + 2], refs[count + 2 : count + 4]
    gate_query, value, key, marks, x_all, w_all, tok_sem, w_sem = refs[count + 4 :]
    z, y, u = where[0], where[1], where[3]
    copies, base = [], 0
    for side, (at, srcs) in enumerate(((u, w_own), (1 - u, w_other))):
        for e, src in enumerate(srcs):
            size = src.shape[0] // 2
            for j in range(2):
                start = ((2 * at + (e ^ (z & 1))) * 2 + (y ^ j)) * size
                to = w_all.at[pl.ds(pl.multiple_of(start, size), size), :]
                sem = w_sem.at[4 * side + 2 * e + j]
                copies.append(pltpu.make_async_copy(src.at[pl.ds(j * size, size), :], to, sem))
    for i, ref in enumerate(tok):
        rows = pl.ds(base, ref.shape[0])
        copies.append(pltpu.make_async_copy(ref, x_all.at[rows, :], tok_sem.at[i]))
        base += ref.shape[0]
    run_copies(copies)
    model = w_all.shape[0]
    total = jnp.dot(x_all[:, :model], w_all[...], preferred_element_type=F32)
    proj = silu(total).astype(BF16)
    gate_query[:, :W] = proj[:, :W]
    value[...] = proj[:, W : 2 * W]
    gate_query[:, W:] = proj[:, 2 * W : 3 * W]
    key[...] = proj[:, 3 * W :]
    marks[...] = x_all[:, model:]


def pick_columns(*weights):
    lane = lax.broadcasted_iota(jnp.int32, (8, W), 1)
    line = lax.broadcasted_iota(jnp.int32, (8, W), 0)
    pick = jnp.zeros((8, W), F32)
    for i, row in enumerate(weights):
        for at, weight in row.items():
            pick = jnp.where((line == i) & (lane == at), weight, pick)
    return pick.astype(BF16)


def attend_kernel(*refs):
    sources, gated, copied, sems = refs[:6], refs[6], refs[7:13], refs[13]
    run_copies(
        [
            pltpu.make_async_copy(src, dst, sems.at[i])
            for i, (src, dst) in enumerate(zip(sources, copied))
        ]
    )
    gate_query, key, value, key_theirs, value_theirs, marks = copied
    pick = pick_columns({0: 128.0, 1: 1.0}, {2: 128.0, 3: 1.0})
    piece = gated.shape[2]
    tile = NZ * piece
    key_pos = lax.dot_general(pick, marks[...], ACROSS, preferred_element_type=F32)
    for k in range(len(PLANE)):
        span = pl.ds(k * tile, tile)
        query = gate_query[span, W:]
        q_pos = lax.dot_general(marks[span, :], pick, ACROSS, preferred_element_type=F32)[:, :1]
        attn = jnp.zeros((tile, W), F32)
        for side, (keys, values) in enumerate(((key, value), (key_theirs, value_theirs))):
            scores = lax.dot_general(
                query, keys[...], ACROSS, preferred_element_type=F32
            ) * W ** (-0.5)
            visible = key_pos[side : side + 1] <= q_pos
            weight = jnp.where(visible, silu(scores), 0.0).astype(BF16)
            attn += jnp.dot(weight, values[...], preferred_element_type=F32)
        normed = attn * lax.rsqrt(jnp.mean(attn * attn, axis=-1, keepdims=True) + 1e-06)
        out = (normed * gate_query[span, :W].astype(F32)).astype(BF16)
        for s in range(NZ):
            gated[s, k] = out[s * piece : (s + 1) * piece]


def hidden_kernel(where, *refs):
    n = len(PLANE)
    gated, w_own, w_other, tok = refs[:5], refs[5:7], refs[7:9], refs[9:13]
    hidden, g_raw, g_all, t_all, w_all, sems = refs[13:]
    z, y, x, u = (where[i] for i in range(4))
    c = chip_at(z, y, x)
    rows = hidden.shape[1]
    half = w_all.shape[1]
    copies = [(src, g_raw.at[k]) for k, src in enumerate(gated[:3])]
    copies += [(src, g_raw.at[3, pl.ds(2 * i, 2)]) for i, src in enumerate(gated[3:])]
    for s in range(NZ):
        cols = pl.ds(s * W, W)
        for side, src in enumerate((w_own, w_other)):
            copies.append((src[s // 2].at[s % 2], w_all.at[side, :, cols]))
        block = relative_chip(c, 0, 0, s)
        from_cols = pl.ds(pl.multiple_of(block * W, W), W)
        for k in range(n):
            copies.append((tok[k].at[pl.ds(0, rows), from_cols], t_all.at[k, :, cols]))
    copies = [pltpu.make_async_copy(src, dst, sems.at[i]) for i, (src, dst) in enumerate(copies)]
    for copy in copies:
        copy.start()
    for copy in copies[:5]:
        copy.wait()
    for k, (by, bx) in enumerate(PLANE):
        for s in range(NZ):
            head = relative_chip(c, by, bx, s)
            cols = pl.ds(pl.multiple_of(head * W, W), W)
            for j in range(n):
                block = j ^ k
                g_all[block * rows : (block + 1) * rows, cols] = g_raw[k, s, j]
    for copy in copies[5:]:
        copy.wait()
    total = 0.0
    for side, at in enumerate((u, 1 - u)):
        part = g_all[:, pl.ds(pl.multiple_of(at * half, half), half)]
        total += jnp.dot(part, w_all[side], preferred_element_type=F32)
    for k in range(n):
        for s in range(NZ):
            term = total[k * rows : (k + 1) * rows, s * W : (s + 1) * W]
            cols = pl.ds(pl.multiple_of((z ^ s) * W, W), W)
            hidden[k, :, cols] = (t_all[k, :, s * W : (s + 1) * W].astype(F32) + term).astype(BF16)


def as_line(column):
    size = column.shape[0]
    line = lax.broadcasted_iota(jnp.int32, (size, size), 0)
    lane = lax.broadcasted_iota(jnp.int32, (size, size), 1)
    return jnp.sum(jnp.where(line == lane, column, 0.0), axis=0, keepdims=True)


def mass_kernel(where, *refs):
    n = len(PLANE)
    pieces, (n_own, n_other, t_keep, t_send, marks) = refs[:5], refs[5:10]
    keep, send, positive, mass, h_all = refs[10:]
    y, x, u = (where[i] for i in range(1, 4))
    rows, half = keep.shape
    for k, (by, bx) in enumerate(PLANE):
        for at in range(NZ):
            block = chip_at(at, y ^ by, x ^ bx)
            cols = pl.ds(pl.multiple_of(block * W, W), W)
            for j in range(n):
                row = (j ^ k) * rows
                ref, i = (pieces[k], j) if k < n - 1 else (pieces[k + j // 2], j % 2)
                h_all[row : row + rows, cols] = ref[i, :, at * W : (at + 1) * W]
    mine = pl.ds(pl.multiple_of(u * half, half), half)
    theirs = pl.ds(pl.multiple_of((1 - u) * half, half), half)
    keep[...] = h_all[:rows, mine]
    send[...] = h_all[:rows, theirs]
    hh, dots, lines = 0.0, 0.0, []
    pick = pick_columns({0: 1.0, 1: 1.0, 2: 1.0}, {3: 256.0, 4: 1.0})
    for part, neg in ((mine, n_own), (theirs, n_other)):
        h_part = h_all[:, part]
        h_f = h_part.astype(F32)
        hh += jnp.sum(h_f * h_f, axis=1, keepdims=True)
        dots += lax.dot_general(h_part, neg[:, :half], ACROSS, preferred_element_type=F32)
        lines.append(lax.dot_general(pick, neg[:, half:], ACROSS, preferred_element_type=F32))
    h_scale = lax.rsqrt(hh + 1e-06) * 20.0
    he = ee = 0.0
    for h_ref, ref in ((keep, t_keep), (send, t_send)):
        h_f, t_f = h_ref[...].astype(F32), ref[...].astype(F32)
        he += jnp.sum(h_f * t_f, axis=1, keepdims=True)
        ee += jnp.sum(t_f * t_f, axis=1, keepdims=True)
    positive[...] = as_line(he * lax.rsqrt(ee + 1e-06) * h_scale[:rows])
    first = [marks[k * NZ * rows : (k * NZ + 1) * rows] for k in range(n)]
    pick = pick_columns({4: 256.0, 5: 1.0})
    t_ids = lax.dot_general(
        jnp.concatenate(first), pick, ACROSS, preferred_element_type=F32
    )[:, :1]
    neg_logit = dots * h_scale * lax.rsqrt(lines[0][0:1] + lines[1][0:1] + 1e-06)
    kept = jnp.where(lines[0][1:2] != t_ids, jnp.exp(neg_logit), 0.0)
    total = jnp.sum(kept, axis=1, keepdims=True)
    for k in range(n):
        mass[k] = as_line(total[k * rows : (k + 1) * rows])


def final_kernel(where, keep, theirs, positive, *refs):
    masses, (hidden, loss) = refs[:-2], refs[-2:]
    u, rows = where[3], keep.shape[0]
    hidden[pl.ds(pl.multiple_of(u * rows, rows), rows), :] = keep[...]
    hidden[pl.ds(pl.multiple_of((1 - u) * rows, rows), rows), :] = theirs[...]
    total = jnp.exp(positive[...])
    for mass in masses:
        total += mass[...]
    loss[...] = jnp.log(total) - positive[...]


def call(kernel, name, outs, scratch, args, places, flops):
    space = {"s": pltpu.SMEM, "v": pltpu.VMEM, "h": pl.ANY}
    moved = sum(a.size * a.dtype.itemsize for a in args)
    return pl.pallas_call(
        kernel,
        out_shape=[jax.ShapeDtypeStruct(shape, dtype) for shape, dtype in outs],
        in_specs=[pl.BlockSpec(memory_space=space[p]) for p in places],
        out_specs=[pl.BlockSpec(memory_space=pltpu.VMEM)] * len(outs),
        scratch_shapes=scratch,
        compiler_params=pltpu.CompilerParams(vmem_limit_bytes=VMEM_LIMIT),
        cost_estimate=pl.CostEstimate(flops=flops, bytes_accessed=moved, transcendentals=0),
        name=name,
    )(*args)


def whole_parts(value, base):
    return [(value // base).astype(BF16), (value % base).astype(BF16)]


def float_parts(value):
    parts = []
    for _ in range(3):
        parts.append(lax.reduce_precision(value, 8, 7))
        value = value - parts[-1]
    return [part.astype(BF16) for part in parts]


def with_marks(rows, marks):
    marks = jnp.stack(marks, 1)
    marks = jnp.pad(marks, ((0, 0), (0, W - marks.shape[1])))
    return jnp.concatenate([rows, marks], 1)


def head_shards(
    tokens, w_proj, w_out, positions, neg_emb, neg_ids, target_emb, target_ids
):
    c, u = lax.axis_index("ctx"), lax.axis_index("tp")
    z, y, x = coords(c)
    where = jnp.stack([z, y, x, u]).astype(jnp.int32)
    model = tokens.shape[1]
    rows = tokens.shape[0] // 2
    events = rows * CHIPS
    half = model // 2
    negs = neg_emb.shape[0]
    plane = len(PLANE)

    (mine,) = call(
        mark_kernel,
        "mark",
        [((rows, model + W), BF16)],
        [],
        [where, tokens, positions.reshape(2, rows), target_ids.reshape(1, rows)],
        "svvv",
        0,
    )
    line = [mine] + [hop(mine, flip(0, 0, s)) for s in range(1, NZ)]

    to_x, to_y = flip(0, 1), flip(1, 0)
    w_rows = heads_in_plane(w_proj, y, x, mine)
    w_pieces = [
        jnp.concatenate([pick_row(w, e ^ (z & 1)) for w in w_rows]).reshape(-1, 4 * W)
        for e in range(2)
    ]

    own_ids = lax.dynamic_slice_in_dim(neg_ids, c * negs, negs, 0)
    norms = jnp.sum(jnp.square(neg_emb.astype(F32)), axis=1)
    neg = with_marks(neg_emb, float_parts(norms) + whole_parts(own_ids, 256))

    out_pair = pair_up(after(w_out[None], mine))
    low = jnp.concatenate(line[:2])
    low_x, low_y = hop(low, to_x), hop(low, to_y)
    low_xy = across(low_x, low_y)
    w_pieces, neg, out_pair, high = lax.optimization_barrier((w_pieces, neg, out_pair, line[2:]))
    high = jnp.concatenate(high)
    high_x, high_y = hop(high, to_x), hop(high, to_y)
    high_xy = across(high_x, high_y)
    tok = [low, high, low_x, high_x, low_y, high_y, *low_xy, *high_xy]
    w_mine = heads_along_z(w_pieces)
    w_mine = after(w_mine, low_xy, high_xy)
    w_theirs = [swap_cores(w) for w in w_mine]
    out_own = [out_pair, hop(after(out_pair, w_mine), flip(0, 0, 2))]
    t_rows = after(target_emb.reshape(2, rows, -1), w_theirs)
    t_keep = pick_row(t_rows, u)
    t_send = swap_cores(pick_row(t_rows, 1 - u))

    def project(pieces):
        count = sum(p.shape[0] for p in pieces)
        return call(
            proj_kernel,
            "project",
            [((count, 2 * W), BF16)] + [((count, W), BF16)] * 3,
            [
                pltpu.VMEM((count, model + W), BF16),
                pltpu.VMEM((model, 4 * W), BF16),
                pltpu.SemaphoreType.DMA((len(pieces),)),
                pltpu.SemaphoreType.DMA((8,)),
            ],
            [where, *pieces, *w_mine, *w_theirs],
            "s" + (len(pieces) + 4) * "h",
            0,
        )

    gate_query, value, key, marks = project(tok)
    key_theirs, value_theirs = swap_cores(key), swap_cores(value)
    out_pair_theirs = swap_cores(after(out_pair, value))
    (gated,) = call(
        attend_kernel,
        "attend",
        [((NZ, plane, rows, W), BF16)],
        [pltpu.VMEM((events, 2 * W), BF16)]
        + [pltpu.VMEM((events, W), BF16)] * 5
        + [pltpu.SemaphoreType.DMA((6,))],
        [gate_query, key, value, key_theirs, value_theirs, marks],
        6 * "h",
        0,
    )
    out_own, out_pair_theirs, gated = lax.optimization_barrier((out_own, out_pair_theirs, gated))
    gated = jnp.stack([gated[0]] + [hop(gated[s], flip(0, 0, s)) for s in range(1, NZ)])
    neg_pair = pair_up(after(neg, gated))
    neg_far = hop(neg_pair, flip(0, 0, 2))
    out_other = [out_pair_theirs, swap_cores(after(out_own[1], gated))]
    gated = [gated, hop(gated, to_x), hop(gated, to_y)]
    gated += across(gated[1], gated[2])
    (hidden,) = call(
        hidden_kernel,
        "hidden",
        [((plane, rows, NZ * W), BF16)],
        [
            pltpu.VMEM((plane, NZ, plane, rows, W), BF16),
            pltpu.VMEM((plane * rows, model), BF16),
            pltpu.VMEM((plane, rows, NZ * W), BF16),
            pltpu.VMEM((2, half, NZ * W), BF16),
            pltpu.SemaphoreType.DMA((29,)),
        ],
        [where, *gated, *out_own, *out_other, *tok[:7:2]],
        "s" + 13 * "h",
        2 * plane * rows * model * NZ * W,
    )
    neg_own = jnp.concatenate([neg_pair, after(neg_far, hidden, t_send)])
    neg_other = swap_cores(neg_own)
    pieces = [hidden, hop(hidden, to_x), hop(hidden, to_y)]
    pieces += across(pieces[1], pieces[2])
    h_keep, h_send, positive, mass = call(
        mass_kernel,
        "mass",
        [((rows, half), BF16)] * 2 + [((1, rows), F32), ((plane, 1, rows), F32)],
        [pltpu.VMEM((plane * rows, model), BF16)],
        [where, *pieces, neg_own, neg_other, t_keep, t_send, marks],
        "s" + 10 * "v",
        2 * plane * rows * model * NZ * negs,
    )
    masses = [mass[0]] + [hop(mass[k], flip(*PLANE[k])) for k in range(1, plane)]
    h_theirs = swap_cores(h_send)
    hidden, loss = call(
        final_kernel,
        "final",
        [((2 * rows, half), BF16), ((1, rows), F32)],
        [],
        [where, h_keep, h_theirs, positive, *masses],
        "s" + 7 * "v",
        0,
    )
    return hidden, loss.reshape(-1)


def shards(tokens, w_proj, *rest):
    n_ctx, n_tp = lax.axis_size("ctx"), lax.axis_size("tp")
    heads = w_proj.shape[2] * n_tp // HEAD_DIM
    plan = head_shards if (n_ctx, n_tp, heads) == (CHIPS, 2, CHIPS) else general_shards
    return plan(tokens, w_proj, *rest)


def solution(mesh):
    placed = (
        P("ctx", None),
        P("ctx", None, "tp"),
        P("tp", "ctx"),
        P("ctx"),
        P("ctx", "tp"),
        P(),
        P("ctx", "tp"),
        P(("ctx", "tp")),
    )
    return jax.shard_map(
        shards,
        mesh=mesh,
        in_specs=placed,
        out_specs=(P("ctx", "tp"), P(("ctx", "tp"))),
        check_vma=False,
    )
```

```python
import jax
import jax.numpy as jnp
from jax import lax
from jax.experimental import pallas as pl
from jax.experimental.pallas import tpu as pltpu
from jax.sharding import PartitionSpec as P

HEAD_DIM = 128
VMEM_LIMIT = 24 * 1024 * 1024
BF16 = jnp.bfloat16
F32 = jnp.float32


def attend_piece(q_group, q_pos, k_piece, v_piece, p_piece):
    heads = q_group.shape[1]
    width = q_group.shape[2]
    key_heads = k_piece.reshape(k_piece.shape[0], heads, width)
    value_heads = v_piece.reshape(v_piece.shape[0], heads, width)
    scores = jnp.einsum(
        "thd,khd->htk", q_group, key_heads, preferred_element_type=jnp.float32
    ) * width ** (-0.5)
    visible = p_piece[None, None, :] <= q_pos[None, :, None]
    weight = jnp.where(visible, jax.nn.silu(scores), 0.0).astype(jnp.bfloat16)
    return jnp.einsum("htk,khd->thd", weight, value_heads, preferred_element_type=jnp.float32)


def general_shards(
    tokens, w_proj, w_out, positions, neg_emb, neg_ids, target_emb, target_ids
):
    tok_rows = tokens.shape[0]
    head_cols = w_proj.shape[2]
    local_heads = head_cols // HEAD_DIM
    proj_sum = jnp.einsum(
        "td,dfh->tfh",
        tokens,
        lax.all_gather(w_proj, "ctx", axis=0, tiled=True),
        preferred_element_type=jnp.float32,
    )
    proj = jax.nn.silu(proj_sum).astype(jnp.bfloat16)
    gate = proj[:, 0].reshape(tok_rows, local_heads, HEAD_DIM)
    query = proj[:, 2].reshape(tok_rows, local_heads, HEAD_DIM)
    v_piece = lax.all_gather(proj[:, 1], "ctx", axis=0, tiled=True)
    k_piece = lax.all_gather(proj[:, 3], "ctx", axis=0, tiled=True)
    p_piece = lax.all_gather(positions, "ctx", axis=0, tiled=True)
    attn = attend_piece(query, positions, k_piece, v_piece, p_piece)
    normed = attn * lax.rsqrt(jnp.mean(attn * attn, axis=-1, keepdims=True) + 1e-06)
    gated = (normed * gate.astype(jnp.float32)).astype(jnp.bfloat16).reshape(tok_rows, head_cols)
    out_terms = jnp.dot(
        gated, lax.all_gather(w_out, "ctx", axis=1, tiled=True), preferred_element_type=jnp.float32
    )
    out_share = lax.psum_scatter(out_terms, "tp", scatter_dimension=1, tiled=True)
    feat_cols = out_share.shape[1]
    own_tokens = lax.dynamic_slice_in_dim(tokens, lax.axis_index("tp") * feat_cols, feat_cols, 1)
    hidden = (own_tokens.astype(jnp.float32) + out_share).astype(jnp.bfloat16)
    piece = lax.all_gather(neg_emb, "ctx", axis=0, tiled=True)
    panel_dots = lax.dot_general(
        hidden, piece, (((1,), (1,)), ((), ())), preferred_element_type=jnp.float32
    )
    panel_norms = jnp.sum(jnp.square(piece.astype(jnp.float32)), axis=1)
    hidden_f = hidden.astype(jnp.float32)
    target_f = target_emb.astype(jnp.float32)
    part_hh = jnp.sum(hidden_f * hidden_f, axis=1)
    part_he = jnp.sum(hidden_f * target_f, axis=1)
    part_ee = jnp.sum(target_f * target_f, axis=1)
    dots, hh_sum, he_sum, ee_sum = (
        lax.psum_scatter(panel_dots, "tp", scatter_dimension=0, tiled=True),
        lax.psum_scatter(part_hh, "tp", scatter_dimension=0, tiled=True),
        lax.psum_scatter(part_he, "tp", scatter_dimension=0, tiled=True),
        lax.psum_scatter(part_ee, "tp", scatter_dimension=0, tiled=True),
    )
    neg_sq = lax.psum(panel_norms, "tp")
    pos_logit = he_sum / jnp.sqrt(hh_sum + 1e-06) / jnp.sqrt(ee_sum + 1e-06) / 0.05
    neg_logit = dots / jnp.sqrt(hh_sum + 1e-06)[:, None] / jnp.sqrt(neg_sq + 1e-06)[None, :] / 0.05
    keep_mask = neg_ids[None, :] != target_ids[:, None]
    total_mass = jnp.exp(pos_logit) + jnp.sum(jnp.where(keep_mask, jnp.exp(neg_logit), 0.0), axis=1)
    loss = jnp.log(total_mass) - pos_logit
    return (hidden, loss)


NZ, NY, NX = 4, 2, 2
CHIPS = NZ * NY * NX
PLANE = [(by, bx) for by in range(NY) for bx in range(NX)]
SWAP = [(0, 1), (1, 0)]
W = HEAD_DIM
ACROSS = (((1,), (1,)), ((), ()))


def chip_at(z, y, x):
    return (z * NY + y) * NX + x


def coords(c):
    return c // (NY * NX), (c // NX) % NY, c % NX


def relative_chip(c, by, bx, s):
    z, y, x = coords(c)
    return chip_at(z ^ s, y ^ by, x ^ bx)


def flip(by, bx, s=0):
    return [(c, relative_chip(c, by, bx, s)) for c in range(CHIPS)]


def hop(value, perm):
    return lax.ppermute(value, "ctx", perm)


def swap_cores(value):
    return lax.ppermute(value, "tp", SWAP)


def pick_row(value, at):
    return lax.dynamic_index_in_dim(value, at, 0, keepdims=False)


def after(values, *others):
    return lax.optimization_barrier((values, others))[0]


def pair_up(own):
    return jnp.concatenate([own, hop(own, flip(0, 0, 1))])


def across(value_x, value_y):
    half = value_x.shape[0] // 2
    return [hop(value_x[:half], flip(1, 0)), hop(value_y[half:], flip(0, 1))]


def heads_in_plane(w_proj, y, x, first):
    plane = NY * NX
    heads = w_proj.reshape(-1, 4, 2, plane, W).transpose(3, 2, 0, 1, 4)
    heads = heads.reshape(plane, 2, -1, 4 * W)
    out = []
    for by, bx in PLANE:
        piece = pick_row(heads, (y ^ by) * NX + (x ^ bx))
        if (by, bx) != (0, 0):
            piece = hop(after(piece, first if len(out) < plane - 1 else out[1:]), flip(by, bx))
        out.append(piece)
    return out


def heads_along_z(pieces):
    arrived = []
    for e, piece in enumerate(pieces):
        perm = []
        for src in range(CHIPS):
            sz, sy, sx = coords(src)
            for t in range(2):
                dst = chip_at(2 * t + (e ^ (sz & 1)), sy, sx)
                perm.append((2 * src + t, 2 * dst + (sz >> 1)))
        arrived.append(lax.ppermute(piece, ("ctx", "tp"), perm))
    return arrived


def silu(v):
    return 0.5 * v * (1.0 + jnp.tanh(0.5 * v))


def run_copies(copies):
    for copy in copies:
        copy.start()
    for copy in copies:
        copy.wait()


def mark_kernel(where, tokens, positions, ids, mine):
    u = where[3]
    rows, model = mine.shape[0], tokens.shape[1]
    mine[:, :model] = tokens[pl.ds(pl.multiple_of(u * rows, rows), rows), :]
    line = lax.broadcasted_iota(jnp.int32, (rows, rows), 0)
    across = lax.broadcasted_iota(jnp.int32, (rows, rows), 1)
    lane = lax.broadcasted_iota(jnp.int32, (rows, W), 1)
    marks = jnp.zeros((rows, W), F32)
    values = (positions[pl.ds(u, 1)], positions[pl.ds(1 - u, 1)], ids[...])
    for i, (value, bits) in enumerate(zip(values, (7, 7, 8))):
        column = jnp.sum(jnp.where(line == across, value, 0), axis=1, keepdims=True)
        high = lax.shift_right_logical(column, bits)
        marks = jnp.where(lane == 2 * i, high.astype(F32), marks)
        marks = jnp.where(lane == 2 * i + 1, (column - high * 2**bits).astype(F32), marks)
    mine[:, model:] = marks.astype(BF16)


def proj_kernel(where, *refs):
    count = len(refs) - 12
    tok, w_own, w_other = refs[:count], refs[count : count + 2], refs[count + 2 : count + 4]
    gate_query, value, key, marks, x_all, w_all, tok_sem, w_sem = refs[count + 4 :]
    z, y, x, u = (where[i] for i in range(4))
    copies, base = [], 0
    for side, (at, srcs) in enumerate(((u, w_own), (1 - u, w_other))):
        for e, src in enumerate(srcs):
            size = src.shape[0] // len(PLANE)
            for j, (by, bx) in enumerate(PLANE):
                start = chip_at(2 * at + (e ^ (z & 1)), y ^ by, x ^ bx) * size
                to = w_all.at[pl.ds(pl.multiple_of(start, size), size), :]
                sem = w_sem.at[(2 * side + e) * len(PLANE) + j]
                copies.append(pltpu.make_async_copy(src.at[pl.ds(j * size, size), :], to, sem))
    for i, ref in enumerate(tok):
        rows = pl.ds(base, ref.shape[0])
        copies.append(pltpu.make_async_copy(ref, x_all.at[rows, :], tok_sem.at[i]))
        base += ref.shape[0]
    run_copies(copies)
    model = w_all.shape[0]
    total = jnp.dot(x_all[:, :model], w_all[...], preferred_element_type=F32)
    proj = silu(total).astype(BF16)
    gate_query[:, :W] = proj[:, :W]
    value[...] = proj[:, W : 2 * W]
    gate_query[:, W:] = proj[:, 2 * W : 3 * W]
    key[...] = proj[:, 3 * W :]
    marks[...] = x_all[:, model:]


def pick_columns(*weights):
    lane = lax.broadcasted_iota(jnp.int32, (8, W), 1)
    line = lax.broadcasted_iota(jnp.int32, (8, W), 0)
    pick = jnp.zeros((8, W), F32)
    for i, row in enumerate(weights):
        for at, weight in row.items():
            pick = jnp.where((line == i) & (lane == at), weight, pick)
    return pick.astype(BF16)


def attend_kernel(*refs):
    sources, gated, copied, sems = refs[:6], refs[6], refs[7:13], refs[13]
    run_copies(
        [
            pltpu.make_async_copy(src, dst, sems.at[i])
            for i, (src, dst) in enumerate(zip(sources, copied))
        ]
    )
    gate_query, key, value, key_theirs, value_theirs, marks = copied
    pick = pick_columns({0: 128.0, 1: 1.0}, {2: 128.0, 3: 1.0})
    piece = gated.shape[2]
    tile = NZ * piece
    key_pos = lax.dot_general(pick, marks[...], ACROSS, preferred_element_type=F32)
    for k in range(len(PLANE)):
        span = pl.ds(k * tile, tile)
        query = gate_query[span, W:]
        q_pos = lax.dot_general(marks[span, :], pick, ACROSS, preferred_element_type=F32)[:, :1]
        attn = jnp.zeros((tile, W), F32)
        for side, (keys, values) in enumerate(((key, value), (key_theirs, value_theirs))):
            scores = lax.dot_general(
                query, keys[...], ACROSS, preferred_element_type=F32
            ) * W ** (-0.5)
            visible = key_pos[side : side + 1] <= q_pos
            weight = jnp.where(visible, silu(scores), 0.0).astype(BF16)
            attn += jnp.dot(weight, values[...], preferred_element_type=F32)
        normed = attn * lax.rsqrt(jnp.mean(attn * attn, axis=-1, keepdims=True) + 1e-06)
        out = (normed * gate_query[span, :W].astype(F32)).astype(BF16)
        for s in range(NZ):
            gated[s, k] = out[s * piece : (s + 1) * piece]


def hidden_kernel(where, *refs):
    n = len(PLANE)
    gated, w_own, w_other, tok = refs[:5], refs[5:7], refs[7:9], refs[9:13]
    hidden, g_raw, g_all, t_all, w_all, sems = refs[13:]
    z, y, x, u = (where[i] for i in range(4))
    c = chip_at(z, y, x)
    rows = hidden.shape[1]
    half = w_all.shape[1]
    copies = [(src, g_raw.at[k]) for k, src in enumerate(gated[:3])]
    copies += [(src, g_raw.at[3, pl.ds(2 * i, 2)]) for i, src in enumerate(gated[3:])]
    for s in range(NZ):
        cols = pl.ds(s * W, W)
        for side, src in enumerate((w_own, w_other)):
            copies.append((src[s // 2].at[s % 2], w_all.at[side, :, cols]))
        block = relative_chip(c, 0, 0, s)
        from_cols = pl.ds(pl.multiple_of(block * W, W), W)
        for k in range(n):
            copies.append((tok[k].at[pl.ds(0, rows), from_cols], t_all.at[k, :, cols]))
    copies = [pltpu.make_async_copy(src, dst, sems.at[i]) for i, (src, dst) in enumerate(copies)]
    for copy in copies:
        copy.start()
    for copy in copies[:5]:
        copy.wait()
    for k, (by, bx) in enumerate(PLANE):
        for s in range(NZ):
            head = relative_chip(c, by, bx, s)
            cols = pl.ds(pl.multiple_of(head * W, W), W)
            for j in range(n):
                block = j ^ k
                g_all[block * rows : (block + 1) * rows, cols] = g_raw[k, s, j]
    for copy in copies[5:]:
        copy.wait()
    total = 0.0
    for side, at in enumerate((u, 1 - u)):
        part = g_all[:, pl.ds(pl.multiple_of(at * half, half), half)]
        total += jnp.dot(part, w_all[side], preferred_element_type=F32)
    for k in range(n):
        for s in range(NZ):
            term = total[k * rows : (k + 1) * rows, s * W : (s + 1) * W]
            cols = pl.ds(pl.multiple_of((z ^ s) * W, W), W)
            hidden[k, :, cols] = (t_all[k, :, s * W : (s + 1) * W].astype(F32) + term).astype(BF16)


def as_line(column):
    size = column.shape[0]
    line = lax.broadcasted_iota(jnp.int32, (size, size), 0)
    lane = lax.broadcasted_iota(jnp.int32, (size, size), 1)
    return jnp.sum(jnp.where(line == lane, column, 0.0), axis=0, keepdims=True)


def mass_kernel(where, *refs):
    n = len(PLANE)
    pieces, (n_own, n_other, t_keep, t_send, marks) = refs[:5], refs[5:10]
    keep, send, positive, mass, h_all = refs[10:]
    y, x, u = (where[i] for i in range(1, 4))
    rows, half = keep.shape
    for k, (by, bx) in enumerate(PLANE):
        for at in range(NZ):
            block = chip_at(at, y ^ by, x ^ bx)
            cols = pl.ds(pl.multiple_of(block * W, W), W)
            for j in range(n):
                row = (j ^ k) * rows
                ref, i = (pieces[k], j) if k < n - 1 else (pieces[k + j // 2], j % 2)
                h_all[row : row + rows, cols] = ref[i, :, at * W : (at + 1) * W]
    mine = pl.ds(pl.multiple_of(u * half, half), half)
    theirs = pl.ds(pl.multiple_of((1 - u) * half, half), half)
    keep[...] = h_all[:rows, mine]
    send[...] = h_all[:rows, theirs]
    hh, dots, lines = 0.0, 0.0, []
    pick = pick_columns({0: 1.0, 1: 1.0, 2: 1.0}, {3: 256.0, 4: 1.0})
    for part, neg in ((mine, n_own), (theirs, n_other)):
        h_part = h_all[:, part]
        h_f = h_part.astype(F32)
        hh += jnp.sum(h_f * h_f, axis=1, keepdims=True)
        dots += lax.dot_general(h_part, neg[:, :half], ACROSS, preferred_element_type=F32)
        lines.append(lax.dot_general(pick, neg[:, half:], ACROSS, preferred_element_type=F32))
    h_scale = lax.rsqrt(hh + 1e-06) * 20.0
    he = ee = 0.0
    for h_ref, ref in ((keep, t_keep), (send, t_send)):
        h_f, t_f = h_ref[...].astype(F32), ref[...].astype(F32)
        he += jnp.sum(h_f * t_f, axis=1, keepdims=True)
        ee += jnp.sum(t_f * t_f, axis=1, keepdims=True)
    positive[...] = as_line(he * lax.rsqrt(ee + 1e-06) * h_scale[:rows])
    first = [marks[k * NZ * rows : (k * NZ + 1) * rows] for k in range(n)]
    pick = pick_columns({4: 256.0, 5: 1.0})
    t_ids = lax.dot_general(
        jnp.concatenate(first), pick, ACROSS, preferred_element_type=F32
    )[:, :1]
    neg_logit = dots * h_scale * lax.rsqrt(lines[0][0:1] + lines[1][0:1] + 1e-06)
    kept = jnp.where(lines[0][1:2] != t_ids, jnp.exp(neg_logit), 0.0)
    total = jnp.sum(kept, axis=1, keepdims=True)
    for k in range(n):
        mass[k] = as_line(total[k * rows : (k + 1) * rows])


def final_kernel(where, keep, theirs, positive, *refs):
    masses, (hidden, loss) = refs[:-2], refs[-2:]
    u, rows = where[3], keep.shape[0]
    hidden[pl.ds(pl.multiple_of(u * rows, rows), rows), :] = keep[...]
    hidden[pl.ds(pl.multiple_of((1 - u) * rows, rows), rows), :] = theirs[...]
    total = jnp.exp(positive[...])
    for mass in masses:
        total += mass[...]
    loss[...] = jnp.log(total) - positive[...]


def call(kernel, name, outs, scratch, args, places, flops):
    space = {"s": pltpu.SMEM, "v": pltpu.VMEM, "h": pl.ANY}
    moved = sum(a.size * a.dtype.itemsize for a in args)
    return pl.pallas_call(
        kernel,
        out_shape=[jax.ShapeDtypeStruct(shape, dtype) for shape, dtype in outs],
        in_specs=[pl.BlockSpec(memory_space=space[p]) for p in places],
        out_specs=[pl.BlockSpec(memory_space=pltpu.VMEM)] * len(outs),
        scratch_shapes=scratch,
        compiler_params=pltpu.CompilerParams(vmem_limit_bytes=VMEM_LIMIT),
        cost_estimate=pl.CostEstimate(flops=flops, bytes_accessed=moved, transcendentals=0),
        name=name,
    )(*args)


def whole_parts(value, base):
    return [(value // base).astype(BF16), (value % base).astype(BF16)]


def float_parts(value):
    parts = []
    for _ in range(3):
        parts.append(lax.reduce_precision(value, 8, 7))
        value = value - parts[-1]
    return [part.astype(BF16) for part in parts]


def with_marks(rows, marks):
    marks = jnp.stack(marks, 1)
    marks = jnp.pad(marks, ((0, 0), (0, W - marks.shape[1])))
    return jnp.concatenate([rows, marks], 1)


def head_shards(
    tokens, w_proj, w_out, positions, neg_emb, neg_ids, target_emb, target_ids
):
    c, u = lax.axis_index("ctx"), lax.axis_index("tp")
    z, y, x = coords(c)
    where = jnp.stack([z, y, x, u]).astype(jnp.int32)
    model = tokens.shape[1]
    rows = tokens.shape[0] // 2
    events = rows * CHIPS
    half = model // 2
    negs = neg_emb.shape[0]
    plane = len(PLANE)

    (mine,) = call(
        mark_kernel,
        "mark",
        [((rows, model + W), BF16)],
        [],
        [where, tokens, positions.reshape(2, rows), target_ids.reshape(1, rows)],
        "svvv",
        0,
    )
    line = [mine] + [hop(mine, flip(0, 0, s)) for s in range(1, NZ)]

    to_x, to_y = flip(0, 1), flip(1, 0)
    w_rows = heads_in_plane(w_proj, y, x, mine)
    w_pieces = [
        jnp.concatenate([pick_row(w, e ^ (z & 1)) for w in w_rows]).reshape(-1, 4 * W)
        for e in range(2)
    ]

    own_ids = lax.dynamic_slice_in_dim(neg_ids, c * negs, negs, 0)
    norms = jnp.sum(jnp.square(neg_emb.astype(F32)), axis=1)
    neg = with_marks(neg_emb, float_parts(norms) + whole_parts(own_ids, 256))

    out_pair = pair_up(after(w_out[None], w_rows[1:3]))
    w_pieces, neg, out_pair, line = lax.optimization_barrier((w_pieces, neg, out_pair, line))
    near = jnp.concatenate(line)
    near_x, near_y = hop(near, to_x), hop(near, to_y)
    tok = [near, near_x, near_y, *across(near_x, near_y)]
    w_mine = heads_along_z(w_pieces)
    w_theirs = [swap_cores(w) for w in w_mine]
    out_own = [out_pair, hop(after(out_pair, w_mine), flip(0, 0, 2))]
    t_rows = after(target_emb.reshape(2, rows, -1), w_theirs)
    t_keep = pick_row(t_rows, u)
    t_send = swap_cores(pick_row(t_rows, 1 - u))

    def project(pieces):
        count = sum(p.shape[0] for p in pieces)
        return call(
            proj_kernel,
            "project",
            [((count, 2 * W), BF16)] + [((count, W), BF16)] * 3,
            [
                pltpu.VMEM((count, model + W), BF16),
                pltpu.VMEM((model, 4 * W), BF16),
                pltpu.SemaphoreType.DMA((len(pieces),)),
                pltpu.SemaphoreType.DMA((16,)),
            ],
            [where, *pieces, *w_mine, *w_theirs],
            "s" + (len(pieces) + 4) * "h",
            0,
        )

    gate_query, value, key, marks = project(tok)
    key_theirs, value_theirs = swap_cores(key), swap_cores(value)
    out_pair_theirs = swap_cores(after(out_pair, value))
    (gated,) = call(
        attend_kernel,
        "attend",
        [((NZ, plane, rows, W), BF16)],
        [pltpu.VMEM((events, 2 * W), BF16)]
        + [pltpu.VMEM((events, W), BF16)] * 5
        + [pltpu.SemaphoreType.DMA((6,))],
        [gate_query, key, value, key_theirs, value_theirs, marks],
        6 * "h",
        0,
    )
    out_own, out_pair_theirs, gated = lax.optimization_barrier((out_own, out_pair_theirs, gated))
    gated = jnp.stack([gated[0]] + [hop(gated[s], flip(0, 0, s)) for s in range(1, NZ)])
    neg_pair = pair_up(after(neg, gated))
    neg_far = hop(neg_pair, flip(0, 0, 2))
    out_other = [out_pair_theirs, swap_cores(after(out_own[1], gated))]
    gated = [gated, hop(gated, to_x), hop(gated, to_y)]
    gated += across(gated[1], gated[2])
    (hidden,) = call(
        hidden_kernel,
        "hidden",
        [((plane, rows, NZ * W), BF16)],
        [
            pltpu.VMEM((plane, NZ, plane, rows, W), BF16),
            pltpu.VMEM((plane * rows, model), BF16),
            pltpu.VMEM((plane, rows, NZ * W), BF16),
            pltpu.VMEM((2, half, NZ * W), BF16),
            pltpu.SemaphoreType.DMA((29,)),
        ],
        [where, *gated, *out_own, *out_other, *tok[:4]],
        "s" + 13 * "h",
        2 * plane * rows * model * NZ * W,
    )
    neg_own = jnp.concatenate([neg_pair, after(neg_far, hidden, t_send)])
    neg_other = swap_cores(neg_own)
    pieces = [hidden, hop(hidden, to_x), hop(hidden, to_y)]
    pieces += across(pieces[1], pieces[2])
    h_keep, h_send, positive, mass = call(
        mass_kernel,
        "mass",
        [((rows, half), BF16)] * 2 + [((1, rows), F32), ((plane, 1, rows), F32)],
        [pltpu.VMEM((plane * rows, model), BF16)],
        [where, *pieces, neg_own, neg_other, t_keep, t_send, marks],
        "s" + 10 * "v",
        2 * plane * rows * model * NZ * negs,
    )
    masses = [mass[0]] + [hop(mass[k], flip(*PLANE[k])) for k in range(1, plane)]
    h_theirs = swap_cores(h_send)
    hidden, loss = call(
        final_kernel,
        "final",
        [((2 * rows, half), BF16), ((1, rows), F32)],
        [],
        [where, h_keep, h_theirs, positive, *masses],
        "s" + 7 * "v",
        0,
    )
    return hidden, loss.reshape(-1)


def shards(tokens, w_proj, *rest):
    n_ctx, n_tp = lax.axis_size("ctx"), lax.axis_size("tp")
    heads = w_proj.shape[2] * n_tp // HEAD_DIM
    plan = head_shards if (n_ctx, n_tp, heads) == (CHIPS, 2, CHIPS) else general_shards
    return plan(tokens, w_proj, *rest)


def solution(mesh):
    placed = (
        P("ctx", None),
        P("ctx", None, "tp"),
        P("tp", "ctx"),
        P("ctx"),
        P("ctx", "tp"),
        P(),
        P("ctx", "tp"),
        P(("ctx", "tp")),
    )
    return jax.shard_map(
        shards,
        mesh=mesh,
        in_specs=placed,
        out_specs=(P("ctx", "tp"), P(("ctx", "tp"))),
        check_vma=False,
    )
```

```python
import jax
import jax.numpy as jnp
from jax import lax
from jax.experimental import pallas as pl
from jax.experimental.pallas import tpu as pltpu
from jax.sharding import PartitionSpec as P

HEAD_DIM = 128
VMEM_LIMIT = 14 * 1024 * 1024
BF16 = jnp.bfloat16
F32 = jnp.float32


def attend_piece(q_group, q_pos, k_piece, v_piece, p_piece):
    heads = q_group.shape[1]
    width = q_group.shape[2]
    key_heads = k_piece.reshape(k_piece.shape[0], heads, width)
    value_heads = v_piece.reshape(v_piece.shape[0], heads, width)
    scores = jnp.einsum(
        "thd,khd->htk", q_group, key_heads, preferred_element_type=jnp.float32
    ) * width ** (-0.5)
    visible = p_piece[None, None, :] <= q_pos[None, :, None]
    weight = jnp.where(visible, jax.nn.silu(scores), 0.0).astype(jnp.bfloat16)
    return jnp.einsum("htk,khd->thd", weight, value_heads, preferred_element_type=jnp.float32)


def general_shards(
    tokens, w_proj, w_out, positions, neg_emb, neg_ids, target_emb, target_ids
):
    tok_rows = tokens.shape[0]
    head_cols = w_proj.shape[2]
    local_heads = head_cols // HEAD_DIM
    proj_sum = jnp.einsum(
        "td,dfh->tfh",
        tokens,
        lax.all_gather(w_proj, "ctx", axis=0, tiled=True),
        preferred_element_type=jnp.float32,
    )
    proj = jax.nn.silu(proj_sum).astype(jnp.bfloat16)
    gate = proj[:, 0].reshape(tok_rows, local_heads, HEAD_DIM)
    query = proj[:, 2].reshape(tok_rows, local_heads, HEAD_DIM)
    v_piece = lax.all_gather(proj[:, 1], "ctx", axis=0, tiled=True)
    k_piece = lax.all_gather(proj[:, 3], "ctx", axis=0, tiled=True)
    p_piece = lax.all_gather(positions, "ctx", axis=0, tiled=True)
    attn = attend_piece(query, positions, k_piece, v_piece, p_piece)
    normed = attn * lax.rsqrt(jnp.mean(attn * attn, axis=-1, keepdims=True) + 1e-06)
    gated = (normed * gate.astype(jnp.float32)).astype(jnp.bfloat16).reshape(tok_rows, head_cols)
    out_terms = jnp.dot(
        gated, lax.all_gather(w_out, "ctx", axis=1, tiled=True), preferred_element_type=jnp.float32
    )
    out_share = lax.psum_scatter(out_terms, "tp", scatter_dimension=1, tiled=True)
    feat_cols = out_share.shape[1]
    own_tokens = lax.dynamic_slice_in_dim(tokens, lax.axis_index("tp") * feat_cols, feat_cols, 1)
    hidden = (own_tokens.astype(jnp.float32) + out_share).astype(jnp.bfloat16)
    piece = lax.all_gather(neg_emb, "ctx", axis=0, tiled=True)
    panel_dots = lax.dot_general(
        hidden, piece, (((1,), (1,)), ((), ())), preferred_element_type=jnp.float32
    )
    panel_norms = jnp.sum(jnp.square(piece.astype(jnp.float32)), axis=1)
    hidden_f = hidden.astype(jnp.float32)
    target_f = target_emb.astype(jnp.float32)
    part_hh = jnp.sum(hidden_f * hidden_f, axis=1)
    part_he = jnp.sum(hidden_f * target_f, axis=1)
    part_ee = jnp.sum(target_f * target_f, axis=1)
    dots, hh_sum, he_sum, ee_sum = (
        lax.psum_scatter(panel_dots, "tp", scatter_dimension=0, tiled=True),
        lax.psum_scatter(part_hh, "tp", scatter_dimension=0, tiled=True),
        lax.psum_scatter(part_he, "tp", scatter_dimension=0, tiled=True),
        lax.psum_scatter(part_ee, "tp", scatter_dimension=0, tiled=True),
    )
    neg_sq = lax.psum(panel_norms, "tp")
    pos_logit = he_sum / jnp.sqrt(hh_sum + 1e-06) / jnp.sqrt(ee_sum + 1e-06) / 0.05
    neg_logit = dots / jnp.sqrt(hh_sum + 1e-06)[:, None] / jnp.sqrt(neg_sq + 1e-06)[None, :] / 0.05
    keep_mask = neg_ids[None, :] != target_ids[:, None]
    total_mass = jnp.exp(pos_logit) + jnp.sum(jnp.where(keep_mask, jnp.exp(neg_logit), 0.0), axis=1)
    loss = jnp.log(total_mass) - pos_logit
    return (hidden, loss)


NZ, NY, NX = 4, 2, 2
CHIPS = NZ * NY * NX
PLANE = [(by, bx) for by in range(NY) for bx in range(NX)]
SWAP = [(0, 1), (1, 0)]
W = HEAD_DIM
ACROSS = (((1,), (1,)), ((), ()))


def chip_at(z, y, x):
    return (z * NY + y) * NX + x


def coords(c):
    return c // (NY * NX), (c // NX) % NY, c % NX


def relative_chip(c, by, bx, s):
    z, y, x = coords(c)
    return chip_at(z ^ s, y ^ by, x ^ bx)


def flip(by, bx, s=0):
    return [(c, relative_chip(c, by, bx, s)) for c in range(CHIPS)]


def hop(value, perm):
    return lax.ppermute(value, "ctx", perm)


def swap_cores(value):
    return lax.ppermute(value, "tp", SWAP)


def pick_row(value, at):
    return lax.dynamic_index_in_dim(value, at, 0, keepdims=False)


def after(values, *others):
    return lax.optimization_barrier((values, others))[0]


def pair_up(own):
    return jnp.concatenate([own, hop(own, flip(0, 0, 1))])


def across(value_x, value_y):
    half = value_x.shape[0] // 2
    return [hop(value_x[:half], flip(1, 0)), hop(value_y[half:], flip(0, 1))]


def heads_in_plane(w_proj, y, x, first):
    plane = NY * NX
    heads = w_proj.reshape(-1, 4, 2, plane, W).transpose(3, 2, 0, 1, 4)
    heads = heads.reshape(plane, 2, -1, 4 * W)
    out = []
    for by, bx in PLANE:
        piece = pick_row(heads, (y ^ by) * NX + (x ^ bx))
        if (by, bx) != (0, 0):
            piece = hop(after(piece, first if len(out) < plane - 1 else out[1:]), flip(by, bx))
        out.append(piece)
    return out


def heads_along_z(pieces):
    arrived = []
    for e, piece in enumerate(pieces):
        perm = []
        for src in range(CHIPS):
            sz, sy, sx = coords(src)
            for t in range(2):
                dst = chip_at(2 * t + (e ^ (sz & 1)), sy, sx)
                perm.append((2 * src + t, 2 * dst + (sz >> 1)))
        arrived.append(lax.ppermute(piece, ("ctx", "tp"), perm))
    return arrived


def silu(v):
    return 0.5 * v * (1.0 + jnp.tanh(0.5 * v))


def run_copies(copies):
    for copy in copies:
        copy.start()
    for copy in copies:
        copy.wait()


def mark_kernel(where, tokens, positions, ids, mine, events, sem):
    u = where[3]
    rows, model = events.shape
    own = tokens.at[pl.ds(pl.multiple_of(u * rows, rows), rows), :]
    copy = pltpu.make_async_copy(own, events, sem)
    copy.start()
    lane = lax.broadcasted_iota(jnp.int32, (rows, W), 1)
    marks = jnp.zeros((rows, W), F32)
    values = ((positions, u * rows, 7), (positions, (1 - u) * rows, 7), (ids, 0, 8))
    for i, (ref, first, bits) in enumerate(values):
        line = lax.broadcasted_iota(jnp.int32, (rows, ref.shape[1]), 0)
        across = lax.broadcasted_iota(jnp.int32, (rows, ref.shape[1]), 1)
        picked = jnp.where(across == line + first, ref[...], 0)
        column = jnp.sum(picked, axis=1, keepdims=True)
        high = lax.shift_right_logical(column, bits)
        marks = jnp.where(lane == 2 * i, high.astype(F32), marks)
        marks = jnp.where(lane == 2 * i + 1, (column - high * 2**bits).astype(F32), marks)
    mine[:, model:] = marks.astype(BF16)
    copy.wait()
    mine[:, :model] = events[...]


def proj_kernel(where, *refs):
    count = len(refs) - 11
    tok, w_own, w_other = refs[:count], refs[count : count + 2], refs[count + 2 : count + 4]
    gate_query, value, key, marks, x_all, w_all, tok_sem = refs[count + 4 :]
    z, y, x, u = (where[i] for i in range(4))
    copies, base = [], 0
    for i, ref in enumerate(tok):
        rows = pl.ds(base, ref.shape[0])
        copies.append(pltpu.make_async_copy(ref, x_all.at[rows, :], tok_sem.at[i]))
        base += ref.shape[0]
    for copy in copies:
        copy.start()
    for at, srcs in ((u, w_own), (1 - u, w_other)):
        for e, src in enumerate(srcs):
            size = src.shape[0] // len(PLANE)
            for j, (by, bx) in enumerate(PLANE):
                start = chip_at(2 * at + (e ^ (z & 1)), y ^ by, x ^ bx) * size
                part = src[j * size : (j + 1) * size, :]
                w_all[pl.ds(pl.multiple_of(start, size), size), :] = part
    for copy in copies:
        copy.wait()
    model = w_all.shape[0]
    total = jnp.dot(x_all[:, :model], w_all[...], preferred_element_type=F32)
    proj = silu(total).astype(BF16)
    gate_query[:, :W] = proj[:, :W]
    value[...] = proj[:, W : 2 * W]
    gate_query[:, W:] = proj[:, 2 * W : 3 * W]
    key[...] = proj[:, 3 * W :]
    marks[...] = x_all[:, model:]


def pick_columns(*weights):
    lane = lax.broadcasted_iota(jnp.int32, (8, W), 1)
    line = lax.broadcasted_iota(jnp.int32, (8, W), 0)
    pick = jnp.zeros((8, W), F32)
    for i, row in enumerate(weights):
        for at, weight in row.items():
            pick = jnp.where((line == i) & (lane == at), weight, pick)
    return pick.astype(BF16)


def attend_kernel(*refs):
    sources, gated, copied, sems = refs[:6], refs[6], refs[7:13], refs[13]
    run_copies(
        [
            pltpu.make_async_copy(src, dst, sems.at[i])
            for i, (src, dst) in enumerate(zip(sources, copied))
        ]
    )
    gate_query, key, value, key_theirs, value_theirs, marks = copied
    pick = pick_columns({0: 128.0, 1: 1.0}, {2: 128.0, 3: 1.0})
    piece = gated.shape[2]
    tile = NZ * piece
    key_pos = lax.dot_general(pick, marks[...], ACROSS, preferred_element_type=F32)
    for k in range(len(PLANE)):
        span = pl.ds(k * tile, tile)
        query = gate_query[span, W:]
        q_pos = lax.dot_general(marks[span, :], pick, ACROSS, preferred_element_type=F32)[:, :1]
        attn = jnp.zeros((tile, W), F32)
        for side, (keys, values) in enumerate(((key, value), (key_theirs, value_theirs))):
            scores = lax.dot_general(
                query, keys[...], ACROSS, preferred_element_type=F32
            ) * W ** (-0.5)
            visible = key_pos[side : side + 1] <= q_pos
            weight = jnp.where(visible, silu(scores), 0.0).astype(BF16)
            attn += jnp.dot(weight, values[...], preferred_element_type=F32)
        normed = attn * lax.rsqrt(jnp.mean(attn * attn, axis=-1, keepdims=True) + 1e-06)
        out = (normed * gate_query[span, :W].astype(F32)).astype(BF16)
        for s in range(NZ):
            gated[s, k] = out[s * piece : (s + 1) * piece]


def hidden_kernel(where, *refs):
    n = len(PLANE)
    gated, w_own, w_other, tok = refs[:5], refs[5:7], refs[7:9], refs[9:13]
    hidden, g_raw, g_all, t_all, w_all, sems = refs[13:]
    z, y, x, u = (where[i] for i in range(4))
    c = chip_at(z, y, x)
    rows = hidden.shape[1]
    half = w_all.shape[1]
    copies = [(src, g_raw.at[k]) for k, src in enumerate(gated[:3])]
    copies += [(src, g_raw.at[3, pl.ds(2 * i, 2)]) for i, src in enumerate(gated[3:])]
    for s in range(NZ):
        cols = pl.ds(s * W, W)
        for side, src in enumerate((w_own, w_other)):
            copies.append((src[s // 2].at[s % 2], w_all.at[side, :, cols]))
        block = relative_chip(c, 0, 0, s)
        from_cols = pl.ds(pl.multiple_of(block * W, W), W)
        for k in range(n):
            copies.append((tok[k].at[pl.ds(0, rows), from_cols], t_all.at[k, :, cols]))
    copies = [pltpu.make_async_copy(src, dst, sems.at[i]) for i, (src, dst) in enumerate(copies)]
    for copy in copies:
        copy.start()
    for copy in copies[:5]:
        copy.wait()
    for k, (by, bx) in enumerate(PLANE):
        for s in range(NZ):
            head = relative_chip(c, by, bx, s)
            cols = pl.ds(pl.multiple_of(head * W, W), W)
            for j in range(n):
                block = j ^ k
                g_all[block * rows : (block + 1) * rows, cols] = g_raw[k, s, j]
    for copy in copies[5:]:
        copy.wait()
    total = 0.0
    for side, at in enumerate((u, 1 - u)):
        part = g_all[:, pl.ds(pl.multiple_of(at * half, half), half)]
        total += jnp.dot(part, w_all[side], preferred_element_type=F32)
    for k in range(n):
        for s in range(NZ):
            term = total[k * rows : (k + 1) * rows, s * W : (s + 1) * W]
            cols = pl.ds(pl.multiple_of((z ^ s) * W, W), W)
            hidden[k, :, cols] = (t_all[k, :, s * W : (s + 1) * W].astype(F32) + term).astype(BF16)


def as_line(column):
    size = column.shape[0]
    line = lax.broadcasted_iota(jnp.int32, (size, size), 0)
    lane = lax.broadcasted_iota(jnp.int32, (size, size), 1)
    return jnp.sum(jnp.where(line == lane, column, 0.0), axis=0, keepdims=True)


def mass_kernel(where, *refs):
    n = len(PLANE)
    pieces, (n_own, n_other, t_keep, t_send, marks) = refs[:5], refs[5:10]
    keep, send, positive, mass, h_all = refs[10:]
    y, x, u = (where[i] for i in range(1, 4))
    rows, half = keep.shape
    for k, (by, bx) in enumerate(PLANE):
        for at in range(NZ):
            block = chip_at(at, y ^ by, x ^ bx)
            cols = pl.ds(pl.multiple_of(block * W, W), W)
            for j in range(n):
                row = (j ^ k) * rows
                ref, i = (pieces[k], j) if k < n - 1 else (pieces[k + j // 2], j % 2)
                h_all[row : row + rows, cols] = ref[i, :, at * W : (at + 1) * W]
    mine = pl.ds(pl.multiple_of(u * half, half), half)
    theirs = pl.ds(pl.multiple_of((1 - u) * half, half), half)
    keep[...] = h_all[:rows, mine]
    send[...] = h_all[:rows, theirs]
    hh, dots, lines = 0.0, 0.0, []
    pick = pick_columns({0: 1.0, 1: 1.0, 2: 1.0}, {3: 256.0, 4: 1.0})
    for part, neg in ((mine, n_own), (theirs, n_other)):
        h_part = h_all[:, part]
        h_f = h_part.astype(F32)
        hh += jnp.sum(h_f * h_f, axis=1, keepdims=True)
        dots += lax.dot_general(h_part, neg[:, :half], ACROSS, preferred_element_type=F32)
        lines.append(lax.dot_general(pick, neg[:, half:], ACROSS, preferred_element_type=F32))
    h_scale = lax.rsqrt(hh + 1e-06) * 20.0
    he = ee = 0.0
    for h_ref, ref in ((keep, t_keep), (send, t_send)):
        h_f, t_f = h_ref[...].astype(F32), ref[...].astype(F32)
        he += jnp.sum(h_f * t_f, axis=1, keepdims=True)
        ee += jnp.sum(t_f * t_f, axis=1, keepdims=True)
    positive[...] = as_line(he * lax.rsqrt(ee + 1e-06) * h_scale[:rows])
    first = [marks[k * NZ * rows : (k * NZ + 1) * rows] for k in range(n)]
    pick = pick_columns({4: 256.0, 5: 1.0})
    t_ids = lax.dot_general(
        jnp.concatenate(first), pick, ACROSS, preferred_element_type=F32
    )[:, :1]
    neg_logit = dots * h_scale * lax.rsqrt(lines[0][0:1] + lines[1][0:1] + 1e-06)
    kept = jnp.where(lines[0][1:2] != t_ids, jnp.exp(neg_logit), 0.0)
    total = jnp.sum(kept, axis=1, keepdims=True)
    for k in range(n):
        mass[k] = as_line(total[k * rows : (k + 1) * rows])


def final_kernel(where, keep, theirs, positive, *refs):
    masses, (hidden, loss) = refs[:-2], refs[-2:]
    u, rows = where[3], keep.shape[0]
    hidden[pl.ds(pl.multiple_of(u * rows, rows), rows), :] = keep[...]
    hidden[pl.ds(pl.multiple_of((1 - u) * rows, rows), rows), :] = theirs[...]
    total = jnp.exp(positive[...])
    for mass in masses:
        total += mass[...]
    loss[...] = jnp.log(total) - positive[...]


def call(kernel, name, outs, scratch, args, places, flops):
    space = {"s": pltpu.SMEM, "v": pltpu.VMEM, "h": pl.ANY}
    moved = sum(a.size * a.dtype.itemsize for a in args)
    return pl.pallas_call(
        kernel,
        out_shape=[jax.ShapeDtypeStruct(shape, dtype) for shape, dtype in outs],
        in_specs=[pl.BlockSpec(memory_space=space[p]) for p in places],
        out_specs=[pl.BlockSpec(memory_space=pltpu.VMEM)] * len(outs),
        scratch_shapes=scratch,
        compiler_params=pltpu.CompilerParams(vmem_limit_bytes=VMEM_LIMIT),
        cost_estimate=pl.CostEstimate(flops=flops, bytes_accessed=moved, transcendentals=0),
        name=name,
    )(*args)


def whole_parts(value, base):
    return [(value // base).astype(BF16), (value % base).astype(BF16)]


def float_parts(value):
    parts = []
    for _ in range(3):
        parts.append(lax.reduce_precision(value, 8, 7))
        value = value - parts[-1]
    return [part.astype(BF16) for part in parts]


def with_marks(rows, marks):
    marks = jnp.stack(marks, 1)
    marks = jnp.pad(marks, ((0, 0), (0, W - marks.shape[1])))
    return jnp.concatenate([rows, marks], 1)


def head_shards(
    tokens, w_proj, w_out, positions, neg_emb, neg_ids, target_emb, target_ids
):
    c, u = lax.axis_index("ctx"), lax.axis_index("tp")
    z, y, x = coords(c)
    where = jnp.stack([z, y, x, u]).astype(jnp.int32)
    model = tokens.shape[1]
    rows = tokens.shape[0] // 2
    events = rows * CHIPS
    half = model // 2
    negs = neg_emb.shape[0]
    plane = len(PLANE)

    (mine,) = call(
        mark_kernel,
        "mark",
        [((rows, model + W), BF16)],
        [pltpu.VMEM((rows, model), BF16), pltpu.SemaphoreType.DMA],
        [where, tokens, positions.reshape(1, 2 * rows), target_ids.reshape(1, rows)],
        "shvv",
        0,
    )
    line = [mine] + [hop(mine, flip(0, 0, s)) for s in range(1, NZ)]

    to_x, to_y = flip(0, 1), flip(1, 0)
    w_rows = heads_in_plane(w_proj, y, x, mine)
    w_pieces = [
        jnp.concatenate([pick_row(w, e ^ (z & 1)) for w in w_rows]).reshape(-1, 4 * W)
        for e in range(2)
    ]

    own_ids = lax.dynamic_slice_in_dim(neg_ids, c * negs, negs, 0)
    norms = jnp.sum(jnp.square(neg_emb.astype(F32)), axis=1)
    neg = with_marks(neg_emb, float_parts(norms) + whole_parts(own_ids, 256))

    out_pair = pair_up(after(w_out[None], w_rows[1:3]))
    t_rows = target_emb.reshape(2, rows, -1)
    t_keep, t_mine = pick_row(t_rows, u), pick_row(t_rows, 1 - u)
    early = (w_pieces, neg, out_pair, t_keep, t_mine, line)
    w_pieces, neg, out_pair, t_keep, t_mine, line = lax.optimization_barrier(early)
    near = jnp.concatenate(line)
    near_x, near_y = hop(near, to_x), hop(near, to_y)
    tok = [near, near_x, near_y, *across(near_x, near_y)]
    w_mine = heads_along_z(w_pieces)
    w_theirs = [swap_cores(w) for w in w_mine]
    out_own = [out_pair, hop(after(out_pair, w_mine), flip(0, 0, 2))]
    t_send = swap_cores(after(t_mine, w_theirs))

    def project(pieces):
        count = sum(p.shape[0] for p in pieces)
        return call(
            proj_kernel,
            "project",
            [((count, 2 * W), BF16)] + [((count, W), BF16)] * 3,
            [
                pltpu.VMEM((count, model + W), BF16),
                pltpu.VMEM((model, 4 * W), BF16),
                pltpu.SemaphoreType.DMA((len(pieces),)),
            ],
            [where, *pieces, *w_mine, *w_theirs],
            "s" + len(pieces) * "h" + 4 * "v",
            0,
        )

    gate_query, value, key, marks = project(tok)
    key_theirs, value_theirs = swap_cores(key), swap_cores(value)
    out_pair_theirs = swap_cores(after(out_pair, value))
    (gated,) = call(
        attend_kernel,
        "attend",
        [((NZ, plane, rows, W), BF16)],
        [pltpu.VMEM((events, 2 * W), BF16)]
        + [pltpu.VMEM((events, W), BF16)] * 5
        + [pltpu.SemaphoreType.DMA((6,))],
        [gate_query, key, value, key_theirs, value_theirs, marks],
        6 * "h",
        0,
    )
    out_own, out_pair_theirs, gated = lax.optimization_barrier((out_own, out_pair_theirs, gated))
    gated = jnp.stack([gated[0]] + [hop(gated[s], flip(0, 0, s)) for s in range(1, NZ)])
    neg_pair = pair_up(after(neg, gated))
    neg_far = hop(neg_pair, flip(0, 0, 2))
    out_other = [out_pair_theirs, swap_cores(after(out_own[1], gated))]
    gated = [gated, hop(gated, to_x), hop(gated, to_y)]
    gated += across(gated[1], gated[2])
    (hidden,) = call(
        hidden_kernel,
        "hidden",
        [((plane, rows, NZ * W), BF16)],
        [
            pltpu.VMEM((plane, NZ, plane, rows, W), BF16),
            pltpu.VMEM((plane * rows, model), BF16),
            pltpu.VMEM((plane, rows, NZ * W), BF16),
            pltpu.VMEM((2, half, NZ * W), BF16),
            pltpu.SemaphoreType.DMA((29,)),
        ],
        [where, *gated, *out_own, *out_other, *tok[:4]],
        "s" + 13 * "h",
        2 * plane * rows * model * NZ * W,
    )
    pieces = [hidden, hop(hidden, to_x), hop(hidden, to_y)]
    neg_own = jnp.concatenate([neg_pair, after(neg_far, pieces, t_send)])
    neg_other = swap_cores(neg_own)
    pieces += across(pieces[1], pieces[2])
    h_keep, h_send, positive, mass = call(
        mass_kernel,
        "mass",
        [((rows, half), BF16)] * 2 + [((1, rows), F32), ((plane, 1, rows), F32)],
        [pltpu.VMEM((plane * rows, model), BF16)],
        [where, *pieces, neg_own, neg_other, t_keep, t_send, marks],
        "s" + 10 * "v",
        2 * plane * rows * model * NZ * negs,
    )
    masses = [mass[0]] + [hop(mass[k], flip(*PLANE[k])) for k in range(1, plane)]
    h_theirs = swap_cores(h_send)
    hidden, loss = call(
        final_kernel,
        "final",
        [((2 * rows, half), BF16), ((1, rows), F32)],
        [],
        [where, h_keep, h_theirs, positive, *masses],
        "s" + 7 * "v",
        0,
    )
    return hidden, loss.reshape(-1)


def shards(tokens, w_proj, *rest):
    n_ctx, n_tp = lax.axis_size("ctx"), lax.axis_size("tp")
    heads = w_proj.shape[2] * n_tp // HEAD_DIM
    plan = head_shards if (n_ctx, n_tp, heads) == (CHIPS, 2, CHIPS) else general_shards
    return plan(tokens, w_proj, *rest)


def solution(mesh):
    placed = (
        P("ctx", None),
        P("ctx", None, "tp"),
        P("tp", "ctx"),
        P("ctx"),
        P("ctx", "tp"),
        P(),
        P("ctx", "tp"),
        P(("ctx", "tp")),
    )
    return jax.shard_map(
        shards,
        mesh=mesh,
        in_specs=placed,
        out_specs=(P("ctx", "tp"), P(("ctx", "tp"))),
        check_vma=False,
    )
```

```python
import jax
import jax.numpy as jnp
from jax import lax
from jax.experimental import pallas as pl
from jax.experimental.pallas import tpu as pltpu
from jax.sharding import PartitionSpec as P

HEAD_DIM = 128
VMEM_LIMIT = 14 * 1024 * 1024
BF16 = jnp.bfloat16
F32 = jnp.float32


def attend_piece(q_group, q_pos, k_piece, v_piece, p_piece):
    heads = q_group.shape[1]
    width = q_group.shape[2]
    key_heads = k_piece.reshape(k_piece.shape[0], heads, width)
    value_heads = v_piece.reshape(v_piece.shape[0], heads, width)
    scores = jnp.einsum(
        "thd,khd->htk", q_group, key_heads, preferred_element_type=jnp.float32
    ) * width ** (-0.5)
    visible = p_piece[None, None, :] <= q_pos[None, :, None]
    weight = jnp.where(visible, jax.nn.silu(scores), 0.0).astype(jnp.bfloat16)
    return jnp.einsum("htk,khd->thd", weight, value_heads, preferred_element_type=jnp.float32)


def general_shards(
    tokens, w_proj, w_out, positions, neg_emb, neg_ids, target_emb, target_ids
):
    tok_rows = tokens.shape[0]
    head_cols = w_proj.shape[2]
    local_heads = head_cols // HEAD_DIM
    proj_sum = jnp.einsum(
        "td,dfh->tfh",
        tokens,
        lax.all_gather(w_proj, "ctx", axis=0, tiled=True),
        preferred_element_type=jnp.float32,
    )
    proj = jax.nn.silu(proj_sum).astype(jnp.bfloat16)
    gate = proj[:, 0].reshape(tok_rows, local_heads, HEAD_DIM)
    query = proj[:, 2].reshape(tok_rows, local_heads, HEAD_DIM)
    v_piece = lax.all_gather(proj[:, 1], "ctx", axis=0, tiled=True)
    k_piece = lax.all_gather(proj[:, 3], "ctx", axis=0, tiled=True)
    p_piece = lax.all_gather(positions, "ctx", axis=0, tiled=True)
    attn = attend_piece(query, positions, k_piece, v_piece, p_piece)
    normed = attn * lax.rsqrt(jnp.mean(attn * attn, axis=-1, keepdims=True) + 1e-06)
    gated = (normed * gate.astype(jnp.float32)).astype(jnp.bfloat16).reshape(tok_rows, head_cols)
    out_terms = jnp.dot(
        gated, lax.all_gather(w_out, "ctx", axis=1, tiled=True), preferred_element_type=jnp.float32
    )
    out_share = lax.psum_scatter(out_terms, "tp", scatter_dimension=1, tiled=True)
    feat_cols = out_share.shape[1]
    own_tokens = lax.dynamic_slice_in_dim(tokens, lax.axis_index("tp") * feat_cols, feat_cols, 1)
    hidden = (own_tokens.astype(jnp.float32) + out_share).astype(jnp.bfloat16)
    piece = lax.all_gather(neg_emb, "ctx", axis=0, tiled=True)
    panel_dots = lax.dot_general(
        hidden, piece, (((1,), (1,)), ((), ())), preferred_element_type=jnp.float32
    )
    panel_norms = jnp.sum(jnp.square(piece.astype(jnp.float32)), axis=1)
    hidden_f = hidden.astype(jnp.float32)
    target_f = target_emb.astype(jnp.float32)
    part_hh = jnp.sum(hidden_f * hidden_f, axis=1)
    part_he = jnp.sum(hidden_f * target_f, axis=1)
    part_ee = jnp.sum(target_f * target_f, axis=1)
    dots, hh_sum, he_sum, ee_sum = (
        lax.psum_scatter(panel_dots, "tp", scatter_dimension=0, tiled=True),
        lax.psum_scatter(part_hh, "tp", scatter_dimension=0, tiled=True),
        lax.psum_scatter(part_he, "tp", scatter_dimension=0, tiled=True),
        lax.psum_scatter(part_ee, "tp", scatter_dimension=0, tiled=True),
    )
    neg_sq = lax.psum(panel_norms, "tp")
    pos_logit = he_sum / jnp.sqrt(hh_sum + 1e-06) / jnp.sqrt(ee_sum + 1e-06) / 0.05
    neg_logit = dots / jnp.sqrt(hh_sum + 1e-06)[:, None] / jnp.sqrt(neg_sq + 1e-06)[None, :] / 0.05
    keep_mask = neg_ids[None, :] != target_ids[:, None]
    total_mass = jnp.exp(pos_logit) + jnp.sum(jnp.where(keep_mask, jnp.exp(neg_logit), 0.0), axis=1)
    loss = jnp.log(total_mass) - pos_logit
    return (hidden, loss)


NZ, NY, NX = 4, 2, 2
CHIPS = NZ * NY * NX
PLANE = [(by, bx) for by in range(NY) for bx in range(NX)]
SWAP = [(0, 1), (1, 0)]
W = HEAD_DIM
ACROSS = (((1,), (1,)), ((), ()))


def chip_at(z, y, x):
    return (z * NY + y) * NX + x


def coords(c):
    return c // (NY * NX), (c // NX) % NY, c % NX


def relative_chip(c, by, bx, s):
    z, y, x = coords(c)
    return chip_at(z ^ s, y ^ by, x ^ bx)


def flip(by, bx, s=0):
    return [(c, relative_chip(c, by, bx, s)) for c in range(CHIPS)]


def hop(value, perm):
    return lax.ppermute(value, "ctx", perm)


def swap_cores(value):
    return lax.ppermute(value, "tp", SWAP)


def pick_row(value, at):
    return lax.dynamic_index_in_dim(value, at, 0, keepdims=False)


def after(values, *others):
    return lax.optimization_barrier((values, others))[0]


def pair_up(own):
    return jnp.concatenate([own, hop(own, flip(0, 0, 1))])


def across(value_x, value_y):
    half = value_x.shape[0] // 2
    return [hop(value_x[:half], flip(1, 0)), hop(value_y[half:], flip(0, 1))]


def heads_in_plane(w_proj, y, x, first):
    plane = NY * NX
    heads = w_proj.reshape(-1, 4, 2, plane, W).transpose(3, 2, 0, 1, 4)
    heads = heads.reshape(plane, 2, -1, 4 * W)
    out = []
    for by, bx in PLANE:
        piece = pick_row(heads, (y ^ by) * NX + (x ^ bx))
        if (by, bx) != (0, 0):
            piece = hop(after(piece, first if len(out) < plane - 1 else out[1:]), flip(by, bx))
        out.append(piece)
    return out


def heads_along_z(pieces):
    arrived = []
    for e, piece in enumerate(pieces):
        perm = []
        for src in range(CHIPS):
            sz, sy, sx = coords(src)
            for t in range(2):
                dst = chip_at(2 * t + (e ^ (sz & 1)), sy, sx)
                perm.append((2 * src + t, 2 * dst + (sz >> 1)))
        arrived.append(lax.ppermute(piece, ("ctx", "tp"), perm))
    return arrived


def silu(v):
    return 0.5 * v * (1.0 + jnp.tanh(0.5 * v))


def run_copies(copies):
    for copy in copies:
        copy.start()
    for copy in copies:
        copy.wait()


def mark_kernel(where, tokens, p_hbm, i_hbm, mine, events, positions, ids, sems):
    u = where[3]
    rows, model = events.shape
    own = tokens.at[pl.ds(pl.multiple_of(u * rows, rows), rows), :]
    copies = [(p_hbm, positions), (i_hbm, ids), (own, events)]
    copies = [pltpu.make_async_copy(a, b, sems.at[i]) for i, (a, b) in enumerate(copies)]
    for copy in copies:
        copy.start()
    for copy in copies[:2]:
        copy.wait()
    lane = lax.broadcasted_iota(jnp.int32, (rows, W), 1)
    marks = jnp.zeros((rows, W), F32)
    values = ((positions, u * rows, 7), (positions, (1 - u) * rows, 7), (ids, 0, 8))
    for i, (ref, first, bits) in enumerate(values):
        line = lax.broadcasted_iota(jnp.int32, (rows, ref.shape[1]), 0)
        across = lax.broadcasted_iota(jnp.int32, (rows, ref.shape[1]), 1)
        picked = jnp.where(across == line + first, ref[...], 0)
        column = jnp.sum(picked, axis=1, keepdims=True)
        high = lax.shift_right_logical(column, bits)
        marks = jnp.where(lane == 2 * i, high.astype(F32), marks)
        marks = jnp.where(lane == 2 * i + 1, (column - high * 2**bits).astype(F32), marks)
    mine[:, model:] = marks.astype(BF16)
    copies[2].wait()
    mine[:, :model] = events[...]


def proj_kernel(where, *refs):
    count = len(refs) - 11
    tok, w_own, w_other = refs[:count], refs[count : count + 2], refs[count + 2 : count + 4]
    gate_query, value, key, marks, x_all, w_all, tok_sem = refs[count + 4 :]
    z, y, x, u = (where[i] for i in range(4))
    copies, base = [], 0
    for i, ref in enumerate(tok):
        rows = pl.ds(base, ref.shape[0])
        copies.append(pltpu.make_async_copy(ref, x_all.at[rows, :], tok_sem.at[i]))
        base += ref.shape[0]
    for copy in copies:
        copy.start()
    for at, srcs in ((u, w_own), (1 - u, w_other)):
        for e, src in enumerate(srcs):
            size = src.shape[0] // len(PLANE)
            for j, (by, bx) in enumerate(PLANE):
                start = chip_at(2 * at + (e ^ (z & 1)), y ^ by, x ^ bx) * size
                part = src[j * size : (j + 1) * size, :]
                w_all[pl.ds(pl.multiple_of(start, size), size), :] = part
    for copy in copies:
        copy.wait()
    model = w_all.shape[0]
    total = jnp.dot(x_all[:, :model], w_all[...], preferred_element_type=F32)
    proj = silu(total).astype(BF16)
    gate_query[:, :W] = proj[:, :W]
    value[...] = proj[:, W : 2 * W]
    gate_query[:, W:] = proj[:, 2 * W : 3 * W]
    key[...] = proj[:, 3 * W :]
    marks[...] = x_all[:, model:]


def pick_columns(*weights):
    lane = lax.broadcasted_iota(jnp.int32, (8, W), 1)
    line = lax.broadcasted_iota(jnp.int32, (8, W), 0)
    pick = jnp.zeros((8, W), F32)
    for i, row in enumerate(weights):
        for at, weight in row.items():
            pick = jnp.where((line == i) & (lane == at), weight, pick)
    return pick.astype(BF16)


def attend_kernel(*refs):
    sources, gated, copied, sems = refs[:6], refs[6], refs[7:13], refs[13]
    run_copies(
        [
            pltpu.make_async_copy(src, dst, sems.at[i])
            for i, (src, dst) in enumerate(zip(sources, copied))
        ]
    )
    gate_query, key, value, key_theirs, value_theirs, marks = copied
    pick = pick_columns({0: 128.0, 1: 1.0}, {2: 128.0, 3: 1.0})
    piece = gated.shape[2]
    tile = NZ * piece
    key_pos = lax.dot_general(pick, marks[...], ACROSS, preferred_element_type=F32)
    for k in range(len(PLANE)):
        span = pl.ds(k * tile, tile)
        query = gate_query[span, W:]
        q_pos = lax.dot_general(marks[span, :], pick, ACROSS, preferred_element_type=F32)[:, :1]
        attn = jnp.zeros((tile, W), F32)
        for side, (keys, values) in enumerate(((key, value), (key_theirs, value_theirs))):
            scores = lax.dot_general(
                query, keys[...], ACROSS, preferred_element_type=F32
            ) * W ** (-0.5)
            visible = key_pos[side : side + 1] <= q_pos
            weight = jnp.where(visible, silu(scores), 0.0).astype(BF16)
            attn += jnp.dot(weight, values[...], preferred_element_type=F32)
        normed = attn * lax.rsqrt(jnp.mean(attn * attn, axis=-1, keepdims=True) + 1e-06)
        out = (normed * gate_query[span, :W].astype(F32)).astype(BF16)
        for s in range(NZ):
            gated[s, k] = out[s * piece : (s + 1) * piece]


def hidden_kernel(where, *refs):
    n = len(PLANE)
    gated, w_own, w_other, tok = refs[:5], refs[5:7], refs[7:9], refs[9:13]
    hidden, g_raw, g_all, t_all, w_all, sems = refs[13:]
    z, y, x, u = (where[i] for i in range(4))
    c = chip_at(z, y, x)
    rows = hidden.shape[1]
    half = w_all.shape[1]
    copies = [(src, g_raw.at[k]) for k, src in enumerate(gated[:3])]
    copies += [(src, g_raw.at[3, pl.ds(2 * i, 2)]) for i, src in enumerate(gated[3:])]
    for s in range(NZ):
        cols = pl.ds(s * W, W)
        for side, src in enumerate((w_own, w_other)):
            copies.append((src[s // 2].at[s % 2], w_all.at[side, :, cols]))
        block = relative_chip(c, 0, 0, s)
        from_cols = pl.ds(pl.multiple_of(block * W, W), W)
        for k in range(n):
            copies.append((tok[k].at[pl.ds(0, rows), from_cols], t_all.at[k, :, cols]))
    copies = [pltpu.make_async_copy(src, dst, sems.at[i]) for i, (src, dst) in enumerate(copies)]
    for copy in copies:
        copy.start()
    for copy in copies[:5]:
        copy.wait()
    for k, (by, bx) in enumerate(PLANE):
        for s in range(NZ):
            head = relative_chip(c, by, bx, s)
            cols = pl.ds(pl.multiple_of(head * W, W), W)
            for j in range(n):
                block = j ^ k
                g_all[block * rows : (block + 1) * rows, cols] = g_raw[k, s, j]
    for copy in copies[5:]:
        copy.wait()
    total = 0.0
    for side, at in enumerate((u, 1 - u)):
        part = g_all[:, pl.ds(pl.multiple_of(at * half, half), half)]
        total += jnp.dot(part, w_all[side], preferred_element_type=F32)
    for k in range(n):
        for s in range(NZ):
            term = total[k * rows : (k + 1) * rows, s * W : (s + 1) * W]
            cols = pl.ds(pl.multiple_of((z ^ s) * W, W), W)
            hidden[k, :, cols] = (t_all[k, :, s * W : (s + 1) * W].astype(F32) + term).astype(BF16)


def as_line(column):
    size = column.shape[0]
    line = lax.broadcasted_iota(jnp.int32, (size, size), 0)
    lane = lax.broadcasted_iota(jnp.int32, (size, size), 1)
    return jnp.sum(jnp.where(line == lane, column, 0.0), axis=0, keepdims=True)


def mass_kernel(where, *refs):
    n = len(PLANE)
    pieces, (n_own, n_other, t_keep, t_send, marks) = refs[:5], refs[5:10]
    keep, send, positive, mass, h_all = refs[10:]
    y, x, u = (where[i] for i in range(1, 4))
    rows, half = keep.shape
    for k, (by, bx) in enumerate(PLANE):
        for at in range(NZ):
            block = chip_at(at, y ^ by, x ^ bx)
            cols = pl.ds(pl.multiple_of(block * W, W), W)
            for j in range(n):
                row = (j ^ k) * rows
                ref, i = (pieces[k], j) if k < n - 1 else (pieces[k + j // 2], j % 2)
                h_all[row : row + rows, cols] = ref[i, :, at * W : (at + 1) * W]
    mine = pl.ds(pl.multiple_of(u * half, half), half)
    theirs = pl.ds(pl.multiple_of((1 - u) * half, half), half)
    keep[...] = h_all[:rows, mine]
    send[...] = h_all[:rows, theirs]
    hh, dots, lines = 0.0, 0.0, []
    pick = pick_columns({0: 1.0, 1: 1.0, 2: 1.0}, {3: 256.0, 4: 1.0})
    for part, neg in ((mine, n_own), (theirs, n_other)):
        h_part = h_all[:, part]
        h_f = h_part.astype(F32)
        hh += jnp.sum(h_f * h_f, axis=1, keepdims=True)
        dots += lax.dot_general(h_part, neg[:, :half], ACROSS, preferred_element_type=F32)
        lines.append(lax.dot_general(pick, neg[:, half:], ACROSS, preferred_element_type=F32))
    h_scale = lax.rsqrt(hh + 1e-06) * 20.0
    he = ee = 0.0
    for h_ref, ref in ((keep, t_keep), (send, t_send)):
        h_f, t_f = h_ref[...].astype(F32), ref[...].astype(F32)
        he += jnp.sum(h_f * t_f, axis=1, keepdims=True)
        ee += jnp.sum(t_f * t_f, axis=1, keepdims=True)
    positive[...] = as_line(he * lax.rsqrt(ee + 1e-06) * h_scale[:rows])
    first = [marks[k * NZ * rows : (k * NZ + 1) * rows] for k in range(n)]
    pick = pick_columns({4: 256.0, 5: 1.0})
    t_ids = lax.dot_general(
        jnp.concatenate(first), pick, ACROSS, preferred_element_type=F32
    )[:, :1]
    neg_logit = dots * h_scale * lax.rsqrt(lines[0][0:1] + lines[1][0:1] + 1e-06)
    kept = jnp.where(lines[0][1:2] != t_ids, jnp.exp(neg_logit), 0.0)
    total = jnp.sum(kept, axis=1, keepdims=True)
    for k in range(n):
        mass[k] = as_line(total[k * rows : (k + 1) * rows])


def final_kernel(where, keep, theirs, positive, *refs):
    masses, (hidden, loss) = refs[:-2], refs[-2:]
    u, rows = where[3], keep.shape[0]
    hidden[pl.ds(pl.multiple_of(u * rows, rows), rows), :] = keep[...]
    hidden[pl.ds(pl.multiple_of((1 - u) * rows, rows), rows), :] = theirs[...]
    total = jnp.exp(positive[...])
    for mass in masses:
        total += mass[...]
    loss[...] = jnp.log(total) - positive[...]


def call(kernel, name, outs, scratch, args, places, flops):
    space = {"s": pltpu.SMEM, "v": pltpu.VMEM, "h": pl.ANY, "o": pltpu.HBM}
    moved = sum(a.size * a.dtype.itemsize for a in args)
    return pl.pallas_call(
        kernel,
        out_shape=[jax.ShapeDtypeStruct(shape, dtype) for shape, dtype in outs],
        in_specs=[pl.BlockSpec(memory_space=space[p]) for p in places],
        out_specs=[pl.BlockSpec(memory_space=pltpu.VMEM)] * len(outs),
        scratch_shapes=scratch,
        compiler_params=pltpu.CompilerParams(vmem_limit_bytes=VMEM_LIMIT),
        cost_estimate=pl.CostEstimate(flops=flops, bytes_accessed=moved, transcendentals=0),
        name=name,
    )(*args)


def whole_parts(value, base):
    return [(value // base).astype(BF16), (value % base).astype(BF16)]


def float_parts(value):
    parts = []
    for _ in range(3):
        parts.append(lax.reduce_precision(value, 8, 7))
        value = value - parts[-1]
    return [part.astype(BF16) for part in parts]


def with_marks(rows, marks):
    marks = jnp.stack(marks, 1)
    marks = jnp.pad(marks, ((0, 0), (0, W - marks.shape[1])))
    return jnp.concatenate([rows, marks], 1)


def head_shards(
    tokens, w_proj, w_out, positions, neg_emb, neg_ids, target_emb, target_ids
):
    c, u = lax.axis_index("ctx"), lax.axis_index("tp")
    z, y, x = coords(c)
    where = jnp.stack([z, y, x, u]).astype(jnp.int32)
    model = tokens.shape[1]
    rows = tokens.shape[0] // 2
    events = rows * CHIPS
    half = model // 2
    negs = neg_emb.shape[0]
    plane = len(PLANE)

    (mine,) = call(
        mark_kernel,
        "mark",
        [((rows, model + W), BF16)],
        [
            pltpu.VMEM((rows, model), BF16),
            pltpu.VMEM((1, 2 * rows), jnp.int32),
            pltpu.VMEM((1, rows), jnp.int32),
            pltpu.SemaphoreType.DMA((3,)),
        ],
        [where, tokens, positions.reshape(1, 2 * rows), target_ids.reshape(1, rows)],
        "sooo",
        0,
    )
    line = [mine] + [hop(mine, flip(0, 0, s)) for s in range(1, NZ)]

    to_x, to_y = flip(0, 1), flip(1, 0)
    w_rows = heads_in_plane(w_proj, y, x, mine)
    w_pieces = [
        jnp.concatenate([pick_row(w, e ^ (z & 1)) for w in w_rows]).reshape(-1, 4 * W)
        for e in range(2)
    ]

    own_ids = lax.dynamic_slice_in_dim(neg_ids, c * negs, negs, 0)
    norms = jnp.sum(jnp.square(neg_emb.astype(F32)), axis=1)
    neg = with_marks(neg_emb, float_parts(norms) + whole_parts(own_ids, 256))

    out_pair = pair_up(after(w_out[None], w_rows[1:3]))
    t_rows = target_emb.reshape(2, rows, -1)
    t_keep, t_mine = pick_row(t_rows, u), pick_row(t_rows, 1 - u)
    early = (w_pieces, neg, out_pair, t_keep, t_mine, line)
    w_pieces, neg, out_pair, t_keep, t_mine, line = lax.optimization_barrier(early)
    near = jnp.concatenate(line)
    near_x, near_y = hop(near, to_x), hop(near, to_y)
    tok = [near, near_x, near_y, *across(near_x, near_y)]
    w_mine = heads_along_z(w_pieces)
    w_theirs = [swap_cores(w) for w in w_mine]
    out_own = [out_pair, hop(after(out_pair, w_mine), flip(0, 0, 2))]
    t_send = swap_cores(after(t_mine, w_theirs))

    def project(pieces):
        count = sum(p.shape[0] for p in pieces)
        return call(
            proj_kernel,
            "project",
            [((count, 2 * W), BF16)] + [((count, W), BF16)] * 3,
            [
                pltpu.VMEM((count, model + W), BF16),
                pltpu.VMEM((model, 4 * W), BF16),
                pltpu.SemaphoreType.DMA((len(pieces),)),
            ],
            [where, *pieces, *w_mine, *w_theirs],
            "s" + len(pieces) * "h" + 4 * "v",
            0,
        )

    gate_query, value, key, marks = project(tok)
    key_theirs, value_theirs = swap_cores(key), swap_cores(value)
    out_pair_theirs = swap_cores(after(out_pair, value))
    (gated,) = call(
        attend_kernel,
        "attend",
        [((NZ, plane, rows, W), BF16)],
        [pltpu.VMEM((events, 2 * W), BF16)]
        + [pltpu.VMEM((events, W), BF16)] * 5
        + [pltpu.SemaphoreType.DMA((6,))],
        [gate_query, key, value, key_theirs, value_theirs, marks],
        6 * "h",
        0,
    )
    hops = [hop(gated[s], flip(0, 0, s)) for s in (1, 2)]
    out_own, out_pair_theirs, last = lax.optimization_barrier((out_own, out_pair_theirs, gated[3]))
    gated = jnp.stack([gated[0], *hops, hop(last, flip(0, 0, 3))])
    neg_pair = pair_up(after(neg, gated))
    neg_far = hop(neg_pair, flip(0, 0, 2))
    out_other = [out_pair_theirs, swap_cores(after(out_own[1], gated))]
    gated = [gated, hop(gated, to_x), hop(gated, to_y)]
    gated += across(gated[1], gated[2])
    (hidden,) = call(
        hidden_kernel,
        "hidden",
        [((plane, rows, NZ * W), BF16)],
        [
            pltpu.VMEM((plane, NZ, plane, rows, W), BF16),
            pltpu.VMEM((plane * rows, model), BF16),
            pltpu.VMEM((plane, rows, NZ * W), BF16),
            pltpu.VMEM((2, half, NZ * W), BF16),
            pltpu.SemaphoreType.DMA((29,)),
        ],
        [where, *gated, *out_own, *out_other, *tok[:4]],
        "s" + 13 * "h",
        2 * plane * rows * model * NZ * W,
    )
    pieces = [hidden, hop(hidden, to_x), hop(hidden, to_y)]
    neg_own = jnp.concatenate([neg_pair, after(neg_far, pieces, t_send)])
    neg_other = swap_cores(neg_own)
    pieces += across(pieces[1], pieces[2])
    h_keep, h_send, positive, mass = call(
        mass_kernel,
        "mass",
        [((rows, half), BF16)] * 2 + [((1, rows), F32), ((plane, 1, rows), F32)],
        [pltpu.VMEM((plane * rows, model), BF16)],
        [where, *pieces, neg_own, neg_other, t_keep, t_send, marks],
        "s" + 10 * "v",
        2 * plane * rows * model * NZ * negs,
    )
    masses = [mass[0]] + [hop(mass[k], flip(*PLANE[k])) for k in range(1, plane)]
    h_theirs = swap_cores(h_send)
    hidden, loss = call(
        final_kernel,
        "final",
        [((2 * rows, half), BF16), ((1, rows), F32)],
        [],
        [where, h_keep, h_theirs, positive, *masses],
        "s" + 7 * "v",
        0,
    )
    return hidden, loss.reshape(-1)


def shards(tokens, w_proj, *rest):
    n_ctx, n_tp = lax.axis_size("ctx"), lax.axis_size("tp")
    heads = w_proj.shape[2] * n_tp // HEAD_DIM
    plan = head_shards if (n_ctx, n_tp, heads) == (CHIPS, 2, CHIPS) else general_shards
    return plan(tokens, w_proj, *rest)


def solution(mesh):
    placed = (
        P("ctx", None),
        P("ctx", None, "tp"),
        P("tp", "ctx"),
        P("ctx"),
        P("ctx", "tp"),
        P(),
        P("ctx", "tp"),
        P(("ctx", "tp")),
    )
    return jax.shard_map(
        shards,
        mesh=mesh,
        in_specs=placed,
        out_specs=(P("ctx", "tp"), P(("ctx", "tp"))),
        check_vma=False,
    )
```

```python
import jax
import jax.numpy as jnp
from jax import lax
from jax.experimental import pallas as pl
from jax.experimental.pallas import tpu as pltpu
from jax.sharding import PartitionSpec as P

HEAD_DIM = 128
VMEM_LIMIT = 14 * 1024 * 1024
BF16 = jnp.bfloat16
F32 = jnp.float32


def attend_piece(q_group, q_pos, k_piece, v_piece, p_piece):
    heads = q_group.shape[1]
    width = q_group.shape[2]
    key_heads = k_piece.reshape(k_piece.shape[0], heads, width)
    value_heads = v_piece.reshape(v_piece.shape[0], heads, width)
    scores = jnp.einsum(
        "thd,khd->htk", q_group, key_heads, preferred_element_type=jnp.float32
    ) * width ** (-0.5)
    visible = p_piece[None, None, :] <= q_pos[None, :, None]
    weight = jnp.where(visible, jax.nn.silu(scores), 0.0).astype(jnp.bfloat16)
    return jnp.einsum("htk,khd->thd", weight, value_heads, preferred_element_type=jnp.float32)


def general_shards(
    tokens, w_proj, w_out, positions, neg_emb, neg_ids, target_emb, target_ids
):
    tok_rows = tokens.shape[0]
    head_cols = w_proj.shape[2]
    local_heads = head_cols // HEAD_DIM
    proj_sum = jnp.einsum(
        "td,dfh->tfh",
        tokens,
        lax.all_gather(w_proj, "ctx", axis=0, tiled=True),
        preferred_element_type=jnp.float32,
    )
    proj = jax.nn.silu(proj_sum).astype(jnp.bfloat16)
    gate = proj[:, 0].reshape(tok_rows, local_heads, HEAD_DIM)
    query = proj[:, 2].reshape(tok_rows, local_heads, HEAD_DIM)
    v_piece = lax.all_gather(proj[:, 1], "ctx", axis=0, tiled=True)
    k_piece = lax.all_gather(proj[:, 3], "ctx", axis=0, tiled=True)
    p_piece = lax.all_gather(positions, "ctx", axis=0, tiled=True)
    attn = attend_piece(query, positions, k_piece, v_piece, p_piece)
    normed = attn * lax.rsqrt(jnp.mean(attn * attn, axis=-1, keepdims=True) + 1e-06)
    gated = (normed * gate.astype(jnp.float32)).astype(jnp.bfloat16).reshape(tok_rows, head_cols)
    out_terms = jnp.dot(
        gated, lax.all_gather(w_out, "ctx", axis=1, tiled=True), preferred_element_type=jnp.float32
    )
    out_share = lax.psum_scatter(out_terms, "tp", scatter_dimension=1, tiled=True)
    feat_cols = out_share.shape[1]
    own_tokens = lax.dynamic_slice_in_dim(tokens, lax.axis_index("tp") * feat_cols, feat_cols, 1)
    hidden = (own_tokens.astype(jnp.float32) + out_share).astype(jnp.bfloat16)
    piece = lax.all_gather(neg_emb, "ctx", axis=0, tiled=True)
    panel_dots = lax.dot_general(
        hidden, piece, (((1,), (1,)), ((), ())), preferred_element_type=jnp.float32
    )
    panel_norms = jnp.sum(jnp.square(piece.astype(jnp.float32)), axis=1)
    hidden_f = hidden.astype(jnp.float32)
    target_f = target_emb.astype(jnp.float32)
    part_hh = jnp.sum(hidden_f * hidden_f, axis=1)
    part_he = jnp.sum(hidden_f * target_f, axis=1)
    part_ee = jnp.sum(target_f * target_f, axis=1)
    dots, hh_sum, he_sum, ee_sum = (
        lax.psum_scatter(panel_dots, "tp", scatter_dimension=0, tiled=True),
        lax.psum_scatter(part_hh, "tp", scatter_dimension=0, tiled=True),
        lax.psum_scatter(part_he, "tp", scatter_dimension=0, tiled=True),
        lax.psum_scatter(part_ee, "tp", scatter_dimension=0, tiled=True),
    )
    neg_sq = lax.psum(panel_norms, "tp")
    pos_logit = he_sum / jnp.sqrt(hh_sum + 1e-06) / jnp.sqrt(ee_sum + 1e-06) / 0.05
    neg_logit = dots / jnp.sqrt(hh_sum + 1e-06)[:, None] / jnp.sqrt(neg_sq + 1e-06)[None, :] / 0.05
    keep_mask = neg_ids[None, :] != target_ids[:, None]
    total_mass = jnp.exp(pos_logit) + jnp.sum(jnp.where(keep_mask, jnp.exp(neg_logit), 0.0), axis=1)
    loss = jnp.log(total_mass) - pos_logit
    return (hidden, loss)


NZ, NY, NX = 4, 2, 2
CHIPS = NZ * NY * NX
PLANE = [(by, bx) for by in range(NY) for bx in range(NX)]
SWAP = [(0, 1), (1, 0)]
W = HEAD_DIM
ACROSS = (((1,), (1,)), ((), ()))


def chip_at(z, y, x):
    return (z * NY + y) * NX + x


def coords(c):
    return c // (NY * NX), (c // NX) % NY, c % NX


def relative_chip(c, by, bx, s):
    z, y, x = coords(c)
    return chip_at(z ^ s, y ^ by, x ^ bx)


def flip(by, bx, s=0):
    return [(c, relative_chip(c, by, bx, s)) for c in range(CHIPS)]


def hop(value, perm):
    return lax.ppermute(value, "ctx", perm)


def swap_cores(value):
    return lax.ppermute(value, "tp", SWAP)


def pick_row(value, at):
    return lax.dynamic_index_in_dim(value, at, 0, keepdims=False)


def after(values, *others):
    return lax.optimization_barrier((values, others))[0]


def pair_up(own):
    return jnp.concatenate([own, hop(own, flip(0, 0, 1))])


def across(value_x, value_y):
    half = value_x.shape[0] // 2
    return [hop(value_x[:half], flip(1, 0)), hop(value_y[half:], flip(0, 1))]


def heads_in_plane(w_proj, y, x, first):
    plane = NY * NX
    heads = w_proj.reshape(-1, 4, 2, plane, W).transpose(3, 2, 0, 1, 4)
    heads = heads.reshape(plane, 2, -1, 4 * W)
    out = []
    for by, bx in PLANE:
        piece = pick_row(heads, (y ^ by) * NX + (x ^ bx))
        if (by, bx) != (0, 0):
            piece = hop(after(piece, first if len(out) < plane - 1 else out[1:]), flip(by, bx))
        out.append(piece)
    return out


def heads_along_z(pieces):
    arrived = []
    for e, piece in enumerate(pieces):
        perm = []
        for src in range(CHIPS):
            sz, sy, sx = coords(src)
            for t in range(2):
                dst = chip_at(2 * t + (e ^ (sz & 1)), sy, sx)
                perm.append((2 * src + t, 2 * dst + (sz >> 1)))
        arrived.append(lax.ppermute(piece, ("ctx", "tp"), perm))
    return arrived


def silu(v):
    return 0.5 * v * (1.0 + jnp.tanh(0.5 * v))


def run_copies(copies):
    for copy in copies:
        copy.start()
    for copy in copies:
        copy.wait()


def mark_kernel(where, tokens, p_hbm, i_hbm, mine, events, positions, ids, sems):
    u = where[3]
    rows, model = events.shape
    own = tokens.at[pl.ds(pl.multiple_of(u * rows, rows), rows), :]
    copies = [(p_hbm, positions), (i_hbm, ids), (own, events)]
    copies = [pltpu.make_async_copy(a, b, sems.at[i]) for i, (a, b) in enumerate(copies)]
    for copy in copies:
        copy.start()
    for copy in copies[:2]:
        copy.wait()
    lane = lax.broadcasted_iota(jnp.int32, (rows, W), 1)
    marks = jnp.zeros((rows, W), F32)
    values = ((positions, u * rows, 7), (positions, (1 - u) * rows, 7), (ids, 0, 8))
    for i, (ref, first, bits) in enumerate(values):
        line = lax.broadcasted_iota(jnp.int32, (rows, ref.shape[1]), 0)
        across = lax.broadcasted_iota(jnp.int32, (rows, ref.shape[1]), 1)
        picked = jnp.where(across == line + first, ref[...], 0)
        column = jnp.sum(picked, axis=1, keepdims=True)
        high = lax.shift_right_logical(column, bits)
        marks = jnp.where(lane == 2 * i, high.astype(F32), marks)
        marks = jnp.where(lane == 2 * i + 1, (column - high * 2**bits).astype(F32), marks)
    mine[:, model:] = marks.astype(BF16)
    copies[2].wait()
    mine[:, :model] = events[...]


def proj_kernel(where, *refs):
    count = len(refs) - 11
    tok, w_own, w_other = refs[:count], refs[count : count + 2], refs[count + 2 : count + 4]
    gate_query, value, key, marks, x_all, w_all, tok_sem = refs[count + 4 :]
    z, y, x, u = (where[i] for i in range(4))
    copies, base = [], 0
    for i, ref in enumerate(tok):
        rows = pl.ds(base, ref.shape[0])
        copies.append(pltpu.make_async_copy(ref, x_all.at[rows, :], tok_sem.at[i]))
        base += ref.shape[0]
    for copy in copies:
        copy.start()
    for at, srcs in ((u, w_own), (1 - u, w_other)):
        for e, src in enumerate(srcs):
            size = src.shape[0] // len(PLANE)
            for j, (by, bx) in enumerate(PLANE):
                start = chip_at(2 * at + (e ^ (z & 1)), y ^ by, x ^ bx) * size
                part = src[j * size : (j + 1) * size, :]
                w_all[pl.ds(pl.multiple_of(start, size), size), :] = part
    for copy in copies:
        copy.wait()
    model = w_all.shape[0]
    total = jnp.dot(x_all[:, :model], w_all[...], preferred_element_type=F32)
    proj = silu(total).astype(BF16)
    gate_query[:, :W] = proj[:, :W]
    value[...] = proj[:, W : 2 * W]
    gate_query[:, W:] = proj[:, 2 * W : 3 * W]
    key[...] = proj[:, 3 * W :]
    marks[...] = x_all[:, model:]


def pick_columns(*weights):
    lane = lax.broadcasted_iota(jnp.int32, (8, W), 1)
    line = lax.broadcasted_iota(jnp.int32, (8, W), 0)
    pick = jnp.zeros((8, W), F32)
    for i, row in enumerate(weights):
        for at, weight in row.items():
            pick = jnp.where((line == i) & (lane == at), weight, pick)
    return pick.astype(BF16)


def attend_kernel(*refs):
    sources, gated, copied, sems = refs[:6], refs[6], refs[7:13], refs[13]
    run_copies(
        [
            pltpu.make_async_copy(src, dst, sems.at[i])
            for i, (src, dst) in enumerate(zip(sources, copied))
        ]
    )
    gate_query, key, value, key_theirs, value_theirs, marks = copied
    pick = pick_columns({0: 128.0, 1: 1.0}, {2: 128.0, 3: 1.0})
    piece = gated.shape[2]
    tile = NZ * piece
    key_pos = lax.dot_general(pick, marks[...], ACROSS, preferred_element_type=F32)
    for k in range(len(PLANE)):
        span = pl.ds(k * tile, tile)
        query = gate_query[span, W:]
        q_pos = lax.dot_general(marks[span, :], pick, ACROSS, preferred_element_type=F32)[:, :1]
        attn = jnp.zeros((tile, W), F32)
        for side, (keys, values) in enumerate(((key, value), (key_theirs, value_theirs))):
            scores = lax.dot_general(
                query, keys[...], ACROSS, preferred_element_type=F32
            ) * W ** (-0.5)
            visible = key_pos[side : side + 1] <= q_pos
            weight = jnp.where(visible, silu(scores), 0.0).astype(BF16)
            attn += jnp.dot(weight, values[...], preferred_element_type=F32)
        normed = attn * lax.rsqrt(jnp.mean(attn * attn, axis=-1, keepdims=True) + 1e-06)
        out = (normed * gate_query[span, :W].astype(F32)).astype(BF16)
        for s in range(NZ):
            gated[s, k] = out[s * piece : (s + 1) * piece]


def hidden_kernel(where, *refs):
    n = len(PLANE)
    gated, w_own, w_other, tok = refs[:5], refs[5:7], refs[7:9], refs[9:13]
    hidden, g_raw, g_all, t_all, w_all, sems = refs[13:]
    z, y, x, u = (where[i] for i in range(4))
    c = chip_at(z, y, x)
    rows = hidden.shape[1]
    half = w_all.shape[1]
    copies = [(src, g_raw.at[k]) for k, src in enumerate(gated[:3])]
    copies += [(src, g_raw.at[3, pl.ds(2 * i, 2)]) for i, src in enumerate(gated[3:])]
    for s in range(NZ):
        cols = pl.ds(s * W, W)
        for side, src in enumerate((w_own, w_other)):
            copies.append((src[s // 2].at[s % 2], w_all.at[side, :, cols]))
        block = relative_chip(c, 0, 0, s)
        from_cols = pl.ds(pl.multiple_of(block * W, W), W)
        for k in range(n):
            copies.append((tok[k].at[pl.ds(0, rows), from_cols], t_all.at[k, :, cols]))
    copies = [pltpu.make_async_copy(src, dst, sems.at[i]) for i, (src, dst) in enumerate(copies)]
    for copy in copies:
        copy.start()
    for copy in copies[:5]:
        copy.wait()
    for k, (by, bx) in enumerate(PLANE):
        for s in range(NZ):
            head = relative_chip(c, by, bx, s)
            cols = pl.ds(pl.multiple_of(head * W, W), W)
            for j in range(n):
                block = j ^ k
                g_all[block * rows : (block + 1) * rows, cols] = g_raw[k, s, j]
    for copy in copies[5:]:
        copy.wait()
    total = 0.0
    for side, at in enumerate((u, 1 - u)):
        part = g_all[:, pl.ds(pl.multiple_of(at * half, half), half)]
        total += jnp.dot(part, w_all[side], preferred_element_type=F32)
    for k in range(n):
        for s in range(NZ):
            term = total[k * rows : (k + 1) * rows, s * W : (s + 1) * W]
            cols = pl.ds(pl.multiple_of((z ^ s) * W, W), W)
            hidden[k, :, cols] = (t_all[k, :, s * W : (s + 1) * W].astype(F32) + term).astype(BF16)


def as_line(column):
    size = column.shape[0]
    line = lax.broadcasted_iota(jnp.int32, (size, size), 0)
    lane = lax.broadcasted_iota(jnp.int32, (size, size), 1)
    return jnp.sum(jnp.where(line == lane, column, 0.0), axis=0, keepdims=True)


def mass_kernel(where, *refs):
    n = len(PLANE)
    pieces, (n_own, n_other, t_keep, t_send, marks) = refs[:5], refs[5:10]
    keep, send, positive, mass, h_all = refs[10:]
    y, x, u = (where[i] for i in range(1, 4))
    rows, half = keep.shape
    for k, (by, bx) in enumerate(PLANE):
        for at in range(NZ):
            block = chip_at(at, y ^ by, x ^ bx)
            cols = pl.ds(pl.multiple_of(block * W, W), W)
            for j in range(n):
                row = (j ^ k) * rows
                ref, i = (pieces[k], j) if k < n - 1 else (pieces[k + j // 2], j % 2)
                h_all[row : row + rows, cols] = ref[i, :, at * W : (at + 1) * W]
    mine = pl.ds(pl.multiple_of(u * half, half), half)
    theirs = pl.ds(pl.multiple_of((1 - u) * half, half), half)
    keep[...] = h_all[:rows, mine]
    send[...] = h_all[:rows, theirs]
    hh, dots, lines = 0.0, 0.0, []
    pick = pick_columns({0: 1.0, 1: 1.0, 2: 1.0}, {3: 256.0, 4: 1.0})
    for part, neg in ((mine, n_own), (theirs, n_other)):
        h_part = h_all[:, part]
        h_f = h_part.astype(F32)
        hh += jnp.sum(h_f * h_f, axis=1, keepdims=True)
        dots += lax.dot_general(h_part, neg[:, :half], ACROSS, preferred_element_type=F32)
        lines.append(lax.dot_general(pick, neg[:, half:], ACROSS, preferred_element_type=F32))
    h_scale = lax.rsqrt(hh + 1e-06) * 20.0
    he = ee = 0.0
    for h_ref, ref in ((keep, t_keep), (send, t_send)):
        h_f, t_f = h_ref[...].astype(F32), ref[...].astype(F32)
        he += jnp.sum(h_f * t_f, axis=1, keepdims=True)
        ee += jnp.sum(t_f * t_f, axis=1, keepdims=True)
    positive[...] = as_line(he * lax.rsqrt(ee + 1e-06) * h_scale[:rows])
    first = [marks[k * NZ * rows : (k * NZ + 1) * rows] for k in range(n)]
    pick = pick_columns({4: 256.0, 5: 1.0})
    t_ids = lax.dot_general(
        jnp.concatenate(first), pick, ACROSS, preferred_element_type=F32
    )[:, :1]
    neg_logit = dots * h_scale * lax.rsqrt(lines[0][0:1] + lines[1][0:1] + 1e-06)
    kept = jnp.where(lines[0][1:2] != t_ids, jnp.exp(neg_logit), 0.0)
    total = jnp.sum(kept, axis=1, keepdims=True)
    for k in range(n):
        mass[k] = as_line(total[k * rows : (k + 1) * rows])


def final_kernel(where, keep, theirs, positive, *refs):
    masses, (hidden, loss) = refs[:-2], refs[-2:]
    u, rows = where[3], keep.shape[0]
    hidden[pl.ds(pl.multiple_of(u * rows, rows), rows), :] = keep[...]
    hidden[pl.ds(pl.multiple_of((1 - u) * rows, rows), rows), :] = theirs[...]
    total = jnp.exp(positive[...])
    for mass in masses:
        total += mass[...]
    loss[...] = jnp.log(total) - positive[...]


def call(kernel, name, outs, scratch, args, places, flops, vmem=VMEM_LIMIT):
    space = {"s": pltpu.SMEM, "v": pltpu.VMEM, "h": pl.ANY, "o": pltpu.HBM}
    moved = sum(a.size * a.dtype.itemsize for a in args)
    return pl.pallas_call(
        kernel,
        out_shape=[jax.ShapeDtypeStruct(shape, dtype) for shape, dtype in outs],
        in_specs=[pl.BlockSpec(memory_space=space[p]) for p in places],
        out_specs=[pl.BlockSpec(memory_space=pltpu.VMEM)] * len(outs),
        scratch_shapes=scratch,
        compiler_params=pltpu.CompilerParams(vmem_limit_bytes=vmem),
        cost_estimate=pl.CostEstimate(flops=flops, bytes_accessed=moved, transcendentals=0),
        name=name,
    )(*args)


def whole_parts(value, base):
    return [(value // base).astype(BF16), (value % base).astype(BF16)]


def float_parts(value):
    parts = []
    for _ in range(3):
        parts.append(lax.reduce_precision(value, 8, 7))
        value = value - parts[-1]
    return [part.astype(BF16) for part in parts]


def with_marks(rows, marks):
    marks = jnp.stack(marks, 1)
    marks = jnp.pad(marks, ((0, 0), (0, W - marks.shape[1])))
    return jnp.concatenate([rows, marks], 1)


def head_shards(
    tokens, w_proj, w_out, positions, neg_emb, neg_ids, target_emb, target_ids
):
    c, u = lax.axis_index("ctx"), lax.axis_index("tp")
    z, y, x = coords(c)
    where = jnp.stack([z, y, x, u]).astype(jnp.int32)
    model = tokens.shape[1]
    rows = tokens.shape[0] // 2
    events = rows * CHIPS
    half = model // 2
    negs = neg_emb.shape[0]
    plane = len(PLANE)

    (mine,) = call(
        mark_kernel,
        "mark",
        [((rows, model + W), BF16)],
        [
            pltpu.VMEM((rows, model), BF16),
            pltpu.VMEM((1, 2 * rows), jnp.int32),
            pltpu.VMEM((1, rows), jnp.int32),
            pltpu.SemaphoreType.DMA((3,)),
        ],
        [where, tokens, positions.reshape(1, 2 * rows), target_ids.reshape(1, rows)],
        "sooo",
        0,
        4 * VMEM_LIMIT,
    )
    line = [mine] + [hop(mine, flip(0, 0, s)) for s in range(1, NZ)]

    to_x, to_y = flip(0, 1), flip(1, 0)
    w_rows = heads_in_plane(w_proj, y, x, mine)
    w_pieces = [
        jnp.concatenate([pick_row(w, e ^ (z & 1)) for w in w_rows]).reshape(-1, 4 * W)
        for e in range(2)
    ]

    own_ids = lax.dynamic_slice_in_dim(neg_ids, c * negs, negs, 0)
    norms = jnp.sum(jnp.square(neg_emb.astype(F32)), axis=1)
    neg = with_marks(neg_emb, float_parts(norms) + whole_parts(own_ids, 256))

    out_pair = pair_up(after(w_out[None], w_rows[1:3]))
    t_rows = target_emb.reshape(2, rows, -1)
    t_keep, t_mine = pick_row(t_rows, u), pick_row(t_rows, 1 - u)
    early = (w_pieces, neg, out_pair, t_keep, t_mine, line)
    w_pieces, neg, out_pair, t_keep, t_mine, line = lax.optimization_barrier(early)
    near = jnp.concatenate(line)
    near_x, near_y = hop(near, to_x), hop(near, to_y)
    tok = [near, near_x, near_y, *across(near_x, near_y)]
    w_mine = heads_along_z(w_pieces)
    w_theirs = [swap_cores(w) for w in w_mine]
    out_own = [out_pair, hop(after(out_pair, w_mine), flip(0, 0, 2))]
    t_send = swap_cores(after(t_mine, w_theirs))

    def project(pieces):
        count = sum(p.shape[0] for p in pieces)
        return call(
            proj_kernel,
            "project",
            [((count, 2 * W), BF16)] + [((count, W), BF16)] * 3,
            [
                pltpu.VMEM((count, model + W), BF16),
                pltpu.VMEM((model, 4 * W), BF16),
                pltpu.SemaphoreType.DMA((len(pieces),)),
            ],
            [where, *pieces, *w_mine, *w_theirs],
            "s" + len(pieces) * "h" + 4 * "v",
            0,
        )

    gate_query, value, key, marks = project(tok)
    key_theirs, value_theirs = swap_cores(key), swap_cores(value)
    out_pair_theirs = swap_cores(after(out_pair, value))
    (gated,) = call(
        attend_kernel,
        "attend",
        [((NZ, plane, rows, W), BF16)],
        [pltpu.VMEM((events, 2 * W), BF16)]
        + [pltpu.VMEM((events, W), BF16)] * 5
        + [pltpu.SemaphoreType.DMA((6,))],
        [gate_query, key, value, key_theirs, value_theirs, marks],
        6 * "h",
        0,
    )
    hops = [hop(gated[s], flip(0, 0, s)) for s in (1, 2)]
    out_own, out_pair_theirs, last = lax.optimization_barrier((out_own, out_pair_theirs, gated[3]))
    gated = jnp.stack([gated[0], *hops, hop(last, flip(0, 0, 3))])
    neg_pair = pair_up(after(neg, gated))
    neg_far = hop(neg_pair, flip(0, 0, 2))
    out_other = [out_pair_theirs, swap_cores(after(out_own[1], gated))]
    gated = [gated, hop(gated, to_x), hop(gated, to_y)]
    gated += across(gated[1], gated[2])
    (hidden,) = call(
        hidden_kernel,
        "hidden",
        [((plane, rows, NZ * W), BF16)],
        [
            pltpu.VMEM((plane, NZ, plane, rows, W), BF16),
            pltpu.VMEM((plane * rows, model), BF16),
            pltpu.VMEM((plane, rows, NZ * W), BF16),
            pltpu.VMEM((2, half, NZ * W), BF16),
            pltpu.SemaphoreType.DMA((29,)),
        ],
        [where, *gated, *out_own, *out_other, *tok[:4]],
        "s" + 13 * "h",
        2 * plane * rows * model * NZ * W,
    )
    pieces = [hidden, hop(hidden, to_x), hop(hidden, to_y)]
    neg_own = jnp.concatenate([neg_pair, after(neg_far, pieces, t_send)])
    neg_other = swap_cores(neg_own)
    pieces += across(pieces[1], pieces[2])
    h_keep, h_send, positive, mass = call(
        mass_kernel,
        "mass",
        [((rows, half), BF16)] * 2 + [((1, rows), F32), ((plane, 1, rows), F32)],
        [pltpu.VMEM((plane * rows, model), BF16)],
        [where, *pieces, neg_own, neg_other, t_keep, t_send, marks],
        "s" + 10 * "v",
        2 * plane * rows * model * NZ * negs,
    )
    masses = [mass[0]] + [hop(mass[k], flip(*PLANE[k])) for k in range(1, plane)]
    h_theirs = swap_cores(h_send)
    hidden, loss = call(
        final_kernel,
        "final",
        [((2 * rows, half), BF16), ((1, rows), F32)],
        [],
        [where, h_keep, h_theirs, positive, *masses],
        "s" + 7 * "v",
        0,
    )
    return hidden, loss.reshape(-1)


def shards(tokens, w_proj, *rest):
    n_ctx, n_tp = lax.axis_size("ctx"), lax.axis_size("tp")
    heads = w_proj.shape[2] * n_tp // HEAD_DIM
    plan = head_shards if (n_ctx, n_tp, heads) == (CHIPS, 2, CHIPS) else general_shards
    return plan(tokens, w_proj, *rest)


def solution(mesh):
    placed = (
        P("ctx", None),
        P("ctx", None, "tp"),
        P("tp", "ctx"),
        P("ctx"),
        P("ctx", "tp"),
        P(),
        P("ctx", "tp"),
        P(("ctx", "tp")),
    )
    return jax.shard_map(
        shards,
        mesh=mesh,
        in_specs=placed,
        out_specs=(P("ctx", "tp"), P(("ctx", "tp"))),
        check_vma=False,
    )
```

```python
import jax
import jax.numpy as jnp
from jax import lax
from jax.experimental import pallas as pl
from jax.experimental.pallas import tpu as pltpu
from jax.sharding import PartitionSpec as P

HEAD_DIM = 128
VMEM_LIMIT = 14 * 1024 * 1024
BF16 = jnp.bfloat16
F32 = jnp.float32


def attend_piece(q_group, q_pos, k_piece, v_piece, p_piece):
    heads = q_group.shape[1]
    width = q_group.shape[2]
    key_heads = k_piece.reshape(k_piece.shape[0], heads, width)
    value_heads = v_piece.reshape(v_piece.shape[0], heads, width)
    scores = jnp.einsum(
        "thd,khd->htk", q_group, key_heads, preferred_element_type=jnp.float32
    ) * width ** (-0.5)
    visible = p_piece[None, None, :] <= q_pos[None, :, None]
    weight = jnp.where(visible, jax.nn.silu(scores), 0.0).astype(jnp.bfloat16)
    return jnp.einsum("htk,khd->thd", weight, value_heads, preferred_element_type=jnp.float32)


def general_shards(
    tokens, w_proj, w_out, positions, neg_emb, neg_ids, target_emb, target_ids
):
    tok_rows = tokens.shape[0]
    head_cols = w_proj.shape[2]
    local_heads = head_cols // HEAD_DIM
    proj_sum = jnp.einsum(
        "td,dfh->tfh",
        tokens,
        lax.all_gather(w_proj, "ctx", axis=0, tiled=True),
        preferred_element_type=jnp.float32,
    )
    proj = jax.nn.silu(proj_sum).astype(jnp.bfloat16)
    gate = proj[:, 0].reshape(tok_rows, local_heads, HEAD_DIM)
    query = proj[:, 2].reshape(tok_rows, local_heads, HEAD_DIM)
    v_piece = lax.all_gather(proj[:, 1], "ctx", axis=0, tiled=True)
    k_piece = lax.all_gather(proj[:, 3], "ctx", axis=0, tiled=True)
    p_piece = lax.all_gather(positions, "ctx", axis=0, tiled=True)
    attn = attend_piece(query, positions, k_piece, v_piece, p_piece)
    normed = attn * lax.rsqrt(jnp.mean(attn * attn, axis=-1, keepdims=True) + 1e-06)
    gated = (normed * gate.astype(jnp.float32)).astype(jnp.bfloat16).reshape(tok_rows, head_cols)
    out_terms = jnp.dot(
        gated, lax.all_gather(w_out, "ctx", axis=1, tiled=True), preferred_element_type=jnp.float32
    )
    out_share = lax.psum_scatter(out_terms, "tp", scatter_dimension=1, tiled=True)
    feat_cols = out_share.shape[1]
    own_tokens = lax.dynamic_slice_in_dim(tokens, lax.axis_index("tp") * feat_cols, feat_cols, 1)
    hidden = (own_tokens.astype(jnp.float32) + out_share).astype(jnp.bfloat16)
    piece = lax.all_gather(neg_emb, "ctx", axis=0, tiled=True)
    panel_dots = lax.dot_general(
        hidden, piece, (((1,), (1,)), ((), ())), preferred_element_type=jnp.float32
    )
    panel_norms = jnp.sum(jnp.square(piece.astype(jnp.float32)), axis=1)
    hidden_f = hidden.astype(jnp.float32)
    target_f = target_emb.astype(jnp.float32)
    part_hh = jnp.sum(hidden_f * hidden_f, axis=1)
    part_he = jnp.sum(hidden_f * target_f, axis=1)
    part_ee = jnp.sum(target_f * target_f, axis=1)
    dots, hh_sum, he_sum, ee_sum = (
        lax.psum_scatter(panel_dots, "tp", scatter_dimension=0, tiled=True),
        lax.psum_scatter(part_hh, "tp", scatter_dimension=0, tiled=True),
        lax.psum_scatter(part_he, "tp", scatter_dimension=0, tiled=True),
        lax.psum_scatter(part_ee, "tp", scatter_dimension=0, tiled=True),
    )
    neg_sq = lax.psum(panel_norms, "tp")
    pos_logit = he_sum / jnp.sqrt(hh_sum + 1e-06) / jnp.sqrt(ee_sum + 1e-06) / 0.05
    neg_logit = dots / jnp.sqrt(hh_sum + 1e-06)[:, None] / jnp.sqrt(neg_sq + 1e-06)[None, :] / 0.05
    keep_mask = neg_ids[None, :] != target_ids[:, None]
    total_mass = jnp.exp(pos_logit) + jnp.sum(jnp.where(keep_mask, jnp.exp(neg_logit), 0.0), axis=1)
    loss = jnp.log(total_mass) - pos_logit
    return (hidden, loss)


NZ, NY, NX = 4, 2, 2
CHIPS = NZ * NY * NX
PLANE = [(by, bx) for by in range(NY) for bx in range(NX)]
SWAP = [(0, 1), (1, 0)]
W = HEAD_DIM
ACROSS = (((1,), (1,)), ((), ()))


def chip_at(z, y, x):
    return (z * NY + y) * NX + x


def coords(c):
    return c // (NY * NX), (c // NX) % NY, c % NX


def relative_chip(c, by, bx, s):
    z, y, x = coords(c)
    return chip_at(z ^ s, y ^ by, x ^ bx)


def flip(by, bx, s=0):
    return [(c, relative_chip(c, by, bx, s)) for c in range(CHIPS)]


def hop(value, perm):
    return lax.ppermute(value, "ctx", perm)


def swap_cores(value):
    return lax.ppermute(value, "tp", SWAP)


def pick_row(value, at):
    return lax.dynamic_index_in_dim(value, at, 0, keepdims=False)


def after(values, *others):
    return lax.optimization_barrier((values, others))[0]


def pair_up(own):
    return jnp.concatenate([own, hop(own, flip(0, 0, 1))])


def is_inner(z):
    return ((z + 1) // 2) % 2 == 1


def inner_hop(pair):
    return hop(pair, [(c, relative_chip(c, 0, 0, 3)) for c in range(CHIPS) if is_inner(coords(c)[0])])


def outer_hop(pair):
    return hop(pair, [(c, relative_chip(c, 0, 0, 1)) for c in range(CHIPS) if is_inner(coords(c)[0])])


def across(value_x, value_y):
    half = value_x.shape[0] // 2
    return [hop(value_x[:half], flip(1, 0)), hop(value_y[half:], flip(0, 1))]


def heads_in_plane(w_proj, y, x, first):
    plane = NY * NX
    heads = w_proj.reshape(-1, 4, 2, plane, W).transpose(3, 2, 0, 1, 4)
    heads = heads.reshape(plane, 2, -1, 4 * W)
    out = []
    for by, bx in PLANE:
        piece = pick_row(heads, (y ^ by) * NX + (x ^ bx))
        if (by, bx) != (0, 0):
            piece = hop(after(piece, first if len(out) < plane - 1 else out[1:]), flip(by, bx))
        out.append(piece)
    return out


def heads_along_z(pieces):
    arrived = []
    for e, piece in enumerate(pieces):
        perm = []
        for src in range(CHIPS):
            sz, sy, sx = coords(src)
            for t in range(2):
                dst = chip_at(2 * t + (e ^ (sz & 1)), sy, sx)
                perm.append((2 * src + t, 2 * dst + (sz >> 1)))
        arrived.append(lax.ppermute(piece, ("ctx", "tp"), perm))
    return arrived


def silu(v):
    return 0.5 * v * (1.0 + jnp.tanh(0.5 * v))


def run_copies(copies):
    for copy in copies:
        copy.start()
    for copy in copies:
        copy.wait()


def mark_kernel(where, tokens, p_hbm, i_hbm, mine, events, positions, ids, sems):
    u = where[3]
    rows, model = events.shape
    own = tokens.at[pl.ds(pl.multiple_of(u * rows, rows), rows), :]
    copies = [(p_hbm, positions), (i_hbm, ids), (own, events)]
    copies = [pltpu.make_async_copy(a, b, sems.at[i]) for i, (a, b) in enumerate(copies)]
    for copy in copies:
        copy.start()
    for copy in copies[:2]:
        copy.wait()
    lane = lax.broadcasted_iota(jnp.int32, (rows, W), 1)
    marks = jnp.zeros((rows, W), F32)
    values = ((positions, u * rows, 7), (positions, (1 - u) * rows, 7), (ids, 0, 8))
    for i, (ref, first, bits) in enumerate(values):
        line = lax.broadcasted_iota(jnp.int32, (rows, ref.shape[1]), 0)
        across = lax.broadcasted_iota(jnp.int32, (rows, ref.shape[1]), 1)
        picked = jnp.where(across == line + first, ref[...], 0)
        column = jnp.sum(picked, axis=1, keepdims=True)
        high = lax.shift_right_logical(column, bits)
        marks = jnp.where(lane == 2 * i, high.astype(F32), marks)
        marks = jnp.where(lane == 2 * i + 1, (column - high * 2**bits).astype(F32), marks)
    mine[:, model:] = marks.astype(BF16)
    copies[2].wait()
    mine[:, :model] = events[...]


def proj_kernel(where, *refs):
    count = len(refs) - 11
    tok, w_own, w_other = refs[:count], refs[count : count + 2], refs[count + 2 : count + 4]
    gate_query, value, key, marks, x_all, w_all, tok_sem = refs[count + 4 :]
    z, y, x, u = (where[i] for i in range(4))
    copies, base = [], 0
    for i, ref in enumerate(tok):
        rows = pl.ds(base, ref.shape[0])
        copies.append(pltpu.make_async_copy(ref, x_all.at[rows, :], tok_sem.at[i]))
        base += ref.shape[0]
    for copy in copies:
        copy.start()
    for at, srcs in ((u, w_own), (1 - u, w_other)):
        for e, src in enumerate(srcs):
            size = src.shape[0] // len(PLANE)
            for j, (by, bx) in enumerate(PLANE):
                start = chip_at(2 * at + (e ^ (z & 1)), y ^ by, x ^ bx) * size
                part = src[j * size : (j + 1) * size, :]
                w_all[pl.ds(pl.multiple_of(start, size), size), :] = part
    for copy in copies:
        copy.wait()
    model = w_all.shape[0]
    total = jnp.dot(x_all[:, :model], w_all[...], preferred_element_type=F32)
    proj = silu(total).astype(BF16)
    gate_query[:, :W] = proj[:, :W]
    value[...] = proj[:, W : 2 * W]
    gate_query[:, W:] = proj[:, 2 * W : 3 * W]
    key[...] = proj[:, 3 * W :]
    marks[...] = x_all[:, model:]


def pick_columns(*weights):
    lane = lax.broadcasted_iota(jnp.int32, (8, W), 1)
    line = lax.broadcasted_iota(jnp.int32, (8, W), 0)
    pick = jnp.zeros((8, W), F32)
    for i, row in enumerate(weights):
        for at, weight in row.items():
            pick = jnp.where((line == i) & (lane == at), weight, pick)
    return pick.astype(BF16)


def attend_kernel(*refs):
    sources, gated, copied, sems = refs[:6], refs[6], refs[7:13], refs[13]
    run_copies(
        [
            pltpu.make_async_copy(src, dst, sems.at[i])
            for i, (src, dst) in enumerate(zip(sources, copied))
        ]
    )
    gate_query, key, value, key_theirs, value_theirs, marks = copied
    pick = pick_columns({0: 128.0, 1: 1.0}, {2: 128.0, 3: 1.0})
    piece = gated.shape[2]
    tile = NZ * piece
    key_pos = lax.dot_general(pick, marks[...], ACROSS, preferred_element_type=F32)
    for k in range(len(PLANE)):
        span = pl.ds(k * tile, tile)
        query = gate_query[span, W:]
        q_pos = lax.dot_general(marks[span, :], pick, ACROSS, preferred_element_type=F32)[:, :1]
        attn = jnp.zeros((tile, W), F32)
        for side, (keys, values) in enumerate(((key, value), (key_theirs, value_theirs))):
            scores = lax.dot_general(
                query, keys[...], ACROSS, preferred_element_type=F32
            ) * W ** (-0.5)
            visible = key_pos[side : side + 1] <= q_pos
            weight = jnp.where(visible, silu(scores), 0.0).astype(BF16)
            attn += jnp.dot(weight, values[...], preferred_element_type=F32)
        normed = attn * lax.rsqrt(jnp.mean(attn * attn, axis=-1, keepdims=True) + 1e-06)
        out = (normed * gate_query[span, :W].astype(F32)).astype(BF16)
        for s in range(NZ):
            gated[s, k] = out[s * piece : (s + 1) * piece]


def hidden_kernel(where, *refs):
    n = len(PLANE)
    gated, w_own, w_other, tok = refs[:5], refs[5:7], refs[7:9], refs[9:13]
    hidden, g_raw, g_all, t_all, w_all, sems = refs[13:]
    z, y, x, u = (where[i] for i in range(4))
    c = chip_at(z, y, x)
    rows = hidden.shape[1]
    half = w_all.shape[1]
    flipped = ((z + 1) // 2) % 2
    copies = [(src, g_raw.at[k]) for k, src in enumerate(gated[:3])]
    copies += [(src, g_raw.at[3, pl.ds(2 * i, 2)]) for i, src in enumerate(gated[3:])]
    for s in range(NZ):
        cols = pl.ds(s * W, W)
        for side, src in enumerate((w_own, w_other)):
            panel = src[0].at[s] if s < 2 else src[1].at[(s % 2) ^ flipped]
            copies.append((panel, w_all.at[side, :, cols]))
        block = relative_chip(c, 0, 0, s)
        from_cols = pl.ds(pl.multiple_of(block * W, W), W)
        for k in range(n):
            copies.append((tok[k].at[pl.ds(0, rows), from_cols], t_all.at[k, :, cols]))
    copies = [pltpu.make_async_copy(src, dst, sems.at[i]) for i, (src, dst) in enumerate(copies)]
    for copy in copies:
        copy.start()
    for copy in copies[:5]:
        copy.wait()
    for k, (by, bx) in enumerate(PLANE):
        for s in range(NZ):
            head = relative_chip(c, by, bx, s)
            cols = pl.ds(pl.multiple_of(head * W, W), W)
            for j in range(n):
                block = j ^ k
                g_all[block * rows : (block + 1) * rows, cols] = g_raw[k, s, j]
    for copy in copies[5:]:
        copy.wait()
    total = 0.0
    for side, at in enumerate((u, 1 - u)):
        part = g_all[:, pl.ds(pl.multiple_of(at * half, half), half)]
        total += jnp.dot(part, w_all[side], preferred_element_type=F32)
    for k in range(n):
        for s in range(NZ):
            term = total[k * rows : (k + 1) * rows, s * W : (s + 1) * W]
            cols = pl.ds(pl.multiple_of((z ^ s) * W, W), W)
            hidden[k, :, cols] = (t_all[k, :, s * W : (s + 1) * W].astype(F32) + term).astype(BF16)


def as_line(column):
    size = column.shape[0]
    line = lax.broadcasted_iota(jnp.int32, (size, size), 0)
    lane = lax.broadcasted_iota(jnp.int32, (size, size), 1)
    return jnp.sum(jnp.where(line == lane, column, 0.0), axis=0, keepdims=True)


def mass_kernel(where, *refs):
    n = len(PLANE)
    pieces, (n_own, n_other, t_keep, t_send, marks) = refs[:5], refs[5:10]
    keep, send, positive, mass, h_all = refs[10:]
    y, x, u = (where[i] for i in range(1, 4))
    rows, half = keep.shape
    for k, (by, bx) in enumerate(PLANE):
        for at in range(NZ):
            block = chip_at(at, y ^ by, x ^ bx)
            cols = pl.ds(pl.multiple_of(block * W, W), W)
            for j in range(n):
                row = (j ^ k) * rows
                ref, i = (pieces[k], j) if k < n - 1 else (pieces[k + j // 2], j % 2)
                h_all[row : row + rows, cols] = ref[i, :, at * W : (at + 1) * W]
    mine = pl.ds(pl.multiple_of(u * half, half), half)
    theirs = pl.ds(pl.multiple_of((1 - u) * half, half), half)
    keep[...] = h_all[:rows, mine]
    send[...] = h_all[:rows, theirs]
    hh, dots, lines = 0.0, 0.0, []
    pick = pick_columns({0: 1.0, 1: 1.0, 2: 1.0}, {3: 256.0, 4: 1.0})
    for part, neg in ((mine, n_own), (theirs, n_other)):
        h_part = h_all[:, part]
        h_f = h_part.astype(F32)
        hh += jnp.sum(h_f * h_f, axis=1, keepdims=True)
        dots += lax.dot_general(h_part, neg[:, :half], ACROSS, preferred_element_type=F32)
        lines.append(lax.dot_general(pick, neg[:, half:], ACROSS, preferred_element_type=F32))
    h_scale = lax.rsqrt(hh + 1e-06) * 20.0
    he = ee = 0.0
    for h_ref, ref in ((keep, t_keep), (send, t_send)):
        h_f, t_f = h_ref[...].astype(F32), ref[...].astype(F32)
        he += jnp.sum(h_f * t_f, axis=1, keepdims=True)
        ee += jnp.sum(t_f * t_f, axis=1, keepdims=True)
    positive[...] = as_line(he * lax.rsqrt(ee + 1e-06) * h_scale[:rows])
    first = [marks[k * NZ * rows : (k * NZ + 1) * rows] for k in range(n)]
    pick = pick_columns({4: 256.0, 5: 1.0})
    t_ids = lax.dot_general(
        jnp.concatenate(first), pick, ACROSS, preferred_element_type=F32
    )[:, :1]
    neg_logit = dots * h_scale * lax.rsqrt(lines[0][0:1] + lines[1][0:1] + 1e-06)
    kept = jnp.where(lines[0][1:2] != t_ids, jnp.exp(neg_logit), 0.0)
    total = jnp.sum(kept, axis=1, keepdims=True)
    for k in range(n):
        mass[k] = as_line(total[k * rows : (k + 1) * rows])


def final_kernel(where, keep, theirs, positive, *refs):
    masses, (hidden, loss) = refs[:-2], refs[-2:]
    u, rows = where[3], keep.shape[0]
    hidden[pl.ds(pl.multiple_of(u * rows, rows), rows), :] = keep[...]
    hidden[pl.ds(pl.multiple_of((1 - u) * rows, rows), rows), :] = theirs[...]
    total = jnp.exp(positive[...])
    for mass in masses:
        total += mass[...]
    loss[...] = jnp.log(total) - positive[...]


def call(kernel, name, outs, scratch, args, places, flops):
    space = {"s": pltpu.SMEM, "v": pltpu.VMEM, "h": pl.ANY, "o": pltpu.HBM}
    moved = sum(a.size * a.dtype.itemsize for a in args)
    return pl.pallas_call(
        kernel,
        out_shape=[jax.ShapeDtypeStruct(shape, dtype) for shape, dtype in outs],
        in_specs=[pl.BlockSpec(memory_space=space[p]) for p in places],
        out_specs=[pl.BlockSpec(memory_space=pltpu.VMEM)] * len(outs),
        scratch_shapes=scratch,
        compiler_params=pltpu.CompilerParams(vmem_limit_bytes=VMEM_LIMIT),
        cost_estimate=pl.CostEstimate(flops=flops, bytes_accessed=moved, transcendentals=0),
        name=name,
    )(*args)


def whole_parts(value, base):
    return [(value // base).astype(BF16), (value % base).astype(BF16)]


def float_parts(value):
    parts = []
    for _ in range(3):
        parts.append(lax.reduce_precision(value, 8, 7))
        value = value - parts[-1]
    return [part.astype(BF16) for part in parts]


def with_marks(rows, marks):
    marks = jnp.stack(marks, 1)
    marks = jnp.pad(marks, ((0, 0), (0, W - marks.shape[1])))
    return jnp.concatenate([rows, marks], 1)


def head_shards(
    tokens, w_proj, w_out, positions, neg_emb, neg_ids, target_emb, target_ids
):
    c, u = lax.axis_index("ctx"), lax.axis_index("tp")
    z, y, x = coords(c)
    where = jnp.stack([z, y, x, u]).astype(jnp.int32)
    model = tokens.shape[1]
    rows = tokens.shape[0] // 2
    events = rows * CHIPS
    half = model // 2
    negs = neg_emb.shape[0]
    plane = len(PLANE)

    (mine,) = call(
        mark_kernel,
        "mark",
        [((rows, model + W), BF16)],
        [
            pltpu.VMEM((rows, model), BF16),
            pltpu.VMEM((1, 2 * rows), jnp.int32),
            pltpu.VMEM((1, rows), jnp.int32),
            pltpu.SemaphoreType.DMA((3,)),
        ],
        [where, tokens, positions.reshape(1, 2 * rows), target_ids.reshape(1, rows)],
        "sooo",
        0,
    )
    line = [mine] + [hop(mine, flip(0, 0, s)) for s in range(1, NZ)]

    to_x, to_y = flip(0, 1), flip(1, 0)
    w_rows = heads_in_plane(w_proj, y, x, mine)
    w_pieces = [
        jnp.concatenate([pick_row(w, e ^ (z & 1)) for w in w_rows]).reshape(-1, 4 * W)
        for e in range(2)
    ]

    own_ids = lax.dynamic_slice_in_dim(neg_ids, c * negs, negs, 0)
    norms = jnp.sum(jnp.square(neg_emb.astype(F32)), axis=1)
    neg = with_marks(neg_emb, float_parts(norms) + whole_parts(own_ids, 256))

    out_pair = pair_up(after(w_out[None], w_rows[1:3]))
    t_rows = target_emb.reshape(2, rows, -1)
    t_keep, t_mine = pick_row(t_rows, u), pick_row(t_rows, 1 - u)
    early = (w_pieces, neg, out_pair, t_keep, t_mine, line)
    w_pieces, neg, out_pair, t_keep, t_mine, line = lax.optimization_barrier(early)
    near = jnp.concatenate(line)
    near_x, near_y = hop(near, to_x), hop(near, to_y)
    tok = [near, near_x, near_y, *across(near_x, near_y)]
    w_mine = heads_along_z(w_pieces)
    w_theirs = [swap_cores(w) for w in w_mine]
    out_met = inner_hop(after(out_pair, w_mine))
    t_send = swap_cores(after(t_mine, w_theirs))

    def project(pieces):
        count = sum(p.shape[0] for p in pieces)
        return call(
            proj_kernel,
            "project",
            [((count, 2 * W), BF16)] + [((count, W), BF16)] * 3,
            [
                pltpu.VMEM((count, model + W), BF16),
                pltpu.VMEM((model, 4 * W), BF16),
                pltpu.SemaphoreType.DMA((len(pieces),)),
            ],
            [where, *pieces, *w_mine, *w_theirs],
            "s" + len(pieces) * "h" + 4 * "v",
            0,
        )

    gate_query, value, key, marks = project(tok)
    key_theirs, value_theirs = swap_cores(key), swap_cores(value)
    out_pair_theirs = swap_cores(after(out_pair, value))
    (gated,) = call(
        attend_kernel,
        "attend",
        [((NZ, plane, rows, W), BF16)],
        [pltpu.VMEM((events, 2 * W), BF16)]
        + [pltpu.VMEM((events, W), BF16)] * 5
        + [pltpu.SemaphoreType.DMA((6,))],
        [gate_query, key, value, key_theirs, value_theirs, marks],
        6 * "h",
        0,
    )
    hops = [hop(gated[s], flip(0, 0, s)) for s in (1, 2)]
    out_met, out_pair_theirs, last = lax.optimization_barrier((out_met, out_pair_theirs, gated[3]))
    gated = jnp.stack([gated[0], *hops, hop(last, flip(0, 0, 3))])
    neg_pair = pair_up(after(neg, gated))
    neg_far = hop(neg_pair, flip(0, 0, 2))
    out_passed = outer_hop(after(out_met, gated))
    gated = [gated, hop(gated, to_x), hop(gated, to_y)]
    out_passed = after(out_passed, gated)
    out_own = [out_pair, jnp.where(is_inner(z), out_met, out_passed)]
    out_other = [out_pair_theirs, swap_cores(out_own[1])]
    gated += across(gated[1], gated[2])
    (hidden,) = call(
        hidden_kernel,
        "hidden",
        [((plane, rows, NZ * W), BF16)],
        [
            pltpu.VMEM((plane, NZ, plane, rows, W), BF16),
            pltpu.VMEM((plane * rows, model), BF16),
            pltpu.VMEM((plane, rows, NZ * W), BF16),
            pltpu.VMEM((2, half, NZ * W), BF16),
            pltpu.SemaphoreType.DMA((29,)),
        ],
        [where, *gated, *out_own, *out_other, *tok[:4]],
        "s" + 13 * "h",
        2 * plane * rows * model * NZ * W,
    )
    pieces = [hidden, hop(hidden, to_x), hop(hidden, to_y)]
    neg_own = jnp.concatenate([neg_pair, after(neg_far, pieces, t_send)])
    neg_other = swap_cores(neg_own)
    pieces += across(pieces[1], pieces[2])
    h_keep, h_send, positive, mass = call(
        mass_kernel,
        "mass",
        [((rows, half), BF16)] * 2 + [((1, rows), F32), ((plane, 1, rows), F32)],
        [pltpu.VMEM((plane * rows, model), BF16)],
        [where, *pieces, neg_own, neg_other, t_keep, t_send, marks],
        "s" + 10 * "v",
        2 * plane * rows * model * NZ * negs,
    )
    masses = [mass[0]] + [hop(mass[k], flip(*PLANE[k])) for k in range(1, plane)]
    h_theirs = swap_cores(h_send)
    hidden, loss = call(
        final_kernel,
        "final",
        [((2 * rows, half), BF16), ((1, rows), F32)],
        [],
        [where, h_keep, h_theirs, positive, *masses],
        "s" + 7 * "v",
        0,
    )
    return hidden, loss.reshape(-1)


def shards(tokens, w_proj, *rest):
    n_ctx, n_tp = lax.axis_size("ctx"), lax.axis_size("tp")
    heads = w_proj.shape[2] * n_tp // HEAD_DIM
    plan = head_shards if (n_ctx, n_tp, heads) == (CHIPS, 2, CHIPS) else general_shards
    return plan(tokens, w_proj, *rest)


def solution(mesh):
    placed = (
        P("ctx", None),
        P("ctx", None, "tp"),
        P("tp", "ctx"),
        P("ctx"),
        P("ctx", "tp"),
        P(),
        P("ctx", "tp"),
        P(("ctx", "tp")),
    )
    return jax.shard_map(
        shards,
        mesh=mesh,
        in_specs=placed,
        out_specs=(P("ctx", "tp"), P(("ctx", "tp"))),
        check_vma=False,
    )
```

```python
import jax
import jax.numpy as jnp
from jax import lax
from jax.experimental import pallas as pl
from jax.experimental.pallas import tpu as pltpu
from jax.sharding import PartitionSpec as P

HEAD_DIM = 128
VMEM_LIMIT = 14 * 1024 * 1024
BF16 = jnp.bfloat16
F32 = jnp.float32


def attend_piece(q_group, q_pos, k_piece, v_piece, p_piece):
    heads = q_group.shape[1]
    width = q_group.shape[2]
    key_heads = k_piece.reshape(k_piece.shape[0], heads, width)
    value_heads = v_piece.reshape(v_piece.shape[0], heads, width)
    scores = jnp.einsum(
        "thd,khd->htk", q_group, key_heads, preferred_element_type=jnp.float32
    ) * width ** (-0.5)
    visible = p_piece[None, None, :] <= q_pos[None, :, None]
    weight = jnp.where(visible, jax.nn.silu(scores), 0.0).astype(jnp.bfloat16)
    return jnp.einsum("htk,khd->thd", weight, value_heads, preferred_element_type=jnp.float32)


def general_shards(
    tokens, w_proj, w_out, positions, neg_emb, neg_ids, target_emb, target_ids
):
    tok_rows = tokens.shape[0]
    head_cols = w_proj.shape[2]
    local_heads = head_cols // HEAD_DIM
    proj_sum = jnp.einsum(
        "td,dfh->tfh",
        tokens,
        lax.all_gather(w_proj, "ctx", axis=0, tiled=True),
        preferred_element_type=jnp.float32,
    )
    proj = jax.nn.silu(proj_sum).astype(jnp.bfloat16)
    gate = proj[:, 0].reshape(tok_rows, local_heads, HEAD_DIM)
    query = proj[:, 2].reshape(tok_rows, local_heads, HEAD_DIM)
    v_piece = lax.all_gather(proj[:, 1], "ctx", axis=0, tiled=True)
    k_piece = lax.all_gather(proj[:, 3], "ctx", axis=0, tiled=True)
    p_piece = lax.all_gather(positions, "ctx", axis=0, tiled=True)
    attn = attend_piece(query, positions, k_piece, v_piece, p_piece)
    normed = attn * lax.rsqrt(jnp.mean(attn * attn, axis=-1, keepdims=True) + 1e-06)
    gated = (normed * gate.astype(jnp.float32)).astype(jnp.bfloat16).reshape(tok_rows, head_cols)
    out_terms = jnp.dot(
        gated, lax.all_gather(w_out, "ctx", axis=1, tiled=True), preferred_element_type=jnp.float32
    )
    out_share = lax.psum_scatter(out_terms, "tp", scatter_dimension=1, tiled=True)
    feat_cols = out_share.shape[1]
    own_tokens = lax.dynamic_slice_in_dim(tokens, lax.axis_index("tp") * feat_cols, feat_cols, 1)
    hidden = (own_tokens.astype(jnp.float32) + out_share).astype(jnp.bfloat16)
    piece = lax.all_gather(neg_emb, "ctx", axis=0, tiled=True)
    panel_dots = lax.dot_general(
        hidden, piece, (((1,), (1,)), ((), ())), preferred_element_type=jnp.float32
    )
    panel_norms = jnp.sum(jnp.square(piece.astype(jnp.float32)), axis=1)
    hidden_f = hidden.astype(jnp.float32)
    target_f = target_emb.astype(jnp.float32)
    part_hh = jnp.sum(hidden_f * hidden_f, axis=1)
    part_he = jnp.sum(hidden_f * target_f, axis=1)
    part_ee = jnp.sum(target_f * target_f, axis=1)
    dots, hh_sum, he_sum, ee_sum = (
        lax.psum_scatter(panel_dots, "tp", scatter_dimension=0, tiled=True),
        lax.psum_scatter(part_hh, "tp", scatter_dimension=0, tiled=True),
        lax.psum_scatter(part_he, "tp", scatter_dimension=0, tiled=True),
        lax.psum_scatter(part_ee, "tp", scatter_dimension=0, tiled=True),
    )
    neg_sq = lax.psum(panel_norms, "tp")
    pos_logit = he_sum / jnp.sqrt(hh_sum + 1e-06) / jnp.sqrt(ee_sum + 1e-06) / 0.05
    neg_logit = dots / jnp.sqrt(hh_sum + 1e-06)[:, None] / jnp.sqrt(neg_sq + 1e-06)[None, :] / 0.05
    keep_mask = neg_ids[None, :] != target_ids[:, None]
    total_mass = jnp.exp(pos_logit) + jnp.sum(jnp.where(keep_mask, jnp.exp(neg_logit), 0.0), axis=1)
    loss = jnp.log(total_mass) - pos_logit
    return (hidden, loss)


NZ, NY, NX = 4, 2, 2
CHIPS = NZ * NY * NX
PLANE = [(by, bx) for by in range(NY) for bx in range(NX)]
SWAP = [(0, 1), (1, 0)]
W = HEAD_DIM
ACROSS = (((1,), (1,)), ((), ()))


def chip_at(z, y, x):
    return (z * NY + y) * NX + x


def coords(c):
    return c // (NY * NX), (c // NX) % NY, c % NX


def relative_chip(c, by, bx, s):
    z, y, x = coords(c)
    return chip_at(z ^ s, y ^ by, x ^ bx)


def flip(by, bx, s=0):
    return [(c, relative_chip(c, by, bx, s)) for c in range(CHIPS)]


def hop(value, perm):
    return lax.ppermute(value, "ctx", perm)


def swap_cores(value):
    return lax.ppermute(value, "tp", SWAP)


def pick_row(value, at):
    return lax.dynamic_index_in_dim(value, at, 0, keepdims=False)


def after(values, *others):
    return lax.optimization_barrier((values, others))[0]


def pair_up(own):
    return jnp.concatenate([own, hop(own, flip(0, 0, 1))])


def across(value_x, value_y):
    half = value_x.shape[0] // 2
    return [hop(value_x[:half], flip(1, 0)), hop(value_y[half:], flip(0, 1))]


def heads_in_plane(w_proj, y, x, first):
    plane = NY * NX
    heads = w_proj.reshape(-1, 4, 2, plane, W).transpose(3, 2, 0, 1, 4)
    heads = heads.reshape(plane, 2, -1, 4 * W)
    out = []
    for by, bx in PLANE:
        piece = pick_row(heads, (y ^ by) * NX + (x ^ bx))
        if (by, bx) != (0, 0):
            piece = hop(after(piece, first if len(out) < plane - 1 else out[1:]), flip(by, bx))
        out.append(piece)
    return out


def heads_along_z(pieces):
    arrived = []
    for e, piece in enumerate(pieces):
        perm = []
        for src in range(CHIPS):
            sz, sy, sx = coords(src)
            for t in range(2):
                dst = chip_at(2 * t + (e ^ (sz & 1)), sy, sx)
                perm.append((2 * src + t, 2 * dst + (sz >> 1)))
        arrived.append(lax.ppermute(piece, ("ctx", "tp"), perm))
    return arrived


def silu(v):
    return 0.5 * v * (1.0 + jnp.tanh(0.5 * v))


def run_copies(copies):
    for copy in copies:
        copy.start()
    for copy in copies:
        copy.wait()


def mark_kernel(where, tokens, p_hbm, i_hbm, mine, events, positions, ids, sems):
    u = where[3]
    rows, model = events.shape
    own = tokens.at[pl.ds(pl.multiple_of(u * rows, rows), rows), :]
    copies = [(p_hbm, positions), (i_hbm, ids), (own, events)]
    copies = [pltpu.make_async_copy(a, b, sems.at[i]) for i, (a, b) in enumerate(copies)]
    for copy in copies:
        copy.start()
    for copy in copies[:2]:
        copy.wait()
    lane = lax.broadcasted_iota(jnp.int32, (rows, W), 1)
    marks = jnp.zeros((rows, W), F32)
    values = ((positions, u * rows, 7), (positions, (1 - u) * rows, 7), (ids, 0, 8))
    for i, (ref, first, bits) in enumerate(values):
        line = lax.broadcasted_iota(jnp.int32, (rows, ref.shape[1]), 0)
        across = lax.broadcasted_iota(jnp.int32, (rows, ref.shape[1]), 1)
        picked = jnp.where(across == line + first, ref[...], 0)
        column = jnp.sum(picked, axis=1, keepdims=True)
        high = lax.shift_right_logical(column, bits)
        marks = jnp.where(lane == 2 * i, high.astype(F32), marks)
        marks = jnp.where(lane == 2 * i + 1, (column - high * 2**bits).astype(F32), marks)
    mine[:, model:] = marks.astype(BF16)
    copies[2].wait()
    mine[:, :model] = events[...]


def proj_kernel(where, *refs):
    count = len(refs) - 11
    tok, w_own, w_other = refs[:count], refs[count : count + 2], refs[count + 2 : count + 4]
    gate_query, value, key, marks, x_all, w_all, tok_sem = refs[count + 4 :]
    z, y, x, u = (where[i] for i in range(4))
    copies, base = [], 0
    for i, ref in enumerate(tok):
        rows = pl.ds(base, ref.shape[0])
        copies.append(pltpu.make_async_copy(ref, x_all.at[rows, :], tok_sem.at[i]))
        base += ref.shape[0]
    for copy in copies:
        copy.start()
    for at, srcs in ((u, w_own), (1 - u, w_other)):
        for e, src in enumerate(srcs):
            size = src.shape[0] // len(PLANE)
            for j, (by, bx) in enumerate(PLANE):
                start = chip_at(2 * at + (e ^ (z & 1)), y ^ by, x ^ bx) * size
                part = src[j * size : (j + 1) * size, :]
                w_all[pl.ds(pl.multiple_of(start, size), size), :] = part
    for copy in copies:
        copy.wait()
    model = w_all.shape[0]
    total = jnp.dot(x_all[:, :model], w_all[...], preferred_element_type=F32)
    proj = silu(total).astype(BF16)
    gate_query[:, :W] = proj[:, :W]
    value[...] = proj[:, W : 2 * W]
    gate_query[:, W:] = proj[:, 2 * W : 3 * W]
    key[...] = proj[:, 3 * W :]
    marks[...] = x_all[:, model:]


def pick_columns(*weights):
    lane = lax.broadcasted_iota(jnp.int32, (8, W), 1)
    line = lax.broadcasted_iota(jnp.int32, (8, W), 0)
    pick = jnp.zeros((8, W), F32)
    for i, row in enumerate(weights):
        for at, weight in row.items():
            pick = jnp.where((line == i) & (lane == at), weight, pick)
    return pick.astype(BF16)


def attend_kernel(*refs):
    sources, gated, copied, sems = refs[:6], refs[6], refs[7:13], refs[13]
    run_copies(
        [
            pltpu.make_async_copy(src, dst, sems.at[i])
            for i, (src, dst) in enumerate(zip(sources, copied))
        ]
    )
    gate_query, key, value, key_theirs, value_theirs, marks = copied
    pick = pick_columns({0: 128.0, 1: 1.0}, {2: 128.0, 3: 1.0})
    piece = gated.shape[2]
    tile = NZ * piece
    key_pos = lax.dot_general(pick, marks[...], ACROSS, preferred_element_type=F32)
    for k in range(len(PLANE)):
        span = pl.ds(k * tile, tile)
        query = gate_query[span, W:]
        q_pos = lax.dot_general(marks[span, :], pick, ACROSS, preferred_element_type=F32)[:, :1]
        attn = jnp.zeros((tile, W), F32)
        for side, (keys, values) in enumerate(((key, value), (key_theirs, value_theirs))):
            scores = lax.dot_general(
                query, keys[...], ACROSS, preferred_element_type=F32
            ) * W ** (-0.5)
            visible = key_pos[side : side + 1] <= q_pos
            weight = jnp.where(visible, silu(scores), 0.0).astype(BF16)
            attn += jnp.dot(weight, values[...], preferred_element_type=F32)
        normed = attn * lax.rsqrt(jnp.mean(attn * attn, axis=-1, keepdims=True) + 1e-06)
        out = (normed * gate_query[span, :W].astype(F32)).astype(BF16)
        for s in range(NZ):
            gated[s, k] = out[s * piece : (s + 1) * piece]


def hidden_kernel(where, *refs):
    n = len(PLANE)
    gated, w_own, w_other, tok = refs[:5], refs[5:7], refs[7:9], refs[9:13]
    hidden, g_raw, g_all, t_all, w_all, sems = refs[13:]
    z, y, x, u = (where[i] for i in range(4))
    c = chip_at(z, y, x)
    rows = hidden.shape[1]
    half = w_all.shape[1]
    copies = [(src, g_raw.at[k]) for k, src in enumerate(gated[:3])]
    copies += [(src, g_raw.at[3, pl.ds(2 * i, 2)]) for i, src in enumerate(gated[3:])]
    for s in range(NZ):
        cols = pl.ds(s * W, W)
        for side, src in enumerate((w_own, w_other)):
            copies.append((src[s // 2].at[s % 2], w_all.at[side, :, cols]))
        block = relative_chip(c, 0, 0, s)
        from_cols = pl.ds(pl.multiple_of(block * W, W), W)
        for k in range(n):
            copies.append((tok[k].at[pl.ds(0, rows), from_cols], t_all.at[k, :, cols]))
    copies = [pltpu.make_async_copy(src, dst, sems.at[i]) for i, (src, dst) in enumerate(copies)]
    for copy in copies:
        copy.start()
    for copy in copies[:5]:
        copy.wait()
    for k, (by, bx) in enumerate(PLANE):
        for s in range(NZ):
            head = relative_chip(c, by, bx, s)
            cols = pl.ds(pl.multiple_of(head * W, W), W)
            for j in range(n):
                block = j ^ k
                g_all[block * rows : (block + 1) * rows, cols] = g_raw[k, s, j]
    for copy in copies[5:]:
        copy.wait()
    total = 0.0
    for side, at in enumerate((u, 1 - u)):
        part = g_all[:, pl.ds(pl.multiple_of(at * half, half), half)]
        total += jnp.dot(part, w_all[side], preferred_element_type=F32)
    for k in range(n):
        for s in range(NZ):
            term = total[k * rows : (k + 1) * rows, s * W : (s + 1) * W]
            cols = pl.ds(pl.multiple_of((z ^ s) * W, W), W)
            hidden[k, :, cols] = (t_all[k, :, s * W : (s + 1) * W].astype(F32) + term).astype(BF16)


def as_line(column):
    size = column.shape[0]
    line = lax.broadcasted_iota(jnp.int32, (size, size), 0)
    lane = lax.broadcasted_iota(jnp.int32, (size, size), 1)
    return jnp.sum(jnp.where(line == lane, column, 0.0), axis=0, keepdims=True)


def mass_kernel(where, *refs):
    n = len(PLANE)
    pieces, (n_own, n_other, t_keep, t_send, marks) = refs[:5], refs[5:10]
    keep, send, positive, mass, h_all = refs[10:]
    y, x, u = (where[i] for i in range(1, 4))
    rows, half = keep.shape
    for k, (by, bx) in enumerate(PLANE):
        for at in range(NZ):
            block = chip_at(at, y ^ by, x ^ bx)
            cols = pl.ds(pl.multiple_of(block * W, W), W)
            for j in range(n):
                row = (j ^ k) * rows
                ref, i = (pieces[k], j) if k < n - 1 else (pieces[k + j // 2], j % 2)
                h_all[row : row + rows, cols] = ref[i, :, at * W : (at + 1) * W]
    mine = pl.ds(pl.multiple_of(u * half, half), half)
    theirs = pl.ds(pl.multiple_of((1 - u) * half, half), half)
    keep[...] = h_all[:rows, mine]
    send[...] = h_all[:rows, theirs]
    hh, dots, lines = 0.0, 0.0, []
    pick = pick_columns({0: 1.0, 1: 1.0, 2: 1.0}, {3: 256.0, 4: 1.0})
    for part, neg in ((mine, n_own), (theirs, n_other)):
        h_part = h_all[:, part]
        h_f = h_part.astype(F32)
        hh += jnp.sum(h_f * h_f, axis=1, keepdims=True)
        dots += lax.dot_general(h_part, neg[:, :half], ACROSS, preferred_element_type=F32)
        lines.append(lax.dot_general(pick, neg[:, half:], ACROSS, preferred_element_type=F32))
    h_scale = lax.rsqrt(hh + 1e-06) * 20.0
    he = ee = 0.0
    for h_ref, ref in ((keep, t_keep), (send, t_send)):
        h_f, t_f = h_ref[...].astype(F32), ref[...].astype(F32)
        he += jnp.sum(h_f * t_f, axis=1, keepdims=True)
        ee += jnp.sum(t_f * t_f, axis=1, keepdims=True)
    positive[...] = as_line(he * lax.rsqrt(ee + 1e-06) * h_scale[:rows])
    first = [marks[k * NZ * rows : (k * NZ + 1) * rows] for k in range(n)]
    pick = pick_columns({4: 256.0, 5: 1.0})
    t_ids = lax.dot_general(
        jnp.concatenate(first), pick, ACROSS, preferred_element_type=F32
    )[:, :1]
    neg_logit = dots * h_scale * lax.rsqrt(lines[0][0:1] + lines[1][0:1] + 1e-06)
    kept = jnp.where(lines[0][1:2] != t_ids, jnp.exp(neg_logit), 0.0)
    total = jnp.sum(kept, axis=1, keepdims=True)
    for k in range(n):
        mass[k] = as_line(total[k * rows : (k + 1) * rows])


def final_kernel(where, keep, theirs, positive, *refs):
    masses, (hidden, loss) = refs[:-2], refs[-2:]
    u, rows = where[3], keep.shape[0]
    hidden[pl.ds(pl.multiple_of(u * rows, rows), rows), :] = keep[...]
    hidden[pl.ds(pl.multiple_of((1 - u) * rows, rows), rows), :] = theirs[...]
    total = jnp.exp(positive[...])
    for mass in masses:
        total += mass[...]
    loss[...] = jnp.log(total) - positive[...]


def call(kernel, name, outs, scratch, args, places, flops):
    space = {"s": pltpu.SMEM, "v": pltpu.VMEM, "h": pl.ANY, "o": pltpu.HBM}
    moved = sum(a.size * a.dtype.itemsize for a in args)
    return pl.pallas_call(
        kernel,
        out_shape=[jax.ShapeDtypeStruct(shape, dtype) for shape, dtype in outs],
        in_specs=[pl.BlockSpec(memory_space=space[p]) for p in places],
        out_specs=[pl.BlockSpec(memory_space=pltpu.VMEM)] * len(outs),
        scratch_shapes=scratch,
        compiler_params=pltpu.CompilerParams(vmem_limit_bytes=VMEM_LIMIT),
        cost_estimate=pl.CostEstimate(flops=flops, bytes_accessed=moved, transcendentals=0),
        name=name,
    )(*args)


def whole_parts(value, base):
    return [(value // base).astype(BF16), (value % base).astype(BF16)]


def float_parts(value):
    parts = []
    for _ in range(3):
        parts.append(lax.reduce_precision(value, 8, 7))
        value = value - parts[-1]
    return [part.astype(BF16) for part in parts]


def with_marks(rows, marks):
    marks = jnp.stack(marks, 1)
    marks = jnp.pad(marks, ((0, 0), (0, W - marks.shape[1])))
    return jnp.concatenate([rows, marks], 1)


def head_shards(
    tokens, w_proj, w_out, positions, neg_emb, neg_ids, target_emb, target_ids
):
    c, u = lax.axis_index("ctx"), lax.axis_index("tp")
    z, y, x = coords(c)
    where = jnp.stack([z, y, x, u]).astype(jnp.int32)
    model = tokens.shape[1]
    rows = tokens.shape[0] // 2
    events = rows * CHIPS
    half = model // 2
    negs = neg_emb.shape[0]
    plane = len(PLANE)

    (mine,) = call(
        mark_kernel,
        "mark",
        [((rows, model + W), BF16)],
        [
            pltpu.VMEM((rows, model), BF16),
            pltpu.VMEM((1, 2 * rows), jnp.int32),
            pltpu.VMEM((1, rows), jnp.int32),
            pltpu.SemaphoreType.DMA((3,)),
        ],
        [where, tokens, positions.reshape(1, 2 * rows), target_ids.reshape(1, rows)],
        "sooo",
        0,
    )
    line = [mine] + [hop(mine, flip(0, 0, s)) for s in range(1, NZ)]

    to_x, to_y = flip(0, 1), flip(1, 0)
    w_rows = heads_in_plane(w_proj, y, x, mine)
    w_pieces = [
        jnp.concatenate([pick_row(w, e ^ (z & 1)) for w in w_rows]).reshape(-1, 4 * W)
        for e in range(2)
    ]

    own_ids = lax.dynamic_slice_in_dim(neg_ids, c * negs, negs, 0)
    norms = jnp.sum(jnp.square(neg_emb.astype(F32)), axis=1)
    neg = with_marks(neg_emb, float_parts(norms) + whole_parts(own_ids, 256))

    out_pair = pair_up(after(w_out[None], w_rows[1:3]))
    t_rows = target_emb.reshape(2, rows, -1)
    t_keep, t_mine = pick_row(t_rows, u), pick_row(t_rows, 1 - u)
    early = (w_pieces, neg, out_pair, t_keep, t_mine, line)
    w_pieces, neg, out_pair, t_keep, t_mine, line = lax.optimization_barrier(early)
    near = jnp.concatenate(line)
    near_x, near_y = hop(near, to_x), hop(near, to_y)
    tok = [near, near_x, near_y, *across(near_x, near_y)]
    w_mine = heads_along_z(w_pieces)
    neg_pair = pair_up(neg)
    w_theirs = [swap_cores(w) for w in after(w_mine, neg_pair)]
    out_own = [out_pair, hop(after(out_pair, w_mine), flip(0, 0, 2))]
    t_send = swap_cores(after(t_mine, w_theirs))

    def project(pieces):
        count = sum(p.shape[0] for p in pieces)
        return call(
            proj_kernel,
            "project",
            [((count, 2 * W), BF16)] + [((count, W), BF16)] * 3,
            [
                pltpu.VMEM((count, model + W), BF16),
                pltpu.VMEM((model, 4 * W), BF16),
                pltpu.SemaphoreType.DMA((len(pieces),)),
            ],
            [where, *pieces, *w_mine, *w_theirs],
            "s" + len(pieces) * "h" + 4 * "v",
            0,
        )

    gate_query, value, key, marks = project(tok)
    key_theirs, value_theirs = swap_cores(key), swap_cores(value)
    out_pair_theirs = swap_cores(after(out_pair, value))
    (gated,) = call(
        attend_kernel,
        "attend",
        [((NZ, plane, rows, W), BF16)],
        [pltpu.VMEM((events, 2 * W), BF16)]
        + [pltpu.VMEM((events, W), BF16)] * 5
        + [pltpu.SemaphoreType.DMA((6,))],
        [gate_query, key, value, key_theirs, value_theirs, marks],
        6 * "h",
        0,
    )
    hops = [hop(gated[s], flip(0, 0, s)) for s in (1, 2)]
    out_own, out_pair_theirs, last = lax.optimization_barrier((out_own, out_pair_theirs, gated[3]))
    gated = jnp.stack([gated[0], *hops, hop(last, flip(0, 0, 3))])
    neg_far = hop(after(neg_pair, gated), flip(0, 0, 2))
    out_other = [out_pair_theirs, swap_cores(after(out_own[1], gated))]
    gated = [gated, hop(gated, to_x), hop(gated, to_y)]
    gated += across(gated[1], gated[2])
    (hidden,) = call(
        hidden_kernel,
        "hidden",
        [((plane, rows, NZ * W), BF16)],
        [
            pltpu.VMEM((plane, NZ, plane, rows, W), BF16),
            pltpu.VMEM((plane * rows, model), BF16),
            pltpu.VMEM((plane, rows, NZ * W), BF16),
            pltpu.VMEM((2, half, NZ * W), BF16),
            pltpu.SemaphoreType.DMA((29,)),
        ],
        [where, *gated, *out_own, *out_other, *tok[:4]],
        "s" + 13 * "h",
        2 * plane * rows * model * NZ * W,
    )
    pieces = [hidden, hop(hidden, to_x), hop(hidden, to_y)]
    neg_own = jnp.concatenate([neg_pair, after(neg_far, pieces, t_send)])
    neg_other = swap_cores(neg_own)
    pieces += across(pieces[1], pieces[2])
    h_keep, h_send, positive, mass = call(
        mass_kernel,
        "mass",
        [((rows, half), BF16)] * 2 + [((1, rows), F32), ((plane, 1, rows), F32)],
        [pltpu.VMEM((plane * rows, model), BF16)],
        [where, *pieces, neg_own, neg_other, t_keep, t_send, marks],
        "s" + 10 * "v",
        2 * plane * rows * model * NZ * negs,
    )
    masses = [mass[0]] + [hop(mass[k], flip(*PLANE[k])) for k in range(1, plane)]
    h_theirs = swap_cores(h_send)
    hidden, loss = call(
        final_kernel,
        "final",
        [((2 * rows, half), BF16), ((1, rows), F32)],
        [],
        [where, h_keep, h_theirs, positive, *masses],
        "s" + 7 * "v",
        0,
    )
    return hidden, loss.reshape(-1)


def shards(tokens, w_proj, *rest):
    n_ctx, n_tp = lax.axis_size("ctx"), lax.axis_size("tp")
    heads = w_proj.shape[2] * n_tp // HEAD_DIM
    plan = head_shards if (n_ctx, n_tp, heads) == (CHIPS, 2, CHIPS) else general_shards
    return plan(tokens, w_proj, *rest)


def solution(mesh):
    placed = (
        P("ctx", None),
        P("ctx", None, "tp"),
        P("tp", "ctx"),
        P("ctx"),
        P("ctx", "tp"),
        P(),
        P("ctx", "tp"),
        P(("ctx", "tp")),
    )
    return jax.shard_map(
        shards,
        mesh=mesh,
        in_specs=placed,
        out_specs=(P("ctx", "tp"), P(("ctx", "tp"))),
        check_vma=False,
    )
```
